32 devices in a mesh: ctx: 8 (over z, y), ws: 4 (over x, core).
Axes of the slice: x: 2, y: 2, z: 4, core: 2. Of those that a mesh axis runs over, the one named last changes fastest.
Arguments:
- inputs: bfloat16 [2, 4096, 1152], P(None, ('ctx', 'ws')), may hold values from -6 to 6
- attn_gain: bfloat16 [1152], P(('ctx', 'ws')), may hold values from 0.25 to 1.75
- query_weight: bfloat16 [1152, 1152], P(('ctx', 'ws')), may hold values from -0.1875 to 0.1875
- key_matrix: bfloat16 [1152, 384], P(('ctx', 'ws')), may hold values from -0.1875 to 0.1875
- value_matrix: bfloat16 [1152, 384], P(('ctx', 'ws')), may hold values from -0.1875 to 0.1875
- out_weight: bfloat16 [1152, 1152], P(('ctx', 'ws')), may hold values from -3.5 to 3.5
- ffn_gain: bfloat16 [1152], P(('ctx', 'ws')), may hold values from 0.25 to 1.75
- gate_weight: bfloat16 [1152, 3072], P(('ctx', 'ws')), may hold values from -0.1875 to 0.1875
- up_weight: bfloat16 [1152, 3072], P(('ctx', 'ws')), may hold values from -0.1875 to 0.1875
- down_weight: bfloat16 [3072, 1152], P(('ctx', 'ws')), may hold values from -0.109375 to 0.109375
- cotangent: bfloat16 [2, 4096, 1152], P(None, ('ctx', 'ws')), may hold values from -6 to 6
Outputs:
- layer_out: bfloat16 [2, 4096, 1152], P(None, ('ctx', 'ws'))
- input_grad: bfloat16 [2, 4096, 1152], P(None, ('ctx', 'ws'))
- attn_gain_grad: float32 [1152], P(('ctx', 'ws'))
- query_grad: float32 [1152, 1152], P(('ctx', 'ws'))
- key_grad: float32 [1152, 384], P(('ctx', 'ws'))
- value_grad: float32 [1152, 384], P(('ctx', 'ws'))
- out_grad: float32 [1152, 1152], P(('ctx', 'ws'))
- ffn_gain_grad: float32 [1152], P(('ctx', 'ws'))
- gate_grad: float32 [1152, 3072], P(('ctx', 'ws'))
- up_grad: float32 [1152, 3072], P(('ctx', 'ws'))
- down_grad: float32 [3072, 1152], P(('ctx', 'ws'))
The draws below stay inside these ranges and needn't reach their ends.
All inputs are finite; a program needn't handle non-finite values.
Results may differ from the reference program's by a relative error of at most 0.02.
Values may be sent and summed in bfloat16 or wider, within the bound.
A program may use at most 256 MiB of HBM per device.

```python
import math
import jax
import jax.numpy as jnp
from jax import lax

MODEL_WIDTH = 1152
QUERY_HEADS = 18
KEY_VALUE_HEADS = 6
HEAD_SIZE = 64
FF = 3072
TOK_DEV = 128
MB = 2
SEQ = 4096
N_CTX = 8
N_WS = 4


def levels(key, shape, shards, least, largest):
    def one(axis_at, parts):
        draws = jax.random.uniform(jax.random.fold_in(jax.random.fold_in(key, 6), axis_at), (parts,), jnp.float32, least / len(shards), largest / len(shards))
        return jnp.repeat(jnp.exp(draws), shape[axis_at] // parts).reshape((-1,) + (1,) * (len(shape) - axis_at - 1))

    gain = one(*shards[0])
    for cut in shards[1:]:
        gain = gain * one(*cut)
    return gain


def gaussian(rng, extent, scale, bound, cuts=(), kind=jnp.bfloat16):
    result = scale * jax.random.normal(rng, extent, jnp.float32)
    if cuts:
        result = result * levels(rng, extent, cuts, -0.22, 0.18)
    return jnp.clip(result, -bound, bound).astype(kind)


def setup_inputs(seed: int = 0) -> dict:
    streams_of = jax.random.split(jax.random.key(seed), 12)
    inputs = gaussian(streams_of[0], (MB, SEQ, MODEL_WIDTH), 1.0, 6.0, ((1, 32),))
    attn_gain = jnp.clip(1.0 + 0.15 * jax.random.normal(streams_of[1], (MODEL_WIDTH,), jnp.float32), 0.25, 1.75).astype(jnp.bfloat16)
    query_weight = gaussian(streams_of[2], (MODEL_WIDTH, QUERY_HEADS * HEAD_SIZE), MODEL_WIDTH ** -0.5, 0.1875, ((0, 32),))
    key_matrix = gaussian(streams_of[3], (MODEL_WIDTH, KEY_VALUE_HEADS * HEAD_SIZE), MODEL_WIDTH ** -0.5, 0.1875, ((0, 32),))
    value_matrix = gaussian(streams_of[4], (MODEL_WIDTH, KEY_VALUE_HEADS * HEAD_SIZE), MODEL_WIDTH ** -0.5, 0.1875, ((0, 32),))
    out_weight = gaussian(streams_of[5], (QUERY_HEADS * HEAD_SIZE, MODEL_WIDTH), (max(1.0, 10.0 * QUERY_HEADS * HEAD_SIZE / SEQ)) ** -0.5, 3.5, ((0, 32),))
    ffn_gain = jnp.clip(1.0 + 0.15 * jax.random.normal(streams_of[6], (MODEL_WIDTH,), jnp.float32), 0.25, 1.75).astype(jnp.bfloat16)
    gate_weight = gaussian(streams_of[7], (MODEL_WIDTH, FF), MODEL_WIDTH ** -0.5, 0.1875, ((0, 32),))
    up_weight = gaussian(streams_of[8], (MODEL_WIDTH, FF), MODEL_WIDTH ** -0.5, 0.1875, ((0, 32),))
    down_weight = gaussian(streams_of[9], (FF, MODEL_WIDTH), FF ** -0.5, 0.109375, ((0, 32),))
    cotangent = gaussian(streams_of[10], (MB, SEQ, MODEL_WIDTH), 1.0, 6.0, ((1, 32),))
    return {"inputs": inputs, "attn_gain": attn_gain, "query_weight": query_weight, "key_matrix": key_matrix, "value_matrix": value_matrix, "out_weight": out_weight, "ffn_gain": ffn_gain, "gate_weight": gate_weight, "up_weight": up_weight, "down_weight": down_weight, "cotangent": cotangent}


@jax.custom_vjp
def reduced_input(v):
    return lax.optimization_barrier(v.astype(jnp.bfloat16)).astype(jnp.float32)

@jax.custom_vjp
def reduced_backward(v):
    return v

def low_keep(v):
    return (reduced_input(v), None)

def low_pass(kept, grad):
    return (grad,)

def back_keep(v):
    return (v, None)

def back_low(kept, grad):
    return (reduced_input(grad),)
reduced_input.defvjp(low_keep, low_pass)
reduced_backward.defvjp(back_keep, back_low)
EPSILON = 1e-05
MASKED_SCORE = -1e+30

def score_product(left, right):
    return jnp.dot(left, right, preferred_element_type=jnp.float32, precision=lax.Precision.HIGHEST)

def positions():
    rows_per_half = TOK_DEV // 2
    row_index = jnp.arange(SEQ, dtype=jnp.int32)
    group_index = row_index // TOK_DEV
    ctx_index = group_index // N_WS
    member_index = group_index % N_WS
    local_index = row_index % TOK_DEV
    span_index = jnp.where(local_index < rows_per_half, ctx_index, 2 * N_CTX - 1 - ctx_index)
    return (span_index * (N_WS * rows_per_half) + member_index * rows_per_half + local_index % rows_per_half).astype(jnp.int32)

def rotary_embedding(heads, token_positions):
    quarter = HEAD_SIZE // 2
    frequency = 10000.0 ** (-2.0 * jnp.arange(quarter, dtype=jnp.float32) / HEAD_SIZE)
    angles = token_positions.astype(jnp.float32)[:, None] * frequency[None, :]
    cosine_table = jnp.cos(angles)[:, None, :]
    sine_table = jnp.sin(angles)[:, None, :]
    first_half = heads[..., :quarter]
    second_half = heads[..., quarter:]
    return jnp.concatenate([first_half * cosine_table - second_half * sine_table, second_half * cosine_table + first_half * sine_table], axis=-1)

def root_norm(layer_rows, gain_vector):
    return layer_rows * lax.rsqrt(lax.optimization_barrier(jnp.mean(layer_rows * layer_rows, axis=-1, keepdims=True)) + EPSILON) * gain_vector

def block_forward(layer_rows, params, token_positions):
    attn_gain, query_weight, key_matrix, value_matrix, out_weight, ffn_gain, gate_weight, up_weight, down_weight = params
    count_of_rows = layer_rows.shape[0]
    queries_per_group = QUERY_HEADS // KEY_VALUE_HEADS
    normalized_rows = reduced_input(root_norm(layer_rows, attn_gain))
    query_rows = reduced_input(rotary_embedding(reduced_backward(score_product(normalized_rows, query_weight)).reshape(count_of_rows, QUERY_HEADS, HEAD_SIZE), token_positions))
    rows_of_keys = reduced_input(rotary_embedding(reduced_backward(score_product(normalized_rows, key_matrix)).reshape(count_of_rows, KEY_VALUE_HEADS, HEAD_SIZE), token_positions))
    rows_of_values = reduced_input(reduced_backward(score_product(normalized_rows, value_matrix))).reshape(count_of_rows, KEY_VALUE_HEADS, HEAD_SIZE)
    rows_per_block = math.gcd(count_of_rows, 512)
    grouped_heads = query_rows.reshape(count_of_rows // rows_per_block, rows_per_block, KEY_VALUE_HEADS, queries_per_group, HEAD_SIZE)
    block_places = token_positions.reshape(count_of_rows // rows_per_block, rows_per_block)

    def attend_block(block_pair):
        query_block, query_places = block_pair
        scores = reduced_backward(jnp.einsum('bgjd,kgd->gbjk', query_block, rows_of_keys, precision=lax.Precision.HIGHEST) * HEAD_SIZE ** (-0.5))
        causal_visible = query_places[:, None] >= token_positions[None, :]
        scores = jnp.where(causal_visible[None, :, None, :], scores, MASKED_SCORE)
        attn_probs = reduced_input(jax.nn.softmax(scores, axis=-1))
        return jnp.einsum('gbjk,kgd->bgjd', attn_probs, rows_of_values, precision=lax.Precision.HIGHEST)
    attended = lax.map(jax.checkpoint(attend_block), (grouped_heads, block_places))
    attended = reduced_input(reduced_backward(attended.reshape(count_of_rows, QUERY_HEADS * HEAD_SIZE)))
    middle = layer_rows + reduced_backward(score_product(attended, out_weight))
    hidden = reduced_input(root_norm(middle, ffn_gain))
    gate_rows = reduced_backward(score_product(hidden, gate_weight))
    up_rows = reduced_backward(score_product(hidden, up_weight))
    activated = reduced_input(jax.nn.silu(gate_rows) * up_rows)
    return middle + reduced_backward(score_product(activated, down_weight))

def reference(inputs, attn_gain, query_weight, key_matrix, value_matrix, out_weight, ffn_gain, gate_weight, up_weight, down_weight, cotangent):
    params = (attn_gain.astype(jnp.float32), query_weight.astype(jnp.float32), key_matrix.astype(jnp.float32), value_matrix.astype(jnp.float32), out_weight.astype(jnp.float32), ffn_gain.astype(jnp.float32), gate_weight.astype(jnp.float32), up_weight.astype(jnp.float32), down_weight.astype(jnp.float32))
    token_positions = positions()

    def forward(sequences, weights_all):
        return lax.map(lambda sequence: block_forward(sequence, weights_all, token_positions), sequences)
    layer_out, pullback = jax.vjp(forward, inputs.astype(jnp.float32), params)
    input_grad, weight_grads = pullback(cotangent.astype(jnp.float32))
    return (layer_out.astype(jnp.bfloat16), input_grad.astype(jnp.bfloat16), weight_grads[0], weight_grads[1], weight_grads[2], weight_grads[3], weight_grads[4], weight_grads[5], weight_grads[6], weight_grads[7], weight_grads[8])
```

```python
import jax
import jax.numpy as jnp
from jax import lax
from jax.experimental import pallas as pl
from jax.experimental.pallas import tpu as pltpu
from jax.sharding import PartitionSpec as P
import functools

QUERY_HEADS = 18
KEY_VALUE_HEADS = 6
HEAD_SIZE = 64


EPSILON = 1e-05
MASKED_SCORE = -1e30


def shifted(block, axis, distance):
    devices = range(lax.axis_size(axis))
    route = [((i - distance) % len(devices), i) for i in devices]
    return lax.ppermute(block, axis, route)


def as_sent(x):

    def short(part):
        return part.astype(jnp.bfloat16) if part.dtype == jnp.float32 else part

    return jax.tree.map(short, x)


def matrix_multiply(left, right):
    return jnp.dot(left, right, preferred_element_type=jnp.float32)


def outer_sum(left, right):
    return jnp.einsum("ri,rj->ij", left, right, preferred_element_type=jnp.float32)


def back_product(gradient, weight):
    return jnp.einsum("rj,ij->ri", gradient, weight, preferred_element_type=jnp.float32)


def normalize(layer_rows, gain_vector):
    inverse = lax.rsqrt(jnp.mean(layer_rows * layer_rows, axis=-1, keepdims=True) + EPSILON)
    return (layer_rows * inverse * gain_vector, inverse)


def normalize_back(layer_rows, inverse, gain_vector, gradient):
    weighted = gradient * gain_vector
    inner_mean = jnp.mean(weighted * layer_rows, axis=-1, keepdims=True)
    row_grad = inverse * weighted - layer_rows * (inverse * inverse * inverse) * inner_mean
    gain_grad = jnp.sum(gradient * layer_rows * inverse, axis=0)
    return (row_grad, gain_grad)


def rotary_tables(token_positions):
    quarter = HEAD_SIZE // 2
    frequency = 10000.0 ** (-2.0 * jnp.arange(quarter, dtype=jnp.float32) / HEAD_SIZE)
    angles = token_positions.astype(jnp.float32)[:, None] * frequency[None, :]
    return (jnp.cos(angles)[:, None, :], jnp.sin(angles)[:, None, :])


def rotate(heads, cosine_table, sine_table):
    quarter = HEAD_SIZE // 2
    first_half = heads[..., :quarter]
    second_half = heads[..., quarter:]
    return jnp.concatenate(
        [
            first_half * cosine_table - second_half * sine_table,
            second_half * cosine_table + first_half * sine_table,
        ],
        axis=-1,
    )


def rotate_back(heads, cosine_table, sine_table):
    quarter = HEAD_SIZE // 2
    first_half = heads[..., :quarter]
    second_half = heads[..., quarter:]
    return jnp.concatenate(
        [
            first_half * cosine_table + second_half * sine_table,
            second_half * cosine_table - first_half * sine_table,
        ],
        axis=-1,
    )


def query_places(own_ctx, own_member, count_of_rows, ctx_count, device_count):
    rows_per_half = count_of_rows // 2
    local_index = jnp.arange(count_of_rows, dtype=jnp.int32)
    span_index = jnp.where(local_index < rows_per_half, own_ctx, 2 * ctx_count - 1 - own_ctx)
    return (
        span_index * (device_count * rows_per_half)
        + own_member * rows_per_half
        + local_index % rows_per_half
    )


def block_places(source_ctx, count_of_rows, ctx_count, device_count):
    rows_per_half = count_of_rows // 2
    member_index = jnp.arange(device_count, dtype=jnp.int32)[:, None, None]
    half_index = jnp.arange(2, dtype=jnp.int32)[None, :, None]
    inner_index = jnp.arange(rows_per_half, dtype=jnp.int32)[None, None, :]
    span_index = jnp.where(half_index == 0, source_ctx, 2 * ctx_count - 1 - source_ctx)
    return (
        span_index * (device_count * rows_per_half) + member_index * rows_per_half + inner_index
    ).reshape(-1)


def split_block(block_of_keys):
    hidden_width = KEY_VALUE_HEADS * HEAD_SIZE
    device_count, _, rows_per_half, _ = block_of_keys.shape
    rows_of_keys = block_of_keys[..., :hidden_width].reshape(
        device_count, 2, rows_per_half, KEY_VALUE_HEADS, HEAD_SIZE
    )
    rows_of_values = block_of_keys[..., hidden_width:].reshape(
        device_count, 2, rows_per_half, KEY_VALUE_HEADS, HEAD_SIZE
    )
    return (rows_of_keys, rows_of_values)


def attend(query_rows, rows_of_keys, rows_of_values, causal_visible):
    scores = jnp.einsum(
        "rgjd,kgd->grjk", query_rows, rows_of_keys, preferred_element_type=jnp.float32
    ) * HEAD_SIZE ** (-0.5)
    if causal_visible is not None:
        scores = jnp.where(causal_visible[None, :, None, :], scores, MASKED_SCORE)
    row_max = jnp.max(scores, axis=-1)
    exponentials = jnp.exp(scores - row_max[..., None])
    row_total = jnp.sum(exponentials, axis=-1)
    mixture = jnp.einsum(
        "grjk,kgd->rgjd",
        exponentials.astype(jnp.bfloat16),
        rows_of_values,
        preferred_element_type=jnp.float32,
    )
    return (jnp.transpose(row_max, (1, 0, 2)), jnp.transpose(row_total, (1, 0, 2)), mixture)


def empty_part(count_of_rows):
    queries_per_group = QUERY_HEADS // KEY_VALUE_HEADS
    return (
        jnp.full((count_of_rows, KEY_VALUE_HEADS, queries_per_group), MASKED_SCORE, jnp.float32),
        jnp.zeros((count_of_rows, KEY_VALUE_HEADS, queries_per_group), jnp.float32),
        jnp.zeros((count_of_rows, KEY_VALUE_HEADS, queries_per_group, HEAD_SIZE), jnp.float32),
    )


def combine(carried, incoming):
    carried_max, carried_total, carried_mix = carried
    incoming_max, incoming_total, incoming_mix = incoming
    new_max = jnp.maximum(carried_max, incoming_max)
    carried_scale = jnp.exp(carried_max - new_max)
    incoming_scale = jnp.exp(incoming_max - new_max)
    return (
        new_max,
        carried_total * carried_scale + incoming_total * incoming_scale,
        carried_mix * carried_scale[..., None] + incoming_mix * incoming_scale[..., None],
    )


def forward_block(carried, block_of_keys, source_ctx, own_ctx, query_rows, own_places, ctx_count):
    rows_of_keys, rows_of_values = split_block(block_of_keys)
    device_count, _, rows_per_half, _ = block_of_keys.shape

    def forward_earlier():
        return attend(
            query_rows,
            rows_of_keys[:, 0].reshape(-1, KEY_VALUE_HEADS, HEAD_SIZE),
            rows_of_values[:, 0].reshape(-1, KEY_VALUE_HEADS, HEAD_SIZE),
            None,
        )

    def forward_later():
        late_part = attend(
            query_rows[rows_per_half:],
            rows_of_keys.reshape(-1, KEY_VALUE_HEADS, HEAD_SIZE),
            rows_of_values.reshape(-1, KEY_VALUE_HEADS, HEAD_SIZE),
            None,
        )
        early_part = empty_part(rows_per_half)
        return tuple(
            (
                jnp.concatenate([early_piece, late_piece], axis=0)
                for early_piece, late_piece in zip(early_part, late_part)
            )
        )

    def forward_diagonal():
        key_places = block_places(source_ctx, 2 * rows_per_half, ctx_count, device_count)
        causal_visible = own_places[:, None] >= key_places[None, :]
        return attend(
            query_rows,
            rows_of_keys.reshape(-1, KEY_VALUE_HEADS, HEAD_SIZE),
            rows_of_values.reshape(-1, KEY_VALUE_HEADS, HEAD_SIZE),
            causal_visible,
        )

    branch_index = jnp.where(source_ctx == own_ctx, 2, jnp.where(source_ctx > own_ctx, 1, 0))
    return combine(
        carried, lax.switch(branch_index, [forward_earlier, forward_later, forward_diagonal])
    )


def attend_back(
    query_rows, attended_grad, log_total, delta_rows, rows_of_keys, rows_of_values, causal_visible
):
    scores = jnp.einsum(
        "rgjd,kgd->grjk", query_rows, rows_of_keys, preferred_element_type=jnp.float32
    ) * HEAD_SIZE ** (-0.5)
    if causal_visible is not None:
        scores = jnp.where(causal_visible[None, :, None, :], scores, MASKED_SCORE)
    probabilities = jnp.exp(scores - jnp.transpose(log_total, (1, 0, 2))[..., None])
    prob_grad = jnp.einsum(
        "rgjd,kgd->grjk", attended_grad, rows_of_values, preferred_element_type=jnp.float32
    )
    score_grad = (
        probabilities * (prob_grad - jnp.transpose(delta_rows, (1, 0, 2))[..., None])
    ).astype(jnp.bfloat16)
    query_part = jnp.einsum(
        "grjk,kgd->rgjd", score_grad, rows_of_keys, preferred_element_type=jnp.float32
    ) * HEAD_SIZE ** (-0.5)
    key_part = jnp.einsum(
        "grjk,rgjd->kgd", score_grad, query_rows, preferred_element_type=jnp.float32
    ) * HEAD_SIZE ** (-0.5)
    value_part = jnp.einsum(
        "grjk,rgjd->kgd",
        probabilities.astype(jnp.bfloat16),
        attended_grad,
        preferred_element_type=jnp.float32,
    )
    return (query_part, key_part, value_part)


def backward_block(
    block_of_keys,
    source_ctx,
    own_ctx,
    query_rows,
    attended_grad,
    log_total,
    delta_rows,
    own_places,
    ctx_count,
):
    rows_of_keys, rows_of_values = split_block(block_of_keys)
    device_count, _, rows_per_half, _ = block_of_keys.shape
    hidden_width = KEY_VALUE_HEADS * HEAD_SIZE

    def backward_earlier():
        query_part, key_part, value_part = attend_back(
            query_rows,
            attended_grad,
            log_total,
            delta_rows,
            rows_of_keys[:, 0].reshape(-1, KEY_VALUE_HEADS, HEAD_SIZE),
            rows_of_values[:, 0].reshape(-1, KEY_VALUE_HEADS, HEAD_SIZE),
            None,
        )
        early_grad = jnp.concatenate(
            [
                key_part.reshape(device_count, 1, rows_per_half, hidden_width),
                value_part.reshape(device_count, 1, rows_per_half, hidden_width),
            ],
            axis=-1,
        )
        return (query_part, jnp.concatenate([early_grad, jnp.zeros_like(early_grad)], axis=1))

    def backward_later():
        query_part, key_part, value_part = attend_back(
            query_rows[rows_per_half:],
            attended_grad[rows_per_half:],
            log_total[rows_per_half:],
            delta_rows[rows_per_half:],
            rows_of_keys.reshape(-1, KEY_VALUE_HEADS, HEAD_SIZE),
            rows_of_values.reshape(-1, KEY_VALUE_HEADS, HEAD_SIZE),
            None,
        )
        query_part = jnp.concatenate([jnp.zeros_like(query_part), query_part], axis=0)
        return (
            query_part,
            jnp.concatenate(
                [
                    key_part.reshape(device_count, 2, rows_per_half, hidden_width),
                    value_part.reshape(device_count, 2, rows_per_half, hidden_width),
                ],
                axis=-1,
            ),
        )

    def backward_diagonal():
        key_places = block_places(source_ctx, 2 * rows_per_half, ctx_count, device_count)
        causal_visible = own_places[:, None] >= key_places[None, :]
        query_part, key_part, value_part = attend_back(
            query_rows,
            attended_grad,
            log_total,
            delta_rows,
            rows_of_keys.reshape(-1, KEY_VALUE_HEADS, HEAD_SIZE),
            rows_of_values.reshape(-1, KEY_VALUE_HEADS, HEAD_SIZE),
            causal_visible,
        )
        return (
            query_part,
            jnp.concatenate(
                [
                    key_part.reshape(device_count, 2, rows_per_half, hidden_width),
                    value_part.reshape(device_count, 2, rows_per_half, hidden_width),
                ],
                axis=-1,
            ),
        )

    branch_index = jnp.where(source_ctx == own_ctx, 2, jnp.where(source_ctx > own_ctx, 1, 0))
    return lax.switch(branch_index, [backward_earlier, backward_later, backward_diagonal])


def per_device(
    inputs,
    attn_gain,
    query_weight,
    key_matrix,
    value_matrix,
    out_weight,
    ffn_gain,
    gate_weight,
    up_weight,
    down_weight,
    cotangent,
):
    ctx_count = lax.axis_size("ctx")
    device_count = lax.axis_size("ws")
    own_ctx = lax.axis_index("ctx")
    own_member = lax.axis_index("ws")
    micro_count, count_of_rows, _ = inputs.shape
    rows_per_half = count_of_rows // 2
    queries_per_group = QUERY_HEADS // KEY_VALUE_HEADS
    hidden_width = KEY_VALUE_HEADS * HEAD_SIZE
    own_places = query_places(own_ctx, own_member, count_of_rows, ctx_count, device_count)
    cosine_table, sine_table = rotary_tables(own_places)
    grad_sums = None
    layer_outs = []
    input_grads = []
    for micro_batch in range(micro_count):
        gathered = (
            lax.all_gather(attn_gain, ("ctx", "ws"), axis=0, tiled=True),
            lax.all_gather(query_weight, ("ctx", "ws"), axis=0, tiled=True),
            lax.all_gather(key_matrix, ("ctx", "ws"), axis=0, tiled=True),
            lax.all_gather(value_matrix, ("ctx", "ws"), axis=0, tiled=True),
            lax.all_gather(out_weight, ("ctx", "ws"), axis=0, tiled=True),
            lax.all_gather(ffn_gain, ("ctx", "ws"), axis=0, tiled=True),
            lax.all_gather(gate_weight, ("ctx", "ws"), axis=0, tiled=True),
            lax.all_gather(up_weight, ("ctx", "ws"), axis=0, tiled=True),
            lax.all_gather(down_weight, ("ctx", "ws"), axis=0, tiled=True),
        )
        (
            full_attn_gain,
            full_query,
            complete_key,
            full_value,
            full_out,
            full_ffn_gain,
            full_gate,
            full_up,
            full_down,
        ) = gathered
        first_gain = full_attn_gain.astype(jnp.float32)
        second_gain = full_ffn_gain.astype(jnp.float32)
        layer_rows = inputs[micro_batch].astype(jnp.float32)
        normalized_rows, first_inverse = normalize(layer_rows, first_gain)
        normalized_reduced = normalized_rows.astype(jnp.bfloat16)
        query_rows = rotate(
            matrix_multiply(normalized_reduced, full_query).reshape(
                count_of_rows, QUERY_HEADS, HEAD_SIZE
            ),
            cosine_table,
            sine_table,
        )
        query_rows = query_rows.astype(jnp.bfloat16).reshape(
            count_of_rows, KEY_VALUE_HEADS, queries_per_group, HEAD_SIZE
        )
        rows_of_keys = rotate(
            matrix_multiply(normalized_reduced, complete_key).reshape(
                count_of_rows, KEY_VALUE_HEADS, HEAD_SIZE
            ),
            cosine_table,
            sine_table,
        ).astype(jnp.bfloat16)
        rows_of_values = matrix_multiply(normalized_reduced, full_value).astype(jnp.bfloat16)
        local_block = jnp.concatenate(
            [rows_of_keys.reshape(count_of_rows, hidden_width), rows_of_values], axis=-1
        )
        group_block = lax.all_gather(local_block, "ws", axis=0, tiled=True).reshape(
            device_count, 2, rows_per_half, 2 * hidden_width
        )

        def fold_step(carried, shard_piece):

            def visit_block(state_now, block_entry):
                block_of_keys, source_ctx = block_entry
                return (
                    forward_block(
                        state_now,
                        block_of_keys,
                        source_ctx,
                        own_ctx,
                        query_rows,
                        own_places,
                        ctx_count,
                    ),
                    None,
                )

            source_list = jnp.arange(shard_piece.shape[0], dtype=jnp.int32)
            result_state, _ = lax.scan(visit_block, carried, (shard_piece, source_list))
            return result_state

        row_max, row_total, mixture = fold_step(
            empty_part(count_of_rows), lax.all_gather(group_block[None], "ctx", axis=0, tiled=True)
        )
        attended = mixture / row_total[..., None]
        log_total = row_max + jnp.log(row_total)
        attended_low = attended.astype(jnp.bfloat16).reshape(count_of_rows, QUERY_HEADS * HEAD_SIZE)
        middle = layer_rows + matrix_multiply(attended_low, full_out)
        hidden, second_inverse = normalize(middle, second_gain)
        hidden_low = hidden.astype(jnp.bfloat16)
        gate_rows = matrix_multiply(hidden_low, full_gate)
        up_rows = matrix_multiply(hidden_low, full_up)
        sigmoid_gate = jax.nn.sigmoid(gate_rows)
        silu_gate = gate_rows * sigmoid_gate
        activated = (silu_gate * up_rows).astype(jnp.bfloat16)
        layer_outs.append((middle + matrix_multiply(activated, full_down)).astype(jnp.bfloat16))
        upstream_low = cotangent[micro_batch]
        upstream = upstream_low.astype(jnp.float32)
        down_sum = outer_sum(activated, upstream_low)
        act_grad = back_product(upstream_low, full_down)
        gate_low = (
            act_grad * up_rows * sigmoid_gate * (1.0 + gate_rows * (1.0 - sigmoid_gate))
        ).astype(jnp.bfloat16)
        up_low = (act_grad * silu_gate).astype(jnp.bfloat16)
        gate_sum = outer_sum(hidden_low, gate_low)
        up_sum = outer_sum(hidden_low, up_low)
        hidden_grad = back_product(gate_low, full_gate) + back_product(up_low, full_up)
        middle_part, ffn_gain_sum = normalize_back(middle, second_inverse, second_gain, hidden_grad)
        middle_grad = middle_part + upstream
        branch_low = middle_grad.astype(jnp.bfloat16)
        out_sum = outer_sum(attended_low, branch_low)
        attended_grad = (
            back_product(branch_low, full_out)
            .reshape(count_of_rows, KEY_VALUE_HEADS, queries_per_group, HEAD_SIZE)
            .astype(jnp.bfloat16)
        )
        delta_rows = jnp.sum(attended_grad.astype(jnp.float32) * attended, axis=-1)

        def cycle_step(turn_index, carried):
            block_of_keys, block_grad, query_total = carried
            source_ctx = (own_ctx - turn_index) % ctx_count
            query_part, block_part = backward_block(
                block_of_keys,
                source_ctx,
                own_ctx,
                query_rows,
                attended_grad,
                log_total,
                delta_rows,
                own_places,
                ctx_count,
            )
            block_grad = block_grad + block_part
            next_block = shifted(block_of_keys, "ctx", 1)
            next_grad = shifted(as_sent(block_grad), "ctx", 1).astype(block_grad.dtype)
            return (next_block, next_grad, query_total + query_part)

        cycle_start = (
            group_block,
            jnp.zeros(group_block.shape, jnp.float32),
            jnp.zeros((count_of_rows, KEY_VALUE_HEADS, queries_per_group, HEAD_SIZE), jnp.float32),
        )
        _, block_grad, query_total = lax.fori_loop(0, ctx_count, cycle_step, cycle_start)
        local_gradient = (
            lax.psum_scatter(block_grad.astype(jnp.bfloat16), "ws", scatter_dimension=0, tiled=True)
            .astype(jnp.float32)
            .reshape(count_of_rows, 2 * hidden_width)
        )
        key_low = rotate_back(
            local_gradient[:, :hidden_width].reshape(count_of_rows, KEY_VALUE_HEADS, HEAD_SIZE),
            cosine_table,
            sine_table,
        )
        key_low = key_low.astype(jnp.bfloat16).reshape(count_of_rows, hidden_width)
        value_low = local_gradient[:, hidden_width:].astype(jnp.bfloat16)
        query_low = rotate_back(
            query_total.reshape(count_of_rows, QUERY_HEADS, HEAD_SIZE), cosine_table, sine_table
        )
        query_low = query_low.astype(jnp.bfloat16).reshape(count_of_rows, QUERY_HEADS * HEAD_SIZE)
        query_sum = outer_sum(normalized_reduced, query_low)
        key_sum = outer_sum(normalized_reduced, key_low)
        value_sum = outer_sum(normalized_reduced, value_low)
        normed_grad = (
            back_product(query_low, full_query)
            + back_product(key_low, complete_key)
            + back_product(value_low, full_value)
        )
        input_part, attn_gain_sum = normalize_back(
            layer_rows, first_inverse, first_gain, normed_grad
        )
        input_grads.append((middle_grad + input_part).astype(jnp.bfloat16))
        batch_terms = (
            attn_gain_sum,
            query_sum,
            key_sum,
            value_sum,
            out_sum,
            ffn_gain_sum,
            gate_sum,
            up_sum,
            down_sum,
        )
        if grad_sums is None:
            grad_sums = batch_terms
        else:
            grad_sums = tuple(
                (
                    earlier_sum + batch_term
                    for earlier_sum, batch_term in zip(grad_sums, batch_terms)
                )
            )
    owned_grads = (
        lax.psum_scatter(grad_sums[0], ("ctx", "ws"), scatter_dimension=0, tiled=True),
        lax.psum_scatter(grad_sums[1], ("ctx", "ws"), scatter_dimension=0, tiled=True),
        lax.psum_scatter(grad_sums[2], ("ctx", "ws"), scatter_dimension=0, tiled=True),
        lax.psum_scatter(grad_sums[3], ("ctx", "ws"), scatter_dimension=0, tiled=True),
        lax.psum_scatter(grad_sums[4], ("ctx", "ws"), scatter_dimension=0, tiled=True),
        lax.psum_scatter(grad_sums[5], ("ctx", "ws"), scatter_dimension=0, tiled=True),
        lax.psum_scatter(grad_sums[6], ("ctx", "ws"), scatter_dimension=0, tiled=True),
        lax.psum_scatter(grad_sums[7], ("ctx", "ws"), scatter_dimension=0, tiled=True),
        lax.psum_scatter(grad_sums[8], ("ctx", "ws"), scatter_dimension=0, tiled=True),
    )
    return (
        jnp.stack(layer_outs),
        jnp.stack(input_grads),
        owned_grads[0],
        owned_grads[1],
        owned_grads[2],
        owned_grads[3],
        owned_grads[4],
        owned_grads[5],
        owned_grads[6],
        owned_grads[7],
        owned_grads[8],
    )


MESH = pl.DeviceIdType.MESH
NEG = -1e30
WIDE = 128
VMEM_LIMIT = 60 * 1024 * 1024


def fits_fast(mesh):
    return mesh.shape["ctx"] == 8 and mesh.shape["ws"] == 4


def place():
    c = lax.axis_index("ctx")
    w = lax.axis_index("ws")
    return c // 2, lax.rem(c, 2), w // 2, lax.rem(w, 2)


def device(z, y, x, k):
    return (z * 2 + y, x * 2 + k)


def greet(zn):
    z, y, x, k = place()
    others = [device(lax.rem(z + j, zn), y, x, k) for j in range(1, zn)]
    others += [device(z, y, 1 - x, k), device(z, 1 - y, x, k), device(z, y, x, 1 - k)]
    barrier = pltpu.get_barrier_semaphore()
    for other in others:
        pl.semaphore_signal(barrier, inc=1, device_id=other, device_id_type=MESH)
    pl.semaphore_wait(barrier, len(others))


def remote(src, dst, send, recv, where):
    return pltpu.make_async_remote_copy(
        src_ref=src, dst_ref=dst, send_sem=send, recv_sem=recv, device_id=where, device_id_type=MESH
    )


class Gather:
    SEMS = 12

    def __init__(self, src, dst, send, recv, zn):
        z, y, x, k = place()
        own = dst.at[z, y, x, k]
        hz = zn // 2
        xn, yn, sib = device(z, y, 1 - x, k), device(z, 1 - y, x, k), device(z, y, x, 1 - k)

        def push(i, ref, where):
            return remote(ref, ref, send.at[i], recv.at[i], where)

        def col(yy, xx, lo=0, n=zn):
            return dst.at[pl.ds(lo, n), yy, xx, k]

        self.local = pltpu.make_async_copy(src, own, send.at[0])
        self.along = [
            remote(src, own, send.at[j], recv.at[j], device(lax.rem(z + j, zn), y, x, k))
            for j in range(1, zn)
        ]
        self.cols = [push(4, col(y, x), xn), push(5, col(y, x), yn)]
        self.corner = [push(7, col(1 - y, x, 0, hz), xn), push(8, col(y, 1 - x, hz, hz), yn)]
        self.twin_own = push(6, col(y, x), sib)
        self.twin_cols = [push(9, col(y, 1 - x), sib), push(10, col(1 - y, x), sib)]
        self.twin_corner = push(11, col(1 - y, 1 - x), sib)

    def stage(self, n):
        if n == 0:
            self.local.start()
            for c in self.along:
                c.start()
        elif n == 1:
            self.local.wait()
            for c in self.along:
                c.wait_recv()
            for c in self.cols:
                c.start()
            self.twin_own.start()
        elif n == 2:
            for c in self.cols:
                c.wait_recv()
            for c in self.corner:
                c.start()
            for c in self.twin_cols:
                c.start()
        elif n == 3:
            for c in self.corner:
                c.wait_recv()
            self.twin_corner.start()
        elif n == 4:
            for c in [self.twin_own] + self.twin_cols + [self.twin_corner]:
                c.wait_recv()
            for c in (
                self.along
                + self.cols
                + self.corner
                + [self.twin_own]
                + self.twin_cols
                + [self.twin_corner]
            ):
                c.wait_send()


def run_stages(items, stages):
    for t in range(len(items) + stages - 1):
        for n in range(stages):
            if 0 <= t - n < len(items):
                items[t - n].stage(n)


def pieces_of(rows, cols, nrow, ncol):
    return [
        (i * (rows // nrow), rows // nrow, j * (cols // ncol), cols // ncol)
        for i in range(nrow)
        for j in range(ncol)
    ]


def gather_all(arrays, rows_used, cuts, collective_id):
    zn = lax.axis_size("ctx") // 2
    n = len(arrays)
    work = [
        (a, piece)
        for a in range(n)
        for piece in pieces_of(rows_used[a], arrays[a].shape[1], *cuts[a])
    ]

    def kernel(*refs):
        ins, outs, (send, recv) = refs[:n], refs[n : 2 * n], refs[2 * n :]
        greet(zn)
        items = []
        for i, (a, (r0, nr, c0, nc)) in enumerate(work):
            src = ins[a].at[pl.ds(r0, nr), pl.ds(c0, nc)]
            dst = outs[a].at[:, :, :, :, pl.ds(r0, nr), pl.ds(c0, nc)]
            items.append(Gather(src, dst, send.at[i], recv.at[i], zn))
        run_stages(items, 5)

    return pl.pallas_call(
        kernel,
        out_shape=[
            jax.ShapeDtypeStruct((zn, 2, 2, 2, rows_used[a], arrays[a].shape[1]), arrays[a].dtype)
            for a in range(n)
        ],
        in_specs=[pl.BlockSpec(memory_space=pl.ANY)] * n,
        out_specs=[pl.BlockSpec(memory_space=pl.ANY)] * n,
        scratch_shapes=[
            pltpu.SemaphoreType.DMA((len(work), Gather.SEMS)),
            pltpu.SemaphoreType.DMA((len(work), Gather.SEMS)),
        ],
        compiler_params=pltpu.CompilerParams(
            collective_id=collective_id, has_side_effects=True, vmem_limit_bytes=VMEM_LIMIT
        ),
    )(*arrays)


class Scatter:
    SEMS = 10

    @staticmethod
    def scratch(zn, nr, nc):
        b = jnp.bfloat16
        return [
            pltpu.VMEM((zn, 2, 2, nr, nc), b),
            pltpu.VMEM((zn, 2, 2, nr, nc), b),
            pltpu.VMEM((2, zn // 2, nr, nc), b),
            pltpu.VMEM((2, zn, nr, nc), b),
            pltpu.VMEM((zn - 1, nr, nc), b),
        ]

    def __init__(self, part, out, bufs, send, recv, zn):
        z, y, x, k = self.at = place()
        self.zn = zn
        hz = zn // 2
        xn, yn, sib = device(z, y, 1 - x, k), device(z, 1 - y, x, k), device(z, y, x, 1 - k)
        self.held, self.twin, self.corners, self.colsums, self.ends = held, twin, corners, colsums, ends = bufs
        self.out = out
        self.load = pltpu.make_async_copy(part.at[:, :, :, k], held, send.at[0])
        self.to_twin = remote(part.at[:, :, :, 1 - k], twin, send.at[1], recv.at[1], sib)
        self.to_corner = [
            remote(held.at[pl.ds(0, hz), 1 - y, 1 - x], corners.at[0], send.at[2], recv.at[2], yn),
            remote(held.at[pl.ds(hz, hz), 1 - y, 1 - x], corners.at[1], send.at[3], recv.at[3], xn),
        ]
        self.to_col = [
            remote(held.at[:, y, 1 - x], colsums.at[0], send.at[4], recv.at[4], xn),
            remote(held.at[:, 1 - y, x], colsums.at[1], send.at[5], recv.at[5], yn),
        ]
        self.along = []
        for j in range(1, zn):
            zz = lax.rem(z + j, zn)
            self.along.append(
                remote(held.at[zz, y, x], ends.at[j - 1], send.at[5 + j], recv.at[5 + j], device(zz, y, x, k))
            )

    def stage(self, n):
        z, y, x, k = self.at
        zn, hz = self.zn, self.zn // 2
        held = self.held
        if n == 0:
            self.to_twin.start()
            self.load.start()
        elif n == 1:
            self.load.wait()
            self.to_twin.wait_recv()

            def add(i, _):
                for yy in range(2):
                    for xx in range(2):
                        held[i, yy, xx] = held[i, yy, xx] + self.twin[i, yy, xx]
                return 0

            lax.fori_loop(0, zn, add, 0)
            for c in self.to_corner:
                c.start()
        elif n == 2:
            for c in self.to_corner:
                c.wait_recv()
            for i in range(hz):
                held[i, y, 1 - x] = held[i, y, 1 - x] + self.corners[0, i]
                held[hz + i, 1 - y, x] = held[hz + i, 1 - y, x] + self.corners[1, i]
            for c in self.to_col:
                c.start()
        elif n == 3:
            for c in self.to_col:
                c.wait_recv()

            def add(i, _):
                f = jnp.float32
                held[i, y, x] = (
                    held[i, y, x].astype(f) + self.colsums[0, i].astype(f) + self.colsums[1, i].astype(f)
                ).astype(jnp.bfloat16)
                return 0

            lax.fori_loop(0, zn, add, 0)
            for c in self.along:
                c.start()
        elif n == 4:
            for c in self.along:
                c.wait_recv()
            total = held[z, y, x].astype(jnp.float32)
            for j in range(zn - 1):
                total = total + self.ends[j].astype(jnp.float32)
            self.out[...] = total
            for c in [self.to_twin] + self.to_corner + self.to_col + self.along:
                c.wait_send()


def scatter_all(parts, cuts, collective_id):
    zn = lax.axis_size("ctx") // 2
    n = len(parts)
    work = [
        (a, piece) for a in range(n) for piece in pieces_of(*parts[a].shape[4:], *cuts[a])
    ]
    scratch = []
    for a, (r0, nr, c0, nc) in work:
        scratch += Scatter.scratch(zn, nr, nc)

    def kernel(*refs):
        ins, outs, bufs, (send, recv) = refs[:n], refs[n : 2 * n], refs[2 * n : -2], refs[-2:]
        greet(zn)
        items = []
        for i, (a, (r0, nr, c0, nc)) in enumerate(work):
            part = ins[a].at[:, :, :, :, pl.ds(r0, nr), pl.ds(c0, nc)]
            out = outs[a].at[pl.ds(r0, nr), pl.ds(c0, nc)]
            items.append(Scatter(part, out, bufs[5 * i : 5 * i + 5], send.at[i], recv.at[i], zn))
        run_stages(items, 5)

    return pl.pallas_call(
        kernel,
        out_shape=[jax.ShapeDtypeStruct(p.shape[4:], jnp.float32) for p in parts],
        in_specs=[pl.BlockSpec(memory_space=pl.ANY)] * n,
        out_specs=[pl.BlockSpec(memory_space=pltpu.VMEM)] * n,
        scratch_shapes=scratch
        + [
            pltpu.SemaphoreType.DMA((len(work), Scatter.SEMS)),
            pltpu.SemaphoreType.DMA((len(work), Scatter.SEMS)),
        ],
        compiler_params=pltpu.CompilerParams(
            collective_id=collective_id, has_side_effects=True, vmem_limit_bytes=VMEM_LIMIT
        ),
    )(*parts)


def head_lanes(block, head, group):
    t = block.astype(jnp.float32)
    if head % 2 != group % 2:
        t = pltpu.roll(t, HEAD_SIZE, 1)
    lane = lax.broadcasted_iota(jnp.int32, t.shape, 1)
    return jnp.where((lane // HEAD_SIZE) == group % 2, t, 0.0)


def spread_heads(src, dst, mb, scale):
    per = QUERY_HEADS // KEY_VALUE_HEADS
    rows = src.shape[1] // 2
    for half in range(2):
        for g in range(KEY_VALUE_HEADS):
            for j in range(per):
                h = per * g + j
                block = src[mb, half * rows : (half + 1) * rows, WIDE * (h // 2) : WIDE * (h // 2) + WIDE]
                t = head_lanes(block, h, g) * scale
                dst[half, g, j * rows : (j + 1) * rows, :] = t.astype(dst.dtype)


def join_heads(get, half, mb, dst, rows):
    per = QUERY_HEADS // KEY_VALUE_HEADS
    vals = {}
    for g in range(KEY_VALUE_HEADS):
        t = get(g)
        for j in range(per):
            vals[per * g + j] = (t[j * rows : (j + 1) * rows], g)
    lane = lax.broadcasted_iota(jnp.int32, (rows, WIDE), 1)
    for m in range(QUERY_HEADS // 2):
        sides = []
        for h in (2 * m, 2 * m + 1):
            t, g = vals[h]
            if h % 2 != g % 2:
                t = pltpu.roll(t, HEAD_SIZE, 1)
            sides.append(t)
        both = jnp.where(lane < HEAD_SIZE, sides[0], sides[1])
        dst[mb, half * rows : (half + 1) * rows, WIDE * m : WIDE * m + WIDE] = both.astype(dst.dtype)


def span_of(t, c, cn):
    half = (t > c).astype(jnp.int32)
    j = jnp.where(half == 1, t - c - 1, t)
    last = jnp.where(half == 1, 2 * cn - 1 - c, c)
    late = (j >= cn).astype(jnp.int32)
    src = jnp.where(late == 1, 2 * cn - 1 - j, j)
    return half, src, late, j == last


def hidden_bias(diag, w, rows, per, wn):
    shape = (per * rows, wn * rows)
    i = lax.rem(lax.broadcasted_iota(jnp.int32, shape, 0), rows)
    key = lax.broadcasted_iota(jnp.int32, shape, 1)
    limit = jnp.where(diag, w * rows, wn * rows)
    return jnp.where(key <= i + limit, 0.0, NEG)


NT = (((1,), (1,)), ((), ()))
TN = (((0,), (0,)), ((), ()))


def nt(a, b):
    return lax.dot_general(a, b, NT, preferred_element_type=jnp.float32)


def tn(a, b):
    return lax.dot_general(a, b, TN, preferred_element_type=jnp.float32)


def attention(q, kv):
    mbs, tokens, qw = q.shape
    cn, wn = kv.shape[:2]
    rows = tokens // 2
    per = QUERY_HEADS // KEY_VALUE_HEADS
    hid = KEY_VALUE_HEADS * HEAD_SIZE
    groups = range(KEY_VALUE_HEADS)

    def kernel(q_ref, kv_ref, o_ref, lse_ref, qs, m_s, l_s, acc):
        c, w = lax.axis_index("ctx"), lax.axis_index("ws")

        def one(mb, _):
            spread_heads(q_ref, qs, mb, HEAD_SIZE**-0.5)
            m_s[...] = jnp.full(m_s.shape, NEG, jnp.float32)
            l_s[...] = jnp.zeros(l_s.shape, jnp.float32)
            acc[...] = jnp.zeros(acc.shape, jnp.float32)

            def step(t, _):
                half, src, late, diag = span_of(t, c, cn)
                bias = hidden_bias(diag, w, rows, per, wn)
                for g in groups:
                    lo = WIDE * (g // 2)
                    kb = kv_ref[src, :, mb, late, :, lo : lo + WIDE].reshape(wn * rows, WIDE)
                    vb = kv_ref[src, :, mb, late, :, hid + lo : hid + lo + WIDE].reshape(wn * rows, WIDE)
                    s = nt(qs[half, g], kb) + bias
                    m_old = m_s[half, g]
                    m_new = jnp.maximum(m_old, jnp.max(s, axis=1, keepdims=True))
                    alpha = jnp.exp(m_old - m_new)
                    p = jnp.exp(s - m_new[:, :1])
                    m_s[half, g] = m_new
                    l_s[half, g] = l_s[half, g] * alpha + jnp.sum(p, axis=1, keepdims=True)
                    acc[half, g] = acc[half, g] * alpha + jnp.dot(
                        p.astype(jnp.bfloat16), vb, preferred_element_type=jnp.float32
                    )
                return 0

            lax.fori_loop(0, 2 * cn + 1, step, 0)
            for half in range(2):
                join_heads(lambda g: acc[half, g] / l_s[half, g], half, mb, o_ref, rows)
                for g in groups:
                    lse_ref[mb, half, g] = m_s[half, g] + jnp.log(l_s[half, g])
            return 0

        lax.fori_loop(0, mbs, one, 0)

    stat = (2, KEY_VALUE_HEADS, per * rows, WIDE)
    return pl.pallas_call(
        kernel,
        out_shape=[
            jax.ShapeDtypeStruct(q.shape, jnp.bfloat16),
            jax.ShapeDtypeStruct((mbs,) + stat, jnp.float32),
        ],
        in_specs=[pl.BlockSpec(memory_space=pltpu.VMEM)] * 2,
        out_specs=[pl.BlockSpec(memory_space=pltpu.VMEM)] * 2,
        scratch_shapes=[
            pltpu.VMEM(stat, jnp.bfloat16),
            pltpu.VMEM(stat, jnp.float32),
            pltpu.VMEM(stat, jnp.float32),
            pltpu.VMEM(stat, jnp.float32),
        ],
        compiler_params=pltpu.CompilerParams(vmem_limit_bytes=VMEM_LIMIT),
    )(q, kv)


def attention_back(q, kv, o, do, lse):
    mbs, tokens, qw = q.shape
    cn, wn = kv.shape[:2]
    rows = tokens // 2
    per = QUERY_HEADS // KEY_VALUE_HEADS
    hid = KEY_VALUE_HEADS * HEAD_SIZE
    groups = range(KEY_VALUE_HEADS)
    scale = HEAD_SIZE**-0.5

    def kernel(q_ref, kv_ref, o_ref, do_ref, lse_ref, dq_ref, dkv_ref, qs, dos, delta, dq, dkv, stage, sems):
        c, w = lax.axis_index("ctx"), lax.axis_index("ws")

        def flush(mb):
            return pltpu.make_async_copy(stage, dkv_ref.at[:, :, mb], sems.at[0])

        for mb in range(mbs):
            spread_heads(q_ref, qs, mb, scale)
            spread_heads(do_ref, dos, mb, 1.0)
            for half in range(2):
                for g in groups:
                    for j in range(per):
                        h = per * g + j
                        lo = WIDE * (h // 2)
                        block = o_ref[mb, half * rows : (half + 1) * rows, lo : lo + WIDE]
                        oh = head_lanes(block, h, g)
                        d = jnp.sum(oh * dos[half, g, j * rows : (j + 1) * rows, :].astype(jnp.float32), axis=1, keepdims=True)
                        delta[half, g, j * rows : (j + 1) * rows, :] = jnp.broadcast_to(d, (rows, WIDE))
            dq[...] = jnp.zeros(dq.shape, jnp.float32)

            def clear(i, _):
                dkv[i] = jnp.zeros(dkv.shape[1:], jnp.float32)
                return 0

            lax.fori_loop(0, cn, clear, 0)

            def step(t, _):
                half, src, late, diag = span_of(t, c, cn)
                bias = hidden_bias(diag, w, rows, per, wn)
                for g in groups:
                    lo = WIDE * (g // 2)
                    kb = kv_ref[src, :, mb, late, :, lo : lo + WIDE].reshape(wn * rows, WIDE)
                    vb = kv_ref[src, :, mb, late, :, hid + lo : hid + lo + WIDE].reshape(wn * rows, WIDE)
                    qg, dog = qs[half, g], dos[half, g]
                    p = jnp.exp(nt(qg, kb) + bias - lse_ref[mb, half, g][:, :1])
                    ds = (p * (nt(dog, vb) - delta[half, g][:, :1])).astype(jnp.bfloat16)
                    dq[half, g] += jnp.dot(ds, kb, preferred_element_type=jnp.float32)
                    dk = tn(ds, qg).reshape(wn, rows, WIDE)
                    dv = tn(p.astype(jnp.bfloat16), dog).reshape(wn, rows, WIDE)
                    dkv[src, :, late, :, lo : lo + WIDE] += dk
                    dkv[src, :, late, :, hid + lo : hid + lo + WIDE] += dv
                return 0

            lax.fori_loop(0, 2 * cn + 1, step, 0)
            for half in range(2):
                join_heads(lambda g: dq[half, g] * scale, half, mb, dq_ref, rows)
            if mb > 0:
                flush(mb - 1).wait()

            def pack(i, _):
                stage[i] = dkv[i].astype(jnp.bfloat16)
                return 0

            lax.fori_loop(0, cn, pack, 0)
            flush(mb).start()
        flush(mbs - 1).wait()

    stat = (2, KEY_VALUE_HEADS, per * rows, WIDE)
    return pl.pallas_call(
        kernel,
        out_shape=[
            jax.ShapeDtypeStruct(q.shape, jnp.float32),
            jax.ShapeDtypeStruct(kv.shape, jnp.bfloat16),
        ],
        in_specs=[pl.BlockSpec(memory_space=pltpu.VMEM)] * 5,
        out_specs=[pl.BlockSpec(memory_space=pltpu.VMEM), pl.BlockSpec(memory_space=pl.ANY)],
        scratch_shapes=[
            pltpu.VMEM(stat, jnp.bfloat16),
            pltpu.VMEM(stat, jnp.bfloat16),
            pltpu.VMEM(stat, jnp.float32),
            pltpu.VMEM(stat, jnp.float32),
            pltpu.VMEM((cn, wn, 2, rows, 2 * hid), jnp.float32),
            pltpu.VMEM((cn, wn, 2, rows, 2 * hid), jnp.bfloat16),
            pltpu.SemaphoreType.DMA((1,)),
        ],
        compiler_params=pltpu.CompilerParams(vmem_limit_bytes=VMEM_LIMIT),
    )(q, kv, o, do, lse)


def rotate_lanes(t, cos, low, high):
    quarter = HEAD_SIZE // 2
    return t * cos + jnp.roll(t, -quarter, axis=-1) * low + jnp.roll(t, quarter, axis=-1) * high


def lane_tables(positions, heads):
    quarter = HEAD_SIZE // 2
    frequency = 10000.0 ** (-2.0 * jnp.arange(quarter, dtype=jnp.float32) / HEAD_SIZE)
    angles = positions.astype(jnp.float32)[:, None] * frequency[None, :]
    cos, sin = jnp.cos(angles), jnp.sin(angles)
    none = jnp.zeros_like(sin)
    full = lambda a, b: jnp.tile(jnp.concatenate([a, b], axis=1), (1, heads))
    return full(cos, cos), full(-sin, none), full(none, sin)


def fast_device(
    inputs,
    attn_gain,
    query_weight,
    key_matrix,
    value_matrix,
    out_weight,
    ffn_gain,
    gate_weight,
    up_weight,
    down_weight,
    cotangent,
):
    f32, b16 = jnp.float32, jnp.bfloat16
    cn, wn = lax.axis_size("ctx"), lax.axis_size("ws")
    dn = cn * wn
    zn = cn // 2
    mbs, tokens, width = inputs.shape
    own = query_weight.shape[0]
    ra = own // 16 * 16
    rb = own - ra
    q_width = query_weight.shape[1]
    hid = KEY_VALUE_HEADS * HEAD_SIZE
    ff = gate_weight.shape[1]
    rows = mbs * tokens
    wa = dn * ra

    new = jnp.arange(width)
    old = jnp.where(
        new < wa, own * (new // ra) + new % ra, own * ((new - wa) // rb) + ra + (new - wa) % rb
    )
    order = (jnp.arange(width)[:, None] == old[None, :]).astype(b16)

    def to_order(t):
        return jnp.dot(t, order, preferred_element_type=f32).astype(t.dtype)

    def from_order(t):
        return lax.dot_general(t, order, NT, preferred_element_type=f32).astype(t.dtype)

    fold = 16 // rb

    def folded(t):
        return t.reshape(t.shape[0], fold, -1).transpose(1, 0, 2).reshape(16, -1)

    qkv_w = q_width + 2 * hid
    pad1 = -qkv_w % (fold * WIDE)
    rest_w = width + 2 * ff
    pad2 = -rest_w % (fold * WIDE)
    moved = to_order(
        jnp.concatenate(
            [inputs.reshape(rows, width), cotangent.reshape(rows, width), out_weight, down_weight]
        )
    )
    x_low, gy_low = moved[:rows], moved[rows : 2 * rows]
    out_p, down_p = moved[2 * rows : 2 * rows + own], moved[2 * rows + own :]
    qkv = jnp.concatenate([query_weight, key_matrix, value_matrix], axis=1)
    gains = jnp.stack([attn_gain, ffn_gain])
    gains = jnp.pad(gains, ((0, rb - 2), (0, pad1 - own)))
    b1 = folded(jnp.concatenate([qkv[ra:], gains], axis=1))
    b2 = folded(
        jnp.pad(
            jnp.concatenate([out_p[ra:], gate_weight[ra:], up_weight[ra:]], axis=1), ((0, 0), (0, pad2))
        )
    )
    arrays = [qkv, b1, out_p, gate_weight, up_weight, down_p, b2]
    used = [ra, 16, ra, ra, ra, down_p.shape[0], 16]
    cuts = [(1, 1), (1, 1), (1, 1), (1, 2), (1, 2), (2, 1), (1, 1)]
    qkv_a, b1g, out_a, gate_a, up_a, down_a, b2g = gather_all(arrays, used, cuts, 1)

    def unfolded(t):
        cols = t.shape[-1]
        return t.reshape(dn, fold, rb, cols).transpose(0, 2, 1, 3).reshape(dn * rb, fold * cols)

    flat = lambda t: t.reshape(-1, t.shape[-1])
    qkv_a, out_a, gate_a, up_a, down_w = map(flat, (qkv_a, out_a, gate_a, up_a, down_a))
    b1u, b2u = unfolded(b1g), unfolded(b2g)
    qkv_b, out_b = b1u[:, :qkv_w], b2u[:, :width]
    gate_b, up_b = b2u[:, width : width + ff], b2u[:, width + ff : width + 2 * ff]
    gains_all = b1u[:, qkv_w : qkv_w + own].reshape(dn, rb, own)
    in_order = lambda t: jnp.concatenate([t[:, :ra].reshape(-1), t[:, ra:].reshape(-1)]).astype(f32)
    gain1, gain2 = in_order(gains_all[:, 0]), in_order(gains_all[:, 1])

    def mm(h, a, b):
        return matrix_multiply(h[:, :wa], a) + matrix_multiply(h[:, wa:], b)

    def mm_back(g, a, b):
        return jnp.concatenate([back_product(g, a), back_product(g, b)], axis=1)

    c, w = lax.axis_index("ctx"), lax.axis_index("ws")
    places = query_places(c, w, tokens, cn, wn)
    cos, low, high = (jnp.tile(t, (mbs, 1)) for t in lane_tables(places, QUERY_HEADS))
    x = x_low.astype(f32)
    hn, inv1 = normalize(x, gain1)
    hn = hn.astype(b16)
    proj = mm(hn, qkv_a, qkv_b)
    q = rotate_lanes(proj[:, :q_width], cos, low, high).astype(b16)
    k = rotate_lanes(proj[:, q_width : q_width + hid], cos[:, :hid], low[:, :hid], high[:, :hid]).astype(b16)
    v = proj[:, q_width + hid :].astype(b16)
    kv = jnp.concatenate([k, v], axis=1)
    (kv_all,) = gather_all([kv], [rows], [(2, 2)], 2)
    kv_all = kv_all.reshape(cn, wn, mbs, 2, tokens // 2, 2 * hid)
    q3 = q.reshape(mbs, tokens, q_width)
    o3, lse = attention(q3, kv_all)
    o_p = to_order(o3.reshape(rows, q_width))
    x1 = x + mm(o_p, out_a, out_b)
    h2, inv2 = normalize(x1, gain2)
    h2 = h2.astype(b16)
    gate = mm(h2, gate_a, gate_b)
    up = mm(h2, up_a, up_b)
    sig = jax.nn.sigmoid(gate)
    silu = gate * sig
    act = (silu * up).astype(b16)
    out = from_order((x1 + matrix_multiply(act, down_w)).astype(b16))
    gy = gy_low.astype(f32)
    ga = back_product(gy_low, down_w)
    g_gate = (ga * up * sig * (1.0 + gate * (1.0 - sig))).astype(b16)
    g_up = (ga * silu).astype(b16)
    gh2 = mm_back(g_gate, gate_a, gate_b) + mm_back(g_up, up_a, up_b)
    mid, gain2_sum = normalize_back(x1, inv2, gain2, gh2)
    gx1 = mid + gy
    gb = gx1.astype(b16)
    gattn = from_order(mm_back(gb, out_a, out_b).astype(b16))
    dq, dkv = attention_back(q3, kv_all, o3, gattn.reshape(q3.shape), lse)

    gb_plain = from_order(gb)
    gy_plain = cotangent.reshape(rows, width)

    def sums(h, g):
        s = outer_sum(h, g).astype(b16)
        return s[:wa].reshape(zn, 2, 2, 2, ra, -1), s[wa:]

    def fold_sums(parts):
        t = jnp.concatenate(parts, axis=1)
        return (
            t.reshape(dn, rb, fold, -1).transpose(0, 2, 1, 3).reshape(zn, 2, 2, 2, 16, -1)
        )

    d_out_a, d_out_b = sums(o_p, gb_plain)
    d_gate_a, d_gate_b = sums(h2, g_gate)
    d_up_a, d_up_b = sums(h2, g_up)
    d_down = outer_sum(act, gy_plain).astype(b16).reshape(zn, 2, 2, 2, -1, width)
    d_b2 = fold_sums([d_out_b, d_gate_b, d_up_b, jnp.zeros((dn * rb, pad2), b16)])

    (dkv_own,) = scatter_all([dkv.reshape(zn, 2, 2, 2, rows, 2 * hid)], [(2, 2)], 3)
    dk, dv = dkv_own[:, :hid], dkv_own[:, hid:].astype(b16)
    gkr = rotate_lanes(dk, cos[:, :hid], -low[:, :hid], -high[:, :hid]).astype(b16)
    gqr = rotate_lanes(dq.reshape(rows, q_width), cos, -low, -high).astype(b16)
    g_qkv = jnp.concatenate([gqr, gkr, dv], axis=1)
    ghn = mm_back(g_qkv, qkv_a, qkv_b)
    first, gain1_sum = normalize_back(x, inv1, gain1, ghn)
    input_grad = from_order((gx1 + first).astype(b16))
    d_qkv_a, d_qkv_b = sums(hn, g_qkv)
    by_owner = lambda t: jnp.concatenate([t[:wa].reshape(dn, ra), t[wa:].reshape(dn, rb)], axis=1)
    gain_sums = jnp.stack([by_owner(gain1_sum), by_owner(gain2_sum)], axis=1).astype(b16)
    gain_sums = jnp.pad(gain_sums, ((0, 0), (0, rb - 2), (0, pad1 - own))).reshape(dn * rb, pad1)
    d_b1 = fold_sums([d_qkv_b, gain_sums])
    r_out, r_gate, r_up, r_down, r_b2, r_qkv, r_b1 = scatter_all(
        [d_out_a, d_gate_a, d_up_a, d_down, d_b2, d_qkv_a, d_b1],
        [(1, 1), (1, 2), (1, 2), (2, 1), (1, 1), (1, 1), (1, 1)],
        4,
    )

    def own_rows(t):
        return t.reshape(fold, rb, -1).transpose(1, 0, 2).reshape(rb, -1)

    e1, e2 = own_rows(r_b1), own_rows(r_b2)
    whole = lambda a, b: jnp.concatenate([a, b], axis=0)
    d_qkv = whole(r_qkv, e1[:, :qkv_w])
    return (
        out.reshape(inputs.shape),
        input_grad.reshape(inputs.shape),
        e1[0, qkv_w : qkv_w + own],
        d_qkv[:, :q_width],
        d_qkv[:, q_width : q_width + hid],
        d_qkv[:, q_width + hid :],
        whole(r_out, e2[:, :width]),
        e1[1, qkv_w : qkv_w + own],
        whole(r_gate, e2[:, width : width + ff]),
        whole(r_up, e2[:, width + ff : width + 2 * ff]),
        r_down,
    )


def solution(mesh):
    in_specs = (
        P(None, ("ctx", "ws"), None),
        P(("ctx", "ws")),
        P(("ctx", "ws"), None),
        P(("ctx", "ws"), None),
        P(("ctx", "ws"), None),
        P(("ctx", "ws"), None),
        P(("ctx", "ws")),
        P(("ctx", "ws"), None),
        P(("ctx", "ws"), None),
        P(("ctx", "ws"), None),
        P(None, ("ctx", "ws"), None),
    )
    out_specs = (
        P(None, ("ctx", "ws"), None),
        P(None, ("ctx", "ws"), None),
        P(("ctx", "ws")),
        P(("ctx", "ws"), None),
        P(("ctx", "ws"), None),
        P(("ctx", "ws"), None),
        P(("ctx", "ws"), None),
        P(("ctx", "ws")),
        P(("ctx", "ws"), None),
        P(("ctx", "ws"), None),
        P(("ctx", "ws"), None),
    )
    body = fast_device if fits_fast(mesh) else per_device
    return jax.shard_map(
        body, mesh=mesh, in_specs=in_specs, out_specs=out_specs, check_vma=False
    )
```

```python
import jax
import jax.numpy as jnp
from jax import lax
from jax.experimental import pallas as pl
from jax.experimental.pallas import tpu as pltpu
from jax.sharding import PartitionSpec as P
import functools

QUERY_HEADS = 18
KEY_VALUE_HEADS = 6
HEAD_SIZE = 64


EPSILON = 1e-05
MASKED_SCORE = -1e30


def shifted(block, axis, distance):
    devices = range(lax.axis_size(axis))
    route = [((i - distance) % len(devices), i) for i in devices]
    return lax.ppermute(block, axis, route)


def as_sent(x):

    def short(part):
        return part.astype(jnp.bfloat16) if part.dtype == jnp.float32 else part

    return jax.tree.map(short, x)


def matrix_multiply(left, right):
    return jnp.dot(left, right, preferred_element_type=jnp.float32)


def outer_sum(left, right):
    return jnp.einsum("ri,rj->ij", left, right, preferred_element_type=jnp.float32)


def back_product(gradient, weight):
    return jnp.einsum("rj,ij->ri", gradient, weight, preferred_element_type=jnp.float32)


def normalize(layer_rows, gain_vector):
    inverse = lax.rsqrt(jnp.mean(layer_rows * layer_rows, axis=-1, keepdims=True) + EPSILON)
    return (layer_rows * inverse * gain_vector, inverse)


def normalize_back(layer_rows, inverse, gain_vector, gradient):
    weighted = gradient * gain_vector
    inner_mean = jnp.mean(weighted * layer_rows, axis=-1, keepdims=True)
    row_grad = inverse * weighted - layer_rows * (inverse * inverse * inverse) * inner_mean
    gain_grad = jnp.sum(gradient * layer_rows * inverse, axis=0)
    return (row_grad, gain_grad)


def rotary_tables(token_positions):
    quarter = HEAD_SIZE // 2
    frequency = 10000.0 ** (-2.0 * jnp.arange(quarter, dtype=jnp.float32) / HEAD_SIZE)
    angles = token_positions.astype(jnp.float32)[:, None] * frequency[None, :]
    return (jnp.cos(angles)[:, None, :], jnp.sin(angles)[:, None, :])


def rotate(heads, cosine_table, sine_table):
    quarter = HEAD_SIZE // 2
    first_half = heads[..., :quarter]
    second_half = heads[..., quarter:]
    return jnp.concatenate(
        [
            first_half * cosine_table - second_half * sine_table,
            second_half * cosine_table + first_half * sine_table,
        ],
        axis=-1,
    )


def rotate_back(heads, cosine_table, sine_table):
    quarter = HEAD_SIZE // 2
    first_half = heads[..., :quarter]
    second_half = heads[..., quarter:]
    return jnp.concatenate(
        [
            first_half * cosine_table + second_half * sine_table,
            second_half * cosine_table - first_half * sine_table,
        ],
        axis=-1,
    )


def query_places(own_ctx, own_member, count_of_rows, ctx_count, device_count):
    rows_per_half = count_of_rows // 2
    local_index = jnp.arange(count_of_rows, dtype=jnp.int32)
    span_index = jnp.where(local_index < rows_per_half, own_ctx, 2 * ctx_count - 1 - own_ctx)
    return (
        span_index * (device_count * rows_per_half)
        + own_member * rows_per_half
        + local_index % rows_per_half
    )


def block_places(source_ctx, count_of_rows, ctx_count, device_count):
    rows_per_half = count_of_rows // 2
    member_index = jnp.arange(device_count, dtype=jnp.int32)[:, None, None]
    half_index = jnp.arange(2, dtype=jnp.int32)[None, :, None]
    inner_index = jnp.arange(rows_per_half, dtype=jnp.int32)[None, None, :]
    span_index = jnp.where(half_index == 0, source_ctx, 2 * ctx_count - 1 - source_ctx)
    return (
        span_index * (device_count * rows_per_half) + member_index * rows_per_half + inner_index
    ).reshape(-1)


def split_block(block_of_keys):
    hidden_width = KEY_VALUE_HEADS * HEAD_SIZE
    device_count, _, rows_per_half, _ = block_of_keys.shape
    rows_of_keys = block_of_keys[..., :hidden_width].reshape(
        device_count, 2, rows_per_half, KEY_VALUE_HEADS, HEAD_SIZE
    )
    rows_of_values = block_of_keys[..., hidden_width:].reshape(
        device_count, 2, rows_per_half, KEY_VALUE_HEADS, HEAD_SIZE
    )
    return (rows_of_keys, rows_of_values)


def attend(query_rows, rows_of_keys, rows_of_values, causal_visible):
    scores = jnp.einsum(
        "rgjd,kgd->grjk", query_rows, rows_of_keys, preferred_element_type=jnp.float32
    ) * HEAD_SIZE ** (-0.5)
    if causal_visible is not None:
        scores = jnp.where(causal_visible[None, :, None, :], scores, MASKED_SCORE)
    row_max = jnp.max(scores, axis=-1)
    exponentials = jnp.exp(scores - row_max[..., None])
    row_total = jnp.sum(exponentials, axis=-1)
    mixture = jnp.einsum(
        "grjk,kgd->rgjd",
        exponentials.astype(jnp.bfloat16),
        rows_of_values,
        preferred_element_type=jnp.float32,
    )
    return (jnp.transpose(row_max, (1, 0, 2)), jnp.transpose(row_total, (1, 0, 2)), mixture)


def empty_part(count_of_rows):
    queries_per_group = QUERY_HEADS // KEY_VALUE_HEADS
    return (
        jnp.full((count_of_rows, KEY_VALUE_HEADS, queries_per_group), MASKED_SCORE, jnp.float32),
        jnp.zeros((count_of_rows, KEY_VALUE_HEADS, queries_per_group), jnp.float32),
        jnp.zeros((count_of_rows, KEY_VALUE_HEADS, queries_per_group, HEAD_SIZE), jnp.float32),
    )


def combine(carried, incoming):
    carried_max, carried_total, carried_mix = carried
    incoming_max, incoming_total, incoming_mix = incoming
    new_max = jnp.maximum(carried_max, incoming_max)
    carried_scale = jnp.exp(carried_max - new_max)
    incoming_scale = jnp.exp(incoming_max - new_max)
    return (
        new_max,
        carried_total * carried_scale + incoming_total * incoming_scale,
        carried_mix * carried_scale[..., None] + incoming_mix * incoming_scale[..., None],
    )


def forward_block(carried, block_of_keys, source_ctx, own_ctx, query_rows, own_places, ctx_count):
    rows_of_keys, rows_of_values = split_block(block_of_keys)
    device_count, _, rows_per_half, _ = block_of_keys.shape

    def forward_earlier():
        return attend(
            query_rows,
            rows_of_keys[:, 0].reshape(-1, KEY_VALUE_HEADS, HEAD_SIZE),
            rows_of_values[:, 0].reshape(-1, KEY_VALUE_HEADS, HEAD_SIZE),
            None,
        )

    def forward_later():
        late_part = attend(
            query_rows[rows_per_half:],
            rows_of_keys.reshape(-1, KEY_VALUE_HEADS, HEAD_SIZE),
            rows_of_values.reshape(-1, KEY_VALUE_HEADS, HEAD_SIZE),
            None,
        )
        early_part = empty_part(rows_per_half)
        return tuple(
            (
                jnp.concatenate([early_piece, late_piece], axis=0)
                for early_piece, late_piece in zip(early_part, late_part)
            )
        )

    def forward_diagonal():
        key_places = block_places(source_ctx, 2 * rows_per_half, ctx_count, device_count)
        causal_visible = own_places[:, None] >= key_places[None, :]
        return attend(
            query_rows,
            rows_of_keys.reshape(-1, KEY_VALUE_HEADS, HEAD_SIZE),
            rows_of_values.reshape(-1, KEY_VALUE_HEADS, HEAD_SIZE),
            causal_visible,
        )

    branch_index = jnp.where(source_ctx == own_ctx, 2, jnp.where(source_ctx > own_ctx, 1, 0))
    return combine(
        carried, lax.switch(branch_index, [forward_earlier, forward_later, forward_diagonal])
    )


def attend_back(
    query_rows, attended_grad, log_total, delta_rows, rows_of_keys, rows_of_values, causal_visible
):
    scores = jnp.einsum(
        "rgjd,kgd->grjk", query_rows, rows_of_keys, preferred_element_type=jnp.float32
    ) * HEAD_SIZE ** (-0.5)
    if causal_visible is not None:
        scores = jnp.where(causal_visible[None, :, None, :], scores, MASKED_SCORE)
    probabilities = jnp.exp(scores - jnp.transpose(log_total, (1, 0, 2))[..., None])
    prob_grad = jnp.einsum(
        "rgjd,kgd->grjk", attended_grad, rows_of_values, preferred_element_type=jnp.float32
    )
    score_grad = (
        probabilities * (prob_grad - jnp.transpose(delta_rows, (1, 0, 2))[..., None])
    ).astype(jnp.bfloat16)
    query_part = jnp.einsum(
        "grjk,kgd->rgjd", score_grad, rows_of_keys, preferred_element_type=jnp.float32
    ) * HEAD_SIZE ** (-0.5)
    key_part = jnp.einsum(
        "grjk,rgjd->kgd", score_grad, query_rows, preferred_element_type=jnp.float32
    ) * HEAD_SIZE ** (-0.5)
    value_part = jnp.einsum(
        "grjk,rgjd->kgd",
        probabilities.astype(jnp.bfloat16),
        attended_grad,
        preferred_element_type=jnp.float32,
    )
    return (query_part, key_part, value_part)


def backward_block(
    block_of_keys,
    source_ctx,
    own_ctx,
    query_rows,
    attended_grad,
    log_total,
    delta_rows,
    own_places,
    ctx_count,
):
    rows_of_keys, rows_of_values = split_block(block_of_keys)
    device_count, _, rows_per_half, _ = block_of_keys.shape
    hidden_width = KEY_VALUE_HEADS * HEAD_SIZE

    def backward_earlier():
        query_part, key_part, value_part = attend_back(
            query_rows,
            attended_grad,
            log_total,
            delta_rows,
            rows_of_keys[:, 0].reshape(-1, KEY_VALUE_HEADS, HEAD_SIZE),
            rows_of_values[:, 0].reshape(-1, KEY_VALUE_HEADS, HEAD_SIZE),
            None,
        )
        early_grad = jnp.concatenate(
            [
                key_part.reshape(device_count, 1, rows_per_half, hidden_width),
                value_part.reshape(device_count, 1, rows_per_half, hidden_width),
            ],
            axis=-1,
        )
        return (query_part, jnp.concatenate([early_grad, jnp.zeros_like(early_grad)], axis=1))

    def backward_later():
        query_part, key_part, value_part = attend_back(
            query_rows[rows_per_half:],
            attended_grad[rows_per_half:],
            log_total[rows_per_half:],
            delta_rows[rows_per_half:],
            rows_of_keys.reshape(-1, KEY_VALUE_HEADS, HEAD_SIZE),
            rows_of_values.reshape(-1, KEY_VALUE_HEADS, HEAD_SIZE),
            None,
        )
        query_part = jnp.concatenate([jnp.zeros_like(query_part), query_part], axis=0)
        return (
            query_part,
            jnp.concatenate(
                [
                    key_part.reshape(device_count, 2, rows_per_half, hidden_width),
                    value_part.reshape(device_count, 2, rows_per_half, hidden_width),
                ],
                axis=-1,
            ),
        )

    def backward_diagonal():
        key_places = block_places(source_ctx, 2 * rows_per_half, ctx_count, device_count)
        causal_visible = own_places[:, None] >= key_places[None, :]
        query_part, key_part, value_part = attend_back(
            query_rows,
            attended_grad,
            log_total,
            delta_rows,
            rows_of_keys.reshape(-1, KEY_VALUE_HEADS, HEAD_SIZE),
            rows_of_values.reshape(-1, KEY_VALUE_HEADS, HEAD_SIZE),
            causal_visible,
        )
        return (
            query_part,
            jnp.concatenate(
                [
                    key_part.reshape(device_count, 2, rows_per_half, hidden_width),
                    value_part.reshape(device_count, 2, rows_per_half, hidden_width),
                ],
                axis=-1,
            ),
        )

    branch_index = jnp.where(source_ctx == own_ctx, 2, jnp.where(source_ctx > own_ctx, 1, 0))
    return lax.switch(branch_index, [backward_earlier, backward_later, backward_diagonal])


def per_device(
    inputs,
    attn_gain,
    query_weight,
    key_matrix,
    value_matrix,
    out_weight,
    ffn_gain,
    gate_weight,
    up_weight,
    down_weight,
    cotangent,
):
    ctx_count = lax.axis_size("ctx")
    device_count = lax.axis_size("ws")
    own_ctx = lax.axis_index("ctx")
    own_member = lax.axis_index("ws")
    micro_count, count_of_rows, _ = inputs.shape
    rows_per_half = count_of_rows // 2
    queries_per_group = QUERY_HEADS // KEY_VALUE_HEADS
    hidden_width = KEY_VALUE_HEADS * HEAD_SIZE
    own_places = query_places(own_ctx, own_member, count_of_rows, ctx_count, device_count)
    cosine_table, sine_table = rotary_tables(own_places)
    grad_sums = None
    layer_outs = []
    input_grads = []
    for micro_batch in range(micro_count):
        gathered = (
            lax.all_gather(attn_gain, ("ctx", "ws"), axis=0, tiled=True),
            lax.all_gather(query_weight, ("ctx", "ws"), axis=0, tiled=True),
            lax.all_gather(key_matrix, ("ctx", "ws"), axis=0, tiled=True),
            lax.all_gather(value_matrix, ("ctx", "ws"), axis=0, tiled=True),
            lax.all_gather(out_weight, ("ctx", "ws"), axis=0, tiled=True),
            lax.all_gather(ffn_gain, ("ctx", "ws"), axis=0, tiled=True),
            lax.all_gather(gate_weight, ("ctx", "ws"), axis=0, tiled=True),
            lax.all_gather(up_weight, ("ctx", "ws"), axis=0, tiled=True),
            lax.all_gather(down_weight, ("ctx", "ws"), axis=0, tiled=True),
        )
        (
            full_attn_gain,
            full_query,
            complete_key,
            full_value,
            full_out,
            full_ffn_gain,
            full_gate,
            full_up,
            full_down,
        ) = gathered
        first_gain = full_attn_gain.astype(jnp.float32)
        second_gain = full_ffn_gain.astype(jnp.float32)
        layer_rows = inputs[micro_batch].astype(jnp.float32)
        normalized_rows, first_inverse = normalize(layer_rows, first_gain)
        normalized_reduced = normalized_rows.astype(jnp.bfloat16)
        query_rows = rotate(
            matrix_multiply(normalized_reduced, full_query).reshape(
                count_of_rows, QUERY_HEADS, HEAD_SIZE
            ),
            cosine_table,
            sine_table,
        )
        query_rows = query_rows.astype(jnp.bfloat16).reshape(
            count_of_rows, KEY_VALUE_HEADS, queries_per_group, HEAD_SIZE
        )
        rows_of_keys = rotate(
            matrix_multiply(normalized_reduced, complete_key).reshape(
                count_of_rows, KEY_VALUE_HEADS, HEAD_SIZE
            ),
            cosine_table,
            sine_table,
        ).astype(jnp.bfloat16)
        rows_of_values = matrix_multiply(normalized_reduced, full_value).astype(jnp.bfloat16)
        local_block = jnp.concatenate(
            [rows_of_keys.reshape(count_of_rows, hidden_width), rows_of_values], axis=-1
        )
        group_block = lax.all_gather(local_block, "ws", axis=0, tiled=True).reshape(
            device_count, 2, rows_per_half, 2 * hidden_width
        )

        def fold_step(carried, shard_piece):

            def visit_block(state_now, block_entry):
                block_of_keys, source_ctx = block_entry
                return (
                    forward_block(
                        state_now,
                        block_of_keys,
                        source_ctx,
                        own_ctx,
                        query_rows,
                        own_places,
                        ctx_count,
                    ),
                    None,
                )

            source_list = jnp.arange(shard_piece.shape[0], dtype=jnp.int32)
            result_state, _ = lax.scan(visit_block, carried, (shard_piece, source_list))
            return result_state

        row_max, row_total, mixture = fold_step(
            empty_part(count_of_rows), lax.all_gather(group_block[None], "ctx", axis=0, tiled=True)
        )
        attended = mixture / row_total[..., None]
        log_total = row_max + jnp.log(row_total)
        attended_low = attended.astype(jnp.bfloat16).reshape(count_of_rows, QUERY_HEADS * HEAD_SIZE)
        middle = layer_rows + matrix_multiply(attended_low, full_out)
        hidden, second_inverse = normalize(middle, second_gain)
        hidden_low = hidden.astype(jnp.bfloat16)
        gate_rows = matrix_multiply(hidden_low, full_gate)
        up_rows = matrix_multiply(hidden_low, full_up)
        sigmoid_gate = jax.nn.sigmoid(gate_rows)
        silu_gate = gate_rows * sigmoid_gate
        activated = (silu_gate * up_rows).astype(jnp.bfloat16)
        layer_outs.append((middle + matrix_multiply(activated, full_down)).astype(jnp.bfloat16))
        upstream_low = cotangent[micro_batch]
        upstream = upstream_low.astype(jnp.float32)
        down_sum = outer_sum(activated, upstream_low)
        act_grad = back_product(upstream_low, full_down)
        gate_low = (
            act_grad * up_rows * sigmoid_gate * (1.0 + gate_rows * (1.0 - sigmoid_gate))
        ).astype(jnp.bfloat16)
        up_low = (act_grad * silu_gate).astype(jnp.bfloat16)
        gate_sum = outer_sum(hidden_low, gate_low)
        up_sum = outer_sum(hidden_low, up_low)
        hidden_grad = back_product(gate_low, full_gate) + back_product(up_low, full_up)
        middle_part, ffn_gain_sum = normalize_back(middle, second_inverse, second_gain, hidden_grad)
        middle_grad = middle_part + upstream
        branch_low = middle_grad.astype(jnp.bfloat16)
        out_sum = outer_sum(attended_low, branch_low)
        attended_grad = (
            back_product(branch_low, full_out)
            .reshape(count_of_rows, KEY_VALUE_HEADS, queries_per_group, HEAD_SIZE)
            .astype(jnp.bfloat16)
        )
        delta_rows = jnp.sum(attended_grad.astype(jnp.float32) * attended, axis=-1)

        def cycle_step(turn_index, carried):
            block_of_keys, block_grad, query_total = carried
            source_ctx = (own_ctx - turn_index) % ctx_count
            query_part, block_part = backward_block(
                block_of_keys,
                source_ctx,
                own_ctx,
                query_rows,
                attended_grad,
                log_total,
                delta_rows,
                own_places,
                ctx_count,
            )
            block_grad = block_grad + block_part
            next_block = shifted(block_of_keys, "ctx", 1)
            next_grad = shifted(as_sent(block_grad), "ctx", 1).astype(block_grad.dtype)
            return (next_block, next_grad, query_total + query_part)

        cycle_start = (
            group_block,
            jnp.zeros(group_block.shape, jnp.float32),
            jnp.zeros((count_of_rows, KEY_VALUE_HEADS, queries_per_group, HEAD_SIZE), jnp.float32),
        )
        _, block_grad, query_total = lax.fori_loop(0, ctx_count, cycle_step, cycle_start)
        local_gradient = (
            lax.psum_scatter(block_grad.astype(jnp.bfloat16), "ws", scatter_dimension=0, tiled=True)
            .astype(jnp.float32)
            .reshape(count_of_rows, 2 * hidden_width)
        )
        key_low = rotate_back(
            local_gradient[:, :hidden_width].reshape(count_of_rows, KEY_VALUE_HEADS, HEAD_SIZE),
            cosine_table,
            sine_table,
        )
        key_low = key_low.astype(jnp.bfloat16).reshape(count_of_rows, hidden_width)
        value_low = local_gradient[:, hidden_width:].astype(jnp.bfloat16)
        query_low = rotate_back(
            query_total.reshape(count_of_rows, QUERY_HEADS, HEAD_SIZE), cosine_table, sine_table
        )
        query_low = query_low.astype(jnp.bfloat16).reshape(count_of_rows, QUERY_HEADS * HEAD_SIZE)
        query_sum = outer_sum(normalized_reduced, query_low)
        key_sum = outer_sum(normalized_reduced, key_low)
        value_sum = outer_sum(normalized_reduced, value_low)
        normed_grad = (
            back_product(query_low, full_query)
            + back_product(key_low, complete_key)
            + back_product(value_low, full_value)
        )
        input_part, attn_gain_sum = normalize_back(
            layer_rows, first_inverse, first_gain, normed_grad
        )
        input_grads.append((middle_grad + input_part).astype(jnp.bfloat16))
        batch_terms = (
            attn_gain_sum,
            query_sum,
            key_sum,
            value_sum,
            out_sum,
            ffn_gain_sum,
            gate_sum,
            up_sum,
            down_sum,
        )
        if grad_sums is None:
            grad_sums = batch_terms
        else:
            grad_sums = tuple(
                (
                    earlier_sum + batch_term
                    for earlier_sum, batch_term in zip(grad_sums, batch_terms)
                )
            )
    owned_grads = (
        lax.psum_scatter(grad_sums[0], ("ctx", "ws"), scatter_dimension=0, tiled=True),
        lax.psum_scatter(grad_sums[1], ("ctx", "ws"), scatter_dimension=0, tiled=True),
        lax.psum_scatter(grad_sums[2], ("ctx", "ws"), scatter_dimension=0, tiled=True),
        lax.psum_scatter(grad_sums[3], ("ctx", "ws"), scatter_dimension=0, tiled=True),
        lax.psum_scatter(grad_sums[4], ("ctx", "ws"), scatter_dimension=0, tiled=True),
        lax.psum_scatter(grad_sums[5], ("ctx", "ws"), scatter_dimension=0, tiled=True),
        lax.psum_scatter(grad_sums[6], ("ctx", "ws"), scatter_dimension=0, tiled=True),
        lax.psum_scatter(grad_sums[7], ("ctx", "ws"), scatter_dimension=0, tiled=True),
        lax.psum_scatter(grad_sums[8], ("ctx", "ws"), scatter_dimension=0, tiled=True),
    )
    return (
        jnp.stack(layer_outs),
        jnp.stack(input_grads),
        owned_grads[0],
        owned_grads[1],
        owned_grads[2],
        owned_grads[3],
        owned_grads[4],
        owned_grads[5],
        owned_grads[6],
        owned_grads[7],
        owned_grads[8],
    )


MESH = pl.DeviceIdType.MESH
NEG = -1e30
WIDE = 128
VMEM_LIMIT = 61 * 1024 * 1024


def fits_fast(mesh):
    return mesh.shape["ctx"] == 8 and mesh.shape["ws"] == 4


def place():
    c = lax.axis_index("ctx")
    w = lax.axis_index("ws")
    return c // 2, lax.rem(c, 2), w // 2, lax.rem(w, 2)


def device(z, y, x, k):
    return (z * 2 + y, x * 2 + k)


def greet(zn):
    z, y, x, k = place()
    others = [device(lax.rem(z + j, zn), y, x, k) for j in range(1, zn)]
    others += [device(z, y, 1 - x, k), device(z, 1 - y, x, k), device(z, y, x, 1 - k)]
    barrier = pltpu.get_barrier_semaphore()
    for other in others:
        pl.semaphore_signal(barrier, inc=1, device_id=other, device_id_type=MESH)
    pl.semaphore_wait(barrier, len(others))


def remote(src, dst, send, recv, where):
    return pltpu.make_async_remote_copy(
        src_ref=src, dst_ref=dst, send_sem=send, recv_sem=recv, device_id=where, device_id_type=MESH
    )


class Gather:
    SEMS = 12

    def __init__(self, src, dst, send, recv, zn):
        z, y, x, k = place()
        own = dst.at[z, y, x, k]
        hz = zn // 2
        xn, yn, sib = device(z, y, 1 - x, k), device(z, 1 - y, x, k), device(z, y, x, 1 - k)

        def push(i, ref, where):
            return remote(ref, ref, send.at[i], recv.at[i], where)

        def col(yy, xx, lo=0, n=zn):
            return dst.at[pl.ds(lo, n), yy, xx, k]

        self.local = pltpu.make_async_copy(src(z), own, send.at[0])
        self.along = []
        for j in range(1, zn):
            zz = lax.rem(z + j, zn)
            self.along.append(remote(src(zz), own, send.at[j], recv.at[j], device(zz, y, x, k)))
        self.cols = [push(4, col(y, x), xn), push(5, col(y, x), yn)]
        self.corner = [push(7, col(1 - y, x, 0, hz), xn), push(8, col(y, 1 - x, hz, hz), yn)]
        self.twin_own = push(6, col(y, x), sib)
        self.twin_cols = [push(9, col(y, 1 - x), sib), push(10, col(1 - y, x), sib)]
        self.twin_corner = push(11, col(1 - y, 1 - x), sib)

    def stage(self, n):
        if n == 0:
            self.local.start()
            for c in self.along:
                c.start()
        elif n == 1:
            self.local.wait()
            for c in self.along:
                c.wait_recv()
            for c in self.cols:
                c.start()
            self.twin_own.start()
        elif n == 2:
            for c in self.cols:
                c.wait_recv()
            for c in self.corner:
                c.start()
            for c in self.twin_cols:
                c.start()
        elif n == 3:
            for c in self.corner:
                c.wait_recv()
            self.twin_corner.start()
        elif n == 4:
            for c in [self.twin_own] + self.twin_cols + [self.twin_corner]:
                c.wait_recv()
            for c in (
                self.along
                + self.cols
                + self.corner
                + [self.twin_own]
                + self.twin_cols
                + [self.twin_corner]
            ):
                c.wait_send()


def stage_step(items, stages, t):
    for n in range(stages):
        if 0 <= t - n < len(items):
            items[t - n].stage(n)


def run_stages(items, stages):
    for t in range(len(items) + stages - 1):
        stage_step(items, stages, t)


def pieces_of(rows, cols, nrow, ncol):
    return [
        (i * (rows // nrow), rows // nrow, j * (cols // ncol), cols // ncol)
        for i in range(nrow)
        for j in range(ncol)
    ]


def gather_item(ref, out, r0, nr, c0, nc, send, recv, zn):
    src = ref.at[pl.ds(r0, nr), pl.ds(c0, nc)]
    dst = out.at[:, :, :, :, pl.ds(r0, nr), pl.ds(c0, nc)]
    return Gather(lambda zz: src, dst, send, recv, zn)


class Exchange:
    def __init__(self, src, dst, send, recv, zn):
        z, y, x, k = place()
        self.local = pltpu.make_async_copy(src(z), dst(z), send.at[0])
        self.along = []
        for j in range(1, zn):
            zz = lax.rem(z + j, zn)
            self.along.append(remote(src(zz), dst(z), send.at[j], recv.at[j], device(zz, y, x, k)))

    def start(self):
        self.local.start()
        for c in self.along:
            c.start()

    def arrived(self):
        self.local.wait()
        for c in self.along:
            c.wait_recv()

    def sent(self):
        for c in self.along:
            c.wait_send()


def gather_all(arrays, rows_used, cuts, collective_id):
    zn = lax.axis_size("ctx") // 2
    n = len(arrays)
    work = [
        (a, piece)
        for a in range(n)
        for piece in pieces_of(rows_used[a], arrays[a].shape[1], *cuts[a])
    ]

    def kernel(*refs):
        ins, outs, (send, recv) = refs[:n], refs[n : 2 * n], refs[2 * n :]
        greet(zn)
        items = []
        for i, (a, (r0, nr, c0, nc)) in enumerate(work):
            items.append(gather_item(ins[a], outs[a], r0, nr, c0, nc, send.at[i], recv.at[i], zn))
        run_stages(items, 5)

    return pl.pallas_call(
        kernel,
        out_shape=[
            jax.ShapeDtypeStruct((zn, 2, 2, 2, rows_used[a], arrays[a].shape[1]), arrays[a].dtype)
            for a in range(n)
        ],
        in_specs=[pl.BlockSpec(memory_space=pl.ANY)] * n,
        out_specs=[pl.BlockSpec(memory_space=pl.ANY)] * n,
        scratch_shapes=[
            pltpu.SemaphoreType.DMA((len(work), Gather.SEMS)),
            pltpu.SemaphoreType.DMA((len(work), Gather.SEMS)),
        ],
        compiler_params=pltpu.CompilerParams(
            collective_id=collective_id, has_side_effects=True, vmem_limit_bytes=VMEM_LIMIT
        ),
    )(*arrays)


class Scatter:
    SEMS = 10

    @staticmethod
    def scratch(zn, nr, nc):
        b = jnp.bfloat16
        return [
            pltpu.VMEM((zn, 2, 2, nr, nc), b),
            pltpu.VMEM((zn, 2, 2, nr, nc), b),
            pltpu.VMEM((2, zn // 2, nr, nc), b),
            pltpu.VMEM((2, zn, nr, nc), b),
            pltpu.VMEM((zn - 1, nr, nc), b),
        ]

    def __init__(self, part, out, bufs, send, recv, zn, give=None):
        z, y, x, k = self.at = place()
        self.zn = zn
        hz = zn // 2
        xn, yn, sib = device(z, y, 1 - x, k), device(z, 1 - y, x, k), device(z, y, x, 1 - k)
        self.held, self.twin, self.corners, self.colsums, self.ends = held, twin, corners, colsums, ends = bufs
        self.out = out
        self.load = None
        if give is None:
            self.load = pltpu.make_async_copy(part.at[:, :, :, k], held, send.at[0])
            give = part.at[:, :, :, 1 - k]
        self.to_twin = remote(give, twin, send.at[1], recv.at[1], sib)
        self.to_corner = [
            remote(held.at[pl.ds(0, hz), 1 - y, 1 - x], corners.at[0], send.at[2], recv.at[2], yn),
            remote(held.at[pl.ds(hz, hz), 1 - y, 1 - x], corners.at[1], send.at[3], recv.at[3], xn),
        ]
        self.to_col = [
            remote(held.at[:, y, 1 - x], colsums.at[0], send.at[4], recv.at[4], xn),
            remote(held.at[:, 1 - y, x], colsums.at[1], send.at[5], recv.at[5], yn),
        ]
        self.along = []
        for j in range(1, zn):
            zz = lax.rem(z + j, zn)
            dst = out.at[z] if ends is None else ends.at[j - 1]
            self.along.append(
                remote(held.at[zz, y, x], dst, send.at[5 + j], recv.at[5 + j], device(zz, y, x, k))
            )
        self.last = pltpu.make_async_copy(held.at[z, y, x], out.at[z], send.at[0]) if ends is None else None

    def stage(self, n):
        z, y, x, k = self.at
        zn, hz = self.zn, self.zn // 2
        held = self.held
        if n == 0:
            self.to_twin.start()
            if self.load is not None:
                self.load.start()
        elif n == 1:
            if self.load is not None:
                self.load.wait()
            self.to_twin.wait_recv()

            def add(i, _):
                for yy in range(2):
                    for xx in range(2):
                        held[i, yy, xx] = held[i, yy, xx] + self.twin[i, yy, xx]
                return 0

            lax.fori_loop(0, zn, add, 0)
            for c in self.to_corner:
                c.start()
        elif n == 2:
            for c in self.to_corner:
                c.wait_recv()
            for i in range(hz):
                held[i, y, 1 - x] = held[i, y, 1 - x] + self.corners[0, i]
                held[hz + i, 1 - y, x] = held[hz + i, 1 - y, x] + self.corners[1, i]
            for c in self.to_col:
                c.start()
        elif n == 3:
            for c in self.to_col:
                c.wait_recv()

            def add(i, _):
                f = jnp.float32
                held[i, y, x] = (
                    held[i, y, x].astype(f) + self.colsums[0, i].astype(f) + self.colsums[1, i].astype(f)
                ).astype(jnp.bfloat16)
                return 0

            lax.fori_loop(0, zn, add, 0)
            for c in self.along:
                c.start()
            if self.last is not None:
                self.last.start()
        elif n == 4:
            for c in self.along:
                c.wait_recv()
            if self.last is not None:
                self.last.wait()
            else:
                total = held[z, y, x].astype(jnp.float32)
                for j in range(zn - 1):
                    total = total + self.ends[j].astype(jnp.float32)
                self.out[...] = total
            for c in [self.to_twin] + self.to_corner + self.to_col + self.along:
                c.wait_send()


def scatter_all(parts, cuts, collective_id):
    zn = lax.axis_size("ctx") // 2
    n = len(parts)
    work = [
        (a, piece) for a in range(n) for piece in pieces_of(*parts[a].shape[4:], *cuts[a])
    ]
    scratch = []
    for a, (r0, nr, c0, nc) in work:
        scratch += Scatter.scratch(zn, nr, nc)

    def kernel(*refs):
        ins, outs, bufs, (send, recv) = refs[:n], refs[n : 2 * n], refs[2 * n : -2], refs[-2:]
        greet(zn)
        items = []
        for i, (a, (r0, nr, c0, nc)) in enumerate(work):
            part = ins[a].at[:, :, :, :, pl.ds(r0, nr), pl.ds(c0, nc)]
            out = outs[a].at[pl.ds(r0, nr), pl.ds(c0, nc)]
            items.append(Scatter(part, out, bufs[5 * i : 5 * i + 5], send.at[i], recv.at[i], zn))
        run_stages(items, 5)

    return pl.pallas_call(
        kernel,
        out_shape=[jax.ShapeDtypeStruct(p.shape[4:], jnp.float32) for p in parts],
        in_specs=[pl.BlockSpec(memory_space=pl.ANY)] * n,
        out_specs=[pl.BlockSpec(memory_space=pltpu.VMEM)] * n,
        scratch_shapes=scratch
        + [
            pltpu.SemaphoreType.DMA((len(work), Scatter.SEMS)),
            pltpu.SemaphoreType.DMA((len(work), Scatter.SEMS)),
        ],
        compiler_params=pltpu.CompilerParams(
            collective_id=collective_id, has_side_effects=True, vmem_limit_bytes=VMEM_LIMIT
        ),
    )(*parts)


NT = (((1,), (1,)), ((), ()))
PER = QUERY_HEADS // KEY_VALUE_HEADS
HALF_GROUPS = KEY_VALUE_HEADS // 2
HALF_HEADS = QUERY_HEADS // 2
KV_LANES = 2 * HALF_GROUPS * HEAD_SIZE


def lane_slot(n):
    return n // 2, n % 2


def key_slot(g):
    return lane_slot(g)


def value_slot(g):
    return lane_slot(HALF_GROUPS + g)


def pair_index(half, zp):
    return zp if half == 0 else 3 - zp


def pair_tile(src, g, half, zp):
    tiles = []
    for j in range(PER):
        lo = HEAD_SIZE * (PER * g + j)
        a = src[2 * zp, lo : lo + HEAD_SIZE, :].astype(jnp.float32)
        b = src[2 * zp + 1, lo : lo + HEAD_SIZE, :].astype(jnp.float32)
        low = lax.broadcasted_iota(jnp.int32, a.shape, 1) < WIDE // 2
        if half == 0:
            tiles.append(jnp.where(low, a, pltpu.roll(b, WIDE // 2, 1)))
        else:
            tiles.append(jnp.where(low, pltpu.roll(a, WIDE // 2, 1), b))
    return jnp.concatenate(tiles, axis=1)


def unpair(get, dst):
    for zp in range(2):
        for g in range(HALF_GROUPS):
            first, second = get(g, pair_index(0, zp)), get(g, pair_index(1, zp))
            for j in range(PER):
                lo = HEAD_SIZE * (PER * g + j)
                a, b = first[:, WIDE * j : WIDE * j + WIDE], second[:, WIDE * j : WIDE * j + WIDE]
                low = lax.broadcasted_iota(jnp.int32, a.shape, 1) < WIDE // 2
                even = jnp.where(low, a, pltpu.roll(b, WIDE // 2, 1))
                odd = jnp.where(low, pltpu.roll(a, WIDE // 2, 1), b)
                dst[2 * zp, lo : lo + HEAD_SIZE, :] = even.astype(dst.dtype)
                dst[2 * zp + 1, lo : lo + HEAD_SIZE, :] = odd.astype(dst.dtype)


def set_padded(dst, g, p, tile, side):
    tile = tile.astype(dst.dtype)
    dst[g, p, side * HEAD_SIZE : (side + 1) * HEAD_SIZE, :] = tile
    dst[g, p, (1 - side) * HEAD_SIZE : (2 - side) * HEAD_SIZE, :] = jnp.zeros_like(tile)


def walk(t, y, cn):
    b1, b2, b3 = 3 + y, 10 + 2 * y, 22 + y
    p = (t >= b1).astype(jnp.int32) + (t >= b2).astype(jnp.int32) + (t >= b3).astype(jnp.int32)
    j = t - jnp.where(p == 0, 0, jnp.where(p == 1, b1, jnp.where(p == 2, b2, b3)))
    zp = jnp.where(p < 2, p, 3 - p)
    low = jnp.where(p < 2, 4 * zp + y, 2 * cn - 3 - 4 * zp - y)
    late = (j >= cn).astype(jnp.int32)
    src = jnp.where(late == 1, 2 * cn - 1 - j, j)
    return p, j, src // 2, lax.rem(src, 2), pl.multiple_of(late * HEAD_SIZE, HEAD_SIZE), j >= low


STEPS = 38


def visible(p, j, y, w, cn, wn, rows):
    shape = (wn * rows, PER * WIDE)
    lane = lax.rem(lax.broadcasted_iota(jnp.int32, shape, 1), WIDE)
    zp = jnp.where(p < 2, p, 3 - p)
    c = 2 * (2 * zp + lane // rows) + y
    span = jnp.where(p < 2, c, 2 * cn - 1 - c)
    query = span * (wn * rows) + w * rows + lax.rem(lane, rows)
    key = j * (wn * rows) + lax.broadcasted_iota(jnp.int32, shape, 0)
    return key <= query


def key_block(kvg, zz, yy, late, rows, block):
    t = kvg[zz, yy, :, :, pl.ds(late, rows), WIDE * block : WIDE * block + WIDE]
    return t.reshape(4 * rows, WIDE)


def turned(t):
    return t.astype(jnp.float32).T.astype(t.dtype)


def by_span(body, kvg, cn, rows):
    def one(j, _):
        late = (j >= cn).astype(jnp.int32)
        src = jnp.where(late == 1, 2 * cn - 1 - j, j)
        at = pl.multiple_of(late * rows, rows)
        body(j, lambda b: key_block(kvg, src // 2, lax.rem(src, 2), at, rows, b))
        return 0

    lax.fori_loop(0, 2 * cn, one, 0)


def gather_attend(q, kv, arrays, used, cuts, collective_id):
    cn, wn = lax.axis_size("ctx"), lax.axis_size("ws")
    zn = cn // 2
    mbs, q_rows, tokens = q.shape
    rows = tokens // 2
    mine = q_rows // 2
    n = len(arrays)
    f32, b16 = jnp.float32, jnp.bfloat16
    work = [(a, piece) for a in range(n) for piece in pieces_of(used[a], arrays[a].shape[1], *cuts[a])]
    groups = range(HALF_GROUPS)

    def kernel(*refs):
        q_ref, kv_ref = refs[:2]
        ins = refs[2 : 2 + n]
        o_out, q_out, kv_out, oh_out, lse_out = refs[2 + n : 7 + n]
        outs = refs[7 + n : 7 + 2 * n]
        qh, kvg, oh, qpad, vt, m_s, l_s, acc, send, recv, xs, xr, ks, kr, save = refs[7 + 2 * n :]
        greet(zn)
        z, y, x, k = place()
        w = 2 * x + k

        def lanes_of(zz):
            return kv_ref.at[zz // 2, :, pl.ds(pl.multiple_of(lax.rem(zz, 2) * KV_LANES, WIDE), KV_LANES)]

        def heads_of(ref, zz):
            return ref.at[zz // 2, pl.ds(pl.multiple_of(lax.rem(zz, 2) * mine, 16), mine), :]

        items = [
            gather_item(ins[a], outs[a], r0, nr, c0, nc, send.at[i], recv.at[i], zn)
            for i, (a, (r0, nr, c0, nc)) in enumerate(work)
        ]
        kvx = Gather(lanes_of, kvg, ks, kr, zn)
        qx = Exchange(lambda zz: heads_of(q_ref, zz), lambda zz: qh.at[zz], xs.at[0], xr.at[0], zn)
        ox = Exchange(lambda zz: oh.at[zz], lambda zz: heads_of(o_out, zz), xs.at[1], xr.at[1], zn)
        kvx.stage(0)
        qx.start()
        stage_step(items, 5, 0)
        m_s[...] = jnp.full(m_s.shape, NEG, f32)
        l_s[...] = jnp.zeros(l_s.shape, f32)
        acc[...] = jnp.zeros(acc.shape, f32)
        kvx.stage(1)
        kvx.stage(2)
        stage_step(items, 5, 1)
        kvx.stage(3)
        qx.arrived()
        for half in range(2):
            for zp in range(2):
                for g in groups:
                    set_padded(qpad, g, pair_index(half, zp), pair_tile(qh, g, half, zp), key_slot(g)[1])
        kvx.stage(4)

        def turn(j, block):
            flat = {b: turned(block(b)) for b in sorted({value_slot(g)[0] for g in groups})}
            for g in groups:
                b, side = value_slot(g)
                vt[j, g] = flat[b][side * HEAD_SIZE : (side + 1) * HEAD_SIZE]

        by_span(turn, kvg, cn, rows)
        saves = [
            pltpu.make_async_copy(qh, q_out, save.at[0]),
            pltpu.make_async_copy(kvg, kv_out, save.at[1]),
        ]
        for s in saves:
            s.start()

        def step(t, _):
            p, j, zz, yy, late, edge = walk(t, y, cn)

            def run(masked):
                seen = visible(p, j, y, w, cn, wn, rows) if masked else None
                for g in groups:
                    s = jnp.dot(
                        key_block(kvg, zz, yy, late, rows, key_slot(g)[0]), qpad[g, p], preferred_element_type=f32
                    )
                    if masked:
                        s = jnp.where(seen, s, NEG)
                    m_old = m_s[g, p]
                    m_new = jnp.maximum(m_old, jnp.max(s, axis=0, keepdims=True))
                    alpha = jnp.exp(m_old - m_new)
                    e = jnp.exp(s - m_new)
                    m_s[g, p] = m_new
                    l_s[g, p] = l_s[g, p] * alpha + jnp.sum(e, axis=0, keepdims=True)
                    acc[g, p] = acc[g, p] * alpha + jnp.dot(
                        vt[j, g], e.astype(b16), preferred_element_type=f32
                    )

            pl.when(edge)(lambda: run(True))
            pl.when(jnp.logical_not(edge))(lambda: run(False))
            return 0

        last = len(items) + 4
        t = 0
        for s in range(2, last):
            upto = min(STEPS, 5 * (s - 1))
            if t < upto:
                lax.fori_loop(t, upto, step, 0)
                t = upto
                if t == STEPS:
                    unpair(lambda g, p: acc[g, p] / l_s[g, p], oh)
                    ox.start()
                    saves.append(pltpu.make_async_copy(oh, oh_out, save.at[2]))
                    saves[-1].start()
                    lse_out[...] = m_s[...] + jnp.log(l_s[...])
            stage_step(items, 5, s)
        ox.arrived()
        ox.sent()
        qx.sent()
        for s in saves:
            s.wait()

    stat = (HALF_GROUPS, 4, 1, PER * WIDE)
    block = (zn, mine, tokens)
    kv_shape = (zn, 2, 2, 2, tokens, KV_LANES)
    any_ = pl.BlockSpec(memory_space=pl.ANY)
    return pl.pallas_call(
        kernel,
        out_shape=[
            jax.ShapeDtypeStruct(q.shape, b16),
            jax.ShapeDtypeStruct(block, b16),
            jax.ShapeDtypeStruct(kv_shape, b16),
            jax.ShapeDtypeStruct(block, b16),
            jax.ShapeDtypeStruct(stat, f32),
        ]
        + [
            jax.ShapeDtypeStruct((zn, 2, 2, 2, used[a], arrays[a].shape[1]), arrays[a].dtype)
            for a in range(n)
        ],
        in_specs=[any_] * (2 + n),
        out_specs=[any_] * 4 + [pl.BlockSpec(memory_space=pltpu.VMEM)] + [any_] * n,
        scratch_shapes=[
            pltpu.VMEM(block, b16),
            pltpu.VMEM(kv_shape, b16),
            pltpu.VMEM(block, b16),
            pltpu.VMEM((HALF_GROUPS, 4, WIDE, PER * WIDE), b16),
            pltpu.VMEM((2 * cn, HALF_GROUPS, HEAD_SIZE, wn * rows), b16),
            pltpu.VMEM(stat, f32),
            pltpu.VMEM(stat, f32),
            pltpu.VMEM((HALF_GROUPS, 4, HEAD_SIZE, PER * WIDE), f32),
            pltpu.SemaphoreType.DMA((len(work), Gather.SEMS)),
            pltpu.SemaphoreType.DMA((len(work), Gather.SEMS)),
            pltpu.SemaphoreType.DMA((2, zn)),
            pltpu.SemaphoreType.DMA((2, zn)),
            pltpu.SemaphoreType.DMA((Gather.SEMS,)),
            pltpu.SemaphoreType.DMA((Gather.SEMS,)),
            pltpu.SemaphoreType.DMA((3,)),
        ],
        compiler_params=pltpu.CompilerParams(
            collective_id=collective_id, has_side_effects=True, vmem_limit_bytes=VMEM_LIMIT
        ),
    )(q, kv, *arrays)


def scatter_attend(do, qh, kvg, oh, lse, parts, cuts, collective_id):
    cn, wn = lax.axis_size("ctx"), lax.axis_size("ws")
    zn = cn // 2
    mbs, q_rows, tokens = do.shape
    rows = tokens // 2
    mine = q_rows // 2
    n = len(parts)
    f32, b16 = jnp.float32, jnp.bfloat16
    work = [(a, piece) for a in range(n) for piece in pieces_of(*parts[a].shape[4:], *cuts[a])]
    scratch = []
    for a, (r0, nr, c0, nc) in work:
        scratch += Scatter.scratch(zn, nr, nc)
    groups = range(HALF_GROUPS)
    scale = HEAD_SIZE**-0.5

    def kernel(*refs):
        do_ref, qh, kvg, oh, lse_ref = refs[:5]
        ins = refs[5 : 5 + n]
        dq_out, dkv_out = refs[5 + n : 7 + n]
        outs = refs[7 + n : 7 + 2 * n]
        rest = refs[7 + 2 * n :]
        bufs, rest = rest[: len(scratch)], rest[len(scratch) :]
        gh, qt, dot_, qr, dor, kt, delta, dq, dkv, give, kb, send, recv, xs, xr, ks, kr = (
            rest[:10] + (rest[10:14],) + rest[14:]
        )
        dqh = gh
        greet(zn)
        z, y, x, k = place()
        w = 2 * x + k

        def heads_of(ref, zz):
            return ref.at[zz // 2, pl.ds(pl.multiple_of(lax.rem(zz, 2) * mine, 16), mine), :]

        gx = Exchange(lambda zz: heads_of(do_ref, zz), lambda zz: gh.at[zz], xs.at[0], xr.at[0], zn)
        dx = Exchange(lambda zz: dqh.at[zz], lambda zz: heads_of(dq_out, zz), xs.at[1], xr.at[1], zn)
        kvx = Scatter(None, dkv_out, tuple(kb) + (None,), ks, kr, zn, give)
        items = []
        for i, (a, (r0, nr, c0, nc)) in enumerate(work):
            part = ins[a].at[:, :, :, :, pl.ds(r0, nr), pl.ds(c0, nc)]
            out = outs[a].at[pl.ds(r0, nr), pl.ds(c0, nc)]
            items.append(Scatter(part, out, bufs[5 * i : 5 * i + 5], send.at[i], recv.at[i], zn))
        gx.start()
        stage_step(items, 5, 0)
        dq[...] = jnp.zeros(dq.shape, f32)

        def clear(i, _):
            dkv[i] = jnp.zeros(dkv.shape[1:], f32)
            return 0

        lax.fori_loop(0, zn, clear, 0)

        def turn(j, block):
            flat = {b: turned(block(b)) for b in sorted({key_slot(g)[0] for g in groups})}
            for g in groups:
                b, side = key_slot(g)
                kt[j, g] = flat[b][side * HEAD_SIZE : (side + 1) * HEAD_SIZE]

        by_span(turn, kvg, cn, rows)
        stage_step(items, 5, 1)
        gx.arrived()
        for half in range(2):
            for zp in range(2):
                p = pair_index(half, zp)
                for g in groups:
                    g_tile = pair_tile(gh, g, half, zp)
                    o_tile = pair_tile(oh, g, half, zp)
                    delta[g, p] = jnp.sum(g_tile * o_tile, axis=0, keepdims=True)
                    set_padded(qt, g, p, pair_tile(qh, g, half, zp), key_slot(g)[1])
                    set_padded(dot_, g, p, g_tile, value_slot(g)[1])
                    qr[g, p] = turned(qt[g, p])
                    dor[g, p] = turned(dot_[g, p])

        def step(t, _):
            p, j, zz, yy, late, edge = walk(t, y, cn)

            def run(masked):
                seen = visible(p, j, y, w, cn, wn, rows) if masked else None
                blocks = [key_block(kvg, zz, yy, late, rows, b) for b in range(KV_LANES // WIDE)]
                sums = [None] * len(blocks)

                def put(b, v):
                    sums[b] = v if sums[b] is None else sums[b] + v

                for g in groups:
                    s = jnp.dot(blocks[key_slot(g)[0]], qt[g, p], preferred_element_type=f32)
                    if masked:
                        s = jnp.where(seen, s, NEG)
                    e = jnp.exp(s - lse_ref[g, p])
                    dp = jnp.dot(blocks[value_slot(g)[0]], dot_[g, p], preferred_element_type=f32)
                    ds = (e * (dp - delta[g, p])).astype(b16)
                    put(value_slot(g)[0], jnp.dot(e.astype(b16), dor[g, p], preferred_element_type=f32))
                    put(key_slot(g)[0], jnp.dot(ds, qr[g, p], preferred_element_type=f32))
                    dq[g, p] += jnp.dot(kt[j, g], ds, preferred_element_type=f32)
                for b, v in enumerate(sums):
                    dkv[zz, yy, :, :, pl.ds(late, rows), WIDE * b : WIDE * b + WIDE] += v.reshape(
                        2, 2, rows, WIDE
                    )

            pl.when(edge)(lambda: run(True))
            pl.when(jnp.logical_not(edge))(lambda: run(False))
            return 0

        last = len(items) + 4
        t = 0
        kv_stage = 0
        for s in range(2, last):
            upto = min(STEPS, 6 * (s - 1))
            if t < upto:
                lax.fori_loop(t, upto, step, 0)
                t = upto
                if t == STEPS:

                    def pack(i, _):
                        for yy in range(2):
                            for xx in range(2):
                                kb[0][i, yy, xx] = dkv[i, yy, xx, k].astype(b16)
                                give[i, yy, xx] = dkv[i, yy, xx, 1 - k].astype(b16)
                        return 0

                    lax.fori_loop(0, zn, pack, 0)
                    kvx.stage(0)
                    unpair(lambda g, p: dq[g, p] * scale, dqh)
                    dx.start()
                    kv_stage = 1
            elif t == STEPS and kv_stage < 5:
                kvx.stage(kv_stage)
                kv_stage += 1
            stage_step(items, 5, s)
        while kv_stage < 5:
            kvx.stage(kv_stage)
            kv_stage += 1
        dx.arrived()
        dx.sent()
        gx.sent()

    stat = (HALF_GROUPS, 4, 1, PER * WIDE)
    block = (zn, mine, tokens)
    tile = (HALF_GROUPS, 4, WIDE, PER * WIDE)
    tile_t = (HALF_GROUPS, 4, PER * WIDE, WIDE)
    any_ = pl.BlockSpec(memory_space=pl.ANY)
    vmem = pl.BlockSpec(memory_space=pltpu.VMEM)
    return pl.pallas_call(
        kernel,
        out_shape=[
            jax.ShapeDtypeStruct(do.shape, b16),
            jax.ShapeDtypeStruct((zn, tokens, KV_LANES), b16),
        ]
        + [jax.ShapeDtypeStruct(p.shape[4:], f32) for p in parts],
        in_specs=[any_, vmem, vmem, vmem, vmem] + [any_] * n,
        out_specs=[any_, any_] + [vmem] * n,
        scratch_shapes=scratch
        + [
            pltpu.VMEM(block, b16),
            pltpu.VMEM(tile, b16),
            pltpu.VMEM(tile, b16),
            pltpu.VMEM(tile_t, b16),
            pltpu.VMEM(tile_t, b16),
            pltpu.VMEM((2 * cn, HALF_GROUPS, HEAD_SIZE, wn * rows), b16),
            pltpu.VMEM(stat, f32),
            pltpu.VMEM((HALF_GROUPS, 4, HEAD_SIZE, PER * WIDE), f32),
            pltpu.VMEM((zn, 2, 2, 2, tokens, KV_LANES), f32),
            pltpu.VMEM((zn, 2, 2, tokens, KV_LANES), b16),
        ]
        + Scatter.scratch(zn, tokens, KV_LANES)[:4]
        + [
            pltpu.SemaphoreType.DMA((len(work), Scatter.SEMS)),
            pltpu.SemaphoreType.DMA((len(work), Scatter.SEMS)),
            pltpu.SemaphoreType.DMA((2, zn)),
            pltpu.SemaphoreType.DMA((2, zn)),
            pltpu.SemaphoreType.DMA((Scatter.SEMS,)),
            pltpu.SemaphoreType.DMA((Scatter.SEMS,)),
        ],
        compiler_params=pltpu.CompilerParams(
            collective_id=collective_id, has_side_effects=True, vmem_limit_bytes=VMEM_LIMIT
        ),
    )(do, qh, kvg, oh, lse, *parts)


def rotate_lanes(t, cos, low, high):
    quarter = HEAD_SIZE // 2
    return t * cos + jnp.roll(t, -quarter, axis=-1) * low + jnp.roll(t, quarter, axis=-1) * high


def lane_tables(positions):
    quarter = HEAD_SIZE // 2
    frequency = 10000.0 ** (-2.0 * jnp.arange(quarter, dtype=jnp.float32) / HEAD_SIZE)
    angles = positions.astype(jnp.float32)[:, None] * frequency[None, :]
    cos, sin = jnp.cos(angles), jnp.sin(angles)
    none = jnp.zeros_like(sin)

    def full(a, b, still):
        head = jnp.concatenate([a, b], axis=1)
        keys = jnp.tile(head, (1, HALF_GROUPS))
        still = jnp.full_like(keys, still)
        return jnp.concatenate([keys, still, keys, still, jnp.tile(head, (1, QUERY_HEADS))], axis=1)

    return full(cos, cos, 1.0), full(-sin, none, 0.0), full(none, sin, 0.0)


def fast_device(
    inputs,
    attn_gain,
    query_weight,
    key_matrix,
    value_matrix,
    out_weight,
    ffn_gain,
    gate_weight,
    up_weight,
    down_weight,
    cotangent,
):
    f32, b16 = jnp.float32, jnp.bfloat16
    cn, wn = lax.axis_size("ctx"), lax.axis_size("ws")
    dn = cn * wn
    zn = cn // 2
    mbs, tokens, width = inputs.shape
    own = query_weight.shape[0]
    ra = own // 16 * 16
    rb = own - ra
    q_width = query_weight.shape[1]
    hid = KEY_VALUE_HEADS * HEAD_SIZE
    ff = gate_weight.shape[1]
    rows = mbs * tokens
    wa = dn * ra

    new = jnp.arange(width)
    old = jnp.where(
        new < wa, own * (new // ra) + new % ra, own * ((new - wa) // rb) + ra + (new - wa) % rb
    )
    order = (jnp.arange(width)[:, None] == old[None, :]).astype(b16)

    def to_order(t):
        return jnp.dot(t, order, preferred_element_type=f32).astype(t.dtype)

    def from_order(t):
        return lax.dot_general(t, order, NT, preferred_element_type=f32).astype(t.dtype)

    fold = 16 // rb

    def folded(t):
        return t.reshape(t.shape[0], fold, -1).transpose(1, 0, 2).reshape(16, -1)

    qkv_w = q_width + 2 * hid
    pad1 = -qkv_w % (fold * WIDE)
    rest_w = width + 2 * ff
    pad2 = -rest_w % (fold * WIDE)
    moved = to_order(
        jnp.concatenate(
            [inputs.reshape(rows, width), cotangent.reshape(rows, width), out_weight, down_weight]
        )
    )
    x_low, gy_low = moved[:rows], moved[rows : 2 * rows]
    out_p, down_p = moved[2 * rows : 2 * rows + own], moved[2 * rows + own :]
    half_hid = hid // 2
    qkv = jnp.concatenate(
        [
            key_matrix[:, :half_hid],
            value_matrix[:, :half_hid],
            key_matrix[:, half_hid:],
            value_matrix[:, half_hid:],
            query_weight,
        ],
        axis=1,
    )
    gains = jnp.stack([attn_gain, ffn_gain])
    gains = jnp.pad(gains, ((0, rb - 2), (0, pad1 - own)))
    b1 = folded(jnp.concatenate([qkv[ra:], gains], axis=1))
    b2 = folded(
        jnp.pad(
            jnp.concatenate([out_p[ra:], gate_weight[ra:], up_weight[ra:]], axis=1), ((0, 0), (0, pad2))
        )
    )
    qkv_a, b1g = gather_all([qkv, b1], [ra, 16], [(1, 1), (1, 1)], 1)

    def unfolded(t):
        cols = t.shape[-1]
        return t.reshape(dn, fold, rb, cols).transpose(0, 2, 1, 3).reshape(dn * rb, fold * cols)

    flat = lambda t: t.reshape(-1, t.shape[-1])
    qkv_a, b1u = flat(qkv_a), unfolded(b1g)
    qkv_b = b1u[:, :qkv_w]
    gains_all = b1u[:, qkv_w : qkv_w + own].reshape(dn, rb, own)
    in_order = lambda t: jnp.concatenate([t[:, :ra].reshape(-1), t[:, ra:].reshape(-1)]).astype(f32)
    gain1, gain2 = in_order(gains_all[:, 0]), in_order(gains_all[:, 1])

    def mm(h, a, b):
        return matrix_multiply(h[:, :wa], a) + matrix_multiply(h[:, wa:], b)

    def mm_back(g, a, b):
        return jnp.concatenate([back_product(g, a), back_product(g, b)], axis=1)

    c, w = lax.axis_index("ctx"), lax.axis_index("ws")
    places = query_places(c, w, tokens, cn, wn)
    cos, low, high = (jnp.tile(t, (mbs, 1)) for t in lane_tables(places))
    x = x_low.astype(f32)
    hn, inv1 = normalize(x, gain1)
    hn = hn.astype(b16)
    proj = rotate_lanes(mm(hn, qkv_a, qkv_b), cos, low, high)
    kv = proj[:, : 2 * hid].astype(b16).reshape(mbs, tokens, 2 * hid)
    q = (proj[:, 2 * hid :] * HEAD_SIZE**-0.5).astype(b16)
    q = q.reshape(mbs, tokens, q_width).transpose(0, 2, 1)
    o_t, qh, kvg, oh, lse, out_a, gate_a, up_a, down_a, b2g = gather_attend(
        q,
        kv,
        [out_p, gate_weight, up_weight, down_p, b2],
        [ra, ra, ra, down_p.shape[0], 16],
        [(1, 1), (1, 2), (1, 2), (2, 1), (1, 1)],
        2,
    )
    out_a, gate_a, up_a, down_w = map(flat, (out_a, gate_a, up_a, down_a))
    b2u = unfolded(b2g)
    out_b = b2u[:, :width]
    gate_b, up_b = b2u[:, width : width + ff], b2u[:, width + ff : width + 2 * ff]
    o_p = to_order(o_t.transpose(0, 2, 1).reshape(rows, q_width))
    x1 = x + mm(o_p, out_a, out_b)
    h2, inv2 = normalize(x1, gain2)
    h2 = h2.astype(b16)
    gate = mm(h2, gate_a, gate_b)
    up = mm(h2, up_a, up_b)
    sig = jax.nn.sigmoid(gate)
    silu = gate * sig
    act = (silu * up).astype(b16)
    out = from_order((x1 + matrix_multiply(act, down_w)).astype(b16))
    gy = gy_low.astype(f32)
    ga = back_product(gy_low, down_w)
    g_gate = (ga * up * sig * (1.0 + gate * (1.0 - sig))).astype(b16)
    g_up = (ga * silu).astype(b16)
    gh2 = mm_back(g_gate, gate_a, gate_b) + mm_back(g_up, up_a, up_b)
    mid, gain2_sum = normalize_back(x1, inv2, gain2, gh2)
    gx1 = mid + gy
    gb = gx1.astype(b16)
    gattn = from_order(mm_back(gb, out_a, out_b).astype(b16))
    gb_plain = from_order(gb)
    gy_plain = cotangent.reshape(rows, width)

    def sums(h, g):
        first, rest = outer_sum(h[:, :wa], g), outer_sum(h[:, wa:], g)
        return first.astype(b16).reshape(zn, 2, 2, 2, ra, -1), rest.astype(b16)

    def fold_sums(parts):
        t = jnp.concatenate(parts, axis=1)
        return (
            t.reshape(dn, rb, fold, -1).transpose(0, 2, 1, 3).reshape(zn, 2, 2, 2, 16, -1)
        )

    d_out_a, d_out_b = sums(o_p, gb_plain)
    d_gate_a, d_gate_b = sums(h2, g_gate)
    d_up_a, d_up_b = sums(h2, g_up)
    d_down = outer_sum(act, gy_plain).astype(b16).reshape(zn, 2, 2, 2, -1, width)
    d_b2 = fold_sums([d_out_b, d_gate_b, d_up_b, jnp.zeros((dn * rb, pad2), b16)])

    dq, dkv, r_out, r_gate, r_up, r_down, r_b2 = scatter_attend(
        gattn.reshape(mbs, tokens, q_width).transpose(0, 2, 1),
        qh,
        kvg,
        oh,
        lse,
        [d_out_a, d_gate_a, d_up_a, d_down, d_b2],
        [(1, 1), (1, 2), (1, 2), (2, 1), (1, 1)],
        3,
    )
    dkv = dkv.reshape(mbs, 2, tokens, hid).transpose(0, 2, 1, 3).reshape(rows, 2 * hid)
    dq = dq.transpose(0, 2, 1).reshape(rows, q_width)
    g_qkv = rotate_lanes(jnp.concatenate([dkv, dq], axis=1).astype(f32), cos, -low, -high).astype(b16)
    ghn = mm_back(g_qkv, qkv_a, qkv_b)
    first, gain1_sum = normalize_back(x, inv1, gain1, ghn)
    input_grad = from_order((gx1 + first).astype(b16))
    d_qkv_a, d_qkv_b = sums(hn, g_qkv)
    by_owner = lambda t: jnp.concatenate([t[:wa].reshape(dn, ra), t[wa:].reshape(dn, rb)], axis=1)
    gain_sums = jnp.stack([by_owner(gain1_sum), by_owner(gain2_sum)], axis=1).astype(b16)
    gain_sums = jnp.pad(gain_sums, ((0, 0), (0, rb - 2), (0, pad1 - own))).reshape(dn * rb, pad1)
    d_b1 = fold_sums([d_qkv_b, gain_sums])
    r_qkv, r_b1 = scatter_all([d_qkv_a, d_b1], [(1, 1), (1, 1)], 4)

    def own_rows(t):
        return t.reshape(fold, rb, -1).transpose(1, 0, 2).reshape(rb, -1)

    e1, e2 = own_rows(r_b1), own_rows(r_b2)
    whole = lambda a, b: jnp.concatenate([a, b], axis=0)
    d_qkv = whole(r_qkv, e1[:, :qkv_w])
    return (
        out.reshape(inputs.shape),
        input_grad.reshape(inputs.shape),
        e1[0, qkv_w : qkv_w + own],
        d_qkv[:, 2 * hid :],
        jnp.concatenate([d_qkv[:, :half_hid], d_qkv[:, hid : hid + half_hid]], axis=1),
        jnp.concatenate([d_qkv[:, half_hid:hid], d_qkv[:, hid + half_hid : 2 * hid]], axis=1),
        whole(r_out, e2[:, :width]),
        e1[1, qkv_w : qkv_w + own],
        whole(r_gate, e2[:, width : width + ff]),
        whole(r_up, e2[:, width + ff : width + 2 * ff]),
        r_down,
    )


def solution(mesh):
    in_specs = (
        P(None, ("ctx", "ws"), None),
        P(("ctx", "ws")),
        P(("ctx", "ws"), None),
        P(("ctx", "ws"), None),
        P(("ctx", "ws"), None),
        P(("ctx", "ws"), None),
        P(("ctx", "ws")),
        P(("ctx", "ws"), None),
        P(("ctx", "ws"), None),
        P(("ctx", "ws"), None),
        P(None, ("ctx", "ws"), None),
    )
    out_specs = (
        P(None, ("ctx", "ws"), None),
        P(None, ("ctx", "ws"), None),
        P(("ctx", "ws")),
        P(("ctx", "ws"), None),
        P(("ctx", "ws"), None),
        P(("ctx", "ws"), None),
        P(("ctx", "ws"), None),
        P(("ctx", "ws")),
        P(("ctx", "ws"), None),
        P(("ctx", "ws"), None),
        P(("ctx", "ws"), None),
    )
    body = fast_device if fits_fast(mesh) else per_device
    return jax.shard_map(
        body, mesh=mesh, in_specs=in_specs, out_specs=out_specs, check_vma=False
    )
```

```python
import jax
import jax.numpy as jnp
from jax import lax
from jax.experimental import pallas as pl
from jax.experimental.pallas import tpu as pltpu
from jax.sharding import PartitionSpec as P
import functools

QUERY_HEADS = 18
KEY_VALUE_HEADS = 6
HEAD_SIZE = 64


EPSILON = 1e-05
MASKED_SCORE = -1e30


def shifted(block, axis, distance):
    devices = range(lax.axis_size(axis))
    route = [((i - distance) % len(devices), i) for i in devices]
    return lax.ppermute(block, axis, route)


def as_sent(x):

    def short(part):
        return part.astype(jnp.bfloat16) if part.dtype == jnp.float32 else part

    return jax.tree.map(short, x)


def matrix_multiply(left, right):
    return jnp.dot(left, right, preferred_element_type=jnp.float32)


def outer_sum(left, right):
    return jnp.einsum("ri,rj->ij", left, right, preferred_element_type=jnp.float32)


def back_product(gradient, weight):
    return jnp.einsum("rj,ij->ri", gradient, weight, preferred_element_type=jnp.float32)


def normalize(layer_rows, gain_vector):
    inverse = lax.rsqrt(jnp.mean(layer_rows * layer_rows, axis=-1, keepdims=True) + EPSILON)
    return (layer_rows * inverse * gain_vector, inverse)


def normalize_back(layer_rows, inverse, gain_vector, gradient):
    weighted = gradient * gain_vector
    inner_mean = jnp.mean(weighted * layer_rows, axis=-1, keepdims=True)
    row_grad = inverse * weighted - layer_rows * (inverse * inverse * inverse) * inner_mean
    gain_grad = jnp.sum(gradient * layer_rows * inverse, axis=0)
    return (row_grad, gain_grad)


def rotary_tables(token_positions):
    quarter = HEAD_SIZE // 2
    frequency = 10000.0 ** (-2.0 * jnp.arange(quarter, dtype=jnp.float32) / HEAD_SIZE)
    angles = token_positions.astype(jnp.float32)[:, None] * frequency[None, :]
    return (jnp.cos(angles)[:, None, :], jnp.sin(angles)[:, None, :])


def rotate(heads, cosine_table, sine_table):
    quarter = HEAD_SIZE // 2
    first_half = heads[..., :quarter]
    second_half = heads[..., quarter:]
    return jnp.concatenate(
        [
            first_half * cosine_table - second_half * sine_table,
            second_half * cosine_table + first_half * sine_table,
        ],
        axis=-1,
    )


def rotate_back(heads, cosine_table, sine_table):
    quarter = HEAD_SIZE // 2
    first_half = heads[..., :quarter]
    second_half = heads[..., quarter:]
    return jnp.concatenate(
        [
            first_half * cosine_table + second_half * sine_table,
            second_half * cosine_table - first_half * sine_table,
        ],
        axis=-1,
    )


def query_places(own_ctx, own_member, count_of_rows, ctx_count, device_count):
    rows_per_half = count_of_rows // 2
    local_index = jnp.arange(count_of_rows, dtype=jnp.int32)
    span_index = jnp.where(local_index < rows_per_half, own_ctx, 2 * ctx_count - 1 - own_ctx)
    return (
        span_index * (device_count * rows_per_half)
        + own_member * rows_per_half
        + local_index % rows_per_half
    )


def block_places(source_ctx, count_of_rows, ctx_count, device_count):
    rows_per_half = count_of_rows // 2
    member_index = jnp.arange(device_count, dtype=jnp.int32)[:, None, None]
    half_index = jnp.arange(2, dtype=jnp.int32)[None, :, None]
    inner_index = jnp.arange(rows_per_half, dtype=jnp.int32)[None, None, :]
    span_index = jnp.where(half_index == 0, source_ctx, 2 * ctx_count - 1 - source_ctx)
    return (
        span_index * (device_count * rows_per_half) + member_index * rows_per_half + inner_index
    ).reshape(-1)


def split_block(block_of_keys):
    hidden_width = KEY_VALUE_HEADS * HEAD_SIZE
    device_count, _, rows_per_half, _ = block_of_keys.shape
    rows_of_keys = block_of_keys[..., :hidden_width].reshape(
        device_count, 2, rows_per_half, KEY_VALUE_HEADS, HEAD_SIZE
    )
    rows_of_values = block_of_keys[..., hidden_width:].reshape(
        device_count, 2, rows_per_half, KEY_VALUE_HEADS, HEAD_SIZE
    )
    return (rows_of_keys, rows_of_values)


def attend(query_rows, rows_of_keys, rows_of_values, causal_visible):
    scores = jnp.einsum(
        "rgjd,kgd->grjk", query_rows, rows_of_keys, preferred_element_type=jnp.float32
    ) * HEAD_SIZE ** (-0.5)
    if causal_visible is not None:
        scores = jnp.where(causal_visible[None, :, None, :], scores, MASKED_SCORE)
    row_max = jnp.max(scores, axis=-1)
    exponentials = jnp.exp(scores - row_max[..., None])
    row_total = jnp.sum(exponentials, axis=-1)
    mixture = jnp.einsum(
        "grjk,kgd->rgjd",
        exponentials.astype(jnp.bfloat16),
        rows_of_values,
        preferred_element_type=jnp.float32,
    )
    return (jnp.transpose(row_max, (1, 0, 2)), jnp.transpose(row_total, (1, 0, 2)), mixture)


def empty_part(count_of_rows):
    queries_per_group = QUERY_HEADS // KEY_VALUE_HEADS
    return (
        jnp.full((count_of_rows, KEY_VALUE_HEADS, queries_per_group), MASKED_SCORE, jnp.float32),
        jnp.zeros((count_of_rows, KEY_VALUE_HEADS, queries_per_group), jnp.float32),
        jnp.zeros((count_of_rows, KEY_VALUE_HEADS, queries_per_group, HEAD_SIZE), jnp.float32),
    )


def combine(carried, incoming):
    carried_max, carried_total, carried_mix = carried
    incoming_max, incoming_total, incoming_mix = incoming
    new_max = jnp.maximum(carried_max, incoming_max)
    carried_scale = jnp.exp(carried_max - new_max)
    incoming_scale = jnp.exp(incoming_max - new_max)
    return (
        new_max,
        carried_total * carried_scale + incoming_total * incoming_scale,
        carried_mix * carried_scale[..., None] + incoming_mix * incoming_scale[..., None],
    )


def forward_block(carried, block_of_keys, source_ctx, own_ctx, query_rows, own_places, ctx_count):
    rows_of_keys, rows_of_values = split_block(block_of_keys)
    device_count, _, rows_per_half, _ = block_of_keys.shape

    def forward_earlier():
        return attend(
            query_rows,
            rows_of_keys[:, 0].reshape(-1, KEY_VALUE_HEADS, HEAD_SIZE),
            rows_of_values[:, 0].reshape(-1, KEY_VALUE_HEADS, HEAD_SIZE),
            None,
        )

    def forward_later():
        late_part = attend(
            query_rows[rows_per_half:],
            rows_of_keys.reshape(-1, KEY_VALUE_HEADS, HEAD_SIZE),
            rows_of_values.reshape(-1, KEY_VALUE_HEADS, HEAD_SIZE),
            None,
        )
        early_part = empty_part(rows_per_half)
        return tuple(
            (
                jnp.concatenate([early_piece, late_piece], axis=0)
                for early_piece, late_piece in zip(early_part, late_part)
            )
        )

    def forward_diagonal():
        key_places = block_places(source_ctx, 2 * rows_per_half, ctx_count, device_count)
        causal_visible = own_places[:, None] >= key_places[None, :]
        return attend(
            query_rows,
            rows_of_keys.reshape(-1, KEY_VALUE_HEADS, HEAD_SIZE),
            rows_of_values.reshape(-1, KEY_VALUE_HEADS, HEAD_SIZE),
            causal_visible,
        )

    branch_index = jnp.where(source_ctx == own_ctx, 2, jnp.where(source_ctx > own_ctx, 1, 0))
    return combine(
        carried, lax.switch(branch_index, [forward_earlier, forward_later, forward_diagonal])
    )


def attend_back(
    query_rows, attended_grad, log_total, delta_rows, rows_of_keys, rows_of_values, causal_visible
):
    scores = jnp.einsum(
        "rgjd,kgd->grjk", query_rows, rows_of_keys, preferred_element_type=jnp.float32
    ) * HEAD_SIZE ** (-0.5)
    if causal_visible is not None:
        scores = jnp.where(causal_visible[None, :, None, :], scores, MASKED_SCORE)
    probabilities = jnp.exp(scores - jnp.transpose(log_total, (1, 0, 2))[..., None])
    prob_grad = jnp.einsum(
        "rgjd,kgd->grjk", attended_grad, rows_of_values, preferred_element_type=jnp.float32
    )
    score_grad = (
        probabilities * (prob_grad - jnp.transpose(delta_rows, (1, 0, 2))[..., None])
    ).astype(jnp.bfloat16)
    query_part = jnp.einsum(
        "grjk,kgd->rgjd", score_grad, rows_of_keys, preferred_element_type=jnp.float32
    ) * HEAD_SIZE ** (-0.5)
    key_part = jnp.einsum(
        "grjk,rgjd->kgd", score_grad, query_rows, preferred_element_type=jnp.float32
    ) * HEAD_SIZE ** (-0.5)
    value_part = jnp.einsum(
        "grjk,rgjd->kgd",
        probabilities.astype(jnp.bfloat16),
        attended_grad,
        preferred_element_type=jnp.float32,
    )
    return (query_part, key_part, value_part)


def backward_block(
    block_of_keys,
    source_ctx,
    own_ctx,
    query_rows,
    attended_grad,
    log_total,
    delta_rows,
    own_places,
    ctx_count,
):
    rows_of_keys, rows_of_values = split_block(block_of_keys)
    device_count, _, rows_per_half, _ = block_of_keys.shape
    hidden_width = KEY_VALUE_HEADS * HEAD_SIZE

    def backward_earlier():
        query_part, key_part, value_part = attend_back(
            query_rows,
            attended_grad,
            log_total,
            delta_rows,
            rows_of_keys[:, 0].reshape(-1, KEY_VALUE_HEADS, HEAD_SIZE),
            rows_of_values[:, 0].reshape(-1, KEY_VALUE_HEADS, HEAD_SIZE),
            None,
        )
        early_grad = jnp.concatenate(
            [
                key_part.reshape(device_count, 1, rows_per_half, hidden_width),
                value_part.reshape(device_count, 1, rows_per_half, hidden_width),
            ],
            axis=-1,
        )
        return (query_part, jnp.concatenate([early_grad, jnp.zeros_like(early_grad)], axis=1))

    def backward_later():
        query_part, key_part, value_part = attend_back(
            query_rows[rows_per_half:],
            attended_grad[rows_per_half:],
            log_total[rows_per_half:],
            delta_rows[rows_per_half:],
            rows_of_keys.reshape(-1, KEY_VALUE_HEADS, HEAD_SIZE),
            rows_of_values.reshape(-1, KEY_VALUE_HEADS, HEAD_SIZE),
            None,
        )
        query_part = jnp.concatenate([jnp.zeros_like(query_part), query_part], axis=0)
        return (
            query_part,
            jnp.concatenate(
                [
                    key_part.reshape(device_count, 2, rows_per_half, hidden_width),
                    value_part.reshape(device_count, 2, rows_per_half, hidden_width),
                ],
                axis=-1,
            ),
        )

    def backward_diagonal():
        key_places = block_places(source_ctx, 2 * rows_per_half, ctx_count, device_count)
        causal_visible = own_places[:, None] >= key_places[None, :]
        query_part, key_part, value_part = attend_back(
            query_rows,
            attended_grad,
            log_total,
            delta_rows,
            rows_of_keys.reshape(-1, KEY_VALUE_HEADS, HEAD_SIZE),
            rows_of_values.reshape(-1, KEY_VALUE_HEADS, HEAD_SIZE),
            causal_visible,
        )
        return (
            query_part,
            jnp.concatenate(
                [
                    key_part.reshape(device_count, 2, rows_per_half, hidden_width),
                    value_part.reshape(device_count, 2, rows_per_half, hidden_width),
                ],
                axis=-1,
            ),
        )

    branch_index = jnp.where(source_ctx == own_ctx, 2, jnp.where(source_ctx > own_ctx, 1, 0))
    return lax.switch(branch_index, [backward_earlier, backward_later, backward_diagonal])


def per_device(
    inputs,
    attn_gain,
    query_weight,
    key_matrix,
    value_matrix,
    out_weight,
    ffn_gain,
    gate_weight,
    up_weight,
    down_weight,
    cotangent,
):
    ctx_count = lax.axis_size("ctx")
    device_count = lax.axis_size("ws")
    own_ctx = lax.axis_index("ctx")
    own_member = lax.axis_index("ws")
    micro_count, count_of_rows, _ = inputs.shape
    rows_per_half = count_of_rows // 2
    queries_per_group = QUERY_HEADS // KEY_VALUE_HEADS
    hidden_width = KEY_VALUE_HEADS * HEAD_SIZE
    own_places = query_places(own_ctx, own_member, count_of_rows, ctx_count, device_count)
    cosine_table, sine_table = rotary_tables(own_places)
    grad_sums = None
    layer_outs = []
    input_grads = []
    for micro_batch in range(micro_count):
        gathered = (
            lax.all_gather(attn_gain, ("ctx", "ws"), axis=0, tiled=True),
            lax.all_gather(query_weight, ("ctx", "ws"), axis=0, tiled=True),
            lax.all_gather(key_matrix, ("ctx", "ws"), axis=0, tiled=True),
            lax.all_gather(value_matrix, ("ctx", "ws"), axis=0, tiled=True),
            lax.all_gather(out_weight, ("ctx", "ws"), axis=0, tiled=True),
            lax.all_gather(ffn_gain, ("ctx", "ws"), axis=0, tiled=True),
            lax.all_gather(gate_weight, ("ctx", "ws"), axis=0, tiled=True),
            lax.all_gather(up_weight, ("ctx", "ws"), axis=0, tiled=True),
            lax.all_gather(down_weight, ("ctx", "ws"), axis=0, tiled=True),
        )
        (
            full_attn_gain,
            full_query,
            complete_key,
            full_value,
            full_out,
            full_ffn_gain,
            full_gate,
            full_up,
            full_down,
        ) = gathered
        first_gain = full_attn_gain.astype(jnp.float32)
        second_gain = full_ffn_gain.astype(jnp.float32)
        layer_rows = inputs[micro_batch].astype(jnp.float32)
        normalized_rows, first_inverse = normalize(layer_rows, first_gain)
        normalized_reduced = normalized_rows.astype(jnp.bfloat16)
        query_rows = rotate(
            matrix_multiply(normalized_reduced, full_query).reshape(
                count_of_rows, QUERY_HEADS, HEAD_SIZE
            ),
            cosine_table,
            sine_table,
        )
        query_rows = query_rows.astype(jnp.bfloat16).reshape(
            count_of_rows, KEY_VALUE_HEADS, queries_per_group, HEAD_SIZE
        )
        rows_of_keys = rotate(
            matrix_multiply(normalized_reduced, complete_key).reshape(
                count_of_rows, KEY_VALUE_HEADS, HEAD_SIZE
            ),
            cosine_table,
            sine_table,
        ).astype(jnp.bfloat16)
        rows_of_values = matrix_multiply(normalized_reduced, full_value).astype(jnp.bfloat16)
        local_block = jnp.concatenate(
            [rows_of_keys.reshape(count_of_rows, hidden_width), rows_of_values], axis=-1
        )
        group_block = lax.all_gather(local_block, "ws", axis=0, tiled=True).reshape(
            device_count, 2, rows_per_half, 2 * hidden_width
        )

        def fold_step(carried, shard_piece):

            def visit_block(state_now, block_entry):
                block_of_keys, source_ctx = block_entry
                return (
                    forward_block(
                        state_now,
                        block_of_keys,
                        source_ctx,
                        own_ctx,
                        query_rows,
                        own_places,
                        ctx_count,
                    ),
                    None,
                )

            source_list = jnp.arange(shard_piece.shape[0], dtype=jnp.int32)
            result_state, _ = lax.scan(visit_block, carried, (shard_piece, source_list))
            return result_state

        row_max, row_total, mixture = fold_step(
            empty_part(count_of_rows), lax.all_gather(group_block[None], "ctx", axis=0, tiled=True)
        )
        attended = mixture / row_total[..., None]
        log_total = row_max + jnp.log(row_total)
        attended_low = attended.astype(jnp.bfloat16).reshape(count_of_rows, QUERY_HEADS * HEAD_SIZE)
        middle = layer_rows + matrix_multiply(attended_low, full_out)
        hidden, second_inverse = normalize(middle, second_gain)
        hidden_low = hidden.astype(jnp.bfloat16)
        gate_rows = matrix_multiply(hidden_low, full_gate)
        up_rows = matrix_multiply(hidden_low, full_up)
        sigmoid_gate = jax.nn.sigmoid(gate_rows)
        silu_gate = gate_rows * sigmoid_gate
        activated = (silu_gate * up_rows).astype(jnp.bfloat16)
        layer_outs.append((middle + matrix_multiply(activated, full_down)).astype(jnp.bfloat16))
        upstream_low = cotangent[micro_batch]
        upstream = upstream_low.astype(jnp.float32)
        down_sum = outer_sum(activated, upstream_low)
        act_grad = back_product(upstream_low, full_down)
        gate_low = (
            act_grad * up_rows * sigmoid_gate * (1.0 + gate_rows * (1.0 - sigmoid_gate))
        ).astype(jnp.bfloat16)
        up_low = (act_grad * silu_gate).astype(jnp.bfloat16)
        gate_sum = outer_sum(hidden_low, gate_low)
        up_sum = outer_sum(hidden_low, up_low)
        hidden_grad = back_product(gate_low, full_gate) + back_product(up_low, full_up)
        middle_part, ffn_gain_sum = normalize_back(middle, second_inverse, second_gain, hidden_grad)
        middle_grad = middle_part + upstream
        branch_low = middle_grad.astype(jnp.bfloat16)
        out_sum = outer_sum(attended_low, branch_low)
        attended_grad = (
            back_product(branch_low, full_out)
            .reshape(count_of_rows, KEY_VALUE_HEADS, queries_per_group, HEAD_SIZE)
            .astype(jnp.bfloat16)
        )
        delta_rows = jnp.sum(attended_grad.astype(jnp.float32) * attended, axis=-1)

        def cycle_step(turn_index, carried):
            block_of_keys, block_grad, query_total = carried
            source_ctx = (own_ctx - turn_index) % ctx_count
            query_part, block_part = backward_block(
                block_of_keys,
                source_ctx,
                own_ctx,
                query_rows,
                attended_grad,
                log_total,
                delta_rows,
                own_places,
                ctx_count,
            )
            block_grad = block_grad + block_part
            next_block = shifted(block_of_keys, "ctx", 1)
            next_grad = shifted(as_sent(block_grad), "ctx", 1).astype(block_grad.dtype)
            return (next_block, next_grad, query_total + query_part)

        cycle_start = (
            group_block,
            jnp.zeros(group_block.shape, jnp.float32),
            jnp.zeros((count_of_rows, KEY_VALUE_HEADS, queries_per_group, HEAD_SIZE), jnp.float32),
        )
        _, block_grad, query_total = lax.fori_loop(0, ctx_count, cycle_step, cycle_start)
        local_gradient = (
            lax.psum_scatter(block_grad.astype(jnp.bfloat16), "ws", scatter_dimension=0, tiled=True)
            .astype(jnp.float32)
            .reshape(count_of_rows, 2 * hidden_width)
        )
        key_low = rotate_back(
            local_gradient[:, :hidden_width].reshape(count_of_rows, KEY_VALUE_HEADS, HEAD_SIZE),
            cosine_table,
            sine_table,
        )
        key_low = key_low.astype(jnp.bfloat16).reshape(count_of_rows, hidden_width)
        value_low = local_gradient[:, hidden_width:].astype(jnp.bfloat16)
        query_low = rotate_back(
            query_total.reshape(count_of_rows, QUERY_HEADS, HEAD_SIZE), cosine_table, sine_table
        )
        query_low = query_low.astype(jnp.bfloat16).reshape(count_of_rows, QUERY_HEADS * HEAD_SIZE)
        query_sum = outer_sum(normalized_reduced, query_low)
        key_sum = outer_sum(normalized_reduced, key_low)
        value_sum = outer_sum(normalized_reduced, value_low)
        normed_grad = (
            back_product(query_low, full_query)
            + back_product(key_low, complete_key)
            + back_product(value_low, full_value)
        )
        input_part, attn_gain_sum = normalize_back(
            layer_rows, first_inverse, first_gain, normed_grad
        )
        input_grads.append((middle_grad + input_part).astype(jnp.bfloat16))
        batch_terms = (
            attn_gain_sum,
            query_sum,
            key_sum,
            value_sum,
            out_sum,
            ffn_gain_sum,
            gate_sum,
            up_sum,
            down_sum,
        )
        if grad_sums is None:
            grad_sums = batch_terms
        else:
            grad_sums = tuple(
                (
                    earlier_sum + batch_term
                    for earlier_sum, batch_term in zip(grad_sums, batch_terms)
                )
            )
    owned_grads = (
        lax.psum_scatter(grad_sums[0], ("ctx", "ws"), scatter_dimension=0, tiled=True),
        lax.psum_scatter(grad_sums[1], ("ctx", "ws"), scatter_dimension=0, tiled=True),
        lax.psum_scatter(grad_sums[2], ("ctx", "ws"), scatter_dimension=0, tiled=True),
        lax.psum_scatter(grad_sums[3], ("ctx", "ws"), scatter_dimension=0, tiled=True),
        lax.psum_scatter(grad_sums[4], ("ctx", "ws"), scatter_dimension=0, tiled=True),
        lax.psum_scatter(grad_sums[5], ("ctx", "ws"), scatter_dimension=0, tiled=True),
        lax.psum_scatter(grad_sums[6], ("ctx", "ws"), scatter_dimension=0, tiled=True),
        lax.psum_scatter(grad_sums[7], ("ctx", "ws"), scatter_dimension=0, tiled=True),
        lax.psum_scatter(grad_sums[8], ("ctx", "ws"), scatter_dimension=0, tiled=True),
    )
    return (
        jnp.stack(layer_outs),
        jnp.stack(input_grads),
        owned_grads[0],
        owned_grads[1],
        owned_grads[2],
        owned_grads[3],
        owned_grads[4],
        owned_grads[5],
        owned_grads[6],
        owned_grads[7],
        owned_grads[8],
    )


MESH = pl.DeviceIdType.MESH
NEG = -1e30
WIDE = 128
VMEM_LIMIT = 61 * 1024 * 1024


def fits_fast(mesh):
    return mesh.shape["ctx"] == 8 and mesh.shape["ws"] == 4


def place():
    c = lax.axis_index("ctx")
    w = lax.axis_index("ws")
    return c // 2, lax.rem(c, 2), w // 2, lax.rem(w, 2)


def device(z, y, x, k):
    return (z * 2 + y, x * 2 + k)


def greet(zn):
    z, y, x, k = place()
    others = [device(lax.rem(z + j, zn), y, x, k) for j in range(1, zn)]
    others += [device(z, y, 1 - x, k), device(z, 1 - y, x, k), device(z, y, x, 1 - k)]
    barrier = pltpu.get_barrier_semaphore()
    for other in others:
        pl.semaphore_signal(barrier, inc=1, device_id=other, device_id_type=MESH)
    pl.semaphore_wait(barrier, len(others))


def remote(src, dst, send, recv, where):
    return pltpu.make_async_remote_copy(
        src_ref=src, dst_ref=dst, send_sem=send, recv_sem=recv, device_id=where, device_id_type=MESH
    )


class Gather:
    SEMS = 12

    def __init__(self, src, dst, send, recv, zn):
        z, y, x, k = place()
        own = dst.at[z, y, x, k]
        hz = zn // 2
        xn, yn, sib = device(z, y, 1 - x, k), device(z, 1 - y, x, k), device(z, y, x, 1 - k)

        def push(i, ref, where):
            return remote(ref, ref, send.at[i], recv.at[i], where)

        def col(yy, xx, lo=0, n=zn):
            return dst.at[pl.ds(lo, n), yy, xx, k]

        self.local = pltpu.make_async_copy(src(z), own, send.at[0])
        self.along = []
        for j in range(1, zn):
            zz = lax.rem(z + j, zn)
            self.along.append(remote(src(zz), own, send.at[j], recv.at[j], device(zz, y, x, k)))
        self.cols = [push(4, col(y, x), xn), push(5, col(y, x), yn)]
        self.corner = [push(7, col(1 - y, x, 0, hz), xn), push(8, col(y, 1 - x, hz, hz), yn)]
        self.twin_own = push(6, col(y, x), sib)
        self.twin_cols = [push(9, col(y, 1 - x), sib), push(10, col(1 - y, x), sib)]
        self.twin_corner = push(11, col(1 - y, 1 - x), sib)

    def stage(self, n):
        if n == 0:
            self.local.start()
            for c in self.along:
                c.start()
        elif n == 1:
            self.local.wait()
            for c in self.along:
                c.wait_recv()
            for c in self.cols:
                c.start()
            self.twin_own.start()
        elif n == 2:
            for c in self.cols:
                c.wait_recv()
            for c in self.corner:
                c.start()
            for c in self.twin_cols:
                c.start()
        elif n == 3:
            for c in self.corner:
                c.wait_recv()
            self.twin_corner.start()
        elif n == 4:
            for c in [self.twin_own] + self.twin_cols + [self.twin_corner]:
                c.wait_recv()
            for c in (
                self.along
                + self.cols
                + self.corner
                + [self.twin_own]
                + self.twin_cols
                + [self.twin_corner]
            ):
                c.wait_send()


def stage_step(items, stages, t):
    for n in range(stages):
        if 0 <= t - n < len(items) and items[t - n] is not None:
            items[t - n].stage(n)


def run_stages(items, stages):
    for t in range(len(items) + stages - 1):
        stage_step(items, stages, t)


def pieces_of(rows, cols, nrow, ncol):
    return [
        (i * (rows // nrow), rows // nrow, j * (cols // ncol), cols // ncol)
        for i in range(nrow)
        for j in range(ncol)
    ]


def gather_item(ref, out, r0, nr, c0, nc, send, recv, zn):
    src = ref.at[pl.ds(r0, nr), pl.ds(c0, nc)]
    dst = out.at[:, :, :, :, pl.ds(r0, nr), pl.ds(c0, nc)]
    return Gather(lambda zz: src, dst, send, recv, zn)


class Exchange:
    def __init__(self, src, dst, send, recv, zn):
        z, y, x, k = place()
        self.local = pltpu.make_async_copy(src(z), dst(z), send.at[0])
        self.along = []
        for j in range(1, zn):
            zz = lax.rem(z + j, zn)
            self.along.append(remote(src(zz), dst(z), send.at[j], recv.at[j], device(zz, y, x, k)))

    def start(self):
        self.local.start()
        for c in self.along:
            c.start()

    def arrived(self):
        self.local.wait()
        for c in self.along:
            c.wait_recv()

    def sent(self):
        for c in self.along:
            c.wait_send()


def gather_all(arrays, rows_used, cuts, collective_id):
    zn = lax.axis_size("ctx") // 2
    n = len(arrays)
    work = [
        (a, piece)
        for a in range(n)
        for piece in pieces_of(rows_used[a], arrays[a].shape[1], *cuts[a])
    ]

    def kernel(*refs):
        ins, outs, (send, recv) = refs[:n], refs[n : 2 * n], refs[2 * n :]
        greet(zn)
        items = []
        for i, (a, (r0, nr, c0, nc)) in enumerate(work):
            items.append(gather_item(ins[a], outs[a], r0, nr, c0, nc, send.at[i], recv.at[i], zn))
        run_stages(items, 5)

    return pl.pallas_call(
        kernel,
        out_shape=[
            jax.ShapeDtypeStruct((zn, 2, 2, 2, rows_used[a], arrays[a].shape[1]), arrays[a].dtype)
            for a in range(n)
        ],
        in_specs=[pl.BlockSpec(memory_space=pl.ANY)] * n,
        out_specs=[pl.BlockSpec(memory_space=pl.ANY)] * n,
        scratch_shapes=[
            pltpu.SemaphoreType.DMA((len(work), Gather.SEMS)),
            pltpu.SemaphoreType.DMA((len(work), Gather.SEMS)),
        ],
        compiler_params=pltpu.CompilerParams(
            collective_id=collective_id, has_side_effects=True, vmem_limit_bytes=VMEM_LIMIT
        ),
    )(*arrays)


class Scatter:
    SEMS = 10

    @staticmethod
    def scratch(zn, nr, nc):
        b = jnp.bfloat16
        return [
            pltpu.VMEM((zn, 2, 2, nr, nc), b),
            pltpu.VMEM((zn, 2, 2, nr, nc), b),
            pltpu.VMEM((2, zn // 2, nr, nc), b),
            pltpu.VMEM((2, zn, nr, nc), b),
            pltpu.VMEM((zn - 1, nr, nc), b),
        ]

    def __init__(self, part, out, bufs, send, recv, zn, give=None):
        z, y, x, k = self.at = place()
        self.zn = zn
        hz = zn // 2
        xn, yn, sib = device(z, y, 1 - x, k), device(z, 1 - y, x, k), device(z, y, x, 1 - k)
        self.held, self.twin, self.corners, self.colsums, self.ends = held, twin, corners, colsums, ends = bufs
        self.out = out
        self.load = None
        if give is None:
            self.load = pltpu.make_async_copy(part.at[:, :, :, k], held, send.at[0])
            give = part.at[:, :, :, 1 - k]
        self.to_twin = remote(give, twin, send.at[1], recv.at[1], sib)
        self.to_corner = [
            remote(held.at[pl.ds(0, hz), 1 - y, 1 - x], corners.at[0], send.at[2], recv.at[2], yn),
            remote(held.at[pl.ds(hz, hz), 1 - y, 1 - x], corners.at[1], send.at[3], recv.at[3], xn),
        ]
        self.to_col = [
            remote(held.at[:, y, 1 - x], colsums.at[0], send.at[4], recv.at[4], xn),
            remote(held.at[:, 1 - y, x], colsums.at[1], send.at[5], recv.at[5], yn),
        ]
        self.along = []
        for j in range(1, zn):
            zz = lax.rem(z + j, zn)
            dst = out.at[z] if ends is None else ends.at[j - 1]
            self.along.append(
                remote(held.at[zz, y, x], dst, send.at[5 + j], recv.at[5 + j], device(zz, y, x, k))
            )
        self.last = pltpu.make_async_copy(held.at[z, y, x], out.at[z], send.at[0]) if ends is None else None

    def stage(self, n):
        z, y, x, k = self.at
        zn, hz = self.zn, self.zn // 2
        held = self.held
        if n == 0:
            self.to_twin.start()
            if self.load is not None:
                self.load.start()
        elif n == 1:
            if self.load is not None:
                self.load.wait()
            self.to_twin.wait_recv()

            def add(i, _):
                for yy in range(2):
                    for xx in range(2):
                        held[i, yy, xx] = held[i, yy, xx] + self.twin[i, yy, xx]
                return 0

            lax.fori_loop(0, zn, add, 0)
            for c in self.to_corner:
                c.start()
        elif n == 2:
            for c in self.to_corner:
                c.wait_recv()
            for i in range(hz):
                held[i, y, 1 - x] = held[i, y, 1 - x] + self.corners[0, i]
                held[hz + i, 1 - y, x] = held[hz + i, 1 - y, x] + self.corners[1, i]
            for c in self.to_col:
                c.start()
        elif n == 3:
            for c in self.to_col:
                c.wait_recv()

            def add(i, _):
                f = jnp.float32
                held[i, y, x] = (
                    held[i, y, x].astype(f) + self.colsums[0, i].astype(f) + self.colsums[1, i].astype(f)
                ).astype(jnp.bfloat16)
                return 0

            lax.fori_loop(0, zn, add, 0)
            for c in self.along:
                c.start()
            if self.last is not None:
                self.last.start()
        elif n == 4:
            for c in self.along:
                c.wait_recv()
            if self.last is not None:
                self.last.wait()
            else:
                total = held[z, y, x].astype(jnp.float32)
                for j in range(zn - 1):
                    total = total + self.ends[j].astype(jnp.float32)
                self.out[...] = total
            for c in [self.to_twin] + self.to_corner + self.to_col + self.along:
                c.wait_send()


NT = (((1,), (1,)), ((), ()))


def nt(a, b):
    return lax.dot_general(a, b, NT, preferred_element_type=jnp.float32)


PER = QUERY_HEADS // KEY_VALUE_HEADS
HALF_GROUPS = KEY_VALUE_HEADS // 2
HALF_HEADS = QUERY_HEADS // 2
KV_LANES = 2 * HALF_GROUPS * HEAD_SIZE


def lane_slot(n):
    return n // 2, n % 2


def key_slot(g):
    return lane_slot(g)


def value_slot(g):
    return lane_slot(HALF_GROUPS + g)


def pair_index(half, zp):
    return zp if half == 0 else 3 - zp


def pair_tile(src, g, half, zp):
    tiles = []
    for j in range(PER):
        lo = HEAD_SIZE * (PER * g + j)
        a = src[2 * zp, lo : lo + HEAD_SIZE, :].astype(jnp.float32)
        b = src[2 * zp + 1, lo : lo + HEAD_SIZE, :].astype(jnp.float32)
        low = lax.broadcasted_iota(jnp.int32, a.shape, 1) < WIDE // 2
        if half == 0:
            tiles.append(jnp.where(low, a, pltpu.roll(b, WIDE // 2, 1)))
        else:
            tiles.append(jnp.where(low, pltpu.roll(a, WIDE // 2, 1), b))
    return jnp.concatenate(tiles, axis=1)


def unpair(get, dst):
    for zp in range(2):
        for g in range(HALF_GROUPS):
            first, second = get(g, pair_index(0, zp)), get(g, pair_index(1, zp))
            for j in range(PER):
                lo = HEAD_SIZE * (PER * g + j)
                a, b = first[:, WIDE * j : WIDE * j + WIDE], second[:, WIDE * j : WIDE * j + WIDE]
                low = lax.broadcasted_iota(jnp.int32, a.shape, 1) < WIDE // 2
                even = jnp.where(low, a, pltpu.roll(b, WIDE // 2, 1))
                odd = jnp.where(low, pltpu.roll(a, WIDE // 2, 1), b)
                dst[2 * zp, lo : lo + HEAD_SIZE, :] = even.astype(dst.dtype)
                dst[2 * zp + 1, lo : lo + HEAD_SIZE, :] = odd.astype(dst.dtype)


def set_padded(dst, g, p, tile, side):
    tile = tile.astype(dst.dtype)
    dst[g, p, side * HEAD_SIZE : (side + 1) * HEAD_SIZE, :] = tile
    dst[g, p, (1 - side) * HEAD_SIZE : (2 - side) * HEAD_SIZE, :] = jnp.zeros_like(tile)


def walk(t, y, cn):
    b1, b2, b3 = 3 + y, 10 + 2 * y, 22 + y
    p = (t >= b1).astype(jnp.int32) + (t >= b2).astype(jnp.int32) + (t >= b3).astype(jnp.int32)
    j = t - jnp.where(p == 0, 0, jnp.where(p == 1, b1, jnp.where(p == 2, b2, b3)))
    zp = jnp.where(p < 2, p, 3 - p)
    low = jnp.where(p < 2, 4 * zp + y, 2 * cn - 3 - 4 * zp - y)
    late = (j >= cn).astype(jnp.int32)
    src = jnp.where(late == 1, 2 * cn - 1 - j, j)
    return p, j, src // 2, lax.rem(src, 2), pl.multiple_of(late * HEAD_SIZE, HEAD_SIZE), j >= low


STEPS = 38


def visible(p, j, y, w, cn, wn, rows):
    shape = (wn * rows, PER * WIDE)
    lane = lax.rem(lax.broadcasted_iota(jnp.int32, shape, 1), WIDE)
    zp = jnp.where(p < 2, p, 3 - p)
    c = 2 * (2 * zp + lane // rows) + y
    span = jnp.where(p < 2, c, 2 * cn - 1 - c)
    query = span * (wn * rows) + w * rows + lax.rem(lane, rows)
    key = j * (wn * rows) + lax.broadcasted_iota(jnp.int32, shape, 0)
    return key <= query


def key_block(kvg, zz, yy, late, rows, block):
    t = kvg[zz, yy, :, :, pl.ds(late, rows), WIDE * block : WIDE * block + WIDE]
    return t.reshape(4 * rows, WIDE)


def turned(t):
    return t.astype(jnp.float32).T.astype(t.dtype)


def by_span(body, kvg, cn, rows):
    def one(j, _):
        late = (j >= cn).astype(jnp.int32)
        src = jnp.where(late == 1, 2 * cn - 1 - j, j)
        at = pl.multiple_of(late * rows, rows)
        body(j, lambda b: key_block(kvg, src // 2, lax.rem(src, 2), at, rows, b))
        return 0

    lax.fori_loop(0, 2 * cn, one, 0)


def gather_attend(q, kv, arrays, used, cuts, collective_id):
    cn, wn = lax.axis_size("ctx"), lax.axis_size("ws")
    zn = cn // 2
    mbs, q_rows, tokens = q.shape
    rows = tokens // 2
    mine = q_rows // 2
    n = len(arrays)
    f32, b16 = jnp.float32, jnp.bfloat16
    work = [(a, piece) for a in range(n) for piece in pieces_of(used[a], arrays[a].shape[1], *cuts[a])]
    groups = range(HALF_GROUPS)

    def kernel(*refs):
        q_ref, kv_ref = refs[:2]
        ins = refs[2 : 2 + n]
        o_out, q_out, kv_out, oh_out, lse_out = refs[2 + n : 7 + n]
        outs = refs[7 + n : 7 + 2 * n]
        qh, kvg, oh, qpad, vt, m_s, l_s, acc, send, recv, xs, xr, ks, kr, save = refs[7 + 2 * n :]
        greet(zn)
        z, y, x, k = place()
        w = 2 * x + k

        def lanes_of(zz):
            return kv_ref.at[zz // 2, :, pl.ds(pl.multiple_of(lax.rem(zz, 2) * KV_LANES, WIDE), KV_LANES)]

        def heads_of(ref, zz):
            return ref.at[zz // 2, pl.ds(pl.multiple_of(lax.rem(zz, 2) * mine, 16), mine), :]

        items = [
            gather_item(ins[a], outs[a], r0, nr, c0, nc, send.at[i], recv.at[i], zn)
            for i, (a, (r0, nr, c0, nc)) in enumerate(work)
        ]
        kvx = Gather(lanes_of, kvg, ks, kr, zn)
        qx = Exchange(lambda zz: heads_of(q_ref, zz), lambda zz: qh.at[zz], xs.at[0], xr.at[0], zn)
        ox = Exchange(lambda zz: oh.at[zz], lambda zz: heads_of(o_out, zz), xs.at[1], xr.at[1], zn)
        kvx.stage(0)
        qx.start()
        stage_step(items, 5, 0)
        m_s[...] = jnp.full(m_s.shape, NEG, f32)
        l_s[...] = jnp.zeros(l_s.shape, f32)
        acc[...] = jnp.zeros(acc.shape, f32)
        kvx.stage(1)
        kvx.stage(2)
        stage_step(items, 5, 1)
        kvx.stage(3)
        qx.arrived()
        for half in range(2):
            for zp in range(2):
                for g in groups:
                    set_padded(qpad, g, pair_index(half, zp), pair_tile(qh, g, half, zp), key_slot(g)[1])
        kvx.stage(4)

        def turn(j, block):
            flat = {b: turned(block(b)) for b in sorted({value_slot(g)[0] for g in groups})}
            for g in groups:
                b, side = value_slot(g)
                vt[j, g] = flat[b][side * HEAD_SIZE : (side + 1) * HEAD_SIZE]

        by_span(turn, kvg, cn, rows)
        saves = [
            pltpu.make_async_copy(qh, q_out, save.at[0]),
            pltpu.make_async_copy(kvg, kv_out, save.at[1]),
        ]
        for s in saves:
            s.start()

        def step(t, _):
            p, j, zz, yy, late, edge = walk(t, y, cn)

            def run(masked):
                seen = visible(p, j, y, w, cn, wn, rows) if masked else None
                for g in groups:
                    s = jnp.dot(
                        key_block(kvg, zz, yy, late, rows, key_slot(g)[0]), qpad[g, p], preferred_element_type=f32
                    )
                    if masked:
                        s = jnp.where(seen, s, NEG)
                    m_old = m_s[g, p]
                    m_new = jnp.maximum(m_old, jnp.max(s, axis=0, keepdims=True))
                    alpha = jnp.exp(m_old - m_new)
                    e = jnp.exp(s - m_new)
                    m_s[g, p] = m_new
                    l_s[g, p] = l_s[g, p] * alpha + jnp.sum(e, axis=0, keepdims=True)
                    acc[g, p] = acc[g, p] * alpha + jnp.dot(
                        vt[j, g], e.astype(b16), preferred_element_type=f32
                    )

            pl.when(edge)(lambda: run(True))
            pl.when(jnp.logical_not(edge))(lambda: run(False))
            return 0

        last = len(items) + 4
        t = 0
        for s in range(2, last):
            upto = min(STEPS, 5 * (s - 1))
            if t < upto:
                lax.fori_loop(t, upto, step, 0)
                t = upto
                if t == STEPS:
                    unpair(lambda g, p: acc[g, p] / l_s[g, p], oh)
                    ox.start()
                    saves.append(pltpu.make_async_copy(oh, oh_out, save.at[2]))
                    saves[-1].start()
                    lse_out[...] = m_s[...] + jnp.log(l_s[...])
            stage_step(items, 5, s)
        ox.arrived()
        ox.sent()
        qx.sent()
        for s in saves:
            s.wait()

    stat = (HALF_GROUPS, 4, 1, PER * WIDE)
    block = (zn, mine, tokens)
    kv_shape = (zn, 2, 2, 2, tokens, KV_LANES)
    any_ = pl.BlockSpec(memory_space=pl.ANY)
    return pl.pallas_call(
        kernel,
        out_shape=[
            jax.ShapeDtypeStruct(q.shape, b16),
            jax.ShapeDtypeStruct(block, b16),
            jax.ShapeDtypeStruct(kv_shape, b16),
            jax.ShapeDtypeStruct(block, b16),
            jax.ShapeDtypeStruct(stat, f32),
        ]
        + [
            jax.ShapeDtypeStruct((zn, 2, 2, 2, used[a], arrays[a].shape[1]), arrays[a].dtype)
            for a in range(n)
        ],
        in_specs=[any_] * (2 + n),
        out_specs=[any_] * 4 + [pl.BlockSpec(memory_space=pltpu.VMEM)] + [any_] * n,
        scratch_shapes=[
            pltpu.VMEM(block, b16),
            pltpu.VMEM(kv_shape, b16),
            pltpu.VMEM(block, b16),
            pltpu.VMEM((HALF_GROUPS, 4, WIDE, PER * WIDE), b16),
            pltpu.VMEM((2 * cn, HALF_GROUPS, HEAD_SIZE, wn * rows), b16),
            pltpu.VMEM(stat, f32),
            pltpu.VMEM(stat, f32),
            pltpu.VMEM((HALF_GROUPS, 4, HEAD_SIZE, PER * WIDE), f32),
            pltpu.SemaphoreType.DMA((len(work), Gather.SEMS)),
            pltpu.SemaphoreType.DMA((len(work), Gather.SEMS)),
            pltpu.SemaphoreType.DMA((2, zn)),
            pltpu.SemaphoreType.DMA((2, zn)),
            pltpu.SemaphoreType.DMA((Gather.SEMS,)),
            pltpu.SemaphoreType.DMA((Gather.SEMS,)),
            pltpu.SemaphoreType.DMA((3,)),
        ],
        compiler_params=pltpu.CompilerParams(
            collective_id=collective_id, has_side_effects=True, vmem_limit_bytes=VMEM_LIMIT
        ),
    )(q, kv, *arrays)


class Share:
    def __init__(self, src, own, other, local, send, recv, split):
        z, y, x, k = place()
        mine = src.at[:, :, :, k] if split else src
        theirs = src.at[:, :, :, 1 - k] if split else src
        self.load = None if mine is own else pltpu.make_async_copy(mine, own, local)
        self.swap = remote(theirs, other, send, recv, device(z, y, x, 1 - k))
        self.waited = False

    def start(self):
        if self.load is not None:
            self.load.start()
        self.swap.start()

    def ready(self):
        if not self.waited:
            if self.load is not None:
                self.load.wait()
            self.swap.wait_recv()
            self.waited = True

    def sent(self):
        self.swap.wait_send()


class Sum:
    SEMS = 8

    def __init__(self, make, held, bufs, out, send, recv, zn):
        z, y, x, k = self.at = place()
        self.make, self.held, self.out, self.zn = make, held, out, zn
        hz = zn // 2
        xn, yn = device(z, y, 1 - x, k), device(z, 1 - y, x, k)
        self.corners, self.colsums, self.ends = corners, colsums, ends = bufs
        self.to_corner = [
            remote(held.at[pl.ds(0, hz), 1 - y, 1 - x], corners.at[0], send.at[0], recv.at[0], yn),
            remote(held.at[pl.ds(hz, hz), 1 - y, 1 - x], corners.at[1], send.at[1], recv.at[1], xn),
        ]
        self.to_col = [
            remote(held.at[:, y, 1 - x], colsums.at[0], send.at[2], recv.at[2], xn),
            remote(held.at[:, 1 - y, x], colsums.at[1], send.at[3], recv.at[3], yn),
        ]
        self.along = []
        for j in range(1, zn):
            zz = lax.rem(z + j, zn)
            self.along.append(
                remote(held.at[zz, y, x], ends.at[j - 1], send.at[3 + j], recv.at[3 + j], device(zz, y, x, k))
            )

    @staticmethod
    def scratch(zn, nr, nc):
        b = jnp.bfloat16
        return [
            pltpu.VMEM((2, zn // 2, nr, nc), b),
            pltpu.VMEM((2, zn, nr, nc), b),
            pltpu.VMEM((zn - 1, nr, nc), b),
        ]

    def stage(self, n):
        z, y, x, k = self.at
        zn, hz, held = self.zn, self.zn // 2, self.held
        f32, b16 = jnp.float32, jnp.bfloat16
        if n == 0:
            self.make(held)
            for c in self.to_corner:
                c.start()
        elif n == 1:
            for c in self.to_corner:
                c.wait_recv()
            for i in range(hz):
                held[i, y, 1 - x] = held[i, y, 1 - x] + self.corners[0, i]
                held[hz + i, 1 - y, x] = held[hz + i, 1 - y, x] + self.corners[1, i]
            for c in self.to_col:
                c.start()
        elif n == 2:
            for c in self.to_col:
                c.wait_recv()
            for i in range(zn):
                held[i, y, x] = (
                    held[i, y, x].astype(f32)
                    + self.colsums[0, i].astype(f32)
                    + self.colsums[1, i].astype(f32)
                ).astype(b16)
            for c in self.along:
                c.start()
        elif n == 3:
            for c in self.along:
                c.wait_recv()
            total = held[z, y, x].astype(f32)
            for j in range(zn - 1):
                total = total + self.ends[j].astype(f32)
            self.out[...] = total
            for c in self.to_corner + self.to_col + self.along:
                c.wait_send()


def scatter_attend(do, qh, kvg, oh, lse, tables, lefts, rests, rights, plan, collective_id):
    cn, wn = lax.axis_size("ctx"), lax.axis_size("ws")
    zn = cn // 2
    mbs, q_rows, tokens = do.shape
    rows = tokens // 2
    mine = q_rows // 2
    all_rows = mbs * tokens
    f32, b16 = jnp.float32, jnp.bfloat16
    groups = range(HALF_GROUPS)
    scale = HEAD_SIZE**-0.5
    ff = rights[2].shape[1]
    width = rights[0].shape[1]
    qkv_w = q_rows + 2 * KV_LANES
    act_rows = lefts[0].shape[4]
    ra = lefts[1].shape[4]
    rest_w, qkv_rest_w = plan
    n_down = act_rows // ra
    half_ff = ff // 2
    sizes = (
        [(ra, width)] * n_down
        + [(ra, half_ff)] * 4
        + [(ra, width), (16, rest_w), (ra, 2 * KV_LANES), (ra, q_rows), (16, qkv_rest_w)]
    )
    max_cols = max(s[1] for s in sizes)
    ring = 4
    scratch = []
    for nr, nc in sizes:
        scratch += Sum.scratch(zn, nr, nc)
    n_items = len(sizes)
    ins_all = [*lefts, *rests, *rights]
    n_in = len(ins_all)
    split = [True] * len(lefts) + [False] * (n_in - len(lefts))
    half = lambda a, s: (a.shape[:3] + a.shape[4:]) if s else a.shape
    shares = []
    for a, s in zip(ins_all, split):
        shares += [pltpu.VMEM(half(a, s), b16), pltpu.VMEM(half(a, s), b16)]
    outs_shape = [
        (act_rows, width), (ra, ff), (ra, ff), (ra, width), (16, rest_w), (ra, qkv_w), (16, qkv_rest_w)
    ]
    n_out = len(outs_shape)

    def kernel(*refs):
        do_ref, qh, kvg, oh_ref, lse_ref, tab = refs[:6]
        ins = refs[6 : 6 + n_in]
        gq = refs[6 + n_in]
        outs = refs[7 + n_in : 7 + n_in + n_out]
        rest = refs[7 + n_in + n_out :]
        bufs, rest = rest[: len(scratch)], rest[len(scratch) :]
        pairs, rest = rest[: len(shares)], rest[len(shares) :]
        (held, gq_other, dkv_in, oh, gh, qt, dot_, kt, delta, dq, dkv, give) = rest[:12]
        kb = rest[12:16]
        send, recv, ps, pr, pl_, xs, xr, ks, kr = rest[16:]
        dqh, dq_in = gh, oh
        greet(zn)
        z, y, x, k = place()
        w = 2 * x + k

        def heads_of(ref, zz):
            return ref.at[zz // 2, pl.ds(pl.multiple_of(lax.rem(zz, 2) * mine, 16), mine), :]

        gx = Exchange(lambda zz: heads_of(do_ref, zz), lambda zz: gh.at[zz], xs.at[0], xr.at[0], zn)
        dx = Exchange(lambda zz: dqh.at[zz], lambda zz: dq_in.at[zz], xs.at[1], xr.at[1], zn)
        kvx = Scatter(None, dkv_in, tuple(kb) + (None,), ks, kr, zn, give)
        share = [
            Share(ins[i], pairs[2 * i], pairs[2 * i + 1], pl_.at[i], ps.at[i], pr.at[i], split[i])
            for i in range(n_in)
        ]
        gq_share = Share(gq, gq, gq_other, None, ps.at[n_in], pr.at[n_in], False)
        own = lambda i: pairs[2 * i]
        other = lambda i: pairs[2 * i + 1]
        ACT, H2, OT, HN, H2B, OTB, HNB, GY, GB, GG, GU = range(n_in)

        def product(left, right, lo, row0, needs):
            def make(dst):
                for i in needs:
                    share[i].ready()
                nr, nc = dst.shape[3:]
                lefts2 = [
                    r[:, :, :, row0 : row0 + nr, :].reshape(zn * 4 * nr, all_rows)
                    for r in (own(left), other(left))
                ]
                step = 3 * WIDE

                def cols(i, _):
                    at = pl.multiple_of(i * step, WIDE)
                    t = jnp.dot(lefts2[0], right[0][:, pl.ds(lo + at, step)], preferred_element_type=f32)
                    t = t + jnp.dot(lefts2[1], right[1][:, pl.ds(lo + at, step)], preferred_element_type=f32)
                    dst[:, :, :, :, pl.ds(at, step)] = t.astype(b16).reshape(zn, 2, 2, nr, step)
                    return 0

                lax.fori_loop(0, nc // step, cols, 0)

            return make

        def both(i):
            return (own(i), other(i))

        def fold4(quarters):
            row = lax.rem(lax.broadcasted_iota(jnp.int32, quarters[0].shape, 0), 8)
            here = k == 0

            def put(a, b):
                n = a.shape[0]
                low = jnp.where(here, a, pltpu.roll(a, n - 4, 0))
                high = jnp.where(here, pltpu.roll(b, 4, 0), b)
                t = jnp.where(row < 4, low, high)
                return t.reshape(zn * 4, 8, t.shape[1])

            t = jnp.concatenate([put(*quarters[:2]), put(*quarters[2:])], axis=1)
            return t.astype(b16).reshape(zn, 2, 2, 16, t.shape[2])

        def rest_product(dst):
            step = 3 * WIDE
            for i in (H2B, OTB, GB, GG, GU):
                share[i].ready()
            columns = []
            for left, right, n in ((OTB, GB, width), (H2B, GG, ff), (H2B, GU, ff)):
                columns += [(left, right, c) for c in range(0, n, step)]
            per = rest_w // step

            def one(entry):
                if entry is None:
                    return jnp.zeros((own(H2B).shape[0], step), f32)
                left, right, c = entry
                return jnp.dot(own(left)[...], own(right)[:, c : c + step], preferred_element_type=f32) + jnp.dot(
                    other(left)[...], other(right)[:, c : c + step], preferred_element_type=f32
                )

            for c in range(per):
                quarters = []
                for q in range(4):
                    at = q * per + c
                    quarters.append(one(columns[at] if at < len(columns) else None))
                dst[:, :, :, :, c * step : (c + 1) * step] = fold4(quarters)

        def qkv_rest_product(dst):
            for i in (HNB,):
                share[i].ready()
            gq_share.ready()
            quarters = []
            for q in range(4):
                lo, hi = q * qkv_rest_w, min((q + 1) * qkv_rest_w, qkv_w)
                t = jnp.dot(own(HNB)[...], gq[:, lo:hi], preferred_element_type=f32) + jnp.dot(
                    other(HNB)[...], gq_other[:, lo:hi], preferred_element_type=f32
                )
                if hi - lo < qkv_rest_w:
                    t = jnp.concatenate([t, jnp.zeros((t.shape[0], qkv_rest_w - hi + lo), f32)], axis=1)
                quarters.append(t)
            dst[...] = fold4(quarters)

        gq_both = (gq, gq_other)
        makes = [product(ACT, both(GY), 0, ra * i, (ACT, GY)) for i in range(n_down)]
        makes += [product(H2, both(g), lo, 0, (H2, g)) for g in (GG, GU) for lo in (0, half_ff)]
        makes += [product(OT, both(GB), 0, 0, (OT, GB)), rest_product]
        makes += [product(HN, gq_both, 0, 0, (HN,)), product(HN, gq_both, 2 * KV_LANES, 0, (HN,)), qkv_rest_product]
        targets = [outs[0].at[pl.ds(ra * i, ra), :] for i in range(n_down)]
        targets += [outs[g].at[:, pl.ds(lo, half_ff)] for g in (1, 2) for lo in (0, half_ff)]
        targets += [outs[3], outs[4], outs[5].at[:, pl.ds(0, 2 * KV_LANES)], outs[5].at[:, pl.ds(2 * KV_LANES, q_rows)], outs[6]]
        items = []
        for i, (nr, nc) in enumerate(sizes):
            slot = held.at[i % ring, :, :, :, pl.ds(0, nr), pl.ds(0, nc)]
            items.append(
                Sum(makes[i], slot, bufs[3 * i : 3 * i + 3], targets[i], send.at[i], recv.at[i], zn)
            )
        load_o = pltpu.make_async_copy(oh_ref, oh, pl_.at[n_in])
        load_o.start()
        gx.start()
        for i in (ACT, GY, H2, GG, GU, OT, GB, H2B, OTB, HN, HNB):
            share[i].start()
        dq[...] = jnp.zeros(dq.shape, f32)

        def clear(i, _):
            dkv[i] = jnp.zeros(dkv.shape[1:], f32)
            return 0

        lax.fori_loop(0, zn, clear, 0)
        stage_step(items, 4, 0)

        def turn(j, block):
            flat = {b: turned(block(b)) for b in sorted({key_slot(g)[0] for g in groups})}
            for g in groups:
                b, side = key_slot(g)
                kt[j, g] = flat[b][side * HEAD_SIZE : (side + 1) * HEAD_SIZE]

        by_span(turn, kvg, cn, rows)
        stage_step(items, 4, 1)
        gx.arrived()
        load_o.wait()
        for half_ in range(2):
            for zp in range(2):
                p = pair_index(half_, zp)
                for g in groups:
                    g_tile = pair_tile(gh, g, half_, zp)
                    o_tile = pair_tile(oh, g, half_, zp)
                    delta[g, p] = jnp.sum(g_tile * o_tile, axis=0, keepdims=True)
                    set_padded(qt, g, p, pair_tile(qh, g, half_, zp), key_slot(g)[1])
                    set_padded(dot_, g, p, g_tile, value_slot(g)[1])

        def step(t, _):
            p, j, zz, yy, late, edge = walk(t, y, cn)

            def run(masked):
                seen = visible(p, j, y, w, cn, wn, rows) if masked else None
                blocks = [key_block(kvg, zz, yy, late, rows, b) for b in range(KV_LANES // WIDE)]
                sums = [None] * len(blocks)

                def put(b, v):
                    sums[b] = v if sums[b] is None else sums[b] + v

                for g in groups:
                    s = jnp.dot(blocks[key_slot(g)[0]], qt[g, p], preferred_element_type=f32)
                    if masked:
                        s = jnp.where(seen, s, NEG)
                    e = jnp.exp(s - lse_ref[g, p])
                    dp = jnp.dot(blocks[value_slot(g)[0]], dot_[g, p], preferred_element_type=f32)
                    ds = (e * (dp - delta[g, p])).astype(b16)
                    put(value_slot(g)[0], nt(e.astype(b16), dot_[g, p]))
                    put(key_slot(g)[0], nt(ds, qt[g, p]))
                    dq[g, p] += jnp.dot(kt[j, g], ds, preferred_element_type=f32)
                for b, v in enumerate(sums):
                    dkv[zz, yy, :, :, pl.ds(late, rows), WIDE * b : WIDE * b + WIDE] += v.reshape(
                        2, 2, rows, WIDE
                    )

            pl.when(edge)(lambda: run(True))
            pl.when(jnp.logical_not(edge))(lambda: run(False))
            return 0

        def rope_back():
            low_lanes = lax.broadcasted_iota(jnp.int32, (tokens, WIDE), 1) < HEAD_SIZE
            quarter = HEAD_SIZE // 2

            def back(t, kind):
                if kind == "still":
                    return t
                cos, low, high = tab[0], tab[1], tab[2]
                r = t * cos - pltpu.roll(t, WIDE - quarter, 1) * low - pltpu.roll(t, quarter, 1) * high
                return r if kind == "turn" else jnp.where(low_lanes, r, t)

            def heads_block(mb, at):
                n = max(0, min(WIDE, mine - at))
                parts = []
                if n:
                    parts.append(dq_in[2 * mb, at : at + n, :].astype(f32))
                if n < WIDE:
                    lo = at + n - mine
                    parts.append(dq_in[2 * mb + 1, lo : lo + WIDE - n, :].astype(f32))
                return parts[0] if len(parts) == 1 else jnp.concatenate(parts, axis=0)

            kinds = ["turn", "mixed", "still"]
            for mb in range(mbs):
                at = slice(mb * tokens, (mb + 1) * tokens)
                for hh in range(2):
                    for b in range(KV_LANES // WIDE):
                        t = dkv_in[2 * mb + hh, :, WIDE * b : WIDE * b + WIDE].astype(f32)
                        lo = hh * KV_LANES + WIDE * b
                        gq[at, lo : lo + WIDE] = back(t, kinds[b]).astype(b16)
                for b in range(q_rows // WIDE):
                    t = heads_block(mb, WIDE * b).T
                    lo = 2 * KV_LANES + WIDE * b
                    gq[at, lo : lo + WIDE] = back(t, "turn").astype(b16)

        first = n_items - 3
        order = items[:first] + [None, None] + items[first:]
        t = 0
        per_step = -(-STEPS // (first - 3))
        kv_stage = 0
        for s in range(2, len(order) + 3):
            if t < STEPS:
                upto = min(STEPS, t + per_step)
                lax.fori_loop(t, upto, step, 0)
                t = upto
                if t == STEPS:

                    def pack(i, _):
                        for yy in range(2):
                            for xx in range(2):
                                kb[0][i, yy, xx] = dkv[i, yy, xx, k].astype(b16)
                                give[i, yy, xx] = dkv[i, yy, xx, 1 - k].astype(b16)
                        return 0

                    lax.fori_loop(0, zn, pack, 0)
                    kvx.stage(0)
                    kv_stage = 1
                    unpair(lambda g, p: dq[g, p] * scale, dqh)
                    dx.start()
            elif kv_stage < 4 and s <= first + 1:
                kvx.stage(kv_stage)
                kv_stage += 1
            if s == first + 2:
                while kv_stage < 5:
                    kvx.stage(kv_stage)
                    kv_stage += 1
                dx.arrived()
                rope_back()
                gq_share.start()
                gq_share.ready()
            stage_step(order, 4, s)
        dx.sent()
        gx.sent()
        gq_share.sent()
        for i in share:
            i.sent()

    stat = (HALF_GROUPS, 4, 1, PER * WIDE)
    block = (zn, mine, tokens)
    tile = (HALF_GROUPS, 4, WIDE, PER * WIDE)
    any_ = pl.BlockSpec(memory_space=pl.ANY)
    vmem = pl.BlockSpec(memory_space=pltpu.VMEM)
    dma = pltpu.SemaphoreType.DMA
    return pl.pallas_call(
        kernel,
        out_shape=[jax.ShapeDtypeStruct((all_rows, qkv_w), b16)]
        + [jax.ShapeDtypeStruct(s, f32) for s in outs_shape],
        in_specs=[any_, vmem, vmem, any_, vmem, vmem] + [any_] * n_in,
        out_specs=[vmem] * (1 + n_out),
        scratch_shapes=scratch
        + shares
        + [
            pltpu.VMEM((ring, zn, 2, 2, ra, max_cols), b16),
            pltpu.VMEM((all_rows, qkv_w), b16),
            pltpu.VMEM((zn, tokens, KV_LANES), b16),
            pltpu.VMEM(block, b16),
            pltpu.VMEM(block, b16),
            pltpu.VMEM(tile, b16),
            pltpu.VMEM(tile, b16),
            pltpu.VMEM((2 * cn, HALF_GROUPS, HEAD_SIZE, wn * rows), b16),
            pltpu.VMEM(stat, f32),
            pltpu.VMEM((HALF_GROUPS, 4, HEAD_SIZE, PER * WIDE), f32),
            pltpu.VMEM((zn, 2, 2, 2, tokens, KV_LANES), f32),
            pltpu.VMEM((zn, 2, 2, tokens, KV_LANES), b16),
        ]
        + Scatter.scratch(zn, tokens, KV_LANES)[:4]
        + [
            dma((n_items, Sum.SEMS)),
            dma((n_items, Sum.SEMS)),
            dma((n_in + 1,)),
            dma((n_in + 1,)),
            dma((n_in + 1,)),
            dma((2, zn)),
            dma((2, zn)),
            dma((Scatter.SEMS,)),
            dma((Scatter.SEMS,)),
        ],
        compiler_params=pltpu.CompilerParams(
            collective_id=collective_id, has_side_effects=True, vmem_limit_bytes=VMEM_LIMIT
        ),
    )(do, qh, kvg, oh, lse, tables, *ins_all)


def finish(gq, weights, rest, x, inv, gain, gx1, gain_sums, order, collective_id):
    zn = lax.axis_size("ctx") // 2
    f32, b16 = jnp.float32, jnp.bfloat16
    wa = weights.shape[0]
    width = x.shape[1]

    def kernel(gq_ref, w_ref, r_ref, x_ref, inv_ref, gain_ref, gx1_ref, sums_ref, order_ref, out, total, ghn, low, got, send, recv):
        greet(zn)
        z, y, x_, k = place()
        ghn[:, :wa] = lax.dot_general(gq_ref[...], w_ref[...], NT, preferred_element_type=f32)
        ghn[:, wa:] = lax.dot_general(gq_ref[...], r_ref[...], NT, preferred_element_type=f32)
        xf = x_ref[...].astype(f32)
        inv_ = inv_ref[...]
        grad = ghn[...]
        total[...] = jnp.zeros(total.shape, f32)
        total[0:1, :] = jnp.sum(grad * xf * inv_, axis=0, keepdims=True)
        total[1:2, :] = sums_ref[...]
        moves = [
            remote(total, got.at[0], send.at[0], recv.at[0], device(z, y, x_, 1 - k)),
            remote(total, got.at[1], send.at[1], recv.at[1], device(z, y, 1 - x_, k)),
            remote(total, got.at[2], send.at[2], recv.at[2], device(z, 1 - y, x_, k)),
        ]
        moves[0].start()
        weighted = grad * gain_ref[...]
        inner = jnp.mean(weighted * xf, axis=-1, keepdims=True)
        row = inv_ * weighted - xf * (inv_ * inv_ * inv_) * inner
        low[...] = (gx1_ref[...] + row).astype(b16)
        for i in range(3):
            moves[i].wait()
            total[...] = total[...] + got[i]
            if i < 2:
                moves[i + 1].start()
        ends = []
        for j in range(1, zn):
            ends.append(remote(total, got.at[2 + j], send.at[2 + j], recv.at[2 + j], device(lax.rem(z + j, zn), y, x_, k)))
            ends[-1].start()
        out[...] = lax.dot_general(low[...], order_ref[...], NT, preferred_element_type=f32).astype(b16)
        for c in ends:
            c.wait()
        t = total[...]
        for j in range(1, zn):
            t = t + got[2 + j]
        total[...] = t

    vmem = pl.BlockSpec(memory_space=pltpu.VMEM)
    return pl.pallas_call(
        kernel,
        out_shape=[jax.ShapeDtypeStruct(x.shape, b16), jax.ShapeDtypeStruct((8, width), f32)],
        in_specs=[vmem] * 9,
        out_specs=[vmem] * 2,
        scratch_shapes=[
            pltpu.VMEM(x.shape, f32),
            pltpu.VMEM(x.shape, b16),
            pltpu.VMEM((2 + zn, 8, width), f32),
            pltpu.SemaphoreType.DMA((2 + zn,)),
            pltpu.SemaphoreType.DMA((2 + zn,)),
        ],
        compiler_params=pltpu.CompilerParams(
            collective_id=collective_id, has_side_effects=True, vmem_limit_bytes=VMEM_LIMIT
        ),
    )(gq, weights, rest, x, inv, gain, gx1, gain_sums, order)


def rotate_lanes(t, cos, low, high):
    quarter = HEAD_SIZE // 2
    return t * cos + jnp.roll(t, -quarter, axis=-1) * low + jnp.roll(t, quarter, axis=-1) * high


def lane_tables(positions):
    quarter = HEAD_SIZE // 2
    frequency = 10000.0 ** (-2.0 * jnp.arange(quarter, dtype=jnp.float32) / HEAD_SIZE)
    angles = positions.astype(jnp.float32)[:, None] * frequency[None, :]
    cos, sin = jnp.cos(angles), jnp.sin(angles)
    none = jnp.zeros_like(sin)

    def full(a, b, still):
        head = jnp.concatenate([a, b], axis=1)
        keys = jnp.tile(head, (1, HALF_GROUPS))
        still = jnp.full_like(keys, still)
        return jnp.concatenate([keys, still, keys, still, jnp.tile(head, (1, QUERY_HEADS))], axis=1)

    return full(cos, cos, 1.0), full(-sin, none, 0.0), full(none, sin, 0.0)


def fast_device(
    inputs,
    attn_gain,
    query_weight,
    key_matrix,
    value_matrix,
    out_weight,
    ffn_gain,
    gate_weight,
    up_weight,
    down_weight,
    cotangent,
):
    f32, b16 = jnp.float32, jnp.bfloat16
    cn, wn = lax.axis_size("ctx"), lax.axis_size("ws")
    dn = cn * wn
    zn = cn // 2
    mbs, tokens, width = inputs.shape
    own = query_weight.shape[0]
    ra = own // 16 * 16
    rb = own - ra
    q_width = query_weight.shape[1]
    hid = KEY_VALUE_HEADS * HEAD_SIZE
    ff = gate_weight.shape[1]
    rows = mbs * tokens
    wa = dn * ra

    new = jnp.arange(width)
    old = jnp.where(
        new < wa, own * (new // ra) + new % ra, own * ((new - wa) // rb) + ra + (new - wa) % rb
    )
    order = (jnp.arange(width)[:, None] == old[None, :]).astype(b16)

    def to_order(t):
        return jnp.dot(t, order, preferred_element_type=f32).astype(t.dtype)

    def from_order(t):
        return lax.dot_general(t, order, NT, preferred_element_type=f32).astype(t.dtype)

    fold = 16 // rb

    def folded(t):
        return t.reshape(t.shape[0], fold, -1).transpose(1, 0, 2).reshape(16, -1)

    qkv_w = q_width + 2 * hid
    pad1 = -qkv_w % (fold * WIDE)
    rest_w = width + 2 * ff
    pad2 = -rest_w % (fold * WIDE)
    moved = to_order(
        jnp.concatenate(
            [inputs.reshape(rows, width), cotangent.reshape(rows, width), out_weight, down_weight]
        )
    )
    x_low, gy_low = moved[:rows], moved[rows : 2 * rows]
    out_p, down_p = moved[2 * rows : 2 * rows + own], moved[2 * rows + own :]
    half_hid = hid // 2
    qkv = jnp.concatenate(
        [
            key_matrix[:, :half_hid],
            value_matrix[:, :half_hid],
            key_matrix[:, half_hid:],
            value_matrix[:, half_hid:],
            query_weight,
        ],
        axis=1,
    )
    gains = jnp.stack([attn_gain, ffn_gain])
    gains = jnp.pad(gains, ((0, rb - 2), (0, pad1 - own)))
    b1 = folded(jnp.concatenate([qkv[ra:], gains], axis=1))
    b2 = folded(
        jnp.pad(
            jnp.concatenate([out_p[ra:], gate_weight[ra:], up_weight[ra:]], axis=1), ((0, 0), (0, pad2))
        )
    )
    qkv_a, b1g = gather_all([qkv, b1], [ra, 16], [(1, 1), (1, 1)], 1)

    def unfolded(t):
        cols = t.shape[-1]
        return t.reshape(dn, fold, rb, cols).transpose(0, 2, 1, 3).reshape(dn * rb, fold * cols)

    flat = lambda t: t.reshape(-1, t.shape[-1])
    qkv_a, b1u = flat(qkv_a), unfolded(b1g)
    qkv_b = b1u[:, :qkv_w]
    gains_all = b1u[:, qkv_w : qkv_w + own].reshape(dn, rb, own)
    in_order = lambda t: jnp.concatenate([t[:, :ra].reshape(-1), t[:, ra:].reshape(-1)]).astype(f32)
    gain1, gain2 = in_order(gains_all[:, 0]), in_order(gains_all[:, 1])

    def mm(h, a, b):
        return matrix_multiply(h[:, :wa], a) + matrix_multiply(h[:, wa:], b)

    def mm_back(g, a, b):
        return jnp.concatenate([back_product(g, a), back_product(g, b)], axis=1)

    c, w = lax.axis_index("ctx"), lax.axis_index("ws")
    places = query_places(c, w, tokens, cn, wn)
    cos, low, high = (jnp.tile(t, (mbs, 1)) for t in lane_tables(places))
    q_at = 2 * hid
    x = x_low.astype(f32)
    hn, inv1 = normalize(x, gain1)
    hn = hn.astype(b16)
    proj = rotate_lanes(mm(hn, qkv_a, qkv_b), cos, low, high)
    kv = proj[:, : 2 * hid].astype(b16).reshape(mbs, tokens, 2 * hid)
    q = (proj[:, 2 * hid :] * HEAD_SIZE**-0.5).astype(b16)
    q = q.reshape(mbs, tokens, q_width).transpose(0, 2, 1)
    o_t, qh, kvg, oh, lse, out_a, gate_a, up_a, down_a, b2g = gather_attend(
        q,
        kv,
        [out_p, gate_weight, up_weight, down_p, b2],
        [ra, ra, ra, down_p.shape[0], 16],
        [(1, 1), (1, 2), (1, 2), (2, 1), (1, 1)],
        2,
    )
    out_a, gate_a, up_a, down_w = map(flat, (out_a, gate_a, up_a, down_a))
    b2u = unfolded(b2g)
    out_b = b2u[:, :width]
    gate_b, up_b = b2u[:, width : width + ff], b2u[:, width + ff : width + 2 * ff]
    o_p = to_order(o_t.transpose(0, 2, 1).reshape(rows, q_width))
    x1 = x + mm(o_p, out_a, out_b)
    h2, inv2 = normalize(x1, gain2)
    h2 = h2.astype(b16)
    gate = mm(h2, gate_a, gate_b)
    up = mm(h2, up_a, up_b)
    sig = jax.nn.sigmoid(gate)
    silu = gate * sig
    act = (silu * up).astype(b16)
    out = from_order((x1 + matrix_multiply(act, down_w)).astype(b16))
    gy = gy_low.astype(f32)
    ga = back_product(gy_low, down_w)
    g_gate = (ga * up * sig * (1.0 + gate * (1.0 - sig))).astype(b16)
    g_up = (ga * silu).astype(b16)
    gh2 = mm_back(g_gate, gate_a, gate_b) + mm_back(g_up, up_a, up_b)
    mid, gain2_sum = normalize_back(x1, inv2, gain2, gh2)
    gx1 = mid + gy
    gb = gx1.astype(b16)
    gattn = from_order(mm_back(gb, out_a, out_b).astype(b16))
    gb_plain = from_order(gb)
    gy_plain = cotangent.reshape(rows, width)
    left = lambda t: t.T.reshape(zn, 2, 2, 2, -1, rows)
    wide = 2 * HEAD_SIZE
    head_tables = jnp.stack([t[:tokens, q_at : q_at + wide] for t in (cos, low, high)])
    gq, r_down, r_gate, r_up, r_out, r_b2, r_qkv, r_b1 = scatter_attend(
        gattn.reshape(mbs, tokens, q_width).transpose(0, 2, 1),
        qh,
        kvg,
        oh,
        lse,
        head_tables,
        [left(act), left(h2[:, :wa]), left(o_p[:, :wa]), left(hn[:, :wa])],
        [h2[:, wa:].T, o_p[:, wa:].T, hn[:, wa:].T],
        [gy_plain, gb_plain, g_gate, g_up],
        ((rest_w + pad2) // fold, (qkv_w + pad1) // fold),
        3,
    )
    input_grad, gain_sums = finish(
        gq, qkv_a, qkv_b, x_low, inv1, gain1[None], gx1, gain2_sum[None], order, 4
    )
    device_at = c * wn + w

    def own_gain(t):
        first = lax.dynamic_slice(t, (device_at * ra,), (ra,))
        return jnp.concatenate([first, lax.dynamic_slice(t, (wa + device_at * rb,), (rb,))])

    def own_rows(t):
        return t.reshape(fold, rb, -1).transpose(1, 0, 2).reshape(rb, -1)

    e1, e2 = own_rows(r_b1), own_rows(r_b2)
    whole = lambda a, b: jnp.concatenate([a, b], axis=0)
    d_qkv = whole(r_qkv, e1[:, :qkv_w])
    return (
        out.reshape(inputs.shape),
        input_grad.reshape(inputs.shape),
        own_gain(gain_sums[0]),
        d_qkv[:, 2 * hid :],
        jnp.concatenate([d_qkv[:, :half_hid], d_qkv[:, hid : hid + half_hid]], axis=1),
        jnp.concatenate([d_qkv[:, half_hid:hid], d_qkv[:, hid + half_hid : 2 * hid]], axis=1),
        whole(r_out, e2[:, :width]),
        own_gain(gain_sums[1]),
        whole(r_gate, e2[:, width : width + ff]),
        whole(r_up, e2[:, width + ff : width + 2 * ff]),
        r_down,
    )


def solution(mesh):
    in_specs = (
        P(None, ("ctx", "ws"), None),
        P(("ctx", "ws")),
        P(("ctx", "ws"), None),
        P(("ctx", "ws"), None),
        P(("ctx", "ws"), None),
        P(("ctx", "ws"), None),
        P(("ctx", "ws")),
        P(("ctx", "ws"), None),
        P(("ctx", "ws"), None),
        P(("ctx", "ws"), None),
        P(None, ("ctx", "ws"), None),
    )
    out_specs = (
        P(None, ("ctx", "ws"), None),
        P(None, ("ctx", "ws"), None),
        P(("ctx", "ws")),
        P(("ctx", "ws"), None),
        P(("ctx", "ws"), None),
        P(("ctx", "ws"), None),
        P(("ctx", "ws"), None),
        P(("ctx", "ws")),
        P(("ctx", "ws"), None),
        P(("ctx", "ws"), None),
        P(("ctx", "ws"), None),
    )
    body = fast_device if fits_fast(mesh) else per_device
    return jax.shard_map(
        body, mesh=mesh, in_specs=in_specs, out_specs=out_specs, check_vma=False
    )
```

```python
import jax
import jax.numpy as jnp
from jax import lax
from jax.experimental import pallas as pl
from jax.experimental.pallas import tpu as pltpu
from jax.sharding import PartitionSpec as P
import functools

QUERY_HEADS = 18
KEY_VALUE_HEADS = 6
HEAD_SIZE = 64


EPSILON = 1e-05
MASKED_SCORE = -1e30


def shifted(block, axis, distance):
    devices = range(lax.axis_size(axis))
    route = [((i - distance) % len(devices), i) for i in devices]
    return lax.ppermute(block, axis, route)


def as_sent(x):

    def short(part):
        return part.astype(jnp.bfloat16) if part.dtype == jnp.float32 else part

    return jax.tree.map(short, x)


def matrix_multiply(left, right):
    return jnp.dot(left, right, preferred_element_type=jnp.float32)


def outer_sum(left, right):
    return jnp.einsum("ri,rj->ij", left, right, preferred_element_type=jnp.float32)


def back_product(gradient, weight):
    return jnp.einsum("rj,ij->ri", gradient, weight, preferred_element_type=jnp.float32)


def normalize(layer_rows, gain_vector):
    inverse = lax.rsqrt(jnp.mean(layer_rows * layer_rows, axis=-1, keepdims=True) + EPSILON)
    return (layer_rows * inverse * gain_vector, inverse)


def normalize_back(layer_rows, inverse, gain_vector, gradient):
    weighted = gradient * gain_vector
    inner_mean = jnp.mean(weighted * layer_rows, axis=-1, keepdims=True)
    row_grad = inverse * weighted - layer_rows * (inverse * inverse * inverse) * inner_mean
    gain_grad = jnp.sum(gradient * layer_rows * inverse, axis=0)
    return (row_grad, gain_grad)


def rotary_tables(token_positions):
    quarter = HEAD_SIZE // 2
    frequency = 10000.0 ** (-2.0 * jnp.arange(quarter, dtype=jnp.float32) / HEAD_SIZE)
    angles = token_positions.astype(jnp.float32)[:, None] * frequency[None, :]
    return (jnp.cos(angles)[:, None, :], jnp.sin(angles)[:, None, :])


def rotate(heads, cosine_table, sine_table):
    quarter = HEAD_SIZE // 2
    first_half = heads[..., :quarter]
    second_half = heads[..., quarter:]
    return jnp.concatenate(
        [
            first_half * cosine_table - second_half * sine_table,
            second_half * cosine_table + first_half * sine_table,
        ],
        axis=-1,
    )


def rotate_back(heads, cosine_table, sine_table):
    quarter = HEAD_SIZE // 2
    first_half = heads[..., :quarter]
    second_half = heads[..., quarter:]
    return jnp.concatenate(
        [
            first_half * cosine_table + second_half * sine_table,
            second_half * cosine_table - first_half * sine_table,
        ],
        axis=-1,
    )


def query_places(own_ctx, own_member, count_of_rows, ctx_count, device_count):
    rows_per_half = count_of_rows // 2
    local_index = jnp.arange(count_of_rows, dtype=jnp.int32)
    span_index = jnp.where(local_index < rows_per_half, own_ctx, 2 * ctx_count - 1 - own_ctx)
    return (
        span_index * (device_count * rows_per_half)
        + own_member * rows_per_half
        + local_index % rows_per_half
    )


def block_places(source_ctx, count_of_rows, ctx_count, device_count):
    rows_per_half = count_of_rows // 2
    member_index = jnp.arange(device_count, dtype=jnp.int32)[:, None, None]
    half_index = jnp.arange(2, dtype=jnp.int32)[None, :, None]
    inner_index = jnp.arange(rows_per_half, dtype=jnp.int32)[None, None, :]
    span_index = jnp.where(half_index == 0, source_ctx, 2 * ctx_count - 1 - source_ctx)
    return (
        span_index * (device_count * rows_per_half) + member_index * rows_per_half + inner_index
    ).reshape(-1)


def split_block(block_of_keys):
    hidden_width = KEY_VALUE_HEADS * HEAD_SIZE
    device_count, _, rows_per_half, _ = block_of_keys.shape
    rows_of_keys = block_of_keys[..., :hidden_width].reshape(
        device_count, 2, rows_per_half, KEY_VALUE_HEADS, HEAD_SIZE
    )
    rows_of_values = block_of_keys[..., hidden_width:].reshape(
        device_count, 2, rows_per_half, KEY_VALUE_HEADS, HEAD_SIZE
    )
    return (rows_of_keys, rows_of_values)


def attend(query_rows, rows_of_keys, rows_of_values, causal_visible):
    scores = jnp.einsum(
        "rgjd,kgd->grjk", query_rows, rows_of_keys, preferred_element_type=jnp.float32
    ) * HEAD_SIZE ** (-0.5)
    if causal_visible is not None:
        scores = jnp.where(causal_visible[None, :, None, :], scores, MASKED_SCORE)
    row_max = jnp.max(scores, axis=-1)
    exponentials = jnp.exp(scores - row_max[..., None])
    row_total = jnp.sum(exponentials, axis=-1)
    mixture = jnp.einsum(
        "grjk,kgd->rgjd",
        exponentials.astype(jnp.bfloat16),
        rows_of_values,
        preferred_element_type=jnp.float32,
    )
    return (jnp.transpose(row_max, (1, 0, 2)), jnp.transpose(row_total, (1, 0, 2)), mixture)


def empty_part(count_of_rows):
    queries_per_group = QUERY_HEADS // KEY_VALUE_HEADS
    return (
        jnp.full((count_of_rows, KEY_VALUE_HEADS, queries_per_group), MASKED_SCORE, jnp.float32),
        jnp.zeros((count_of_rows, KEY_VALUE_HEADS, queries_per_group), jnp.float32),
        jnp.zeros((count_of_rows, KEY_VALUE_HEADS, queries_per_group, HEAD_SIZE), jnp.float32),
    )


def combine(carried, incoming):
    carried_max, carried_total, carried_mix = carried
    incoming_max, incoming_total, incoming_mix = incoming
    new_max = jnp.maximum(carried_max, incoming_max)
    carried_scale = jnp.exp(carried_max - new_max)
    incoming_scale = jnp.exp(incoming_max - new_max)
    return (
        new_max,
        carried_total * carried_scale + incoming_total * incoming_scale,
        carried_mix * carried_scale[..., None] + incoming_mix * incoming_scale[..., None],
    )


def forward_block(carried, block_of_keys, source_ctx, own_ctx, query_rows, own_places, ctx_count):
    rows_of_keys, rows_of_values = split_block(block_of_keys)
    device_count, _, rows_per_half, _ = block_of_keys.shape

    def forward_earlier():
        return attend(
            query_rows,
            rows_of_keys[:, 0].reshape(-1, KEY_VALUE_HEADS, HEAD_SIZE),
            rows_of_values[:, 0].reshape(-1, KEY_VALUE_HEADS, HEAD_SIZE),
            None,
        )

    def forward_later():
        late_part = attend(
            query_rows[rows_per_half:],
            rows_of_keys.reshape(-1, KEY_VALUE_HEADS, HEAD_SIZE),
            rows_of_values.reshape(-1, KEY_VALUE_HEADS, HEAD_SIZE),
            None,
        )
        early_part = empty_part(rows_per_half)
        return tuple(
            (
                jnp.concatenate([early_piece, late_piece], axis=0)
                for early_piece, late_piece in zip(early_part, late_part)
            )
        )

    def forward_diagonal():
        key_places = block_places(source_ctx, 2 * rows_per_half, ctx_count, device_count)
        causal_visible = own_places[:, None] >= key_places[None, :]
        return attend(
            query_rows,
            rows_of_keys.reshape(-1, KEY_VALUE_HEADS, HEAD_SIZE),
            rows_of_values.reshape(-1, KEY_VALUE_HEADS, HEAD_SIZE),
            causal_visible,
        )

    branch_index = jnp.where(source_ctx == own_ctx, 2, jnp.where(source_ctx > own_ctx, 1, 0))
    return combine(
        carried, lax.switch(branch_index, [forward_earlier, forward_later, forward_diagonal])
    )


def attend_back(
    query_rows, attended_grad, log_total, delta_rows, rows_of_keys, rows_of_values, causal_visible
):
    scores = jnp.einsum(
        "rgjd,kgd->grjk", query_rows, rows_of_keys, preferred_element_type=jnp.float32
    ) * HEAD_SIZE ** (-0.5)
    if causal_visible is not None:
        scores = jnp.where(causal_visible[None, :, None, :], scores, MASKED_SCORE)
    probabilities = jnp.exp(scores - jnp.transpose(log_total, (1, 0, 2))[..., None])
    prob_grad = jnp.einsum(
        "rgjd,kgd->grjk", attended_grad, rows_of_values, preferred_element_type=jnp.float32
    )
    score_grad = (
        probabilities * (prob_grad - jnp.transpose(delta_rows, (1, 0, 2))[..., None])
    ).astype(jnp.bfloat16)
    query_part = jnp.einsum(
        "grjk,kgd->rgjd", score_grad, rows_of_keys, preferred_element_type=jnp.float32
    ) * HEAD_SIZE ** (-0.5)
    key_part = jnp.einsum(
        "grjk,rgjd->kgd", score_grad, query_rows, preferred_element_type=jnp.float32
    ) * HEAD_SIZE ** (-0.5)
    value_part = jnp.einsum(
        "grjk,rgjd->kgd",
        probabilities.astype(jnp.bfloat16),
        attended_grad,
        preferred_element_type=jnp.float32,
    )
    return (query_part, key_part, value_part)


def backward_block(
    block_of_keys,
    source_ctx,
    own_ctx,
    query_rows,
    attended_grad,
    log_total,
    delta_rows,
    own_places,
    ctx_count,
):
    rows_of_keys, rows_of_values = split_block(block_of_keys)
    device_count, _, rows_per_half, _ = block_of_keys.shape
    hidden_width = KEY_VALUE_HEADS * HEAD_SIZE

    def backward_earlier():
        query_part, key_part, value_part = attend_back(
            query_rows,
            attended_grad,
            log_total,
            delta_rows,
            rows_of_keys[:, 0].reshape(-1, KEY_VALUE_HEADS, HEAD_SIZE),
            rows_of_values[:, 0].reshape(-1, KEY_VALUE_HEADS, HEAD_SIZE),
            None,
        )
        early_grad = jnp.concatenate(
            [
                key_part.reshape(device_count, 1, rows_per_half, hidden_width),
                value_part.reshape(device_count, 1, rows_per_half, hidden_width),
            ],
            axis=-1,
        )
        return (query_part, jnp.concatenate([early_grad, jnp.zeros_like(early_grad)], axis=1))

    def backward_later():
        query_part, key_part, value_part = attend_back(
            query_rows[rows_per_half:],
            attended_grad[rows_per_half:],
            log_total[rows_per_half:],
            delta_rows[rows_per_half:],
            rows_of_keys.reshape(-1, KEY_VALUE_HEADS, HEAD_SIZE),
            rows_of_values.reshape(-1, KEY_VALUE_HEADS, HEAD_SIZE),
            None,
        )
        query_part = jnp.concatenate([jnp.zeros_like(query_part), query_part], axis=0)
        return (
            query_part,
            jnp.concatenate(
                [
                    key_part.reshape(device_count, 2, rows_per_half, hidden_width),
                    value_part.reshape(device_count, 2, rows_per_half, hidden_width),
                ],
                axis=-1,
            ),
        )

    def backward_diagonal():
        key_places = block_places(source_ctx, 2 * rows_per_half, ctx_count, device_count)
        causal_visible = own_places[:, None] >= key_places[None, :]
        query_part, key_part, value_part = attend_back(
            query_rows,
            attended_grad,
            log_total,
            delta_rows,
            rows_of_keys.reshape(-1, KEY_VALUE_HEADS, HEAD_SIZE),
            rows_of_values.reshape(-1, KEY_VALUE_HEADS, HEAD_SIZE),
            causal_visible,
        )
        return (
            query_part,
            jnp.concatenate(
                [
                    key_part.reshape(device_count, 2, rows_per_half, hidden_width),
                    value_part.reshape(device_count, 2, rows_per_half, hidden_width),
                ],
                axis=-1,
            ),
        )

    branch_index = jnp.where(source_ctx == own_ctx, 2, jnp.where(source_ctx > own_ctx, 1, 0))
    return lax.switch(branch_index, [backward_earlier, backward_later, backward_diagonal])


def per_device(
    inputs,
    attn_gain,
    query_weight,
    key_matrix,
    value_matrix,
    out_weight,
    ffn_gain,
    gate_weight,
    up_weight,
    down_weight,
    cotangent,
):
    ctx_count = lax.axis_size("ctx")
    device_count = lax.axis_size("ws")
    own_ctx = lax.axis_index("ctx")
    own_member = lax.axis_index("ws")
    micro_count, count_of_rows, _ = inputs.shape
    rows_per_half = count_of_rows // 2
    queries_per_group = QUERY_HEADS // KEY_VALUE_HEADS
    hidden_width = KEY_VALUE_HEADS * HEAD_SIZE
    own_places = query_places(own_ctx, own_member, count_of_rows, ctx_count, device_count)
    cosine_table, sine_table = rotary_tables(own_places)
    grad_sums = None
    layer_outs = []
    input_grads = []
    for micro_batch in range(micro_count):
        gathered = (
            lax.all_gather(attn_gain, ("ctx", "ws"), axis=0, tiled=True),
            lax.all_gather(query_weight, ("ctx", "ws"), axis=0, tiled=True),
            lax.all_gather(key_matrix, ("ctx", "ws"), axis=0, tiled=True),
            lax.all_gather(value_matrix, ("ctx", "ws"), axis=0, tiled=True),
            lax.all_gather(out_weight, ("ctx", "ws"), axis=0, tiled=True),
            lax.all_gather(ffn_gain, ("ctx", "ws"), axis=0, tiled=True),
            lax.all_gather(gate_weight, ("ctx", "ws"), axis=0, tiled=True),
            lax.all_gather(up_weight, ("ctx", "ws"), axis=0, tiled=True),
            lax.all_gather(down_weight, ("ctx", "ws"), axis=0, tiled=True),
        )
        (
            full_attn_gain,
            full_query,
            complete_key,
            full_value,
            full_out,
            full_ffn_gain,
            full_gate,
            full_up,
            full_down,
        ) = gathered
        first_gain = full_attn_gain.astype(jnp.float32)
        second_gain = full_ffn_gain.astype(jnp.float32)
        layer_rows = inputs[micro_batch].astype(jnp.float32)
        normalized_rows, first_inverse = normalize(layer_rows, first_gain)
        normalized_reduced = normalized_rows.astype(jnp.bfloat16)
        query_rows = rotate(
            matrix_multiply(normalized_reduced, full_query).reshape(
                count_of_rows, QUERY_HEADS, HEAD_SIZE
            ),
            cosine_table,
            sine_table,
        )
        query_rows = query_rows.astype(jnp.bfloat16).reshape(
            count_of_rows, KEY_VALUE_HEADS, queries_per_group, HEAD_SIZE
        )
        rows_of_keys = rotate(
            matrix_multiply(normalized_reduced, complete_key).reshape(
                count_of_rows, KEY_VALUE_HEADS, HEAD_SIZE
            ),
            cosine_table,
            sine_table,
        ).astype(jnp.bfloat16)
        rows_of_values = matrix_multiply(normalized_reduced, full_value).astype(jnp.bfloat16)
        local_block = jnp.concatenate(
            [rows_of_keys.reshape(count_of_rows, hidden_width), rows_of_values], axis=-1
        )
        group_block = lax.all_gather(local_block, "ws", axis=0, tiled=True).reshape(
            device_count, 2, rows_per_half, 2 * hidden_width
        )

        def fold_step(carried, shard_piece):

            def visit_block(state_now, block_entry):
                block_of_keys, source_ctx = block_entry
                return (
                    forward_block(
                        state_now,
                        block_of_keys,
                        source_ctx,
                        own_ctx,
                        query_rows,
                        own_places,
                        ctx_count,
                    ),
                    None,
                )

            source_list = jnp.arange(shard_piece.shape[0], dtype=jnp.int32)
            result_state, _ = lax.scan(visit_block, carried, (shard_piece, source_list))
            return result_state

        row_max, row_total, mixture = fold_step(
            empty_part(count_of_rows), lax.all_gather(group_block[None], "ctx", axis=0, tiled=True)
        )
        attended = mixture / row_total[..., None]
        log_total = row_max + jnp.log(row_total)
        attended_low = attended.astype(jnp.bfloat16).reshape(count_of_rows, QUERY_HEADS * HEAD_SIZE)
        middle = layer_rows + matrix_multiply(attended_low, full_out)
        hidden, second_inverse = normalize(middle, second_gain)
        hidden_low = hidden.astype(jnp.bfloat16)
        gate_rows = matrix_multiply(hidden_low, full_gate)
        up_rows = matrix_multiply(hidden_low, full_up)
        sigmoid_gate = jax.nn.sigmoid(gate_rows)
        silu_gate = gate_rows * sigmoid_gate
        activated = (silu_gate * up_rows).astype(jnp.bfloat16)
        layer_outs.append((middle + matrix_multiply(activated, full_down)).astype(jnp.bfloat16))
        upstream_low = cotangent[micro_batch]
        upstream = upstream_low.astype(jnp.float32)
        down_sum = outer_sum(activated, upstream_low)
        act_grad = back_product(upstream_low, full_down)
        gate_low = (
            act_grad * up_rows * sigmoid_gate * (1.0 + gate_rows * (1.0 - sigmoid_gate))
        ).astype(jnp.bfloat16)
        up_low = (act_grad * silu_gate).astype(jnp.bfloat16)
        gate_sum = outer_sum(hidden_low, gate_low)
        up_sum = outer_sum(hidden_low, up_low)
        hidden_grad = back_product(gate_low, full_gate) + back_product(up_low, full_up)
        middle_part, ffn_gain_sum = normalize_back(middle, second_inverse, second_gain, hidden_grad)
        middle_grad = middle_part + upstream
        branch_low = middle_grad.astype(jnp.bfloat16)
        out_sum = outer_sum(attended_low, branch_low)
        attended_grad = (
            back_product(branch_low, full_out)
            .reshape(count_of_rows, KEY_VALUE_HEADS, queries_per_group, HEAD_SIZE)
            .astype(jnp.bfloat16)
        )
        delta_rows = jnp.sum(attended_grad.astype(jnp.float32) * attended, axis=-1)

        def cycle_step(turn_index, carried):
            block_of_keys, block_grad, query_total = carried
            source_ctx = (own_ctx - turn_index) % ctx_count
            query_part, block_part = backward_block(
                block_of_keys,
                source_ctx,
                own_ctx,
                query_rows,
                attended_grad,
                log_total,
                delta_rows,
                own_places,
                ctx_count,
            )
            block_grad = block_grad + block_part
            next_block = shifted(block_of_keys, "ctx", 1)
            next_grad = shifted(as_sent(block_grad), "ctx", 1).astype(block_grad.dtype)
            return (next_block, next_grad, query_total + query_part)

        cycle_start = (
            group_block,
            jnp.zeros(group_block.shape, jnp.float32),
            jnp.zeros((count_of_rows, KEY_VALUE_HEADS, queries_per_group, HEAD_SIZE), jnp.float32),
        )
        _, block_grad, query_total = lax.fori_loop(0, ctx_count, cycle_step, cycle_start)
        local_gradient = (
            lax.psum_scatter(block_grad.astype(jnp.bfloat16), "ws", scatter_dimension=0, tiled=True)
            .astype(jnp.float32)
            .reshape(count_of_rows, 2 * hidden_width)
        )
        key_low = rotate_back(
            local_gradient[:, :hidden_width].reshape(count_of_rows, KEY_VALUE_HEADS, HEAD_SIZE),
            cosine_table,
            sine_table,
        )
        key_low = key_low.astype(jnp.bfloat16).reshape(count_of_rows, hidden_width)
        value_low = local_gradient[:, hidden_width:].astype(jnp.bfloat16)
        query_low = rotate_back(
            query_total.reshape(count_of_rows, QUERY_HEADS, HEAD_SIZE), cosine_table, sine_table
        )
        query_low = query_low.astype(jnp.bfloat16).reshape(count_of_rows, QUERY_HEADS * HEAD_SIZE)
        query_sum = outer_sum(normalized_reduced, query_low)
        key_sum = outer_sum(normalized_reduced, key_low)
        value_sum = outer_sum(normalized_reduced, value_low)
        normed_grad = (
            back_product(query_low, full_query)
            + back_product(key_low, complete_key)
            + back_product(value_low, full_value)
        )
        input_part, attn_gain_sum = normalize_back(
            layer_rows, first_inverse, first_gain, normed_grad
        )
        input_grads.append((middle_grad + input_part).astype(jnp.bfloat16))
        batch_terms = (
            attn_gain_sum,
            query_sum,
            key_sum,
            value_sum,
            out_sum,
            ffn_gain_sum,
            gate_sum,
            up_sum,
            down_sum,
        )
        if grad_sums is None:
            grad_sums = batch_terms
        else:
            grad_sums = tuple(
                (
                    earlier_sum + batch_term
                    for earlier_sum, batch_term in zip(grad_sums, batch_terms)
                )
            )
    owned_grads = (
        lax.psum_scatter(grad_sums[0], ("ctx", "ws"), scatter_dimension=0, tiled=True),
        lax.psum_scatter(grad_sums[1], ("ctx", "ws"), scatter_dimension=0, tiled=True),
        lax.psum_scatter(grad_sums[2], ("ctx", "ws"), scatter_dimension=0, tiled=True),
        lax.psum_scatter(grad_sums[3], ("ctx", "ws"), scatter_dimension=0, tiled=True),
        lax.psum_scatter(grad_sums[4], ("ctx", "ws"), scatter_dimension=0, tiled=True),
        lax.psum_scatter(grad_sums[5], ("ctx", "ws"), scatter_dimension=0, tiled=True),
        lax.psum_scatter(grad_sums[6], ("ctx", "ws"), scatter_dimension=0, tiled=True),
        lax.psum_scatter(grad_sums[7], ("ctx", "ws"), scatter_dimension=0, tiled=True),
        lax.psum_scatter(grad_sums[8], ("ctx", "ws"), scatter_dimension=0, tiled=True),
    )
    return (
        jnp.stack(layer_outs),
        jnp.stack(input_grads),
        owned_grads[0],
        owned_grads[1],
        owned_grads[2],
        owned_grads[3],
        owned_grads[4],
        owned_grads[5],
        owned_grads[6],
        owned_grads[7],
        owned_grads[8],
    )


MESH = pl.DeviceIdType.MESH
NEG = -1e30
WIDE = 128
VMEM_LIMIT = 61 * 1024 * 1024


def fits_fast(mesh):
    return mesh.shape["ctx"] == 8 and mesh.shape["ws"] == 4


def place():
    c = lax.axis_index("ctx")
    w = lax.axis_index("ws")
    return c // 2, lax.rem(c, 2), w // 2, lax.rem(w, 2)


def device(z, y, x, k):
    return (z * 2 + y, x * 2 + k)


def greet(zn):
    z, y, x, k = place()
    others = [device(lax.rem(z + j, zn), y, x, k) for j in range(1, zn)]
    others += [device(z, y, 1 - x, k), device(z, 1 - y, x, k), device(z, y, x, 1 - k)]
    barrier = pltpu.get_barrier_semaphore()
    for other in others:
        pl.semaphore_signal(barrier, inc=1, device_id=other, device_id_type=MESH)
    pl.semaphore_wait(barrier, len(others))


def remote(src, dst, send, recv, where):
    return pltpu.make_async_remote_copy(
        src_ref=src, dst_ref=dst, send_sem=send, recv_sem=recv, device_id=where, device_id_type=MESH
    )


class Gather:
    SEMS = 12

    def __init__(self, src, dst, send, recv, zn):
        z, y, x, k = place()
        own = dst.at[z, y, x, k]
        hz = zn // 2
        xn, yn, sib = device(z, y, 1 - x, k), device(z, 1 - y, x, k), device(z, y, x, 1 - k)

        def push(i, ref, where):
            return remote(ref, ref, send.at[i], recv.at[i], where)

        def col(yy, xx, lo=0, n=zn):
            return dst.at[pl.ds(lo, n), yy, xx, k]

        self.local = pltpu.make_async_copy(src(z), own, send.at[0])
        self.along = []
        for j in range(1, zn):
            zz = lax.rem(z + j, zn)
            self.along.append(remote(src(zz), own, send.at[j], recv.at[j], device(zz, y, x, k)))
        self.cols = [push(4, col(y, x), xn), push(5, col(y, x), yn)]
        self.corner = [push(7, col(1 - y, x, 0, hz), xn), push(8, col(y, 1 - x, hz, hz), yn)]
        self.twin_own = push(6, col(y, x), sib)
        self.twin_cols = [push(9, col(y, 1 - x), sib), push(10, col(1 - y, x), sib)]
        self.twin_corner = push(11, col(1 - y, 1 - x), sib)

    def stage(self, n):
        if n == 0:
            self.local.start()
            for c in self.along:
                c.start()
        elif n == 1:
            self.local.wait()
            for c in self.along:
                c.wait_recv()
            for c in self.cols:
                c.start()
            self.twin_own.start()
        elif n == 2:
            for c in self.cols:
                c.wait_recv()
            for c in self.corner:
                c.start()
            for c in self.twin_cols:
                c.start()
        elif n == 3:
            for c in self.corner:
                c.wait_recv()
            self.twin_corner.start()
        elif n == 4:
            for c in [self.twin_own] + self.twin_cols + [self.twin_corner]:
                c.wait_recv()
            for c in (
                self.along
                + self.cols
                + self.corner
                + [self.twin_own]
                + self.twin_cols
                + [self.twin_corner]
            ):
                c.wait_send()


def stage_step(items, stages, t):
    for n in range(stages):
        if 0 <= t - n < len(items) and items[t - n] is not None:
            items[t - n].stage(n)


def run_stages(items, stages):
    for t in range(len(items) + stages - 1):
        stage_step(items, stages, t)


def pieces_of(rows, cols, nrow, ncol):
    return [
        (i * (rows // nrow), rows // nrow, j * (cols // ncol), cols // ncol)
        for i in range(nrow)
        for j in range(ncol)
    ]


def gather_item(ref, out, r0, nr, c0, nc, send, recv, zn):
    src = ref.at[pl.ds(r0, nr), pl.ds(c0, nc)]
    dst = out.at[:, :, :, :, pl.ds(r0, nr), pl.ds(c0, nc)]
    return Gather(lambda zz: src, dst, send, recv, zn)


class Exchange:
    def __init__(self, src, dst, send, recv, zn):
        z, y, x, k = place()
        self.local = pltpu.make_async_copy(src(z), dst(z), send.at[0])
        self.along = []
        for j in range(1, zn):
            zz = lax.rem(z + j, zn)
            self.along.append(remote(src(zz), dst(z), send.at[j], recv.at[j], device(zz, y, x, k)))

    def start(self):
        self.local.start()
        for c in self.along:
            c.start()

    def arrived(self):
        self.local.wait()
        for c in self.along:
            c.wait_recv()

    def sent(self):
        for c in self.along:
            c.wait_send()


class Scatter:
    SEMS = 10

    @staticmethod
    def scratch(zn, nr, nc):
        b = jnp.bfloat16
        return [
            pltpu.VMEM((zn, 2, 2, nr, nc), b),
            pltpu.VMEM((zn, 2, 2, nr, nc), b),
            pltpu.VMEM((2, zn // 2, nr, nc), b),
            pltpu.VMEM((2, zn, nr, nc), b),
            pltpu.VMEM((zn - 1, nr, nc), b),
        ]

    def __init__(self, part, out, bufs, send, recv, zn, give=None):
        z, y, x, k = self.at = place()
        self.zn = zn
        hz = zn // 2
        xn, yn, sib = device(z, y, 1 - x, k), device(z, 1 - y, x, k), device(z, y, x, 1 - k)
        self.held, self.twin, self.corners, self.colsums, self.ends = held, twin, corners, colsums, ends = bufs
        self.out = out
        self.load = None
        if give is None:
            self.load = pltpu.make_async_copy(part.at[:, :, :, k], held, send.at[0])
            give = part.at[:, :, :, 1 - k]
        self.to_twin = remote(give, twin, send.at[1], recv.at[1], sib)
        self.to_corner = [
            remote(held.at[pl.ds(0, hz), 1 - y, 1 - x], corners.at[0], send.at[2], recv.at[2], yn),
            remote(held.at[pl.ds(hz, hz), 1 - y, 1 - x], corners.at[1], send.at[3], recv.at[3], xn),
        ]
        self.to_col = [
            remote(held.at[:, y, 1 - x], colsums.at[0], send.at[4], recv.at[4], xn),
            remote(held.at[:, 1 - y, x], colsums.at[1], send.at[5], recv.at[5], yn),
        ]
        self.along = []
        for j in range(1, zn):
            zz = lax.rem(z + j, zn)
            dst = out.at[z] if ends is None else ends.at[j - 1]
            self.along.append(
                remote(held.at[zz, y, x], dst, send.at[5 + j], recv.at[5 + j], device(zz, y, x, k))
            )
        self.last = pltpu.make_async_copy(held.at[z, y, x], out.at[z], send.at[0]) if ends is None else None

    def stage(self, n):
        z, y, x, k = self.at
        zn, hz = self.zn, self.zn // 2
        held = self.held
        if n == 0:
            self.to_twin.start()
            if self.load is not None:
                self.load.start()
        elif n == 1:
            if self.load is not None:
                self.load.wait()
            self.to_twin.wait_recv()

            def add(i, _):
                for yy in range(2):
                    for xx in range(2):
                        held[i, yy, xx] = held[i, yy, xx] + self.twin[i, yy, xx]
                return 0

            lax.fori_loop(0, zn, add, 0)
            for c in self.to_corner:
                c.start()
        elif n == 2:
            for c in self.to_corner:
                c.wait_recv()
            for i in range(hz):
                held[i, y, 1 - x] = held[i, y, 1 - x] + self.corners[0, i]
                held[hz + i, 1 - y, x] = held[hz + i, 1 - y, x] + self.corners[1, i]
            for c in self.to_col:
                c.start()
        elif n == 3:
            for c in self.to_col:
                c.wait_recv()

            def add(i, _):
                f = jnp.float32
                held[i, y, x] = (
                    held[i, y, x].astype(f) + self.colsums[0, i].astype(f) + self.colsums[1, i].astype(f)
                ).astype(jnp.bfloat16)
                return 0

            lax.fori_loop(0, zn, add, 0)
            for c in self.along:
                c.start()
            if self.last is not None:
                self.last.start()
        elif n == 4:
            for c in self.along:
                c.wait_recv()
            if self.last is not None:
                self.last.wait()
            else:
                total = held[z, y, x].astype(jnp.float32)
                for j in range(zn - 1):
                    total = total + self.ends[j].astype(jnp.float32)
                self.out[...] = total
            for c in [self.to_twin] + self.to_corner + self.to_col + self.along:
                c.wait_send()


NT = (((1,), (1,)), ((), ()))


def nt(a, b):
    return lax.dot_general(a, b, NT, preferred_element_type=jnp.float32)


PER = QUERY_HEADS // KEY_VALUE_HEADS
HALF_GROUPS = KEY_VALUE_HEADS // 2
HALF_HEADS = QUERY_HEADS // 2
KV_LANES = 2 * HALF_GROUPS * HEAD_SIZE


def lane_slot(n):
    return n // 2, n % 2


def key_slot(g):
    return lane_slot(g)


def value_slot(g):
    return lane_slot(HALF_GROUPS + g)


def pair_index(half, zp):
    return zp if half == 0 else 3 - zp


def pair_tile(src, g, half, zp):
    tiles = []
    for j in range(PER):
        lo = HEAD_SIZE * (PER * g + j)
        a = src[2 * zp, lo : lo + HEAD_SIZE, :].astype(jnp.float32)
        b = src[2 * zp + 1, lo : lo + HEAD_SIZE, :].astype(jnp.float32)
        low = lax.broadcasted_iota(jnp.int32, a.shape, 1) < WIDE // 2
        if half == 0:
            tiles.append(jnp.where(low, a, pltpu.roll(b, WIDE // 2, 1)))
        else:
            tiles.append(jnp.where(low, pltpu.roll(a, WIDE // 2, 1), b))
    return jnp.concatenate(tiles, axis=1)


def unpair(get, dst):
    for zp in range(2):
        for g in range(HALF_GROUPS):
            first, second = get(g, pair_index(0, zp)), get(g, pair_index(1, zp))
            for j in range(PER):
                lo = HEAD_SIZE * (PER * g + j)
                a, b = first[:, WIDE * j : WIDE * j + WIDE], second[:, WIDE * j : WIDE * j + WIDE]
                low = lax.broadcasted_iota(jnp.int32, a.shape, 1) < WIDE // 2
                even = jnp.where(low, a, pltpu.roll(b, WIDE // 2, 1))
                odd = jnp.where(low, pltpu.roll(a, WIDE // 2, 1), b)
                dst[2 * zp, lo : lo + HEAD_SIZE, :] = even.astype(dst.dtype)
                dst[2 * zp + 1, lo : lo + HEAD_SIZE, :] = odd.astype(dst.dtype)


def set_padded(dst, g, p, tile, side):
    tile = tile.astype(dst.dtype)
    dst[g, p, side * HEAD_SIZE : (side + 1) * HEAD_SIZE, :] = tile
    dst[g, p, (1 - side) * HEAD_SIZE : (2 - side) * HEAD_SIZE, :] = jnp.zeros_like(tile)


def walk(t, y, cn):
    b1, b2, b3 = 3 + y, 10 + 2 * y, 22 + y
    p = (t >= b1).astype(jnp.int32) + (t >= b2).astype(jnp.int32) + (t >= b3).astype(jnp.int32)
    j = t - jnp.where(p == 0, 0, jnp.where(p == 1, b1, jnp.where(p == 2, b2, b3)))
    zp = jnp.where(p < 2, p, 3 - p)
    low = jnp.where(p < 2, 4 * zp + y, 2 * cn - 3 - 4 * zp - y)
    late = (j >= cn).astype(jnp.int32)
    src = jnp.where(late == 1, 2 * cn - 1 - j, j)
    return p, j, src // 2, lax.rem(src, 2), pl.multiple_of(late * HEAD_SIZE, HEAD_SIZE), j >= low


STEPS = 38


def visible(p, j, y, w, cn, wn, rows):
    shape = (wn * rows, PER * WIDE)
    lane = lax.rem(lax.broadcasted_iota(jnp.int32, shape, 1), WIDE)
    zp = jnp.where(p < 2, p, 3 - p)
    c = 2 * (2 * zp + lane // rows) + y
    span = jnp.where(p < 2, c, 2 * cn - 1 - c)
    query = span * (wn * rows) + w * rows + lax.rem(lane, rows)
    key = j * (wn * rows) + lax.broadcasted_iota(jnp.int32, shape, 0)
    return key <= query


def key_block(kvg, zz, yy, late, rows, block):
    t = kvg[zz, yy, :, :, pl.ds(late, rows), WIDE * block : WIDE * block + WIDE]
    return t.reshape(4 * rows, WIDE)


def turned(t):
    return t.astype(jnp.float32).T.astype(t.dtype)


def by_span(body, kvg, cn, rows):
    def one(j, _):
        late = (j >= cn).astype(jnp.int32)
        src = jnp.where(late == 1, 2 * cn - 1 - j, j)
        at = pl.multiple_of(late * rows, rows)
        body(j, lambda b: key_block(kvg, src // 2, lax.rem(src, 2), at, rows, b))
        return 0

    lax.fori_loop(0, 2 * cn, one, 0)


def transposed(t):
    return jnp.concatenate([t[:, i : i + WIDE].T for i in range(0, t.shape[1], WIDE)], axis=0)


def unfold_rows(src, dst, rb):
    n = src.shape[0] // 16
    fold = 16 // rb
    cols = src.shape[1]
    shape = (n * rb, n * 16)
    row = lax.broadcasted_iota(jnp.int32, shape, 0)
    at = 16 * (row // rb) + lax.rem(row, rb)
    col = lax.broadcasted_iota(jnp.int32, shape, 1)
    for q in range(fold):
        pick = jnp.where(col == at + rb * q, 1.0, 0.0).astype(jnp.bfloat16)
        t = jnp.dot(pick, src[...], preferred_element_type=jnp.float32)
        dst[:, q * cols : (q + 1) * cols] = t.astype(dst.dtype)


def gather_attend(x, tables, qkv, fold1, arrays, used, cuts, collective_id):
    cn, wn = lax.axis_size("ctx"), lax.axis_size("ws")
    zn = cn // 2
    dn = cn * wn
    tokens = tables.shape[1]
    all_rows, width = x.shape
    mbs = all_rows // tokens
    qkv_w = qkv.shape[1]
    q_rows = qkv_w - 2 * KV_LANES
    rows = tokens // 2
    mine = q_rows // 2
    f32, b16 = jnp.float32, jnp.bfloat16
    ra = qkv.shape[0] // 16 * 16
    rb = qkv.shape[0] - ra
    wa = dn * ra
    wide1 = fold1.shape[1] * (16 // rb)
    n = len(arrays)
    work = [(a, piece) for a in range(n) for piece in pieces_of(used[a], arrays[a].shape[1], *cuts[a])]
    groups = range(HALF_GROUPS)
    n_first = 3

    def kernel(*refs):
        x_ref, tab, qkv_ref, fold_ref = refs[:4]
        ins = refs[4 : 4 + n]
        at = 4 + n
        o_out, q_out, kv_out, oh_out, lse_out, w_out, wb_out, hn_out, hnb_out, inv_out, gains_out = refs[at : at + 11]
        at += 11
        outs = refs[at : at + n]
        at += n
        (wq, f1, wide, hn, q_s, kv_s, qh, kvg, oh, qpad, vt, m_s, l_s, acc, send, recv, xs, xr, ks, kr, save) = refs[at:]
        greet(zn)
        z, y, x_, k = place()
        w = 2 * x_ + k

        def lanes_of(zz):
            return kv_s.at[zz // 2, :, pl.ds(pl.multiple_of(lax.rem(zz, 2) * KV_LANES, WIDE), KV_LANES)]

        def heads_of(ref, zz):
            return ref.at[zz // 2, pl.ds(pl.multiple_of(lax.rem(zz, 2) * mine, 16), mine), :]

        items = [
            gather_item(fold_ref, f1, 0, 16, 0, fold1.shape[1], send.at[0], recv.at[0], zn),
            gather_item(qkv_ref, wq, 0, ra, 0, 2 * KV_LANES, send.at[1], recv.at[1], zn),
            gather_item(qkv_ref, wq, 0, ra, 2 * KV_LANES, q_rows, send.at[2], recv.at[2], zn),
        ]
        items += [
            gather_item(ins[a], outs[a], r0, nr, c0, nc, send.at[n_first + i], recv.at[n_first + i], zn)
            for i, (a, (r0, nr, c0, nc)) in enumerate(work)
        ]
        kvx = Gather(lanes_of, kvg, ks, kr, zn)
        qx = Exchange(lambda zz: heads_of(q_s, zz), lambda zz: qh.at[zz], xs.at[0], xr.at[0], zn)
        ox = Exchange(lambda zz: oh.at[zz], lambda zz: heads_of(o_out, zz), xs.at[1], xr.at[1], zn)
        for s in range(n_first + 1):
            stage_step(items, 5, s)
        xf = x_ref[...].astype(f32)
        inv = lax.rsqrt(jnp.mean(xf * xf, axis=-1, keepdims=True) + EPSILON)
        inv_out[...] = inv
        m_s[...] = jnp.full(m_s.shape, NEG, f32)
        l_s[...] = jnp.zeros(l_s.shape, f32)
        acc[...] = jnp.zeros(acc.shape, f32)
        stage_step(items, 5, n_first + 1)
        unfold_rows(f1[...].reshape(dn * 16, fold1.shape[1]), wide, rb)
        lane = lax.broadcasted_iota(jnp.int32, (WIDE, width), 1)
        local = jnp.where(lane < wa, lax.rem(lane, ra), ra + lax.rem(lane - wa, rb))
        spread = jnp.where(lax.broadcasted_iota(jnp.int32, (WIDE, width), 0) == local, 1.0, 0.0).astype(b16)
        lines = jnp.dot(wide[:, wide1 - WIDE :], spread, preferred_element_type=f32)
        lane = lax.broadcasted_iota(jnp.int32, lines.shape, 1)
        owner = jnp.where(lane < wa, lane // ra, (lane - wa) // rb)
        line = lax.broadcasted_iota(jnp.int32, lines.shape, 0)
        for i in range(2):
            gains_out[i : i + 1, :] = jnp.sum(jnp.where(line == rb * owner + i, lines, 0.0), axis=0, keepdims=True)
        normed = xf * inv * gains_out[0:1, :]
        hn[...] = normed.astype(b16)
        hn_out[...] = transposed(normed[:, :wa]).astype(b16)
        hnb_out[...] = transposed(normed[:, wa:]).astype(b16)
        stage_step(items, 5, n_first + 2)

        low_lanes = lax.broadcasted_iota(jnp.int32, (tokens, WIDE), 1) < HEAD_SIZE
        quarter = HEAD_SIZE // 2

        def turned_heads(t, kind):
            if kind == "still":
                return t
            cos, low, high = tab[0], tab[1], tab[2]
            r = t * cos + pltpu.roll(t, WIDE - quarter, 1) * low + pltpu.roll(t, quarter, 1) * high
            return r if kind == "turn" else jnp.where(low_lanes, r, t)

        def project(c):
            cols = slice(c * KV_LANES, (c + 1) * KV_LANES)
            t = jnp.dot(hn[:, :wa], wq[:, :, :, :, :, cols].reshape(wa, KV_LANES), preferred_element_type=f32)
            t = t + jnp.dot(hn[:, wa:], wide[:, cols], preferred_element_type=f32)
            kinds = ["turn", "mixed", "still"] if c < 2 else ["turn"] * 3
            for mb in range(mbs):
                for b in range(3):
                    r = turned_heads(t[mb * tokens : (mb + 1) * tokens, WIDE * b : WIDE * b + WIDE], kinds[b])
                    at = c * KV_LANES + WIDE * b
                    if c < 2:
                        kv_s[mb, :, at : at + WIDE] = r.astype(b16)
                    else:
                        at -= 2 * KV_LANES
                        q_s[mb, at : at + WIDE, :] = (r * HEAD_SIZE**-0.5).T.astype(b16)

        project(0)
        project(1)
        kvx.stage(0)
        stage_step(items, 5, n_first + 3)
        for c in range(2, qkv_w // KV_LANES):
            project(c)
        qx.start()
        saves = [
            pltpu.make_async_copy(wq, w_out, save.at[3]),
            pltpu.make_async_copy(wide.at[:, pl.ds(0, qkv_w)], wb_out, save.at[4]),
        ]
        for s in saves:
            s.start()
        kvx.stage(1)
        kvx.stage(2)
        stage_step(items, 5, n_first + 4)
        kvx.stage(3)
        qx.arrived()
        for half in range(2):
            for zp in range(2):
                for g in groups:
                    set_padded(qpad, g, pair_index(half, zp), pair_tile(qh, g, half, zp), key_slot(g)[1])
        kvx.stage(4)

        def turn(j, block):
            flat = {b: turned(block(b)) for b in sorted({value_slot(g)[0] for g in groups})}
            for g in groups:
                b, side = value_slot(g)
                vt[j, g] = flat[b][side * HEAD_SIZE : (side + 1) * HEAD_SIZE]

        by_span(turn, kvg, cn, rows)
        saves += [
            pltpu.make_async_copy(qh, q_out, save.at[0]),
            pltpu.make_async_copy(kvg, kv_out, save.at[1]),
        ]
        for s in saves[2:]:
            s.start()

        def step(t, _):
            p, j, zz, yy, late, edge = walk(t, y, cn)

            def run(masked):
                seen = visible(p, j, y, w, cn, wn, rows) if masked else None
                for g in groups:
                    s = jnp.dot(
                        key_block(kvg, zz, yy, late, rows, key_slot(g)[0]), qpad[g, p], preferred_element_type=f32
                    )
                    if masked:
                        s = jnp.where(seen, s, NEG)
                    m_old = m_s[g, p]
                    m_new = jnp.maximum(m_old, jnp.max(s, axis=0, keepdims=True))
                    alpha = jnp.exp(m_old - m_new)
                    e = jnp.exp(s - m_new)
                    m_s[g, p] = m_new
                    l_s[g, p] = l_s[g, p] * alpha + jnp.sum(e, axis=0, keepdims=True)
                    acc[g, p] = acc[g, p] * alpha + jnp.dot(
                        vt[j, g], e.astype(b16), preferred_element_type=f32
                    )

            pl.when(edge)(lambda: run(True))
            pl.when(jnp.logical_not(edge))(lambda: run(False))
            return 0

        last = len(items) + 4
        t = 0
        start = n_first + 5
        per_step = -(-STEPS // (last - start - 2))
        for s in range(start, last):
            upto = min(STEPS, t + per_step)
            if t < upto:
                lax.fori_loop(t, upto, step, 0)
                t = upto
                if t == STEPS:
                    unpair(lambda g, p: acc[g, p] / l_s[g, p], oh)
                    ox.start()
                    saves.append(pltpu.make_async_copy(oh, oh_out, save.at[2]))
                    saves[-1].start()
                    lse_out[...] = m_s[...] + jnp.log(l_s[...])
            stage_step(items, 5, s)
        ox.arrived()
        ox.sent()
        qx.sent()
        for s in saves:
            s.wait()

    stat = (HALF_GROUPS, 4, 1, PER * WIDE)
    block = (zn, mine, tokens)
    kv_shape = (zn, 2, 2, 2, tokens, KV_LANES)
    any_ = pl.BlockSpec(memory_space=pl.ANY)
    vmem = pl.BlockSpec(memory_space=pltpu.VMEM)
    sds = jax.ShapeDtypeStruct
    dma = pltpu.SemaphoreType.DMA
    return pl.pallas_call(
        kernel,
        out_shape=[
            sds((mbs, q_rows, tokens), b16),
            sds(block, b16),
            sds(kv_shape, b16),
            sds(block, b16),
            sds(stat, f32),
            sds((zn, 2, 2, 2, ra, qkv_w), b16),
            sds((dn * rb, qkv_w), b16),
            sds((wa, all_rows), b16),
            sds((width - wa, all_rows), b16),
            sds((all_rows, 1), f32),
            sds((2, width), f32),
        ]
        + [sds((zn, 2, 2, 2, used[a], arrays[a].shape[1]), arrays[a].dtype) for a in range(n)],
        in_specs=[vmem] * 2 + [any_] * (2 + n),
        out_specs=[any_] * 4 + [vmem] + [any_] * 2 + [vmem] * 4 + [any_] * n,
        scratch_shapes=[
            pltpu.VMEM((zn, 2, 2, 2, ra, qkv_w), b16),
            pltpu.VMEM((zn, 2, 2, 2, 16, fold1.shape[1]), b16),
            pltpu.VMEM((dn * rb, wide1), b16),
            pltpu.VMEM((all_rows, width), b16),
            pltpu.VMEM((mbs, q_rows, tokens), b16),
            pltpu.VMEM((mbs, tokens, 2 * KV_LANES), b16),
            pltpu.VMEM(block, b16),
            pltpu.VMEM(kv_shape, b16),
            pltpu.VMEM(block, b16),
            pltpu.VMEM((HALF_GROUPS, 4, WIDE, PER * WIDE), b16),
            pltpu.VMEM((2 * cn, HALF_GROUPS, HEAD_SIZE, wn * rows), b16),
            pltpu.VMEM(stat, f32),
            pltpu.VMEM(stat, f32),
            pltpu.VMEM((HALF_GROUPS, 4, HEAD_SIZE, PER * WIDE), f32),
            dma((n_first + len(work), Gather.SEMS)),
            dma((n_first + len(work), Gather.SEMS)),
            dma((2, zn)),
            dma((2, zn)),
            dma((Gather.SEMS,)),
            dma((Gather.SEMS,)),
            dma((5,)),
        ],
        compiler_params=pltpu.CompilerParams(
            collective_id=collective_id, has_side_effects=True, vmem_limit_bytes=VMEM_LIMIT
        ),
    )(x, tables, qkv, fold1, *arrays)


class Share:
    def __init__(self, src, own, other, local, send, recv, split):
        z, y, x, k = place()
        mine = src.at[:, :, :, k] if split else src
        theirs = src.at[:, :, :, 1 - k] if split else src
        self.load = None if mine is own else pltpu.make_async_copy(mine, own, local)
        self.swap = remote(theirs, other, send, recv, device(z, y, x, 1 - k))
        self.waited = False

    def start(self):
        if self.load is not None:
            self.load.start()
        self.swap.start()

    def ready(self):
        if not self.waited:
            if self.load is not None:
                self.load.wait()
            self.swap.wait_recv()
            self.waited = True

    def sent(self):
        self.swap.wait_send()


class Sum:
    SEMS = 8

    def __init__(self, make, held, bufs, out, send, recv, zn):
        z, y, x, k = self.at = place()
        self.make, self.held, self.out, self.zn = make, held, out, zn
        hz = zn // 2
        xn, yn = device(z, y, 1 - x, k), device(z, 1 - y, x, k)
        self.corners, self.colsums, self.ends = corners, colsums, ends = bufs
        self.to_corner = [
            remote(held.at[pl.ds(0, hz), 1 - y, 1 - x], corners.at[0], send.at[0], recv.at[0], yn),
            remote(held.at[pl.ds(hz, hz), 1 - y, 1 - x], corners.at[1], send.at[1], recv.at[1], xn),
        ]
        self.to_col = [
            remote(held.at[:, y, 1 - x], colsums.at[0], send.at[2], recv.at[2], xn),
            remote(held.at[:, 1 - y, x], colsums.at[1], send.at[3], recv.at[3], yn),
        ]
        self.along = []
        for j in range(1, zn):
            zz = lax.rem(z + j, zn)
            self.along.append(
                remote(held.at[zz, y, x], ends.at[j - 1], send.at[3 + j], recv.at[3 + j], device(zz, y, x, k))
            )

    @staticmethod
    def scratch(zn, nr, nc):
        b = jnp.bfloat16
        return [
            pltpu.VMEM((2, zn // 2, nr, nc), b),
            pltpu.VMEM((2, zn, nr, nc), b),
            pltpu.VMEM((zn - 1, nr, nc), b),
        ]

    def stage(self, n):
        z, y, x, k = self.at
        zn, hz, held = self.zn, self.zn // 2, self.held
        f32, b16 = jnp.float32, jnp.bfloat16
        if n == 0:
            self.make(held)
            for c in self.to_corner:
                c.start()
        elif n == 1:
            for c in self.to_corner:
                c.wait_recv()
            for i in range(hz):
                held[i, y, 1 - x] = held[i, y, 1 - x] + self.corners[0, i]
                held[hz + i, 1 - y, x] = held[hz + i, 1 - y, x] + self.corners[1, i]
            for c in self.to_col:
                c.start()
        elif n == 2:
            for c in self.to_col:
                c.wait_recv()
            for i in range(zn):
                held[i, y, x] = (
                    held[i, y, x].astype(f32)
                    + self.colsums[0, i].astype(f32)
                    + self.colsums[1, i].astype(f32)
                ).astype(b16)
            for c in self.along:
                c.start()
        elif n == 3:
            for c in self.along:
                c.wait_recv()
            total = held[z, y, x].astype(f32)
            for j in range(zn - 1):
                total = total + self.ends[j].astype(f32)
            self.out[...] = total
            for c in self.to_corner + self.to_col + self.along:
                c.wait_send()


def scatter_attend(do, qh, kvg, oh, lse, tables, lefts, rests, rights, plan, collective_id):
    cn, wn = lax.axis_size("ctx"), lax.axis_size("ws")
    zn = cn // 2
    mbs, q_rows, tokens = do.shape
    rows = tokens // 2
    mine = q_rows // 2
    all_rows = mbs * tokens
    f32, b16 = jnp.float32, jnp.bfloat16
    groups = range(HALF_GROUPS)
    scale = HEAD_SIZE**-0.5
    ff = rights[2].shape[1]
    width = rights[0].shape[1]
    qkv_w = q_rows + 2 * KV_LANES
    act_rows = lefts[0].shape[4]
    ra = lefts[1].shape[4]
    rest_w, qkv_rest_w = plan
    n_down = act_rows // ra
    half_ff = ff // 2
    sizes = (
        [(ra, width)] * n_down
        + [(ra, half_ff)] * 4
        + [(ra, width), (16, rest_w), (ra, 2 * KV_LANES), (ra, q_rows), (16, qkv_rest_w)]
    )
    max_cols = max(s[1] for s in sizes)
    ring = 4
    scratch = []
    for nr, nc in sizes:
        scratch += Sum.scratch(zn, nr, nc)
    n_items = len(sizes)
    ins_all = [*lefts, *rests, *rights]
    n_in = len(ins_all)
    split = [True] * len(lefts) + [False] * (n_in - len(lefts))
    half = lambda a, s: (a.shape[:3] + a.shape[4:]) if s else a.shape
    shares = []
    for a, s in zip(ins_all, split):
        shares += [pltpu.VMEM(half(a, s), b16), pltpu.VMEM(half(a, s), b16)]
    outs_shape = [
        (act_rows, width), (ra, ff), (ra, ff), (ra, width), (16, rest_w), (ra, qkv_w), (16, qkv_rest_w)
    ]
    n_out = len(outs_shape)

    def kernel(*refs):
        do_ref, qh, kvg, oh_ref, lse_ref, tab = refs[:6]
        ins = refs[6 : 6 + n_in]
        gq = refs[6 + n_in]
        outs = refs[7 + n_in : 7 + n_in + n_out]
        rest = refs[7 + n_in + n_out :]
        bufs, rest = rest[: len(scratch)], rest[len(scratch) :]
        pairs, rest = rest[: len(shares)], rest[len(shares) :]
        (held, gq_other, dkv_in, oh, gh, qt, dot_, kt, delta, dq, dkv, give) = rest[:12]
        kb = rest[12:16]
        send, recv, ps, pr, pl_, xs, xr, ks, kr = rest[16:]
        dqh, dq_in = gh, oh
        greet(zn)
        z, y, x, k = place()
        w = 2 * x + k

        def heads_of(ref, zz):
            return ref.at[zz // 2, pl.ds(pl.multiple_of(lax.rem(zz, 2) * mine, 16), mine), :]

        gx = Exchange(lambda zz: heads_of(do_ref, zz), lambda zz: gh.at[zz], xs.at[0], xr.at[0], zn)
        dx = Exchange(lambda zz: dqh.at[zz], lambda zz: dq_in.at[zz], xs.at[1], xr.at[1], zn)
        kvx = Scatter(None, dkv_in, tuple(kb) + (None,), ks, kr, zn, give)
        share = [
            Share(ins[i], pairs[2 * i], pairs[2 * i + 1], pl_.at[i], ps.at[i], pr.at[i], split[i])
            for i in range(n_in)
        ]
        gq_share = Share(gq, gq, gq_other, None, ps.at[n_in], pr.at[n_in], False)
        own = lambda i: pairs[2 * i]
        other = lambda i: pairs[2 * i + 1]
        ACT, H2, OT, HN, H2B, OTB, HNB, GY, GB, GG, GU = range(n_in)

        def product(left, right, lo, row0, needs):
            def make(dst):
                for i in needs:
                    share[i].ready()
                nr, nc = dst.shape[3:]
                lefts2 = [
                    r[:, :, :, row0 : row0 + nr, :].reshape(zn * 4 * nr, all_rows)
                    for r in (own(left), other(left))
                ]
                step = 3 * WIDE

                def cols(i, _):
                    at = pl.multiple_of(i * step, WIDE)
                    t = jnp.dot(lefts2[0], right[0][:, pl.ds(lo + at, step)], preferred_element_type=f32)
                    t = t + jnp.dot(lefts2[1], right[1][:, pl.ds(lo + at, step)], preferred_element_type=f32)
                    dst[:, :, :, :, pl.ds(at, step)] = t.astype(b16).reshape(zn, 2, 2, nr, step)
                    return 0

                lax.fori_loop(0, nc // step, cols, 0)

            return make

        def both(i):
            return (own(i), other(i))

        def fold4(quarters):
            row = lax.rem(lax.broadcasted_iota(jnp.int32, quarters[0].shape, 0), 8)
            here = k == 0

            def put(a, b):
                n = a.shape[0]
                low = jnp.where(here, a, pltpu.roll(a, n - 4, 0))
                high = jnp.where(here, pltpu.roll(b, 4, 0), b)
                t = jnp.where(row < 4, low, high)
                return t.reshape(zn * 4, 8, t.shape[1])

            t = jnp.concatenate([put(*quarters[:2]), put(*quarters[2:])], axis=1)
            return t.astype(b16).reshape(zn, 2, 2, 16, t.shape[2])

        def rest_product(dst):
            step = 3 * WIDE
            for i in (H2B, OTB, GB, GG, GU):
                share[i].ready()
            columns = []
            for left, right, n in ((OTB, GB, width), (H2B, GG, ff), (H2B, GU, ff)):
                columns += [(left, right, c) for c in range(0, n, step)]
            per = rest_w // step

            def one(entry):
                if entry is None:
                    return jnp.zeros((own(H2B).shape[0], step), f32)
                left, right, c = entry
                return jnp.dot(own(left)[...], own(right)[:, c : c + step], preferred_element_type=f32) + jnp.dot(
                    other(left)[...], other(right)[:, c : c + step], preferred_element_type=f32
                )

            for c in range(per):
                quarters = []
                for q in range(4):
                    at = q * per + c
                    quarters.append(one(columns[at] if at < len(columns) else None))
                dst[:, :, :, :, c * step : (c + 1) * step] = fold4(quarters)

        def qkv_rest_product(dst):
            for i in (HNB,):
                share[i].ready()
            gq_share.ready()
            quarters = []
            for q in range(4):
                lo, hi = q * qkv_rest_w, min((q + 1) * qkv_rest_w, qkv_w)
                t = jnp.dot(own(HNB)[...], gq[:, lo:hi], preferred_element_type=f32) + jnp.dot(
                    other(HNB)[...], gq_other[:, lo:hi], preferred_element_type=f32
                )
                if hi - lo < qkv_rest_w:
                    t = jnp.concatenate([t, jnp.zeros((t.shape[0], qkv_rest_w - hi + lo), f32)], axis=1)
                quarters.append(t)
            dst[...] = fold4(quarters)

        gq_both = (gq, gq_other)
        makes = [product(ACT, both(GY), 0, ra * i, (ACT, GY)) for i in range(n_down)]
        makes += [product(H2, both(g), lo, 0, (H2, g)) for g in (GG, GU) for lo in (0, half_ff)]
        makes += [product(OT, both(GB), 0, 0, (OT, GB)), rest_product]
        makes += [product(HN, gq_both, 0, 0, (HN,)), product(HN, gq_both, 2 * KV_LANES, 0, (HN,)), qkv_rest_product]
        targets = [outs[0].at[pl.ds(ra * i, ra), :] for i in range(n_down)]
        targets += [outs[g].at[:, pl.ds(lo, half_ff)] for g in (1, 2) for lo in (0, half_ff)]
        targets += [outs[3], outs[4], outs[5].at[:, pl.ds(0, 2 * KV_LANES)], outs[5].at[:, pl.ds(2 * KV_LANES, q_rows)], outs[6]]
        items = []
        for i, (nr, nc) in enumerate(sizes):
            slot = held.at[i % ring, :, :, :, pl.ds(0, nr), pl.ds(0, nc)]
            items.append(
                Sum(makes[i], slot, bufs[3 * i : 3 * i + 3], targets[i], send.at[i], recv.at[i], zn)
            )
        load_o = pltpu.make_async_copy(oh_ref, oh, pl_.at[n_in])
        load_o.start()
        gx.start()
        for i in (ACT, GY, H2, GG, GU, OT, GB, H2B, OTB, HN, HNB):
            share[i].start()
        dq[...] = jnp.zeros(dq.shape, f32)

        def clear(i, _):
            dkv[i] = jnp.zeros(dkv.shape[1:], f32)
            return 0

        lax.fori_loop(0, zn, clear, 0)
        stage_step(items, 4, 0)

        def turn(j, block):
            flat = {b: turned(block(b)) for b in sorted({key_slot(g)[0] for g in groups})}
            for g in groups:
                b, side = key_slot(g)
                kt[j, g] = flat[b][side * HEAD_SIZE : (side + 1) * HEAD_SIZE]

        by_span(turn, kvg, cn, rows)
        stage_step(items, 4, 1)
        gx.arrived()
        load_o.wait()
        for half_ in range(2):
            for zp in range(2):
                p = pair_index(half_, zp)
                for g in groups:
                    g_tile = pair_tile(gh, g, half_, zp)
                    o_tile = pair_tile(oh, g, half_, zp)
                    delta[g, p] = jnp.sum(g_tile * o_tile, axis=0, keepdims=True)
                    set_padded(qt, g, p, pair_tile(qh, g, half_, zp), key_slot(g)[1])
                    set_padded(dot_, g, p, g_tile, value_slot(g)[1])

        def step(t, _):
            p, j, zz, yy, late, edge = walk(t, y, cn)

            def run(masked):
                seen = visible(p, j, y, w, cn, wn, rows) if masked else None
                blocks = [key_block(kvg, zz, yy, late, rows, b) for b in range(KV_LANES // WIDE)]
                sums = [None] * len(blocks)

                def put(b, v):
                    sums[b] = v if sums[b] is None else sums[b] + v

                for g in groups:
                    s = jnp.dot(blocks[key_slot(g)[0]], qt[g, p], preferred_element_type=f32)
                    if masked:
                        s = jnp.where(seen, s, NEG)
                    e = jnp.exp(s - lse_ref[g, p])
                    dp = jnp.dot(blocks[value_slot(g)[0]], dot_[g, p], preferred_element_type=f32)
                    ds = (e * (dp - delta[g, p])).astype(b16)
                    put(value_slot(g)[0], nt(e.astype(b16), dot_[g, p]))
                    put(key_slot(g)[0], nt(ds, qt[g, p]))
                    dq[g, p] += jnp.dot(kt[j, g], ds, preferred_element_type=f32)
                for b, v in enumerate(sums):
                    dkv[zz, yy, :, :, pl.ds(late, rows), WIDE * b : WIDE * b + WIDE] += v.reshape(
                        2, 2, rows, WIDE
                    )

            pl.when(edge)(lambda: run(True))
            pl.when(jnp.logical_not(edge))(lambda: run(False))
            return 0

        def rope_back():
            low_lanes = lax.broadcasted_iota(jnp.int32, (tokens, WIDE), 1) < HEAD_SIZE
            quarter = HEAD_SIZE // 2

            def back(t, kind):
                if kind == "still":
                    return t
                cos, low, high = tab[0], tab[1], tab[2]
                r = t * cos - pltpu.roll(t, WIDE - quarter, 1) * low - pltpu.roll(t, quarter, 1) * high
                return r if kind == "turn" else jnp.where(low_lanes, r, t)

            def heads_block(mb, at):
                n = max(0, min(WIDE, mine - at))
                parts = []
                if n:
                    parts.append(dq_in[2 * mb, at : at + n, :].astype(f32))
                if n < WIDE:
                    lo = at + n - mine
                    parts.append(dq_in[2 * mb + 1, lo : lo + WIDE - n, :].astype(f32))
                return parts[0] if len(parts) == 1 else jnp.concatenate(parts, axis=0)

            kinds = ["turn", "mixed", "still"]
            for mb in range(mbs):
                at = slice(mb * tokens, (mb + 1) * tokens)
                for hh in range(2):
                    for b in range(KV_LANES // WIDE):
                        t = dkv_in[2 * mb + hh, :, WIDE * b : WIDE * b + WIDE].astype(f32)
                        lo = hh * KV_LANES + WIDE * b
                        gq[at, lo : lo + WIDE] = back(t, kinds[b]).astype(b16)
                for b in range(q_rows // WIDE):
                    t = heads_block(mb, WIDE * b).T
                    lo = 2 * KV_LANES + WIDE * b
                    gq[at, lo : lo + WIDE] = back(t, "turn").astype(b16)

        first = n_items - 3
        order = items[:first] + [None, None] + items[first:]
        t = 0
        per_step = -(-STEPS // (first - 3))
        kv_stage = 0
        for s in range(2, len(order) + 3):
            if t < STEPS:
                upto = min(STEPS, t + per_step)
                lax.fori_loop(t, upto, step, 0)
                t = upto
                if t == STEPS:

                    def pack(i, _):
                        for yy in range(2):
                            for xx in range(2):
                                kb[0][i, yy, xx] = dkv[i, yy, xx, k].astype(b16)
                                give[i, yy, xx] = dkv[i, yy, xx, 1 - k].astype(b16)
                        return 0

                    lax.fori_loop(0, zn, pack, 0)
                    kvx.stage(0)
                    kv_stage = 1
                    unpair(lambda g, p: dq[g, p] * scale, dqh)
                    dx.start()
            elif kv_stage < 4 and s <= first + 1:
                kvx.stage(kv_stage)
                kv_stage += 1
            if s == first + 2:
                while kv_stage < 5:
                    kvx.stage(kv_stage)
                    kv_stage += 1
                dx.arrived()
                rope_back()
                gq_share.start()
                gq_share.ready()
            stage_step(order, 4, s)
        dx.sent()
        gx.sent()
        gq_share.sent()
        for i in share:
            i.sent()

    stat = (HALF_GROUPS, 4, 1, PER * WIDE)
    block = (zn, mine, tokens)
    tile = (HALF_GROUPS, 4, WIDE, PER * WIDE)
    any_ = pl.BlockSpec(memory_space=pl.ANY)
    vmem = pl.BlockSpec(memory_space=pltpu.VMEM)
    dma = pltpu.SemaphoreType.DMA
    return pl.pallas_call(
        kernel,
        out_shape=[jax.ShapeDtypeStruct((all_rows, qkv_w), b16)]
        + [jax.ShapeDtypeStruct(s, f32) for s in outs_shape],
        in_specs=[any_, vmem, vmem, any_, vmem, vmem] + [any_] * n_in,
        out_specs=[vmem] * (1 + n_out),
        scratch_shapes=scratch
        + shares
        + [
            pltpu.VMEM((ring, zn, 2, 2, ra, max_cols), b16),
            pltpu.VMEM((all_rows, qkv_w), b16),
            pltpu.VMEM((zn, tokens, KV_LANES), b16),
            pltpu.VMEM(block, b16),
            pltpu.VMEM(block, b16),
            pltpu.VMEM(tile, b16),
            pltpu.VMEM(tile, b16),
            pltpu.VMEM((2 * cn, HALF_GROUPS, HEAD_SIZE, wn * rows), b16),
            pltpu.VMEM(stat, f32),
            pltpu.VMEM((HALF_GROUPS, 4, HEAD_SIZE, PER * WIDE), f32),
            pltpu.VMEM((zn, 2, 2, 2, tokens, KV_LANES), f32),
            pltpu.VMEM((zn, 2, 2, tokens, KV_LANES), b16),
        ]
        + Scatter.scratch(zn, tokens, KV_LANES)[:4]
        + [
            dma((n_items, Sum.SEMS)),
            dma((n_items, Sum.SEMS)),
            dma((n_in + 1,)),
            dma((n_in + 1,)),
            dma((n_in + 1,)),
            dma((2, zn)),
            dma((2, zn)),
            dma((Scatter.SEMS,)),
            dma((Scatter.SEMS,)),
        ],
        compiler_params=pltpu.CompilerParams(
            collective_id=collective_id, has_side_effects=True, vmem_limit_bytes=VMEM_LIMIT
        ),
    )(do, qh, kvg, oh, lse, tables, *ins_all)


def finish(gq, weights, rest, x, inv, gain, gx1, gain_sums, order, collective_id):
    zn = lax.axis_size("ctx") // 2
    f32, b16 = jnp.float32, jnp.bfloat16
    wa = weights.shape[0]
    width = x.shape[1]

    def kernel(gq_ref, w_ref, r_ref, x_ref, inv_ref, gain_ref, gx1_ref, sums_ref, order_ref, out, total, ghn, low, got, send, recv):
        greet(zn)
        z, y, x_, k = place()
        ghn[:, :wa] = lax.dot_general(gq_ref[...], w_ref[...], NT, preferred_element_type=f32)
        ghn[:, wa:] = lax.dot_general(gq_ref[...], r_ref[...], NT, preferred_element_type=f32)
        xf = x_ref[...].astype(f32)
        inv_ = inv_ref[...]
        grad = ghn[...]
        total[...] = jnp.zeros(total.shape, f32)
        total[0:1, :] = jnp.sum(grad * xf * inv_, axis=0, keepdims=True)
        total[1:2, :] = sums_ref[...]
        moves = [
            remote(total, got.at[0], send.at[0], recv.at[0], device(z, y, x_, 1 - k)),
            remote(total, got.at[1], send.at[1], recv.at[1], device(z, y, 1 - x_, k)),
            remote(total, got.at[2], send.at[2], recv.at[2], device(z, 1 - y, x_, k)),
        ]
        moves[0].start()
        weighted = grad * gain_ref[...]
        inner = jnp.mean(weighted * xf, axis=-1, keepdims=True)
        row = inv_ * weighted - xf * (inv_ * inv_ * inv_) * inner
        low[...] = (gx1_ref[...] + row).astype(b16)
        for i in range(3):
            moves[i].wait()
            total[...] = total[...] + got[i]
            if i < 2:
                moves[i + 1].start()
        ends = []
        for j in range(1, zn):
            ends.append(remote(total, got.at[2 + j], send.at[2 + j], recv.at[2 + j], device(lax.rem(z + j, zn), y, x_, k)))
            ends[-1].start()
        out[...] = lax.dot_general(low[...], order_ref[...], NT, preferred_element_type=f32).astype(b16)
        for c in ends:
            c.wait()
        t = total[...]
        for j in range(1, zn):
            t = t + got[2 + j]
        total[...] = t

    vmem = pl.BlockSpec(memory_space=pltpu.VMEM)
    return pl.pallas_call(
        kernel,
        out_shape=[jax.ShapeDtypeStruct(x.shape, b16), jax.ShapeDtypeStruct((8, width), f32)],
        in_specs=[vmem] * 9,
        out_specs=[vmem] * 2,
        scratch_shapes=[
            pltpu.VMEM(x.shape, f32),
            pltpu.VMEM(x.shape, b16),
            pltpu.VMEM((2 + zn, 8, width), f32),
            pltpu.SemaphoreType.DMA((2 + zn,)),
            pltpu.SemaphoreType.DMA((2 + zn,)),
        ],
        compiler_params=pltpu.CompilerParams(
            collective_id=collective_id, has_side_effects=True, vmem_limit_bytes=VMEM_LIMIT
        ),
    )(gq, weights, rest, x, inv, gain, gx1, gain_sums, order)


def ffn(o_t, x, gy, gain, order_t, out_a, gate_a, up_a, down, rest):
    f32, b16 = jnp.float32, jnp.bfloat16
    mbs, width, tokens = o_t.shape
    rows = mbs * tokens
    ff = gate_a.shape[1]
    wa = out_a.shape[0]
    wb = width - wa
    rb = wb * 16 // rest.shape[0]
    chunk = 4 * WIDE

    def kernel(o_ref, x_ref, gy_ref, gain_ref, order_hbm, out_hbm, gate_hbm, up_hbm, down_hbm, rest_hbm,
               y_ref, gx1_ref, gb_ref, gg_ref, gu_ref, act_ref, h2_ref, h2b_ref, op_ref, opb_ref, go_ref, gain_sum,
               order_s, out_s, gate_s, up_s, down_s, rest_s, wide, x1, h2, acc, gh, sems):
        loads = [
            pltpu.make_async_copy(src, dst, sems.at[i])
            for i, (src, dst) in enumerate(
                [(order_hbm, order_s), (rest_hbm, rest_s), (out_hbm, out_s), (gate_hbm, gate_s), (up_hbm, up_s), (down_hbm, down_s)]
            )
        ]
        for c in loads:
            c.start()
        loads[0].wait()
        for mb in range(mbs):
            at = slice(mb * tokens, (mb + 1) * tokens)
            t = jnp.dot(order_s[...], o_ref[mb], preferred_element_type=f32)
            op_ref[:, at] = t[:wa].astype(b16)
            opb_ref[:, at] = t[wa:].astype(b16)
            h2[at, :] = transposed_rows(t).astype(b16)
        loads[1].wait()
        unfold_rows(rest_s, wide, rb)
        loads[2].wait()
        x1[...] = (
            x_ref[...].astype(f32)
            + jnp.dot(h2[:, :wa], out_s[...], preferred_element_type=f32)
            + jnp.dot(h2[:, wa:], wide[:, :width], preferred_element_type=f32)
        )
        u = x1[...]
        inv = lax.rsqrt(jnp.mean(u * u, axis=-1, keepdims=True) + EPSILON)
        hidden = u * inv * gain_ref[...]
        h2[...] = hidden.astype(b16)
        h2_ref[...] = transposed(hidden[:, :wa]).astype(b16)
        h2b_ref[...] = transposed(hidden[:, wa:]).astype(b16)
        acc[...] = jnp.zeros(acc.shape, f32)
        gh[...] = jnp.zeros(gh.shape, f32)
        for c in loads[3:]:
            c.wait()

        def one(i, _):
            at = pl.multiple_of(i * chunk, WIDE)
            cols = pl.ds(at, chunk)
            gcols, ucols = pl.ds(width + at, chunk), pl.ds(width + ff + at, chunk)
            ha, hb = h2[:, :wa], h2[:, wa:]
            gate = jnp.dot(ha, gate_s[:, cols], preferred_element_type=f32) + jnp.dot(
                hb, wide[:, gcols], preferred_element_type=f32
            )
            up = jnp.dot(ha, up_s[:, cols], preferred_element_type=f32) + jnp.dot(
                hb, wide[:, ucols], preferred_element_type=f32
            )
            ga = nt(gy_ref[...], down_s[cols, :])
            sig = jax.nn.sigmoid(gate)
            silu = gate * sig
            act = silu * up
            g_gate = (ga * up * sig * (1.0 + gate * (1.0 - sig))).astype(b16)
            g_up = (ga * silu).astype(b16)
            gg_ref[:, cols] = g_gate
            gu_ref[:, cols] = g_up
            act_ref[cols, :] = transposed(act).astype(b16)
            acc[...] += jnp.dot(act.astype(b16), down_s[cols, :], preferred_element_type=f32)
            gh[:, :wa] += nt(g_gate, gate_s[:, cols]) + nt(g_up, up_s[:, cols])
            gh[:, wa:] += nt(g_gate, wide[:, gcols]) + nt(g_up, wide[:, ucols])
            return 0

        lax.fori_loop(0, ff // chunk, one, 0)
        y = (x1[...] + acc[...]).astype(b16)
        y_ref[...] = jnp.dot(y, order_s[...], preferred_element_type=f32).astype(b16)
        u = x1[...]
        inv = lax.rsqrt(jnp.mean(u * u, axis=-1, keepdims=True) + EPSILON)
        grad = gh[...]
        gain_sum[...] = jnp.sum(grad * u * inv, axis=0, keepdims=True)
        weighted = grad * gain_ref[...]
        inner = jnp.mean(weighted * u, axis=-1, keepdims=True)
        gx1 = inv * weighted - u * (inv * inv * inv) * inner + gy_ref[...].astype(f32)
        gx1_ref[...] = gx1
        gb = gx1.astype(b16)
        gb_ref[...] = jnp.dot(gb, order_s[...], preferred_element_type=f32).astype(b16)
        h2[:, :wa] = nt(gb, out_s[...]).astype(b16)
        h2[:, wa:] = nt(gb, wide[:, :width]).astype(b16)
        go = jnp.dot(h2[...], order_s[...], preferred_element_type=f32)
        for mb in range(mbs):
            go_ref[mb] = transposed(go[mb * tokens : (mb + 1) * tokens]).astype(b16)

    def transposed_rows(t):
        return jnp.concatenate([t[i : i + WIDE].T for i in range(0, t.shape[0], WIDE)], axis=1)

    any_ = pl.BlockSpec(memory_space=pl.ANY)
    vmem = pl.BlockSpec(memory_space=pltpu.VMEM)
    sds = jax.ShapeDtypeStruct
    return pl.pallas_call(
        kernel,
        out_shape=[
            sds((rows, width), b16),
            sds((rows, width), f32),
            sds((rows, width), b16),
            sds((rows, ff), b16),
            sds((rows, ff), b16),
            sds((ff, rows), b16),
            sds((wa, rows), b16),
            sds((wb, rows), b16),
            sds((wa, rows), b16),
            sds((wb, rows), b16),
            sds(o_t.shape, b16),
            sds((1, width), f32),
        ],
        in_specs=[vmem] * 4 + [any_] * 6,
        out_specs=[vmem] * 12,
        scratch_shapes=[
            pltpu.VMEM(order_t.shape, b16),
            pltpu.VMEM(out_a.shape, b16),
            pltpu.VMEM(gate_a.shape, b16),
            pltpu.VMEM(up_a.shape, b16),
            pltpu.VMEM(down.shape, b16),
            pltpu.VMEM(rest.shape, b16),
            pltpu.VMEM((wb, 16 // rb * rest.shape[1]), b16),
            pltpu.VMEM((rows, width), f32),
            pltpu.VMEM((rows, width), b16),
            pltpu.VMEM((rows, width), f32),
            pltpu.VMEM((rows, width), f32),
            pltpu.SemaphoreType.DMA((6,)),
        ],
        compiler_params=pltpu.CompilerParams(vmem_limit_bytes=VMEM_LIMIT),
    )(o_t, x, gy, gain, order_t, out_a, gate_a, up_a, down, rest)


def lane_tables(positions):
    quarter = HEAD_SIZE // 2
    frequency = 10000.0 ** (-2.0 * jnp.arange(quarter, dtype=jnp.float32) / HEAD_SIZE)
    angles = positions.astype(jnp.float32)[:, None] * frequency[None, :]
    cos, sin = jnp.cos(angles), jnp.sin(angles)
    none = jnp.zeros_like(sin)
    full = lambda a, b: jnp.concatenate([a, b, a, b], axis=1)
    return jnp.stack([full(cos, cos), full(-sin, none), full(none, sin)])


def fast_device(
    inputs,
    attn_gain,
    query_weight,
    key_matrix,
    value_matrix,
    out_weight,
    ffn_gain,
    gate_weight,
    up_weight,
    down_weight,
    cotangent,
):
    f32, b16 = jnp.float32, jnp.bfloat16
    cn, wn = lax.axis_size("ctx"), lax.axis_size("ws")
    dn = cn * wn
    zn = cn // 2
    mbs, tokens, width = inputs.shape
    own = query_weight.shape[0]
    ra = own // 16 * 16
    rb = own - ra
    q_width = query_weight.shape[1]
    hid = KEY_VALUE_HEADS * HEAD_SIZE
    ff = gate_weight.shape[1]
    rows = mbs * tokens
    wa = dn * ra

    new = jnp.arange(width)
    old = jnp.where(
        new < wa, own * (new // ra) + new % ra, own * ((new - wa) // rb) + ra + (new - wa) % rb
    )
    order = (jnp.arange(width)[:, None] == old[None, :]).astype(b16)

    def to_order(t):
        return jnp.dot(t, order, preferred_element_type=f32).astype(t.dtype)

    def from_order(t):
        return lax.dot_general(t, order, NT, preferred_element_type=f32).astype(t.dtype)

    fold = 16 // rb

    def folded(t):
        return t.reshape(t.shape[0], fold, -1).transpose(1, 0, 2).reshape(16, -1)

    qkv_w = q_width + 2 * hid
    pad1 = -qkv_w % (fold * WIDE)
    rest_w = width + 2 * ff
    pad2 = -rest_w % (fold * WIDE)
    moved = to_order(
        jnp.concatenate(
            [inputs.reshape(rows, width), cotangent.reshape(rows, width), out_weight, down_weight]
        )
    )
    x_low, gy_low = moved[:rows], moved[rows : 2 * rows]
    out_p, down_p = moved[2 * rows : 2 * rows + own], moved[2 * rows + own :]
    half_hid = hid // 2
    qkv = jnp.concatenate(
        [
            key_matrix[:, :half_hid],
            value_matrix[:, :half_hid],
            key_matrix[:, half_hid:],
            value_matrix[:, half_hid:],
            query_weight,
        ],
        axis=1,
    )
    gains = jnp.stack([attn_gain, ffn_gain])
    gains = jnp.pad(gains, ((0, rb - 2), (0, pad1 - own)))
    b1 = folded(jnp.concatenate([qkv[ra:], gains], axis=1))
    b2 = folded(
        jnp.pad(
            jnp.concatenate([out_p[ra:], gate_weight[ra:], up_weight[ra:]], axis=1), ((0, 0), (0, pad2))
        )
    )
    flat = lambda t: t.reshape(-1, t.shape[-1])
    c, w = lax.axis_index("ctx"), lax.axis_index("ws")
    tables = lane_tables(query_places(c, w, tokens, cn, wn))
    (o_t, qh, kvg, oh, lse, qkv_a, qkv_b, hn_t, hn_bt, inv1, gains, out_a, gate_a, up_a, down_a, b2g) = gather_attend(
        x_low,
        tables,
        qkv,
        b1,
        [out_p, gate_weight, up_weight, down_p, b2],
        [ra, ra, ra, down_p.shape[0], 16],
        [(1, 1), (1, 2), (1, 2), (2, 1), (1, 1)],
        2,
    )
    qkv_a, out_a, gate_a, up_a, down_w = map(flat, (qkv_a, out_a, gate_a, up_a, down_a))
    gain1, gain2 = gains[:1], gains[1:]
    out, gx1, gb_plain, g_gate, g_up, act_t, h2_t, h2_bt, o_pt, o_pbt, go_t, gain2_sum = ffn(
        o_t, x_low, gy_low, gain2, order.T, out_a, gate_a, up_a, down_w, flat(b2g)
    )
    gy_plain = cotangent.reshape(rows, width)
    left = lambda t: t.reshape(zn, 2, 2, 2, -1, rows)
    gq, r_down, r_gate, r_up, r_out, r_b2, r_qkv, r_b1 = scatter_attend(
        go_t,
        qh,
        kvg,
        oh,
        lse,
        tables,
        [left(act_t), left(h2_t), left(o_pt), left(hn_t)],
        [h2_bt, o_pbt, hn_bt],
        [gy_plain, gb_plain, g_gate, g_up],
        ((rest_w + pad2) // fold, (qkv_w + pad1) // fold),
        3,
    )
    input_grad, gain_sums = finish(
        gq, qkv_a, qkv_b, x_low, inv1, gain1, gx1, gain2_sum, order, 4
    )
    device_at = c * wn + w

    def own_gain(t):
        first = lax.dynamic_slice(t, (device_at * ra,), (ra,))
        return jnp.concatenate([first, lax.dynamic_slice(t, (wa + device_at * rb,), (rb,))])

    def own_rows(t):
        return t.reshape(fold, rb, -1).transpose(1, 0, 2).reshape(rb, -1)

    e1, e2 = own_rows(r_b1), own_rows(r_b2)
    whole = lambda a, b: jnp.concatenate([a, b], axis=0)
    d_qkv = whole(r_qkv, e1[:, :qkv_w])
    return (
        out.reshape(inputs.shape),
        input_grad.reshape(inputs.shape),
        own_gain(gain_sums[0]),
        d_qkv[:, 2 * hid :],
        jnp.concatenate([d_qkv[:, :half_hid], d_qkv[:, hid : hid + half_hid]], axis=1),
        jnp.concatenate([d_qkv[:, half_hid:hid], d_qkv[:, hid + half_hid : 2 * hid]], axis=1),
        whole(r_out, e2[:, :width]),
        own_gain(gain_sums[1]),
        whole(r_gate, e2[:, width : width + ff]),
        whole(r_up, e2[:, width + ff : width + 2 * ff]),
        r_down,
    )


def solution(mesh):
    in_specs = (
        P(None, ("ctx", "ws"), None),
        P(("ctx", "ws")),
        P(("ctx", "ws"), None),
        P(("ctx", "ws"), None),
        P(("ctx", "ws"), None),
        P(("ctx", "ws"), None),
        P(("ctx", "ws")),
        P(("ctx", "ws"), None),
        P(("ctx", "ws"), None),
        P(("ctx", "ws"), None),
        P(None, ("ctx", "ws"), None),
    )
    out_specs = (
        P(None, ("ctx", "ws"), None),
        P(None, ("ctx", "ws"), None),
        P(("ctx", "ws")),
        P(("ctx", "ws"), None),
        P(("ctx", "ws"), None),
        P(("ctx", "ws"), None),
        P(("ctx", "ws"), None),
        P(("ctx", "ws")),
        P(("ctx", "ws"), None),
        P(("ctx", "ws"), None),
        P(("ctx", "ws"), None),
    )
    body = fast_device if fits_fast(mesh) else per_device
    return jax.shard_map(
        body, mesh=mesh, in_specs=in_specs, out_specs=out_specs, check_vma=False
    )
```

```python
import jax
import jax.numpy as jnp
from jax import lax
from jax.experimental import pallas as pl
from jax.experimental.pallas import tpu as pltpu
from jax.sharding import PartitionSpec as P
import functools

QUERY_HEADS = 18
KEY_VALUE_HEADS = 6
HEAD_SIZE = 64


EPSILON = 1e-05
MASKED_SCORE = -1e30


def shifted(block, axis, distance):
    devices = range(lax.axis_size(axis))
    route = [((i - distance) % len(devices), i) for i in devices]
    return lax.ppermute(block, axis, route)


def as_sent(x):

    def short(part):
        return part.astype(jnp.bfloat16) if part.dtype == jnp.float32 else part

    return jax.tree.map(short, x)


def matrix_multiply(left, right):
    return jnp.dot(left, right, preferred_element_type=jnp.float32)


def outer_sum(left, right):
    return jnp.einsum("ri,rj->ij", left, right, preferred_element_type=jnp.float32)


def back_product(gradient, weight):
    return jnp.einsum("rj,ij->ri", gradient, weight, preferred_element_type=jnp.float32)


def normalize(layer_rows, gain_vector):
    inverse = lax.rsqrt(jnp.mean(layer_rows * layer_rows, axis=-1, keepdims=True) + EPSILON)
    return (layer_rows * inverse * gain_vector, inverse)


def normalize_back(layer_rows, inverse, gain_vector, gradient):
    weighted = gradient * gain_vector
    inner_mean = jnp.mean(weighted * layer_rows, axis=-1, keepdims=True)
    row_grad = inverse * weighted - layer_rows * (inverse * inverse * inverse) * inner_mean
    gain_grad = jnp.sum(gradient * layer_rows * inverse, axis=0)
    return (row_grad, gain_grad)


def rotary_tables(token_positions):
    quarter = HEAD_SIZE // 2
    frequency = 10000.0 ** (-2.0 * jnp.arange(quarter, dtype=jnp.float32) / HEAD_SIZE)
    angles = token_positions.astype(jnp.float32)[:, None] * frequency[None, :]
    return (jnp.cos(angles)[:, None, :], jnp.sin(angles)[:, None, :])


def rotate(heads, cosine_table, sine_table):
    quarter = HEAD_SIZE // 2
    first_half = heads[..., :quarter]
    second_half = heads[..., quarter:]
    return jnp.concatenate(
        [
            first_half * cosine_table - second_half * sine_table,
            second_half * cosine_table + first_half * sine_table,
        ],
        axis=-1,
    )


def rotate_back(heads, cosine_table, sine_table):
    quarter = HEAD_SIZE // 2
    first_half = heads[..., :quarter]
    second_half = heads[..., quarter:]
    return jnp.concatenate(
        [
            first_half * cosine_table + second_half * sine_table,
            second_half * cosine_table - first_half * sine_table,
        ],
        axis=-1,
    )


def query_places(own_ctx, own_member, count_of_rows, ctx_count, device_count):
    rows_per_half = count_of_rows // 2
    local_index = jnp.arange(count_of_rows, dtype=jnp.int32)
    span_index = jnp.where(local_index < rows_per_half, own_ctx, 2 * ctx_count - 1 - own_ctx)
    return (
        span_index * (device_count * rows_per_half)
        + own_member * rows_per_half
        + local_index % rows_per_half
    )


def block_places(source_ctx, count_of_rows, ctx_count, device_count):
    rows_per_half = count_of_rows // 2
    member_index = jnp.arange(device_count, dtype=jnp.int32)[:, None, None]
    half_index = jnp.arange(2, dtype=jnp.int32)[None, :, None]
    inner_index = jnp.arange(rows_per_half, dtype=jnp.int32)[None, None, :]
    span_index = jnp.where(half_index == 0, source_ctx, 2 * ctx_count - 1 - source_ctx)
    return (
        span_index * (device_count * rows_per_half) + member_index * rows_per_half + inner_index
    ).reshape(-1)


def split_block(block_of_keys):
    hidden_width = KEY_VALUE_HEADS * HEAD_SIZE
    device_count, _, rows_per_half, _ = block_of_keys.shape
    rows_of_keys = block_of_keys[..., :hidden_width].reshape(
        device_count, 2, rows_per_half, KEY_VALUE_HEADS, HEAD_SIZE
    )
    rows_of_values = block_of_keys[..., hidden_width:].reshape(
        device_count, 2, rows_per_half, KEY_VALUE_HEADS, HEAD_SIZE
    )
    return (rows_of_keys, rows_of_values)


def attend(query_rows, rows_of_keys, rows_of_values, causal_visible):
    scores = jnp.einsum(
        "rgjd,kgd->grjk", query_rows, rows_of_keys, preferred_element_type=jnp.float32
    ) * HEAD_SIZE ** (-0.5)
    if causal_visible is not None:
        scores = jnp.where(causal_visible[None, :, None, :], scores, MASKED_SCORE)
    row_max = jnp.max(scores, axis=-1)
    exponentials = jnp.exp(scores - row_max[..., None])
    row_total = jnp.sum(exponentials, axis=-1)
    mixture = jnp.einsum(
        "grjk,kgd->rgjd",
        exponentials.astype(jnp.bfloat16),
        rows_of_values,
        preferred_element_type=jnp.float32,
    )
    return (jnp.transpose(row_max, (1, 0, 2)), jnp.transpose(row_total, (1, 0, 2)), mixture)


def empty_part(count_of_rows):
    queries_per_group = QUERY_HEADS // KEY_VALUE_HEADS
    return (
        jnp.full((count_of_rows, KEY_VALUE_HEADS, queries_per_group), MASKED_SCORE, jnp.float32),
        jnp.zeros((count_of_rows, KEY_VALUE_HEADS, queries_per_group), jnp.float32),
        jnp.zeros((count_of_rows, KEY_VALUE_HEADS, queries_per_group, HEAD_SIZE), jnp.float32),
    )


def combine(carried, incoming):
    carried_max, carried_total, carried_mix = carried
    incoming_max, incoming_total, incoming_mix = incoming
    new_max = jnp.maximum(carried_max, incoming_max)
    carried_scale = jnp.exp(carried_max - new_max)
    incoming_scale = jnp.exp(incoming_max - new_max)
    return (
        new_max,
        carried_total * carried_scale + incoming_total * incoming_scale,
        carried_mix * carried_scale[..., None] + incoming_mix * incoming_scale[..., None],
    )


def forward_block(carried, block_of_keys, source_ctx, own_ctx, query_rows, own_places, ctx_count):
    rows_of_keys, rows_of_values = split_block(block_of_keys)
    device_count, _, rows_per_half, _ = block_of_keys.shape

    def forward_earlier():
        return attend(
            query_rows,
            rows_of_keys[:, 0].reshape(-1, KEY_VALUE_HEADS, HEAD_SIZE),
            rows_of_values[:, 0].reshape(-1, KEY_VALUE_HEADS, HEAD_SIZE),
            None,
        )

    def forward_later():
        late_part = attend(
            query_rows[rows_per_half:],
            rows_of_keys.reshape(-1, KEY_VALUE_HEADS, HEAD_SIZE),
            rows_of_values.reshape(-1, KEY_VALUE_HEADS, HEAD_SIZE),
            None,
        )
        early_part = empty_part(rows_per_half)
        return tuple(
            (
                jnp.concatenate([early_piece, late_piece], axis=0)
                for early_piece, late_piece in zip(early_part, late_part)
            )
        )

    def forward_diagonal():
        key_places = block_places(source_ctx, 2 * rows_per_half, ctx_count, device_count)
        causal_visible = own_places[:, None] >= key_places[None, :]
        return attend(
            query_rows,
            rows_of_keys.reshape(-1, KEY_VALUE_HEADS, HEAD_SIZE),
            rows_of_values.reshape(-1, KEY_VALUE_HEADS, HEAD_SIZE),
            causal_visible,
        )

    branch_index = jnp.where(source_ctx == own_ctx, 2, jnp.where(source_ctx > own_ctx, 1, 0))
    return combine(
        carried, lax.switch(branch_index, [forward_earlier, forward_later, forward_diagonal])
    )


def attend_back(
    query_rows, attended_grad, log_total, delta_rows, rows_of_keys, rows_of_values, causal_visible
):
    scores = jnp.einsum(
        "rgjd,kgd->grjk", query_rows, rows_of_keys, preferred_element_type=jnp.float32
    ) * HEAD_SIZE ** (-0.5)
    if causal_visible is not None:
        scores = jnp.where(causal_visible[None, :, None, :], scores, MASKED_SCORE)
    probabilities = jnp.exp(scores - jnp.transpose(log_total, (1, 0, 2))[..., None])
    prob_grad = jnp.einsum(
        "rgjd,kgd->grjk", attended_grad, rows_of_values, preferred_element_type=jnp.float32
    )
    score_grad = (
        probabilities * (prob_grad - jnp.transpose(delta_rows, (1, 0, 2))[..., None])
    ).astype(jnp.bfloat16)
    query_part = jnp.einsum(
        "grjk,kgd->rgjd", score_grad, rows_of_keys, preferred_element_type=jnp.float32
    ) * HEAD_SIZE ** (-0.5)
    key_part = jnp.einsum(
        "grjk,rgjd->kgd", score_grad, query_rows, preferred_element_type=jnp.float32
    ) * HEAD_SIZE ** (-0.5)
    value_part = jnp.einsum(
        "grjk,rgjd->kgd",
        probabilities.astype(jnp.bfloat16),
        attended_grad,
        preferred_element_type=jnp.float32,
    )
    return (query_part, key_part, value_part)


def backward_block(
    block_of_keys,
    source_ctx,
    own_ctx,
    query_rows,
    attended_grad,
    log_total,
    delta_rows,
    own_places,
    ctx_count,
):
    rows_of_keys, rows_of_values = split_block(block_of_keys)
    device_count, _, rows_per_half, _ = block_of_keys.shape
    hidden_width = KEY_VALUE_HEADS * HEAD_SIZE

    def backward_earlier():
        query_part, key_part, value_part = attend_back(
            query_rows,
            attended_grad,
            log_total,
            delta_rows,
            rows_of_keys[:, 0].reshape(-1, KEY_VALUE_HEADS, HEAD_SIZE),
            rows_of_values[:, 0].reshape(-1, KEY_VALUE_HEADS, HEAD_SIZE),
            None,
        )
        early_grad = jnp.concatenate(
            [
                key_part.reshape(device_count, 1, rows_per_half, hidden_width),
                value_part.reshape(device_count, 1, rows_per_half, hidden_width),
            ],
            axis=-1,
        )
        return (query_part, jnp.concatenate([early_grad, jnp.zeros_like(early_grad)], axis=1))

    def backward_later():
        query_part, key_part, value_part = attend_back(
            query_rows[rows_per_half:],
            attended_grad[rows_per_half:],
            log_total[rows_per_half:],
            delta_rows[rows_per_half:],
            rows_of_keys.reshape(-1, KEY_VALUE_HEADS, HEAD_SIZE),
            rows_of_values.reshape(-1, KEY_VALUE_HEADS, HEAD_SIZE),
            None,
        )
        query_part = jnp.concatenate([jnp.zeros_like(query_part), query_part], axis=0)
        return (
            query_part,
            jnp.concatenate(
                [
                    key_part.reshape(device_count, 2, rows_per_half, hidden_width),
                    value_part.reshape(device_count, 2, rows_per_half, hidden_width),
                ],
                axis=-1,
            ),
        )

    def backward_diagonal():
        key_places = block_places(source_ctx, 2 * rows_per_half, ctx_count, device_count)
        causal_visible = own_places[:, None] >= key_places[None, :]
        query_part, key_part, value_part = attend_back(
            query_rows,
            attended_grad,
            log_total,
            delta_rows,
            rows_of_keys.reshape(-1, KEY_VALUE_HEADS, HEAD_SIZE),
            rows_of_values.reshape(-1, KEY_VALUE_HEADS, HEAD_SIZE),
            causal_visible,
        )
        return (
            query_part,
            jnp.concatenate(
                [
                    key_part.reshape(device_count, 2, rows_per_half, hidden_width),
                    value_part.reshape(device_count, 2, rows_per_half, hidden_width),
                ],
                axis=-1,
            ),
        )

    branch_index = jnp.where(source_ctx == own_ctx, 2, jnp.where(source_ctx > own_ctx, 1, 0))
    return lax.switch(branch_index, [backward_earlier, backward_later, backward_diagonal])


def per_device(
    inputs,
    attn_gain,
    query_weight,
    key_matrix,
    value_matrix,
    out_weight,
    ffn_gain,
    gate_weight,
    up_weight,
    down_weight,
    cotangent,
):
    ctx_count = lax.axis_size("ctx")
    device_count = lax.axis_size("ws")
    own_ctx = lax.axis_index("ctx")
    own_member = lax.axis_index("ws")
    micro_count, count_of_rows, _ = inputs.shape
    rows_per_half = count_of_rows // 2
    queries_per_group = QUERY_HEADS // KEY_VALUE_HEADS
    hidden_width = KEY_VALUE_HEADS * HEAD_SIZE
    own_places = query_places(own_ctx, own_member, count_of_rows, ctx_count, device_count)
    cosine_table, sine_table = rotary_tables(own_places)
    grad_sums = None
    layer_outs = []
    input_grads = []
    for micro_batch in range(micro_count):
        gathered = (
            lax.all_gather(attn_gain, ("ctx", "ws"), axis=0, tiled=True),
            lax.all_gather(query_weight, ("ctx", "ws"), axis=0, tiled=True),
            lax.all_gather(key_matrix, ("ctx", "ws"), axis=0, tiled=True),
            lax.all_gather(value_matrix, ("ctx", "ws"), axis=0, tiled=True),
            lax.all_gather(out_weight, ("ctx", "ws"), axis=0, tiled=True),
            lax.all_gather(ffn_gain, ("ctx", "ws"), axis=0, tiled=True),
            lax.all_gather(gate_weight, ("ctx", "ws"), axis=0, tiled=True),
            lax.all_gather(up_weight, ("ctx", "ws"), axis=0, tiled=True),
            lax.all_gather(down_weight, ("ctx", "ws"), axis=0, tiled=True),
        )
        (
            full_attn_gain,
            full_query,
            complete_key,
            full_value,
            full_out,
            full_ffn_gain,
            full_gate,
            full_up,
            full_down,
        ) = gathered
        first_gain = full_attn_gain.astype(jnp.float32)
        second_gain = full_ffn_gain.astype(jnp.float32)
        layer_rows = inputs[micro_batch].astype(jnp.float32)
        normalized_rows, first_inverse = normalize(layer_rows, first_gain)
        normalized_reduced = normalized_rows.astype(jnp.bfloat16)
        query_rows = rotate(
            matrix_multiply(normalized_reduced, full_query).reshape(
                count_of_rows, QUERY_HEADS, HEAD_SIZE
            ),
            cosine_table,
            sine_table,
        )
        query_rows = query_rows.astype(jnp.bfloat16).reshape(
            count_of_rows, KEY_VALUE_HEADS, queries_per_group, HEAD_SIZE
        )
        rows_of_keys = rotate(
            matrix_multiply(normalized_reduced, complete_key).reshape(
                count_of_rows, KEY_VALUE_HEADS, HEAD_SIZE
            ),
            cosine_table,
            sine_table,
        ).astype(jnp.bfloat16)
        rows_of_values = matrix_multiply(normalized_reduced, full_value).astype(jnp.bfloat16)
        local_block = jnp.concatenate(
            [rows_of_keys.reshape(count_of_rows, hidden_width), rows_of_values], axis=-1
        )
        group_block = lax.all_gather(local_block, "ws", axis=0, tiled=True).reshape(
            device_count, 2, rows_per_half, 2 * hidden_width
        )

        def fold_step(carried, shard_piece):

            def visit_block(state_now, block_entry):
                block_of_keys, source_ctx = block_entry
                return (
                    forward_block(
                        state_now,
                        block_of_keys,
                        source_ctx,
                        own_ctx,
                        query_rows,
                        own_places,
                        ctx_count,
                    ),
                    None,
                )

            source_list = jnp.arange(shard_piece.shape[0], dtype=jnp.int32)
            result_state, _ = lax.scan(visit_block, carried, (shard_piece, source_list))
            return result_state

        row_max, row_total, mixture = fold_step(
            empty_part(count_of_rows), lax.all_gather(group_block[None], "ctx", axis=0, tiled=True)
        )
        attended = mixture / row_total[..., None]
        log_total = row_max + jnp.log(row_total)
        attended_low = attended.astype(jnp.bfloat16).reshape(count_of_rows, QUERY_HEADS * HEAD_SIZE)
        middle = layer_rows + matrix_multiply(attended_low, full_out)
        hidden, second_inverse = normalize(middle, second_gain)
        hidden_low = hidden.astype(jnp.bfloat16)
        gate_rows = matrix_multiply(hidden_low, full_gate)
        up_rows = matrix_multiply(hidden_low, full_up)
        sigmoid_gate = jax.nn.sigmoid(gate_rows)
        silu_gate = gate_rows * sigmoid_gate
        activated = (silu_gate * up_rows).astype(jnp.bfloat16)
        layer_outs.append((middle + matrix_multiply(activated, full_down)).astype(jnp.bfloat16))
        upstream_low = cotangent[micro_batch]
        upstream = upstream_low.astype(jnp.float32)
        down_sum = outer_sum(activated, upstream_low)
        act_grad = back_product(upstream_low, full_down)
        gate_low = (
            act_grad * up_rows * sigmoid_gate * (1.0 + gate_rows * (1.0 - sigmoid_gate))
        ).astype(jnp.bfloat16)
        up_low = (act_grad * silu_gate).astype(jnp.bfloat16)
        gate_sum = outer_sum(hidden_low, gate_low)
        up_sum = outer_sum(hidden_low, up_low)
        hidden_grad = back_product(gate_low, full_gate) + back_product(up_low, full_up)
        middle_part, ffn_gain_sum = normalize_back(middle, second_inverse, second_gain, hidden_grad)
        middle_grad = middle_part + upstream
        branch_low = middle_grad.astype(jnp.bfloat16)
        out_sum = outer_sum(attended_low, branch_low)
        attended_grad = (
            back_product(branch_low, full_out)
            .reshape(count_of_rows, KEY_VALUE_HEADS, queries_per_group, HEAD_SIZE)
            .astype(jnp.bfloat16)
        )
        delta_rows = jnp.sum(attended_grad.astype(jnp.float32) * attended, axis=-1)

        def cycle_step(turn_index, carried):
            block_of_keys, block_grad, query_total = carried
            source_ctx = (own_ctx - turn_index) % ctx_count
            query_part, block_part = backward_block(
                block_of_keys,
                source_ctx,
                own_ctx,
                query_rows,
                attended_grad,
                log_total,
                delta_rows,
                own_places,
                ctx_count,
            )
            block_grad = block_grad + block_part
            next_block = shifted(block_of_keys, "ctx", 1)
            next_grad = shifted(as_sent(block_grad), "ctx", 1).astype(block_grad.dtype)
            return (next_block, next_grad, query_total + query_part)

        cycle_start = (
            group_block,
            jnp.zeros(group_block.shape, jnp.float32),
            jnp.zeros((count_of_rows, KEY_VALUE_HEADS, queries_per_group, HEAD_SIZE), jnp.float32),
        )
        _, block_grad, query_total = lax.fori_loop(0, ctx_count, cycle_step, cycle_start)
        local_gradient = (
            lax.psum_scatter(block_grad.astype(jnp.bfloat16), "ws", scatter_dimension=0, tiled=True)
            .astype(jnp.float32)
            .reshape(count_of_rows, 2 * hidden_width)
        )
        key_low = rotate_back(
            local_gradient[:, :hidden_width].reshape(count_of_rows, KEY_VALUE_HEADS, HEAD_SIZE),
            cosine_table,
            sine_table,
        )
        key_low = key_low.astype(jnp.bfloat16).reshape(count_of_rows, hidden_width)
        value_low = local_gradient[:, hidden_width:].astype(jnp.bfloat16)
        query_low = rotate_back(
            query_total.reshape(count_of_rows, QUERY_HEADS, HEAD_SIZE), cosine_table, sine_table
        )
        query_low = query_low.astype(jnp.bfloat16).reshape(count_of_rows, QUERY_HEADS * HEAD_SIZE)
        query_sum = outer_sum(normalized_reduced, query_low)
        key_sum = outer_sum(normalized_reduced, key_low)
        value_sum = outer_sum(normalized_reduced, value_low)
        normed_grad = (
            back_product(query_low, full_query)
            + back_product(key_low, complete_key)
            + back_product(value_low, full_value)
        )
        input_part, attn_gain_sum = normalize_back(
            layer_rows, first_inverse, first_gain, normed_grad
        )
        input_grads.append((middle_grad + input_part).astype(jnp.bfloat16))
        batch_terms = (
            attn_gain_sum,
            query_sum,
            key_sum,
            value_sum,
            out_sum,
            ffn_gain_sum,
            gate_sum,
            up_sum,
            down_sum,
        )
        if grad_sums is None:
            grad_sums = batch_terms
        else:
            grad_sums = tuple(
                (
                    earlier_sum + batch_term
                    for earlier_sum, batch_term in zip(grad_sums, batch_terms)
                )
            )
    owned_grads = (
        lax.psum_scatter(grad_sums[0], ("ctx", "ws"), scatter_dimension=0, tiled=True),
        lax.psum_scatter(grad_sums[1], ("ctx", "ws"), scatter_dimension=0, tiled=True),
        lax.psum_scatter(grad_sums[2], ("ctx", "ws"), scatter_dimension=0, tiled=True),
        lax.psum_scatter(grad_sums[3], ("ctx", "ws"), scatter_dimension=0, tiled=True),
        lax.psum_scatter(grad_sums[4], ("ctx", "ws"), scatter_dimension=0, tiled=True),
        lax.psum_scatter(grad_sums[5], ("ctx", "ws"), scatter_dimension=0, tiled=True),
        lax.psum_scatter(grad_sums[6], ("ctx", "ws"), scatter_dimension=0, tiled=True),
        lax.psum_scatter(grad_sums[7], ("ctx", "ws"), scatter_dimension=0, tiled=True),
        lax.psum_scatter(grad_sums[8], ("ctx", "ws"), scatter_dimension=0, tiled=True),
    )
    return (
        jnp.stack(layer_outs),
        jnp.stack(input_grads),
        owned_grads[0],
        owned_grads[1],
        owned_grads[2],
        owned_grads[3],
        owned_grads[4],
        owned_grads[5],
        owned_grads[6],
        owned_grads[7],
        owned_grads[8],
    )


MESH = pl.DeviceIdType.MESH
NEG = -1e30
WIDE = 128
VMEM_LIMIT = 61 * 1024 * 1024


def fits_fast(mesh):
    return mesh.shape["ctx"] == 8 and mesh.shape["ws"] == 4


def place():
    c = lax.axis_index("ctx")
    w = lax.axis_index("ws")
    return c // 2, lax.rem(c, 2), w // 2, lax.rem(w, 2)


def device(z, y, x, k):
    return (z * 2 + y, x * 2 + k)


def greet(zn):
    z, y, x, k = place()
    others = [device(lax.rem(z + j, zn), y, x, k) for j in range(1, zn)]
    others += [device(z, y, 1 - x, k), device(z, 1 - y, x, k), device(z, y, x, 1 - k)]
    barrier = pltpu.get_barrier_semaphore()
    for other in others:
        pl.semaphore_signal(barrier, inc=1, device_id=other, device_id_type=MESH)
    pl.semaphore_wait(barrier, len(others))


def remote(src, dst, send, recv, where):
    return pltpu.make_async_remote_copy(
        src_ref=src, dst_ref=dst, send_sem=send, recv_sem=recv, device_id=where, device_id_type=MESH
    )


class Gather:
    SEMS = 12

    def __init__(self, src, dst, send, recv, zn):
        z, y, x, k = place()
        own = dst.at[z, y, x, k]
        hz = zn // 2
        xn, yn, sib = device(z, y, 1 - x, k), device(z, 1 - y, x, k), device(z, y, x, 1 - k)

        def push(i, ref, where):
            return remote(ref, ref, send.at[i], recv.at[i], where)

        def col(yy, xx, lo=0, n=zn):
            return dst.at[pl.ds(lo, n), yy, xx, k]

        self.local = pltpu.make_async_copy(src(z), own, send.at[0])
        self.along = []
        for j in range(1, zn):
            zz = lax.rem(z + j, zn)
            self.along.append(remote(src(zz), own, send.at[j], recv.at[j], device(zz, y, x, k)))
        self.cols = [push(4, col(y, x), xn), push(5, col(y, x), yn)]
        self.corner = [push(7, col(1 - y, x, 0, hz), xn), push(8, col(y, 1 - x, hz, hz), yn)]
        self.twin_own = push(6, col(y, x), sib)
        self.twin_cols = [push(9, col(y, 1 - x), sib), push(10, col(1 - y, x), sib)]
        self.twin_corner = push(11, col(1 - y, 1 - x), sib)

    def stage(self, n):
        if n == 0:
            self.local.start()
            for c in self.along:
                c.start()
        elif n == 1:
            self.local.wait()
            for c in self.along:
                c.wait_recv()
            for c in self.cols:
                c.start()
            self.twin_own.start()
        elif n == 2:
            for c in self.cols:
                c.wait_recv()
            for c in self.corner:
                c.start()
            for c in self.twin_cols:
                c.start()
        elif n == 3:
            for c in self.corner:
                c.wait_recv()
            self.twin_corner.start()
        elif n == 4:
            for c in [self.twin_own] + self.twin_cols + [self.twin_corner]:
                c.wait_recv()
            for c in (
                self.along
                + self.cols
                + self.corner
                + [self.twin_own]
                + self.twin_cols
                + [self.twin_corner]
            ):
                c.wait_send()


def stage_step(items, stages, t, between=None):
    for n in stages:
        if 0 <= t - n < len(items):
            items[t - n].stage(n)
            if between is not None:
                between()


GATHER_STAGES = (0, 1, 2, 3, 4)
SUM_STAGES = (0, 1, 2, 3)


def portions(step, total, parts):
    done = [0]

    def call(all_=False):
        upto = total if all_ else min(total, done[0] + -(-total // parts))
        if upto > done[0]:
            lax.fori_loop(done[0], upto, step, 0)
            done[0] = upto

    return call


def pieces_of(rows, cols, nrow, ncol):
    return [
        (i * (rows // nrow), rows // nrow, j * (cols // ncol), cols // ncol)
        for i in range(nrow)
        for j in range(ncol)
    ]


def gather_item(ref, out, r0, nr, c0, nc, send, recv, zn):
    src = ref.at[pl.ds(r0, nr), pl.ds(c0, nc)]
    dst = out.at[:, :, :, :, pl.ds(r0, nr), pl.ds(c0, nc)]
    return Gather(lambda zz: src, dst, send, recv, zn)


class Exchange:
    def __init__(self, src, dst, send, recv, zn):
        z, y, x, k = place()
        self.local = pltpu.make_async_copy(src(z), dst(z), send.at[0])
        self.along = []
        for j in range(1, zn):
            zz = lax.rem(z + j, zn)
            self.along.append(remote(src(zz), dst(z), send.at[j], recv.at[j], device(zz, y, x, k)))

    def start(self):
        self.local.start()
        for c in self.along:
            c.start()

    def arrived(self):
        self.local.wait()
        for c in self.along:
            c.wait_recv()

    def sent(self):
        for c in self.along:
            c.wait_send()


class Scatter:
    SEMS = 10

    @staticmethod
    def scratch(zn, nr, nc):
        b = jnp.bfloat16
        return [
            pltpu.VMEM((zn, 2, 2, nr, nc), b),
            pltpu.VMEM((zn, 2, 2, nr, nc), b),
            pltpu.VMEM((2, zn // 2, nr, nc), b),
            pltpu.VMEM((2, zn, nr, nc), b),
            pltpu.VMEM((zn - 1, nr, nc), b),
        ]

    def __init__(self, part, out, bufs, send, recv, zn, give=None):
        z, y, x, k = self.at = place()
        self.zn = zn
        hz = zn // 2
        xn, yn, sib = device(z, y, 1 - x, k), device(z, 1 - y, x, k), device(z, y, x, 1 - k)
        self.held, self.twin, self.corners, self.colsums, self.ends = held, twin, corners, colsums, ends = bufs
        self.out = out
        self.load = None
        if give is None:
            self.load = pltpu.make_async_copy(part.at[:, :, :, k], held, send.at[0])
            give = part.at[:, :, :, 1 - k]
        self.to_twin = remote(give, twin, send.at[1], recv.at[1], sib)
        self.to_corner = [
            remote(held.at[pl.ds(0, hz), 1 - y, 1 - x], corners.at[0], send.at[2], recv.at[2], yn),
            remote(held.at[pl.ds(hz, hz), 1 - y, 1 - x], corners.at[1], send.at[3], recv.at[3], xn),
        ]
        self.to_col = [
            remote(held.at[:, y, 1 - x], colsums.at[0], send.at[4], recv.at[4], xn),
            remote(held.at[:, 1 - y, x], colsums.at[1], send.at[5], recv.at[5], yn),
        ]
        self.along = []
        for j in range(1, zn):
            zz = lax.rem(z + j, zn)
            dst = out.at[z] if ends is None else ends.at[j - 1]
            self.along.append(
                remote(held.at[zz, y, x], dst, send.at[5 + j], recv.at[5 + j], device(zz, y, x, k))
            )
        self.last = pltpu.make_async_copy(held.at[z, y, x], out.at[z], send.at[0]) if ends is None else None

    def stage(self, n):
        z, y, x, k = self.at
        zn, hz = self.zn, self.zn // 2
        held = self.held
        if n == 0:
            self.to_twin.start()
            if self.load is not None:
                self.load.start()
        elif n == 1:
            if self.load is not None:
                self.load.wait()
            self.to_twin.wait_recv()

            def add(i, _):
                for yy in range(2):
                    for xx in range(2):
                        held[i, yy, xx] = held[i, yy, xx] + self.twin[i, yy, xx]
                return 0

            lax.fori_loop(0, zn, add, 0)
            for c in self.to_corner:
                c.start()
        elif n == 2:
            for c in self.to_corner:
                c.wait_recv()
            for i in range(hz):
                held[i, y, 1 - x] = held[i, y, 1 - x] + self.corners[0, i]
                held[hz + i, 1 - y, x] = held[hz + i, 1 - y, x] + self.corners[1, i]
            for c in self.to_col:
                c.start()
        elif n == 3:
            for c in self.to_col:
                c.wait_recv()

            def add(i, _):
                f = jnp.float32
                held[i, y, x] = (
                    held[i, y, x].astype(f) + self.colsums[0, i].astype(f) + self.colsums[1, i].astype(f)
                ).astype(jnp.bfloat16)
                return 0

            lax.fori_loop(0, zn, add, 0)
            for c in self.along:
                c.start()
            if self.last is not None:
                self.last.start()
        elif n == 4:
            for c in self.along:
                c.wait_recv()
            if self.last is not None:
                self.last.wait()
            else:
                total = held[z, y, x].astype(jnp.float32)
                for j in range(zn - 1):
                    total = total + self.ends[j].astype(jnp.float32)
                self.out[...] = total
            for c in [self.to_twin] + self.to_corner + self.to_col + self.along:
                c.wait_send()


NT = (((1,), (1,)), ((), ()))


def nt(a, b):
    return lax.dot_general(a, b, NT, preferred_element_type=jnp.float32)


PER = QUERY_HEADS // KEY_VALUE_HEADS
HALF_GROUPS = KEY_VALUE_HEADS // 2
HALF_HEADS = QUERY_HEADS // 2
KV_LANES = 2 * HALF_GROUPS * HEAD_SIZE


def lane_slot(n):
    return n // 2, n % 2


def key_slot(g):
    return lane_slot(g)


def value_slot(g):
    return lane_slot(HALF_GROUPS + g)


def pair_index(half, zp):
    return zp if half == 0 else 3 - zp


def pair_tile(src, g, half, zp):
    tiles = []
    for j in range(PER):
        lo = HEAD_SIZE * (PER * g + j)
        a = src[2 * zp, lo : lo + HEAD_SIZE, :].astype(jnp.float32)
        b = src[2 * zp + 1, lo : lo + HEAD_SIZE, :].astype(jnp.float32)
        low = lax.broadcasted_iota(jnp.int32, a.shape, 1) < WIDE // 2
        if half == 0:
            tiles.append(jnp.where(low, a, pltpu.roll(b, WIDE // 2, 1)))
        else:
            tiles.append(jnp.where(low, pltpu.roll(a, WIDE // 2, 1), b))
    return jnp.concatenate(tiles, axis=1)


def unpair(get, dst):
    for zp in range(2):
        for g in range(HALF_GROUPS):
            first, second = get(g, pair_index(0, zp)), get(g, pair_index(1, zp))
            for j in range(PER):
                lo = HEAD_SIZE * (PER * g + j)
                a, b = first[:, WIDE * j : WIDE * j + WIDE], second[:, WIDE * j : WIDE * j + WIDE]
                low = lax.broadcasted_iota(jnp.int32, a.shape, 1) < WIDE // 2
                even = jnp.where(low, a, pltpu.roll(b, WIDE // 2, 1))
                odd = jnp.where(low, pltpu.roll(a, WIDE // 2, 1), b)
                dst[2 * zp, lo : lo + HEAD_SIZE, :] = even.astype(dst.dtype)
                dst[2 * zp + 1, lo : lo + HEAD_SIZE, :] = odd.astype(dst.dtype)


def set_padded(dst, g, p, tile, side):
    tile = tile.astype(dst.dtype)
    dst[g, p, side * HEAD_SIZE : (side + 1) * HEAD_SIZE, :] = tile
    dst[g, p, (1 - side) * HEAD_SIZE : (2 - side) * HEAD_SIZE, :] = jnp.zeros_like(tile)


def walk(t, y, cn):
    b1, b2, b3 = 3 + y, 10 + 2 * y, 22 + y
    p = (t >= b1).astype(jnp.int32) + (t >= b2).astype(jnp.int32) + (t >= b3).astype(jnp.int32)
    j = t - jnp.where(p == 0, 0, jnp.where(p == 1, b1, jnp.where(p == 2, b2, b3)))
    zp = jnp.where(p < 2, p, 3 - p)
    low = jnp.where(p < 2, 4 * zp + y, 2 * cn - 3 - 4 * zp - y)
    late = (j >= cn).astype(jnp.int32)
    src = jnp.where(late == 1, 2 * cn - 1 - j, j)
    return p, j, src // 2, lax.rem(src, 2), pl.multiple_of(late * HEAD_SIZE, HEAD_SIZE), j >= low


STEPS = 38
FORWARD_PARTS = 20


def visible(p, j, y, w, cn, wn, rows):
    shape = (wn * rows, PER * WIDE)
    lane = lax.rem(lax.broadcasted_iota(jnp.int32, shape, 1), WIDE)
    zp = jnp.where(p < 2, p, 3 - p)
    c = 2 * (2 * zp + lane // rows) + y
    span = jnp.where(p < 2, c, 2 * cn - 1 - c)
    query = span * (wn * rows) + w * rows + lax.rem(lane, rows)
    key = j * (wn * rows) + lax.broadcasted_iota(jnp.int32, shape, 0)
    return key <= query


def key_block(kvg, zz, yy, late, rows, block):
    t = kvg[zz, yy, :, :, pl.ds(late, rows), WIDE * block : WIDE * block + WIDE]
    return t.reshape(4 * rows, WIDE)


def turned(t):
    return t.astype(jnp.float32).T.astype(t.dtype)


def by_span(body, kvg, cn, rows):
    def one(j, _):
        late = (j >= cn).astype(jnp.int32)
        src = jnp.where(late == 1, 2 * cn - 1 - j, j)
        at = pl.multiple_of(late * rows, rows)
        body(j, lambda b: key_block(kvg, src // 2, lax.rem(src, 2), at, rows, b))
        return 0

    lax.fori_loop(0, 2 * cn, one, 0)


def transposed(t):
    return jnp.concatenate([t[:, i : i + WIDE].T for i in range(0, t.shape[1], WIDE)], axis=0)


def unfold_rows(src, dst, rb):
    n = src.shape[0] // 16
    fold = 16 // rb
    cols = src.shape[1]
    shape = (n * rb, n * 16)
    row = lax.broadcasted_iota(jnp.int32, shape, 0)
    at = 16 * (row // rb) + lax.rem(row, rb)
    col = lax.broadcasted_iota(jnp.int32, shape, 1)
    for q in range(fold):
        pick = jnp.where(col == at + rb * q, 1.0, 0.0).astype(jnp.bfloat16)
        t = jnp.dot(pick, src[...], preferred_element_type=jnp.float32)
        dst[:, q * cols : (q + 1) * cols] = t.astype(dst.dtype)


def gather_attend(x, tables, qkv, fold1, arrays, used, cuts, collective_id):
    cn, wn = lax.axis_size("ctx"), lax.axis_size("ws")
    zn = cn // 2
    dn = cn * wn
    tokens = tables.shape[1]
    all_rows, width = x.shape
    mbs = all_rows // tokens
    qkv_w = qkv.shape[1]
    q_rows = qkv_w - 2 * KV_LANES
    rows = tokens // 2
    mine = q_rows // 2
    f32, b16 = jnp.float32, jnp.bfloat16
    ra = qkv.shape[0] // 16 * 16
    rb = qkv.shape[0] - ra
    wa = dn * ra
    wide1 = fold1.shape[1] * (16 // rb)
    n = len(arrays)
    work = [(a, piece) for a in range(n) for piece in pieces_of(used[a], arrays[a].shape[1], *cuts[a])]
    groups = range(HALF_GROUPS)
    n_first = 3

    def kernel(*refs):
        x_ref, tab, qkv_ref, fold_ref = refs[:4]
        ins = refs[4 : 4 + n]
        at = 4 + n
        o_out, q_out, kv_out, oh_out, lse_out, w_out, wb_out, hn_out, hnb_out, inv_out, gains_out = refs[at : at + 11]
        at += 11
        outs = refs[at : at + n]
        at += n
        (wq, f1, wide, hn, q_s, kv_s, qh, kvg, oh, qpad, vt, m_s, l_s, acc, send, recv, xs, xr, ks, kr, save) = refs[at:]
        greet(zn)
        z, y, x_, k = place()
        w = 2 * x_ + k

        def lanes_of(zz):
            return kv_s.at[zz // 2, :, pl.ds(pl.multiple_of(lax.rem(zz, 2) * KV_LANES, WIDE), KV_LANES)]

        def heads_of(ref, zz):
            return ref.at[zz // 2, pl.ds(pl.multiple_of(lax.rem(zz, 2) * mine, 16), mine), :]

        items = [
            gather_item(fold_ref, f1, 0, 16, 0, fold1.shape[1], send.at[0], recv.at[0], zn),
            gather_item(qkv_ref, wq, 0, ra, 0, 2 * KV_LANES, send.at[1], recv.at[1], zn),
            gather_item(qkv_ref, wq, 0, ra, 2 * KV_LANES, q_rows, send.at[2], recv.at[2], zn),
        ]
        items += [
            gather_item(ins[a], outs[a], r0, nr, c0, nc, send.at[n_first + i], recv.at[n_first + i], zn)
            for i, (a, (r0, nr, c0, nc)) in enumerate(work)
        ]
        kvx = Gather(lanes_of, kvg, ks, kr, zn)
        qx = Exchange(lambda zz: heads_of(q_s, zz), lambda zz: qh.at[zz], xs.at[0], xr.at[0], zn)
        ox = Exchange(lambda zz: oh.at[zz], lambda zz: heads_of(o_out, zz), xs.at[1], xr.at[1], zn)
        for s in range(n_first + 1):
            stage_step(items, GATHER_STAGES, s)
        xf = x_ref[...].astype(f32)
        inv = lax.rsqrt(jnp.mean(xf * xf, axis=-1, keepdims=True) + EPSILON)
        inv_out[...] = inv
        m_s[...] = jnp.full(m_s.shape, NEG, f32)
        l_s[...] = jnp.zeros(l_s.shape, f32)
        acc[...] = jnp.zeros(acc.shape, f32)
        stage_step(items, GATHER_STAGES, n_first + 1)
        unfold_rows(f1[...].reshape(dn * 16, fold1.shape[1]), wide, rb)
        lane = lax.broadcasted_iota(jnp.int32, (WIDE, width), 1)
        local = jnp.where(lane < wa, lax.rem(lane, ra), ra + lax.rem(lane - wa, rb))
        spread = jnp.where(lax.broadcasted_iota(jnp.int32, (WIDE, width), 0) == local, 1.0, 0.0).astype(b16)
        lines = jnp.dot(wide[:, wide1 - WIDE :], spread, preferred_element_type=f32)
        lane = lax.broadcasted_iota(jnp.int32, lines.shape, 1)
        owner = jnp.where(lane < wa, lane // ra, (lane - wa) // rb)
        line = lax.broadcasted_iota(jnp.int32, lines.shape, 0)
        for i in range(2):
            gains_out[i : i + 1, :] = jnp.sum(jnp.where(line == rb * owner + i, lines, 0.0), axis=0, keepdims=True)
        normed = xf * inv * gains_out[0:1, :]
        hn[...] = normed.astype(b16)
        hn_out[...] = transposed(normed[:, :wa]).astype(b16)
        hnb_out[...] = transposed(normed[:, wa:]).astype(b16)
        stage_step(items, GATHER_STAGES, n_first + 2)

        low_lanes = lax.broadcasted_iota(jnp.int32, (tokens, WIDE), 1) < HEAD_SIZE
        quarter = HEAD_SIZE // 2

        def turned_heads(t, kind):
            if kind == "still":
                return t
            cos, low, high = tab[0], tab[1], tab[2]
            r = t * cos + pltpu.roll(t, WIDE - quarter, 1) * low + pltpu.roll(t, quarter, 1) * high
            return r if kind == "turn" else jnp.where(low_lanes, r, t)

        def project(c):
            cols = slice(c * KV_LANES, (c + 1) * KV_LANES)
            t = jnp.dot(hn[:, :wa], wq[:, :, :, :, :, cols].reshape(wa, KV_LANES), preferred_element_type=f32)
            t = t + jnp.dot(hn[:, wa:], wide[:, cols], preferred_element_type=f32)
            kinds = ["turn", "mixed", "still"] if c < 2 else ["turn"] * 3
            for mb in range(mbs):
                for b in range(3):
                    r = turned_heads(t[mb * tokens : (mb + 1) * tokens, WIDE * b : WIDE * b + WIDE], kinds[b])
                    at = c * KV_LANES + WIDE * b
                    if c < 2:
                        kv_s[mb, :, at : at + WIDE] = r.astype(b16)
                    else:
                        at -= 2 * KV_LANES
                        q_s[mb, at : at + WIDE, :] = (r * HEAD_SIZE**-0.5).T.astype(b16)

        project(0)
        project(1)
        kvx.stage(0)
        stage_step(items, GATHER_STAGES, n_first + 3)
        for c in range(2, qkv_w // KV_LANES):
            project(c)
        qx.start()
        saves = [
            pltpu.make_async_copy(wq, w_out, save.at[3]),
            pltpu.make_async_copy(wide.at[:, pl.ds(0, qkv_w)], wb_out, save.at[4]),
        ]
        for s in saves:
            s.start()
        kvx.stage(1)
        kvx.stage(2)
        stage_step(items, GATHER_STAGES, n_first + 4)
        kvx.stage(3)
        qx.arrived()
        for half in range(2):
            for zp in range(2):
                for g in groups:
                    set_padded(qpad, g, pair_index(half, zp), pair_tile(qh, g, half, zp), key_slot(g)[1])
        kvx.stage(4)

        def turn(j, block):
            flat = {b: turned(block(b)) for b in sorted({value_slot(g)[0] for g in groups})}
            for g in groups:
                b, side = value_slot(g)
                vt[j, g] = flat[b][side * HEAD_SIZE : (side + 1) * HEAD_SIZE]

        by_span(turn, kvg, cn, rows)
        saves += [
            pltpu.make_async_copy(qh, q_out, save.at[0]),
            pltpu.make_async_copy(kvg, kv_out, save.at[1]),
        ]
        for s in saves[2:]:
            s.start()

        def step(t, _):
            p, j, zz, yy, late, edge = walk(t, y, cn)

            def run(masked):
                seen = visible(p, j, y, w, cn, wn, rows) if masked else None
                for g in groups:
                    s = jnp.dot(
                        key_block(kvg, zz, yy, late, rows, key_slot(g)[0]), qpad[g, p], preferred_element_type=f32
                    )
                    if masked:
                        s = jnp.where(seen, s, NEG)
                    m_old = m_s[g, p]
                    m_new = jnp.maximum(m_old, jnp.max(s, axis=0, keepdims=True))
                    alpha = jnp.exp(m_old - m_new)
                    e = jnp.exp(s - m_new)
                    m_s[g, p] = m_new
                    l_s[g, p] = l_s[g, p] * alpha + jnp.sum(e, axis=0, keepdims=True)
                    acc[g, p] = acc[g, p] * alpha + jnp.dot(
                        vt[j, g], e.astype(b16), preferred_element_type=f32
                    )

            pl.when(edge)(lambda: run(True))
            pl.when(jnp.logical_not(edge))(lambda: run(False))
            return 0

        last = len(items) + 4
        start = n_first + 5
        attend = portions(step, STEPS, FORWARD_PARTS)
        for s in range(start, last):
            stage_step(items, GATHER_STAGES, s, attend if s < last - 2 else None)
            if s == last - 3:
                attend(True)
                unpair(lambda g, p: acc[g, p] / l_s[g, p], oh)
                ox.start()
                saves.append(pltpu.make_async_copy(oh, oh_out, save.at[2]))
                saves[-1].start()
                lse_out[...] = m_s[...] + jnp.log(l_s[...])
        ox.arrived()
        ox.sent()
        qx.sent()
        for s in saves:
            s.wait()

    stat = (HALF_GROUPS, 4, 1, PER * WIDE)
    block = (zn, mine, tokens)
    kv_shape = (zn, 2, 2, 2, tokens, KV_LANES)
    any_ = pl.BlockSpec(memory_space=pl.ANY)
    vmem = pl.BlockSpec(memory_space=pltpu.VMEM)
    sds = jax.ShapeDtypeStruct
    dma = pltpu.SemaphoreType.DMA
    return pl.pallas_call(
        kernel,
        out_shape=[
            sds((mbs, q_rows, tokens), b16),
            sds(block, b16),
            sds(kv_shape, b16),
            sds(block, b16),
            sds(stat, f32),
            sds((zn, 2, 2, 2, ra, qkv_w), b16),
            sds((dn * rb, qkv_w), b16),
            sds((wa, all_rows), b16),
            sds((width - wa, all_rows), b16),
            sds((all_rows, 1), f32),
            sds((2, width), f32),
        ]
        + [sds((zn, 2, 2, 2, used[a], arrays[a].shape[1]), arrays[a].dtype) for a in range(n)],
        in_specs=[vmem] * 2 + [any_] * (2 + n),
        out_specs=[any_] * 4 + [vmem] + [any_] * 2 + [vmem] * 4 + [any_] * n,
        scratch_shapes=[
            pltpu.VMEM((zn, 2, 2, 2, ra, qkv_w), b16),
            pltpu.VMEM((zn, 2, 2, 2, 16, fold1.shape[1]), b16),
            pltpu.VMEM((dn * rb, wide1), b16),
            pltpu.VMEM((all_rows, width), b16),
            pltpu.VMEM((mbs, q_rows, tokens), b16),
            pltpu.VMEM((mbs, tokens, 2 * KV_LANES), b16),
            pltpu.VMEM(block, b16),
            pltpu.VMEM(kv_shape, b16),
            pltpu.VMEM(block, b16),
            pltpu.VMEM((HALF_GROUPS, 4, WIDE, PER * WIDE), b16),
            pltpu.VMEM((2 * cn, HALF_GROUPS, HEAD_SIZE, wn * rows), b16),
            pltpu.VMEM(stat, f32),
            pltpu.VMEM(stat, f32),
            pltpu.VMEM((HALF_GROUPS, 4, HEAD_SIZE, PER * WIDE), f32),
            dma((n_first + len(work), Gather.SEMS)),
            dma((n_first + len(work), Gather.SEMS)),
            dma((2, zn)),
            dma((2, zn)),
            dma((Gather.SEMS,)),
            dma((Gather.SEMS,)),
            dma((5,)),
        ],
        compiler_params=pltpu.CompilerParams(
            collective_id=collective_id, has_side_effects=True, vmem_limit_bytes=VMEM_LIMIT
        ),
    )(x, tables, qkv, fold1, *arrays)


class Share:
    def __init__(self, src, own, other, local, send, recv, split):
        z, y, x, k = place()
        mine = src.at[:, :, :, k] if split else src
        theirs = src.at[:, :, :, 1 - k] if split else src
        self.load = None if mine is own else pltpu.make_async_copy(mine, own, local)
        self.swap = remote(theirs, other, send, recv, device(z, y, x, 1 - k))
        self.waited = False

    def start(self):
        if self.load is not None:
            self.load.start()
        self.swap.start()

    def ready(self):
        if not self.waited:
            if self.load is not None:
                self.load.wait()
            self.swap.wait_recv()
            self.waited = True

    def sent(self):
        self.swap.wait_send()


class Sum:
    SEMS = 8

    def __init__(self, make, held, bufs, out, send, recv, zn):
        z, y, x, k = self.at = place()
        self.make, self.held, self.out, self.zn = make, held, out, zn
        hz = zn // 2
        xn, yn = device(z, y, 1 - x, k), device(z, 1 - y, x, k)
        self.corners, self.colsums, self.ends = corners, colsums, ends = bufs
        self.to_corner = [
            remote(held.at[pl.ds(0, hz), 1 - y, 1 - x], corners.at[0], send.at[0], recv.at[0], yn),
            remote(held.at[pl.ds(hz, hz), 1 - y, 1 - x], corners.at[1], send.at[1], recv.at[1], xn),
        ]
        self.to_col = [
            remote(held.at[:, y, 1 - x], colsums.at[0], send.at[2], recv.at[2], xn),
            remote(held.at[:, 1 - y, x], colsums.at[1], send.at[3], recv.at[3], yn),
        ]
        self.along = []
        for j in range(1, zn):
            zz = lax.rem(z + j, zn)
            self.along.append(
                remote(held.at[zz, y, x], ends.at[j - 1], send.at[3 + j], recv.at[3 + j], device(zz, y, x, k))
            )

    @staticmethod
    def scratch(zn, nr, nc):
        b = jnp.bfloat16
        return [
            pltpu.VMEM((2, zn // 2, nr, nc), b),
            pltpu.VMEM((2, zn, nr, nc), b),
            pltpu.VMEM((zn - 1, nr, nc), b),
        ]

    def stage(self, n):
        z, y, x, k = self.at
        zn, hz, held = self.zn, self.zn // 2, self.held
        f32, b16 = jnp.float32, jnp.bfloat16
        if n == 0:
            self.make(held)
            for c in self.to_corner:
                c.start()
        elif n == 1:
            for c in self.to_corner:
                c.wait_recv()
            for i in range(hz):
                held[i, y, 1 - x] = held[i, y, 1 - x] + self.corners[0, i]
                held[hz + i, 1 - y, x] = held[hz + i, 1 - y, x] + self.corners[1, i]
            for c in self.to_col:
                c.start()
        elif n == 2:
            for c in self.to_col:
                c.wait_recv()
            for i in range(zn):
                held[i, y, x] = (
                    held[i, y, x].astype(f32)
                    + self.colsums[0, i].astype(f32)
                    + self.colsums[1, i].astype(f32)
                ).astype(b16)
            for c in self.along:
                c.start()
        elif n == 3:
            for c in self.along:
                c.wait_recv()
            total = held[z, y, x].astype(f32)
            for j in range(zn - 1):
                total = total + self.ends[j].astype(f32)
            self.out[...] = total
            for c in self.to_corner + self.to_col + self.along:
                c.wait_send()


ORDER = (0, 1, 2, 3, 4, 5, 6, 7, 8, 9, 10, 11, 12)
BACK_SPAN, BACK_PARTS = 3, 10


def scatter_attend(do, qh, kvg, oh, lse, tables, lefts, rests, rights, plan, last, collective_id):
    cn, wn = lax.axis_size("ctx"), lax.axis_size("ws")
    zn = cn // 2
    mbs, q_rows, tokens = do.shape
    rows = tokens // 2
    mine = q_rows // 2
    all_rows = mbs * tokens
    f32, b16 = jnp.float32, jnp.bfloat16
    groups = range(HALF_GROUPS)
    scale = HEAD_SIZE**-0.5
    ff = rights[2].shape[1]
    width = rights[0].shape[1]
    qkv_w = q_rows + 2 * KV_LANES
    act_rows = lefts[0].shape[4]
    ra = lefts[1].shape[4]
    rest_w, qkv_rest_w = plan
    n_down = act_rows // ra
    half_ff = ff // 2
    sizes = (
        [(ra, width)] * n_down
        + [(ra, half_ff)] * 3
        + [(ra, half_ff // 2)] * 2
        + [(ra, width), (16, rest_w), (ra, 2 * KV_LANES), (ra, q_rows), (16, qkv_rest_w)]
    )
    max_cols = max(s[1] for s in sizes)
    ring = 4
    scratch = []
    for nr, nc in sizes:
        scratch += Sum.scratch(zn, nr, nc)
    n_items = len(sizes)
    ins_all = [*lefts, *rests, *rights]
    n_in = len(ins_all)
    split = [True] * len(lefts) + [False] * (n_in - len(lefts))
    half = lambda a, s: (a.shape[:3] + a.shape[4:]) if s else a.shape
    shares = []
    for a, s in zip(ins_all, split):
        shares += [pltpu.VMEM(half(a, s), b16), pltpu.VMEM(half(a, s), b16)]
    outs_shape = [
        (act_rows, width), (ra, ff), (ra, ff), (ra, width), (16, rest_w), (ra, qkv_w), (16, qkv_rest_w)
    ]
    n_out = len(outs_shape)
    n_last = len(last)

    def kernel(*refs):
        do_ref, qh_ref, kvg_ref, oh_ref, lse_ref, tab = refs[:6]
        ins = refs[6 : 6 + n_in]
        at = 6 + n_in
        w_ref, r_ref, x_ref, inv_ref, gain_ref, gx1_ref, gain2_ref, order_ref = refs[at : at + n_last]
        at += n_last
        outs = refs[at : at + n_out]
        input_grad, total = refs[at + n_out : at + n_out + 2]
        rest = refs[at + n_out + 2 :]
        bufs, rest = rest[: len(scratch)], rest[len(scratch) :]
        pairs, rest = rest[: len(shares)], rest[len(shares) :]
        (held, gq, gq_other, dkv_in, oh, gh, give, got) = rest[:8]
        kb = rest[8:12]
        send, recv, ps, pr, pl_, xs, xr, ks, kr, gs, gr, loads = rest[12:]
        dqh, dq_in = gh, oh
        greet(zn)
        z, y, x, k = place()
        w = 2 * x + k

        def heads_of(ref, zz):
            return ref.at[zz // 2, pl.ds(pl.multiple_of(lax.rem(zz, 2) * mine, 16), mine), :]

        gx = Exchange(lambda zz: heads_of(do_ref, zz), lambda zz: gh.at[zz], xs.at[0], xr.at[0], zn)
        dx = Exchange(lambda zz: dqh.at[zz], lambda zz: dq_in.at[zz], xs.at[1], xr.at[1], zn)
        kvx = Scatter(None, dkv_in, tuple(kb) + (None,), ks, kr, zn, give)
        share = [
            Share(ins[i], pairs[2 * i], pairs[2 * i + 1], pl_.at[i], ps.at[i], pr.at[i], split[i])
            for i in range(n_in)
        ]
        gq_share = Share(gq, gq, gq_other, None, ps.at[n_in], pr.at[n_in], False)
        own = lambda i: pairs[2 * i]
        other = lambda i: pairs[2 * i + 1]
        ACT, H2, OT, HN, H2B, OTB, HNB, GY, GB, GG, GU = range(n_in)

        def product(left, right, lo, row0, needs):
            def make(dst):
                for i in needs:
                    share[i].ready()
                nr, nc = dst.shape[3:]
                lefts2 = [
                    r[:, :, :, row0 : row0 + nr, :].reshape(zn * 4 * nr, all_rows)
                    for r in (own(left), other(left))
                ]
                step = 3 * WIDE

                def cols(i, _):
                    at = pl.multiple_of(i * step, WIDE)
                    t = jnp.dot(lefts2[0], right[0][:, pl.ds(lo + at, step)], preferred_element_type=f32)
                    t = t + jnp.dot(lefts2[1], right[1][:, pl.ds(lo + at, step)], preferred_element_type=f32)
                    dst[:, :, :, :, pl.ds(at, step)] = t.astype(b16).reshape(zn, 2, 2, nr, step)
                    return 0

                lax.fori_loop(0, nc // step, cols, 0)

            return make

        def both(i):
            return (own(i), other(i))

        def fold4(quarters):
            row = lax.rem(lax.broadcasted_iota(jnp.int32, quarters[0].shape, 0), 8)
            here = k == 0

            def put(a, b):
                n = a.shape[0]
                low = jnp.where(here, a, pltpu.roll(a, n - 4, 0))
                high = jnp.where(here, pltpu.roll(b, 4, 0), b)
                t = jnp.where(row < 4, low, high)
                return t.reshape(zn * 4, 8, t.shape[1])

            t = jnp.concatenate([put(*quarters[:2]), put(*quarters[2:])], axis=1)
            return t.astype(b16).reshape(zn, 2, 2, 16, t.shape[2])

        def rest_product(dst):
            step = 3 * WIDE
            for i in (H2B, OTB, GB, GG, GU):
                share[i].ready()
            columns = []
            for left, right, n in ((OTB, GB, width), (H2B, GG, ff), (H2B, GU, ff)):
                columns += [(left, right, c) for c in range(0, n, step)]
            per = rest_w // step

            def one(entry):
                if entry is None:
                    return jnp.zeros((own(H2B).shape[0], step), f32)
                left, right, c = entry
                return jnp.dot(own(left)[...], own(right)[:, c : c + step], preferred_element_type=f32) + jnp.dot(
                    other(left)[...], other(right)[:, c : c + step], preferred_element_type=f32
                )

            for c in range(per):
                quarters = []
                for q in range(4):
                    at = q * per + c
                    quarters.append(one(columns[at] if at < len(columns) else None))
                dst[:, :, :, :, c * step : (c + 1) * step] = fold4(quarters)

        def qkv_rest_product(dst):
            for i in (HNB,):
                share[i].ready()
            gq_share.ready()
            quarters = []
            for q in range(4):
                lo, hi = q * qkv_rest_w, min((q + 1) * qkv_rest_w, qkv_w)
                t = jnp.dot(own(HNB)[...], gq[:, lo:hi], preferred_element_type=f32) + jnp.dot(
                    other(HNB)[...], gq_other[:, lo:hi], preferred_element_type=f32
                )
                if hi - lo < qkv_rest_w:
                    t = jnp.concatenate([t, jnp.zeros((t.shape[0], qkv_rest_w - hi + lo), f32)], axis=1)
                quarters.append(t)
            dst[...] = fold4(quarters)

        gq_both = (gq, gq_other)
        makes = [product(ACT, both(GY), 0, ra * i, (ACT, GY)) for i in range(n_down)]
        ffn_parts = [(GG, 0, half_ff), (GG, half_ff, half_ff), (GU, 0, half_ff)]
        ffn_parts += [(GU, half_ff, half_ff // 2), (GU, half_ff + half_ff // 2, half_ff // 2)]
        makes += [product(H2, both(g), lo, 0, (H2, g)) for g, lo, _ in ffn_parts]
        makes += [product(OT, both(GB), 0, 0, (OT, GB)), rest_product]
        makes += [product(HN, gq_both, 0, 0, (HN,)), product(HN, gq_both, 2 * KV_LANES, 0, (HN,)), qkv_rest_product]
        targets = [outs[0].at[pl.ds(ra * i, ra), :] for i in range(n_down)]
        targets += [outs[1 if g == GG else 2].at[:, pl.ds(lo, n)] for g, lo, n in ffn_parts]
        targets += [outs[3], outs[4], outs[5].at[:, pl.ds(0, 2 * KV_LANES)], outs[5].at[:, pl.ds(2 * KV_LANES, q_rows)], outs[6]]
        items = []
        for i, (nr, nc) in enumerate(sizes):
            slot = held.at[ORDER.index(i) % ring, :, :, :, pl.ds(0, nr), pl.ds(0, nc)]
            items.append(
                Sum(makes[i], slot, bufs[3 * i : 3 * i + 3], targets[i], send.at[i], recv.at[i], zn)
            )
        load_o = pltpu.make_async_copy(oh_ref, oh, pl_.at[n_in])
        load_o.start()
        gx.start()
        for i in (ACT, GY, H2, GG, GU, OT, GB, H2B, OTB, HN, HNB):
            share[i].start()
        order = [items[i] for i in ORDER]
        at_qkv = ORDER.index(n_items - 3)
        n_back = BACK_SPAN
        stage_step(order, SUM_STAGES, 0)

        def attention_back(kvg, qh, qt, dot_, kt, delta, dq, dkv):
            load_kv = pltpu.make_async_copy(kvg_ref, kvg, loads.at[0])
            load_q = pltpu.make_async_copy(qh_ref, qh, loads.at[1])
            load_kv.start()
            load_q.start()
            dq[...] = jnp.zeros(dq.shape, f32)

            def clear(i, _):
                dkv[i] = jnp.zeros(dkv.shape[1:], f32)
                return 0

            lax.fori_loop(0, zn, clear, 0)
            def turn(j, block):
                flat = {b: turned(block(b)) for b in sorted({key_slot(g)[0] for g in groups})}
                for g in groups:
                    b, side = key_slot(g)
                    kt[j, g] = flat[b][side * HEAD_SIZE : (side + 1) * HEAD_SIZE]

            load_kv.wait()
            by_span(turn, kvg, cn, rows)
            stage_step(order, SUM_STAGES, 1)
            gx.arrived()
            load_o.wait()
            load_q.wait()
            for half_ in range(2):
                for zp in range(2):
                    p = pair_index(half_, zp)
                    for g in groups:
                        g_tile = pair_tile(gh, g, half_, zp)
                        o_tile = pair_tile(oh, g, half_, zp)
                        delta[g, p] = jnp.sum(g_tile * o_tile, axis=0, keepdims=True)
                        set_padded(qt, g, p, pair_tile(qh, g, half_, zp), key_slot(g)[1])
                        set_padded(dot_, g, p, g_tile, value_slot(g)[1])

            def step(t, _):
                p, j, zz, yy, late, edge = walk(t, y, cn)

                def run(masked):
                    seen = visible(p, j, y, w, cn, wn, rows) if masked else None
                    blocks = [key_block(kvg, zz, yy, late, rows, b) for b in range(KV_LANES // WIDE)]
                    sums = [None] * len(blocks)

                    def put(b, v):
                        sums[b] = v if sums[b] is None else sums[b] + v

                    for g in groups:
                        s = jnp.dot(blocks[key_slot(g)[0]], qt[g, p], preferred_element_type=f32)
                        if masked:
                            s = jnp.where(seen, s, NEG)
                        e = jnp.exp(s - lse_ref[g, p])
                        dp = jnp.dot(blocks[value_slot(g)[0]], dot_[g, p], preferred_element_type=f32)
                        ds = (e * (dp - delta[g, p])).astype(b16)
                        put(value_slot(g)[0], nt(e.astype(b16), dot_[g, p]))
                        put(key_slot(g)[0], nt(ds, qt[g, p]))
                        dq[g, p] += jnp.dot(kt[j, g], ds, preferred_element_type=f32)
                    for b, v in enumerate(sums):
                        dkv[zz, yy, :, :, pl.ds(late, rows), WIDE * b : WIDE * b + WIDE] += v.reshape(
                            2, 2, rows, WIDE
                        )

                pl.when(edge)(lambda: run(True))
                pl.when(jnp.logical_not(edge))(lambda: run(False))
                return 0

            attend = portions(step, STEPS, BACK_PARTS)
            for s in range(2, 2 + n_back):
                stage_step(order, SUM_STAGES, s, attend)
            attend(True)

            def pack(i, _):
                for yy in range(2):
                    for xx in range(2):
                        kb[0][i, yy, xx] = dkv[i, yy, xx, k].astype(b16)
                        give[i, yy, xx] = dkv[i, yy, xx, 1 - k].astype(b16)
                return 0

            lax.fori_loop(0, zn, pack, 0)
            kvx.stage(0)
            unpair(lambda g, p: dq[g, p] * scale, dqh)
            dx.start()

        stat = (HALF_GROUPS, 4, 1, PER * WIDE)
        tile = (HALF_GROUPS, 4, WIDE, PER * WIDE)
        pl.run_scoped(
            attention_back,
            pltpu.VMEM(kvg_ref.shape, b16),
            pltpu.VMEM(qh_ref.shape, b16),
            pltpu.VMEM(tile, b16),
            pltpu.VMEM(tile, b16),
            pltpu.VMEM((2 * cn, HALF_GROUPS, HEAD_SIZE, wn * rows), b16),
            pltpu.VMEM(stat, f32),
            pltpu.VMEM((HALF_GROUPS, 4, HEAD_SIZE, PER * WIDE), f32),
            pltpu.VMEM((zn, 2, 2, 2, tokens, KV_LANES), f32),
        )

        def rope_back():
            low_lanes = lax.broadcasted_iota(jnp.int32, (tokens, WIDE), 1) < HEAD_SIZE
            quarter = HEAD_SIZE // 2

            def back(t, kind):
                if kind == "still":
                    return t
                cos, low, high = tab[0], tab[1], tab[2]
                r = t * cos - pltpu.roll(t, WIDE - quarter, 1) * low - pltpu.roll(t, quarter, 1) * high
                return r if kind == "turn" else jnp.where(low_lanes, r, t)

            def heads_block(mb, at):
                n = max(0, min(WIDE, mine - at))
                parts = []
                if n:
                    parts.append(dq_in[2 * mb, at : at + n, :].astype(f32))
                if n < WIDE:
                    lo = at + n - mine
                    parts.append(dq_in[2 * mb + 1, lo : lo + WIDE - n, :].astype(f32))
                return parts[0] if len(parts) == 1 else jnp.concatenate(parts, axis=0)

            kinds = ["turn", "mixed", "still"]
            for mb in range(mbs):
                at = slice(mb * tokens, (mb + 1) * tokens)
                for hh in range(2):
                    for b in range(KV_LANES // WIDE):
                        t = dkv_in[2 * mb + hh, :, WIDE * b : WIDE * b + WIDE].astype(f32)
                        lo = hh * KV_LANES + WIDE * b
                        gq[at, lo : lo + WIDE] = back(t, kinds[b]).astype(b16)
                for b in range(q_rows // WIDE):
                    t = heads_block(mb, WIDE * b).T
                    lo = 2 * KV_LANES + WIDE * b
                    gq[at, lo : lo + WIDE] = back(t, "turn").astype(b16)

        def gains_and_input(w_s, r_s, order_s, x_s, gx_s, ghn, low):
            moves = [
                pltpu.make_async_copy(src, dst, loads.at[i])
                for i, (src, dst) in enumerate(
                    [(w_ref, w_s), (r_ref, r_s), (order_ref, order_s), (x_ref, x_s), (gx1_ref, gx_s)]
                )
            ]
            for c in moves:
                c.start()
            wa = w_s.shape[0]
            chips = [device(z, y, x, 1 - k), device(z, y, 1 - x, k), device(z, 1 - y, x, k)]
            steps = [remote(total, got.at[i], gs.at[i], gr.at[i], chips[i]) for i in range(3)]
            ends = [
                remote(total, got.at[2 + j], gs.at[2 + j], gr.at[2 + j], device(lax.rem(z + j, zn), y, x, k))
                for j in range(1, zn)
            ]

            def first():
                for c in moves:
                    c.wait()
                ghn[:, :wa] = nt(gq[...], w_s[...])
                ghn[:, wa:] = nt(gq[...], r_s[...])

            def second():
                xf, inv, grad = x_s[...].astype(f32), inv_ref[...], ghn[...]
                total[...] = jnp.zeros(total.shape, f32)
                total[0:1, :] = jnp.sum(grad * xf * inv, axis=0, keepdims=True)
                total[1:2, :] = gain2_ref[...]
                steps[0].start()
                weighted = grad * gain_ref[...]
                inner = jnp.mean(weighted * xf, axis=-1, keepdims=True)
                low[...] = (gx_s[...] + inv * weighted - xf * (inv * inv * inv) * inner).astype(b16)

            def add(i):
                steps[i].wait()
                total[...] = total[...] + got[i]
                for c in [steps[i + 1]] if i < 2 else ends:
                    c.start()

            def third():
                input_grad[...] = jnp.dot(low[...], order_s[...], preferred_element_type=f32).astype(b16)

            jobs = [first, second, lambda: (add(0), third()), lambda: add(1), lambda: add(2)]
            kv_stage = 1
            for s in range(2 + n_back, len(order) + 3):
                if s == at_qkv:
                    while kv_stage < 5:
                        kvx.stage(kv_stage)
                        kv_stage += 1
                    dx.arrived()
                    rope_back()
                    gq_share.start()
                    gq_share.ready()
                stage_step(order, SUM_STAGES, s)
                if kv_stage < 4:
                    kvx.stage(kv_stage)
                    kv_stage += 1
                if s >= at_qkv and jobs:
                    jobs.pop(0)()
            for job in jobs:
                job()
            for c in ends:
                c.wait()
            t = total[...]
            for j in range(1, zn):
                t = t + got[2 + j]
            total[...] = t

        pl.run_scoped(
            gains_and_input,
            pltpu.VMEM(w_ref.shape, b16),
            pltpu.VMEM(r_ref.shape, b16),
            pltpu.VMEM(order_ref.shape, b16),
            pltpu.VMEM(x_ref.shape, b16),
            pltpu.VMEM(gx1_ref.shape, f32),
            pltpu.VMEM(gx1_ref.shape, f32),
            pltpu.VMEM(x_ref.shape, b16),
        )
        dx.sent()
        gx.sent()
        gq_share.sent()
        for i in share:
            i.sent()

    block = (zn, mine, tokens)
    any_ = pl.BlockSpec(memory_space=pl.ANY)
    vmem = pl.BlockSpec(memory_space=pltpu.VMEM)
    dma = pltpu.SemaphoreType.DMA
    return pl.pallas_call(
        kernel,
        out_shape=[jax.ShapeDtypeStruct(s, f32) for s in outs_shape]
        + [jax.ShapeDtypeStruct((all_rows, width), b16), jax.ShapeDtypeStruct((8, width), f32)],
        in_specs=[any_, any_, any_, any_, vmem, vmem]
        + [any_] * n_in
        + [any_, any_, any_, vmem, vmem, any_, vmem, any_],
        out_specs=[vmem] * (n_out + 2),
        scratch_shapes=scratch
        + shares
        + [
            pltpu.VMEM((ring, zn, 2, 2, ra, max_cols), b16),
            pltpu.VMEM((all_rows, qkv_w), b16),
            pltpu.VMEM((all_rows, qkv_w), b16),
            pltpu.VMEM((zn, tokens, KV_LANES), b16),
            pltpu.VMEM(block, b16),
            pltpu.VMEM(block, b16),
            pltpu.VMEM((zn, 2, 2, tokens, KV_LANES), b16),
            pltpu.VMEM((2 + zn, 8, width), f32),
        ]
        + Scatter.scratch(zn, tokens, KV_LANES)[:4]
        + [
            dma((n_items, Sum.SEMS)),
            dma((n_items, Sum.SEMS)),
            dma((n_in + 1,)),
            dma((n_in + 1,)),
            dma((n_in + 1,)),
            dma((2, zn)),
            dma((2, zn)),
            dma((Scatter.SEMS,)),
            dma((Scatter.SEMS,)),
            dma((2 + zn,)),
            dma((2 + zn,)),
            dma((5,)),
        ],
        compiler_params=pltpu.CompilerParams(
            collective_id=collective_id, has_side_effects=True, vmem_limit_bytes=VMEM_LIMIT
        ),
    )(do, qh, kvg, oh, lse, tables, *ins_all, *last)


def ffn(o_t, x, gy, gain, order_t, out_a, gate_a, up_a, down, rest):
    f32, b16 = jnp.float32, jnp.bfloat16
    mbs, width, tokens = o_t.shape
    rows = mbs * tokens
    ff = gate_a.shape[1]
    wa = out_a.shape[0]
    wb = width - wa
    rb = wb * 16 // rest.shape[0]
    chunk = 4 * WIDE

    def kernel(o_ref, x_ref, gy_ref, gain_ref, order_hbm, out_hbm, gate_hbm, up_hbm, down_hbm, rest_hbm,
               y_ref, gx1_ref, gb_ref, gg_ref, gu_ref, act_ref, h2_ref, h2b_ref, op_ref, opb_ref, go_ref, gain_sum,
               order_s, out_s, gate_s, up_s, down_s, rest_s, wide, x1, h2, acc, gh, sems):
        loads = [
            pltpu.make_async_copy(src, dst, sems.at[i])
            for i, (src, dst) in enumerate(
                [(order_hbm, order_s), (rest_hbm, rest_s), (out_hbm, out_s), (gate_hbm, gate_s), (up_hbm, up_s), (down_hbm, down_s)]
            )
        ]
        for c in loads:
            c.start()
        loads[0].wait()
        for mb in range(mbs):
            at = slice(mb * tokens, (mb + 1) * tokens)
            t = jnp.dot(order_s[...], o_ref[mb], preferred_element_type=f32)
            op_ref[:, at] = t[:wa].astype(b16)
            opb_ref[:, at] = t[wa:].astype(b16)
            h2[at, :] = transposed_rows(t).astype(b16)
        loads[1].wait()
        unfold_rows(rest_s, wide, rb)
        loads[2].wait()
        x1[...] = (
            x_ref[...].astype(f32)
            + jnp.dot(h2[:, :wa], out_s[...], preferred_element_type=f32)
            + jnp.dot(h2[:, wa:], wide[:, :width], preferred_element_type=f32)
        )
        u = x1[...]
        inv = lax.rsqrt(jnp.mean(u * u, axis=-1, keepdims=True) + EPSILON)
        hidden = u * inv * gain_ref[...]
        h2[...] = hidden.astype(b16)
        h2_ref[...] = transposed(hidden[:, :wa]).astype(b16)
        h2b_ref[...] = transposed(hidden[:, wa:]).astype(b16)
        acc[...] = jnp.zeros(acc.shape, f32)
        gh[...] = jnp.zeros(gh.shape, f32)
        for c in loads[3:]:
            c.wait()

        def one(i, _):
            at = pl.multiple_of(i * chunk, WIDE)
            cols = pl.ds(at, chunk)
            gcols, ucols = pl.ds(width + at, chunk), pl.ds(width + ff + at, chunk)
            ha, hb = h2[:, :wa], h2[:, wa:]
            gate = jnp.dot(ha, gate_s[:, cols], preferred_element_type=f32) + jnp.dot(
                hb, wide[:, gcols], preferred_element_type=f32
            )
            up = jnp.dot(ha, up_s[:, cols], preferred_element_type=f32) + jnp.dot(
                hb, wide[:, ucols], preferred_element_type=f32
            )
            ga = nt(gy_ref[...], down_s[cols, :])
            sig = jax.nn.sigmoid(gate)
            silu = gate * sig
            act = silu * up
            g_gate = (ga * up * sig * (1.0 + gate * (1.0 - sig))).astype(b16)
            g_up = (ga * silu).astype(b16)
            gg_ref[:, cols] = g_gate
            gu_ref[:, cols] = g_up
            act_ref[cols, :] = transposed(act).astype(b16)
            acc[...] += jnp.dot(act.astype(b16), down_s[cols, :], preferred_element_type=f32)
            gh[:, :wa] += nt(g_gate, gate_s[:, cols]) + nt(g_up, up_s[:, cols])
            gh[:, wa:] += nt(g_gate, wide[:, gcols]) + nt(g_up, wide[:, ucols])
            return 0

        lax.fori_loop(0, ff // chunk, one, 0)
        y = (x1[...] + acc[...]).astype(b16)
        y_ref[...] = jnp.dot(y, order_s[...], preferred_element_type=f32).astype(b16)
        u = x1[...]
        inv = lax.rsqrt(jnp.mean(u * u, axis=-1, keepdims=True) + EPSILON)
        grad = gh[...]
        gain_sum[...] = jnp.sum(grad * u * inv, axis=0, keepdims=True)
        weighted = grad * gain_ref[...]
        inner = jnp.mean(weighted * u, axis=-1, keepdims=True)
        gx1 = inv * weighted - u * (inv * inv * inv) * inner + gy_ref[...].astype(f32)
        gx1_ref[...] = gx1
        gb = gx1.astype(b16)
        gb_ref[...] = jnp.dot(gb, order_s[...], preferred_element_type=f32).astype(b16)
        h2[:, :wa] = nt(gb, out_s[...]).astype(b16)
        h2[:, wa:] = nt(gb, wide[:, :width]).astype(b16)
        go = jnp.dot(h2[...], order_s[...], preferred_element_type=f32)
        for mb in range(mbs):
            go_ref[mb] = transposed(go[mb * tokens : (mb + 1) * tokens]).astype(b16)

    def transposed_rows(t):
        return jnp.concatenate([t[i : i + WIDE].T for i in range(0, t.shape[0], WIDE)], axis=1)

    any_ = pl.BlockSpec(memory_space=pl.ANY)
    vmem = pl.BlockSpec(memory_space=pltpu.VMEM)
    sds = jax.ShapeDtypeStruct
    return pl.pallas_call(
        kernel,
        out_shape=[
            sds((rows, width), b16),
            sds((rows, width), f32),
            sds((rows, width), b16),
            sds((rows, ff), b16),
            sds((rows, ff), b16),
            sds((ff, rows), b16),
            sds((wa, rows), b16),
            sds((wb, rows), b16),
            sds((wa, rows), b16),
            sds((wb, rows), b16),
            sds(o_t.shape, b16),
            sds((1, width), f32),
        ],
        in_specs=[vmem] * 4 + [any_] * 6,
        out_specs=[vmem] * 12,
        scratch_shapes=[
            pltpu.VMEM(order_t.shape, b16),
            pltpu.VMEM(out_a.shape, b16),
            pltpu.VMEM(gate_a.shape, b16),
            pltpu.VMEM(up_a.shape, b16),
            pltpu.VMEM(down.shape, b16),
            pltpu.VMEM(rest.shape, b16),
            pltpu.VMEM((wb, 16 // rb * rest.shape[1]), b16),
            pltpu.VMEM((rows, width), f32),
            pltpu.VMEM((rows, width), b16),
            pltpu.VMEM((rows, width), f32),
            pltpu.VMEM((rows, width), f32),
            pltpu.SemaphoreType.DMA((6,)),
        ],
        compiler_params=pltpu.CompilerParams(vmem_limit_bytes=VMEM_LIMIT),
    )(o_t, x, gy, gain, order_t, out_a, gate_a, up_a, down, rest)


def lane_tables(positions):
    quarter = HEAD_SIZE // 2
    frequency = 10000.0 ** (-2.0 * jnp.arange(quarter, dtype=jnp.float32) / HEAD_SIZE)
    angles = positions.astype(jnp.float32)[:, None] * frequency[None, :]
    cos, sin = jnp.cos(angles), jnp.sin(angles)
    none = jnp.zeros_like(sin)
    full = lambda a, b: jnp.concatenate([a, b, a, b], axis=1)
    return jnp.stack([full(cos, cos), full(-sin, none), full(none, sin)])


def fast_device(
    inputs,
    attn_gain,
    query_weight,
    key_matrix,
    value_matrix,
    out_weight,
    ffn_gain,
    gate_weight,
    up_weight,
    down_weight,
    cotangent,
):
    f32, b16 = jnp.float32, jnp.bfloat16
    cn, wn = lax.axis_size("ctx"), lax.axis_size("ws")
    dn = cn * wn
    zn = cn // 2
    mbs, tokens, width = inputs.shape
    own = query_weight.shape[0]
    ra = own // 16 * 16
    rb = own - ra
    q_width = query_weight.shape[1]
    hid = KEY_VALUE_HEADS * HEAD_SIZE
    ff = gate_weight.shape[1]
    rows = mbs * tokens
    wa = dn * ra

    new = jnp.arange(width)
    old = jnp.where(
        new < wa, own * (new // ra) + new % ra, own * ((new - wa) // rb) + ra + (new - wa) % rb
    )
    order = (jnp.arange(width)[:, None] == old[None, :]).astype(b16)

    def to_order(t):
        return jnp.dot(t, order, preferred_element_type=f32).astype(t.dtype)

    def from_order(t):
        return lax.dot_general(t, order, NT, preferred_element_type=f32).astype(t.dtype)

    fold = 16 // rb

    def folded(t):
        return t.reshape(t.shape[0], fold, -1).transpose(1, 0, 2).reshape(16, -1)

    qkv_w = q_width + 2 * hid
    pad1 = -qkv_w % (fold * WIDE)
    rest_w = width + 2 * ff
    pad2 = -rest_w % (fold * WIDE)
    moved = to_order(
        jnp.concatenate(
            [inputs.reshape(rows, width), cotangent.reshape(rows, width), out_weight, down_weight]
        )
    )
    x_low, gy_low = moved[:rows], moved[rows : 2 * rows]
    out_p, down_p = moved[2 * rows : 2 * rows + own], moved[2 * rows + own :]
    half_hid = hid // 2
    qkv = jnp.concatenate(
        [
            key_matrix[:, :half_hid],
            value_matrix[:, :half_hid],
            key_matrix[:, half_hid:],
            value_matrix[:, half_hid:],
            query_weight,
        ],
        axis=1,
    )
    gains = jnp.stack([attn_gain, ffn_gain])
    gains = jnp.pad(gains, ((0, rb - 2), (0, pad1 - own)))
    b1 = folded(jnp.concatenate([qkv[ra:], gains], axis=1))
    b2 = folded(
        jnp.pad(
            jnp.concatenate([out_p[ra:], gate_weight[ra:], up_weight[ra:]], axis=1), ((0, 0), (0, pad2))
        )
    )
    flat = lambda t: t.reshape(-1, t.shape[-1])
    c, w = lax.axis_index("ctx"), lax.axis_index("ws")
    tables = lane_tables(query_places(c, w, tokens, cn, wn))
    (o_t, qh, kvg, oh, lse, qkv_a, qkv_b, hn_t, hn_bt, inv1, gains, out_a, gate_a, up_a, down_a, b2g) = gather_attend(
        x_low,
        tables,
        qkv,
        b1,
        [out_p, gate_weight, up_weight, down_p, b2],
        [ra, ra, ra, down_p.shape[0], 16],
        [(1, 1), (1, 2), (1, 2), (2, 1), (1, 1)],
        2,
    )
    qkv_a, out_a, gate_a, up_a, down_w = map(flat, (qkv_a, out_a, gate_a, up_a, down_a))
    gain1, gain2 = gains[:1], gains[1:]
    order_t = order.T
    out, gx1, gb_plain, g_gate, g_up, act_t, h2_t, h2_bt, o_pt, o_pbt, go_t, gain2_sum = ffn(
        o_t, x_low, gy_low, gain2, order_t, out_a, gate_a, up_a, down_w, flat(b2g)
    )
    gy_plain = cotangent.reshape(rows, width)
    left = lambda t: t.reshape(zn, 2, 2, 2, -1, rows)
    r_down, r_gate, r_up, r_out, r_b2, r_qkv, r_b1, input_grad, gain_sums = scatter_attend(
        go_t,
        qh,
        kvg,
        oh,
        lse,
        tables,
        [left(act_t), left(h2_t), left(o_pt), left(hn_t)],
        [h2_bt, o_pbt, hn_bt],
        [gy_plain, gb_plain, g_gate, g_up],
        ((rest_w + pad2) // fold, (qkv_w + pad1) // fold),
        [qkv_a, qkv_b, x_low, inv1, gain1, gx1, gain2_sum, order_t],
        3,
    )
    device_at = c * wn + w

    def own_gain(t):
        first = lax.dynamic_slice(t, (device_at * ra,), (ra,))
        return jnp.concatenate([first, lax.dynamic_slice(t, (wa + device_at * rb,), (rb,))])

    def own_rows(t):
        return t.reshape(fold, rb, -1).transpose(1, 0, 2).reshape(rb, -1)

    e1, e2 = own_rows(r_b1), own_rows(r_b2)
    whole = lambda a, b: jnp.concatenate([a, b], axis=0)
    d_qkv = whole(r_qkv, e1[:, :qkv_w])
    return (
        out.reshape(inputs.shape),
        input_grad.reshape(inputs.shape),
        own_gain(gain_sums[0]),
        d_qkv[:, 2 * hid :],
        jnp.concatenate([d_qkv[:, :half_hid], d_qkv[:, hid : hid + half_hid]], axis=1),
        jnp.concatenate([d_qkv[:, half_hid:hid], d_qkv[:, hid + half_hid : 2 * hid]], axis=1),
        whole(r_out, e2[:, :width]),
        own_gain(gain_sums[1]),
        whole(r_gate, e2[:, width : width + ff]),
        whole(r_up, e2[:, width + ff : width + 2 * ff]),
        r_down,
    )


def solution(mesh):
    in_specs = (
        P(None, ("ctx", "ws"), None),
        P(("ctx", "ws")),
        P(("ctx", "ws"), None),
        P(("ctx", "ws"), None),
        P(("ctx", "ws"), None),
        P(("ctx", "ws"), None),
        P(("ctx", "ws")),
        P(("ctx", "ws"), None),
        P(("ctx", "ws"), None),
        P(("ctx", "ws"), None),
        P(None, ("ctx", "ws"), None),
    )
    out_specs = (
        P(None, ("ctx", "ws"), None),
        P(None, ("ctx", "ws"), None),
        P(("ctx", "ws")),
        P(("ctx", "ws"), None),
        P(("ctx", "ws"), None),
        P(("ctx", "ws"), None),
        P(("ctx", "ws"), None),
        P(("ctx", "ws")),
        P(("ctx", "ws"), None),
        P(("ctx", "ws"), None),
        P(("ctx", "ws"), None),
    )
    body = fast_device if fits_fast(mesh) else per_device
    return jax.shard_map(
        body, mesh=mesh, in_specs=in_specs, out_specs=out_specs, check_vma=False
    )
```

```python
import jax
import jax.numpy as jnp
from jax import lax
from jax.experimental import pallas as pl
from jax.experimental.pallas import tpu as pltpu
from jax.sharding import PartitionSpec as P
import functools

QUERY_HEADS = 18
KEY_VALUE_HEADS = 6
HEAD_SIZE = 64


EPSILON = 1e-05
MASKED_SCORE = -1e30


def shifted(block, axis, distance):
    devices = range(lax.axis_size(axis))
    route = [((i - distance) % len(devices), i) for i in devices]
    return lax.ppermute(block, axis, route)


def as_sent(x):

    def short(part):
        return part.astype(jnp.bfloat16) if part.dtype == jnp.float32 else part

    return jax.tree.map(short, x)


def matrix_multiply(left, right):
    return jnp.dot(left, right, preferred_element_type=jnp.float32)


def outer_sum(left, right):
    return jnp.einsum("ri,rj->ij", left, right, preferred_element_type=jnp.float32)


def back_product(gradient, weight):
    return jnp.einsum("rj,ij->ri", gradient, weight, preferred_element_type=jnp.float32)


def normalize(layer_rows, gain_vector):
    inverse = lax.rsqrt(jnp.mean(layer_rows * layer_rows, axis=-1, keepdims=True) + EPSILON)
    return (layer_rows * inverse * gain_vector, inverse)


def normalize_back(layer_rows, inverse, gain_vector, gradient):
    weighted = gradient * gain_vector
    inner_mean = jnp.mean(weighted * layer_rows, axis=-1, keepdims=True)
    row_grad = inverse * weighted - layer_rows * (inverse * inverse * inverse) * inner_mean
    gain_grad = jnp.sum(gradient * layer_rows * inverse, axis=0)
    return (row_grad, gain_grad)


def rotary_tables(token_positions):
    quarter = HEAD_SIZE // 2
    frequency = 10000.0 ** (-2.0 * jnp.arange(quarter, dtype=jnp.float32) / HEAD_SIZE)
    angles = token_positions.astype(jnp.float32)[:, None] * frequency[None, :]
    return (jnp.cos(angles)[:, None, :], jnp.sin(angles)[:, None, :])


def rotate(heads, cosine_table, sine_table):
    quarter = HEAD_SIZE // 2
    first_half = heads[..., :quarter]
    second_half = heads[..., quarter:]
    return jnp.concatenate(
        [
            first_half * cosine_table - second_half * sine_table,
            second_half * cosine_table + first_half * sine_table,
        ],
        axis=-1,
    )


def rotate_back(heads, cosine_table, sine_table):
    quarter = HEAD_SIZE // 2
    first_half = heads[..., :quarter]
    second_half = heads[..., quarter:]
    return jnp.concatenate(
        [
            first_half * cosine_table + second_half * sine_table,
            second_half * cosine_table - first_half * sine_table,
        ],
        axis=-1,
    )


def query_places(own_ctx, own_member, count_of_rows, ctx_count, device_count):
    rows_per_half = count_of_rows // 2
    local_index = jnp.arange(count_of_rows, dtype=jnp.int32)
    span_index = jnp.where(local_index < rows_per_half, own_ctx, 2 * ctx_count - 1 - own_ctx)
    return (
        span_index * (device_count * rows_per_half)
        + own_member * rows_per_half
        + local_index % rows_per_half
    )


def block_places(source_ctx, count_of_rows, ctx_count, device_count):
    rows_per_half = count_of_rows // 2
    member_index = jnp.arange(device_count, dtype=jnp.int32)[:, None, None]
    half_index = jnp.arange(2, dtype=jnp.int32)[None, :, None]
    inner_index = jnp.arange(rows_per_half, dtype=jnp.int32)[None, None, :]
    span_index = jnp.where(half_index == 0, source_ctx, 2 * ctx_count - 1 - source_ctx)
    return (
        span_index * (device_count * rows_per_half) + member_index * rows_per_half + inner_index
    ).reshape(-1)


def split_block(block_of_keys):
    hidden_width = KEY_VALUE_HEADS * HEAD_SIZE
    device_count, _, rows_per_half, _ = block_of_keys.shape
    rows_of_keys = block_of_keys[..., :hidden_width].reshape(
        device_count, 2, rows_per_half, KEY_VALUE_HEADS, HEAD_SIZE
    )
    rows_of_values = block_of_keys[..., hidden_width:].reshape(
        device_count, 2, rows_per_half, KEY_VALUE_HEADS, HEAD_SIZE
    )
    return (rows_of_keys, rows_of_values)


def attend(query_rows, rows_of_keys, rows_of_values, causal_visible):
    scores = jnp.einsum(
        "rgjd,kgd->grjk", query_rows, rows_of_keys, preferred_element_type=jnp.float32
    ) * HEAD_SIZE ** (-0.5)
    if causal_visible is not None:
        scores = jnp.where(causal_visible[None, :, None, :], scores, MASKED_SCORE)
    row_max = jnp.max(scores, axis=-1)
    exponentials = jnp.exp(scores - row_max[..., None])
    row_total = jnp.sum(exponentials, axis=-1)
    mixture = jnp.einsum(
        "grjk,kgd->rgjd",
        exponentials.astype(jnp.bfloat16),
        rows_of_values,
        preferred_element_type=jnp.float32,
    )
    return (jnp.transpose(row_max, (1, 0, 2)), jnp.transpose(row_total, (1, 0, 2)), mixture)


def empty_part(count_of_rows):
    queries_per_group = QUERY_HEADS // KEY_VALUE_HEADS
    return (
        jnp.full((count_of_rows, KEY_VALUE_HEADS, queries_per_group), MASKED_SCORE, jnp.float32),
        jnp.zeros((count_of_rows, KEY_VALUE_HEADS, queries_per_group), jnp.float32),
        jnp.zeros((count_of_rows, KEY_VALUE_HEADS, queries_per_group, HEAD_SIZE), jnp.float32),
    )


def combine(carried, incoming):
    carried_max, carried_total, carried_mix = carried
    incoming_max, incoming_total, incoming_mix = incoming
    new_max = jnp.maximum(carried_max, incoming_max)
    carried_scale = jnp.exp(carried_max - new_max)
    incoming_scale = jnp.exp(incoming_max - new_max)
    return (
        new_max,
        carried_total * carried_scale + incoming_total * incoming_scale,
        carried_mix * carried_scale[..., None] + incoming_mix * incoming_scale[..., None],
    )


def forward_block(carried, block_of_keys, source_ctx, own_ctx, query_rows, own_places, ctx_count):
    rows_of_keys, rows_of_values = split_block(block_of_keys)
    device_count, _, rows_per_half, _ = block_of_keys.shape

    def forward_earlier():
        return attend(
            query_rows,
            rows_of_keys[:, 0].reshape(-1, KEY_VALUE_HEADS, HEAD_SIZE),
            rows_of_values[:, 0].reshape(-1, KEY_VALUE_HEADS, HEAD_SIZE),
            None,
        )

    def forward_later():
        late_part = attend(
            query_rows[rows_per_half:],
            rows_of_keys.reshape(-1, KEY_VALUE_HEADS, HEAD_SIZE),
            rows_of_values.reshape(-1, KEY_VALUE_HEADS, HEAD_SIZE),
            None,
        )
        early_part = empty_part(rows_per_half)
        return tuple(
            (
                jnp.concatenate([early_piece, late_piece], axis=0)
                for early_piece, late_piece in zip(early_part, late_part)
            )
        )

    def forward_diagonal():
        key_places = block_places(source_ctx, 2 * rows_per_half, ctx_count, device_count)
        causal_visible = own_places[:, None] >= key_places[None, :]
        return attend(
            query_rows,
            rows_of_keys.reshape(-1, KEY_VALUE_HEADS, HEAD_SIZE),
            rows_of_values.reshape(-1, KEY_VALUE_HEADS, HEAD_SIZE),
            causal_visible,
        )

    branch_index = jnp.where(source_ctx == own_ctx, 2, jnp.where(source_ctx > own_ctx, 1, 0))
    return combine(
        carried, lax.switch(branch_index, [forward_earlier, forward_later, forward_diagonal])
    )


def attend_back(
    query_rows, attended_grad, log_total, delta_rows, rows_of_keys, rows_of_values, causal_visible
):
    scores = jnp.einsum(
        "rgjd,kgd->grjk", query_rows, rows_of_keys, preferred_element_type=jnp.float32
    ) * HEAD_SIZE ** (-0.5)
    if causal_visible is not None:
        scores = jnp.where(causal_visible[None, :, None, :], scores, MASKED_SCORE)
    probabilities = jnp.exp(scores - jnp.transpose(log_total, (1, 0, 2))[..., None])
    prob_grad = jnp.einsum(
        "rgjd,kgd->grjk", attended_grad, rows_of_values, preferred_element_type=jnp.float32
    )
    score_grad = (
        probabilities * (prob_grad - jnp.transpose(delta_rows, (1, 0, 2))[..., None])
    ).astype(jnp.bfloat16)
    query_part = jnp.einsum(
        "grjk,kgd->rgjd", score_grad, rows_of_keys, preferred_element_type=jnp.float32
    ) * HEAD_SIZE ** (-0.5)
    key_part = jnp.einsum(
        "grjk,rgjd->kgd", score_grad, query_rows, preferred_element_type=jnp.float32
    ) * HEAD_SIZE ** (-0.5)
    value_part = jnp.einsum(
        "grjk,rgjd->kgd",
        probabilities.astype(jnp.bfloat16),
        attended_grad,
        preferred_element_type=jnp.float32,
    )
    return (query_part, key_part, value_part)


def backward_block(
    block_of_keys,
    source_ctx,
    own_ctx,
    query_rows,
    attended_grad,
    log_total,
    delta_rows,
    own_places,
    ctx_count,
):
    rows_of_keys, rows_of_values = split_block(block_of_keys)
    device_count, _, rows_per_half, _ = block_of_keys.shape
    hidden_width = KEY_VALUE_HEADS * HEAD_SIZE

    def backward_earlier():
        query_part, key_part, value_part = attend_back(
            query_rows,
            attended_grad,
            log_total,
            delta_rows,
            rows_of_keys[:, 0].reshape(-1, KEY_VALUE_HEADS, HEAD_SIZE),
            rows_of_values[:, 0].reshape(-1, KEY_VALUE_HEADS, HEAD_SIZE),
            None,
        )
        early_grad = jnp.concatenate(
            [
                key_part.reshape(device_count, 1, rows_per_half, hidden_width),
                value_part.reshape(device_count, 1, rows_per_half, hidden_width),
            ],
            axis=-1,
        )
        return (query_part, jnp.concatenate([early_grad, jnp.zeros_like(early_grad)], axis=1))

    def backward_later():
        query_part, key_part, value_part = attend_back(
            query_rows[rows_per_half:],
            attended_grad[rows_per_half:],
            log_total[rows_per_half:],
            delta_rows[rows_per_half:],
            rows_of_keys.reshape(-1, KEY_VALUE_HEADS, HEAD_SIZE),
            rows_of_values.reshape(-1, KEY_VALUE_HEADS, HEAD_SIZE),
            None,
        )
        query_part = jnp.concatenate([jnp.zeros_like(query_part), query_part], axis=0)
        return (
            query_part,
            jnp.concatenate(
                [
                    key_part.reshape(device_count, 2, rows_per_half, hidden_width),
                    value_part.reshape(device_count, 2, rows_per_half, hidden_width),
                ],
                axis=-1,
            ),
        )

    def backward_diagonal():
        key_places = block_places(source_ctx, 2 * rows_per_half, ctx_count, device_count)
        causal_visible = own_places[:, None] >= key_places[None, :]
        query_part, key_part, value_part = attend_back(
            query_rows,
            attended_grad,
            log_total,
            delta_rows,
            rows_of_keys.reshape(-1, KEY_VALUE_HEADS, HEAD_SIZE),
            rows_of_values.reshape(-1, KEY_VALUE_HEADS, HEAD_SIZE),
            causal_visible,
        )
        return (
            query_part,
            jnp.concatenate(
                [
                    key_part.reshape(device_count, 2, rows_per_half, hidden_width),
                    value_part.reshape(device_count, 2, rows_per_half, hidden_width),
                ],
                axis=-1,
            ),
        )

    branch_index = jnp.where(source_ctx == own_ctx, 2, jnp.where(source_ctx > own_ctx, 1, 0))
    return lax.switch(branch_index, [backward_earlier, backward_later, backward_diagonal])


def per_device(
    inputs,
    attn_gain,
    query_weight,
    key_matrix,
    value_matrix,
    out_weight,
    ffn_gain,
    gate_weight,
    up_weight,
    down_weight,
    cotangent,
):
    ctx_count = lax.axis_size("ctx")
    device_count = lax.axis_size("ws")
    own_ctx = lax.axis_index("ctx")
    own_member = lax.axis_index("ws")
    micro_count, count_of_rows, _ = inputs.shape
    rows_per_half = count_of_rows // 2
    queries_per_group = QUERY_HEADS // KEY_VALUE_HEADS
    hidden_width = KEY_VALUE_HEADS * HEAD_SIZE
    own_places = query_places(own_ctx, own_member, count_of_rows, ctx_count, device_count)
    cosine_table, sine_table = rotary_tables(own_places)
    grad_sums = None
    layer_outs = []
    input_grads = []
    for micro_batch in range(micro_count):
        gathered = (
            lax.all_gather(attn_gain, ("ctx", "ws"), axis=0, tiled=True),
            lax.all_gather(query_weight, ("ctx", "ws"), axis=0, tiled=True),
            lax.all_gather(key_matrix, ("ctx", "ws"), axis=0, tiled=True),
            lax.all_gather(value_matrix, ("ctx", "ws"), axis=0, tiled=True),
            lax.all_gather(out_weight, ("ctx", "ws"), axis=0, tiled=True),
            lax.all_gather(ffn_gain, ("ctx", "ws"), axis=0, tiled=True),
            lax.all_gather(gate_weight, ("ctx", "ws"), axis=0, tiled=True),
            lax.all_gather(up_weight, ("ctx", "ws"), axis=0, tiled=True),
            lax.all_gather(down_weight, ("ctx", "ws"), axis=0, tiled=True),
        )
        (
            full_attn_gain,
            full_query,
            complete_key,
            full_value,
            full_out,
            full_ffn_gain,
            full_gate,
            full_up,
            full_down,
        ) = gathered
        first_gain = full_attn_gain.astype(jnp.float32)
        second_gain = full_ffn_gain.astype(jnp.float32)
        layer_rows = inputs[micro_batch].astype(jnp.float32)
        normalized_rows, first_inverse = normalize(layer_rows, first_gain)
        normalized_reduced = normalized_rows.astype(jnp.bfloat16)
        query_rows = rotate(
            matrix_multiply(normalized_reduced, full_query).reshape(
                count_of_rows, QUERY_HEADS, HEAD_SIZE
            ),
            cosine_table,
            sine_table,
        )
        query_rows = query_rows.astype(jnp.bfloat16).reshape(
            count_of_rows, KEY_VALUE_HEADS, queries_per_group, HEAD_SIZE
        )
        rows_of_keys = rotate(
            matrix_multiply(normalized_reduced, complete_key).reshape(
                count_of_rows, KEY_VALUE_HEADS, HEAD_SIZE
            ),
            cosine_table,
            sine_table,
        ).astype(jnp.bfloat16)
        rows_of_values = matrix_multiply(normalized_reduced, full_value).astype(jnp.bfloat16)
        local_block = jnp.concatenate(
            [rows_of_keys.reshape(count_of_rows, hidden_width), rows_of_values], axis=-1
        )
        group_block = lax.all_gather(local_block, "ws", axis=0, tiled=True).reshape(
            device_count, 2, rows_per_half, 2 * hidden_width
        )

        def fold_step(carried, shard_piece):

            def visit_block(state_now, block_entry):
                block_of_keys, source_ctx = block_entry
                return (
                    forward_block(
                        state_now,
                        block_of_keys,
                        source_ctx,
                        own_ctx,
                        query_rows,
                        own_places,
                        ctx_count,
                    ),
                    None,
                )

            source_list = jnp.arange(shard_piece.shape[0], dtype=jnp.int32)
            result_state, _ = lax.scan(visit_block, carried, (shard_piece, source_list))
            return result_state

        row_max, row_total, mixture = fold_step(
            empty_part(count_of_rows), lax.all_gather(group_block[None], "ctx", axis=0, tiled=True)
        )
        attended = mixture / row_total[..., None]
        log_total = row_max + jnp.log(row_total)
        attended_low = attended.astype(jnp.bfloat16).reshape(count_of_rows, QUERY_HEADS * HEAD_SIZE)
        middle = layer_rows + matrix_multiply(attended_low, full_out)
        hidden, second_inverse = normalize(middle, second_gain)
        hidden_low = hidden.astype(jnp.bfloat16)
        gate_rows = matrix_multiply(hidden_low, full_gate)
        up_rows = matrix_multiply(hidden_low, full_up)
        sigmoid_gate = jax.nn.sigmoid(gate_rows)
        silu_gate = gate_rows * sigmoid_gate
        activated = (silu_gate * up_rows).astype(jnp.bfloat16)
        layer_outs.append((middle + matrix_multiply(activated, full_down)).astype(jnp.bfloat16))
        upstream_low = cotangent[micro_batch]
        upstream = upstream_low.astype(jnp.float32)
        down_sum = outer_sum(activated, upstream_low)
        act_grad = back_product(upstream_low, full_down)
        gate_low = (
            act_grad * up_rows * sigmoid_gate * (1.0 + gate_rows * (1.0 - sigmoid_gate))
        ).astype(jnp.bfloat16)
        up_low = (act_grad * silu_gate).astype(jnp.bfloat16)
        gate_sum = outer_sum(hidden_low, gate_low)
        up_sum = outer_sum(hidden_low, up_low)
        hidden_grad = back_product(gate_low, full_gate) + back_product(up_low, full_up)
        middle_part, ffn_gain_sum = normalize_back(middle, second_inverse, second_gain, hidden_grad)
        middle_grad = middle_part + upstream
        branch_low = middle_grad.astype(jnp.bfloat16)
        out_sum = outer_sum(attended_low, branch_low)
        attended_grad = (
            back_product(branch_low, full_out)
            .reshape(count_of_rows, KEY_VALUE_HEADS, queries_per_group, HEAD_SIZE)
            .astype(jnp.bfloat16)
        )
        delta_rows = jnp.sum(attended_grad.astype(jnp.float32) * attended, axis=-1)

        def cycle_step(turn_index, carried):
            block_of_keys, block_grad, query_total = carried
            source_ctx = (own_ctx - turn_index) % ctx_count
            query_part, block_part = backward_block(
                block_of_keys,
                source_ctx,
                own_ctx,
                query_rows,
                attended_grad,
                log_total,
                delta_rows,
                own_places,
                ctx_count,
            )
            block_grad = block_grad + block_part
            next_block = shifted(block_of_keys, "ctx", 1)
            next_grad = shifted(as_sent(block_grad), "ctx", 1).astype(block_grad.dtype)
            return (next_block, next_grad, query_total + query_part)

        cycle_start = (
            group_block,
            jnp.zeros(group_block.shape, jnp.float32),
            jnp.zeros((count_of_rows, KEY_VALUE_HEADS, queries_per_group, HEAD_SIZE), jnp.float32),
        )
        _, block_grad, query_total = lax.fori_loop(0, ctx_count, cycle_step, cycle_start)
        local_gradient = (
            lax.psum_scatter(block_grad.astype(jnp.bfloat16), "ws", scatter_dimension=0, tiled=True)
            .astype(jnp.float32)
            .reshape(count_of_rows, 2 * hidden_width)
        )
        key_low = rotate_back(
            local_gradient[:, :hidden_width].reshape(count_of_rows, KEY_VALUE_HEADS, HEAD_SIZE),
            cosine_table,
            sine_table,
        )
        key_low = key_low.astype(jnp.bfloat16).reshape(count_of_rows, hidden_width)
        value_low = local_gradient[:, hidden_width:].astype(jnp.bfloat16)
        query_low = rotate_back(
            query_total.reshape(count_of_rows, QUERY_HEADS, HEAD_SIZE), cosine_table, sine_table
        )
        query_low = query_low.astype(jnp.bfloat16).reshape(count_of_rows, QUERY_HEADS * HEAD_SIZE)
        query_sum = outer_sum(normalized_reduced, query_low)
        key_sum = outer_sum(normalized_reduced, key_low)
        value_sum = outer_sum(normalized_reduced, value_low)
        normed_grad = (
            back_product(query_low, full_query)
            + back_product(key_low, complete_key)
            + back_product(value_low, full_value)
        )
        input_part, attn_gain_sum = normalize_back(
            layer_rows, first_inverse, first_gain, normed_grad
        )
        input_grads.append((middle_grad + input_part).astype(jnp.bfloat16))
        batch_terms = (
            attn_gain_sum,
            query_sum,
            key_sum,
            value_sum,
            out_sum,
            ffn_gain_sum,
            gate_sum,
            up_sum,
            down_sum,
        )
        if grad_sums is None:
            grad_sums = batch_terms
        else:
            grad_sums = tuple(
                (
                    earlier_sum + batch_term
                    for earlier_sum, batch_term in zip(grad_sums, batch_terms)
                )
            )
    owned_grads = (
        lax.psum_scatter(grad_sums[0], ("ctx", "ws"), scatter_dimension=0, tiled=True),
        lax.psum_scatter(grad_sums[1], ("ctx", "ws"), scatter_dimension=0, tiled=True),
        lax.psum_scatter(grad_sums[2], ("ctx", "ws"), scatter_dimension=0, tiled=True),
        lax.psum_scatter(grad_sums[3], ("ctx", "ws"), scatter_dimension=0, tiled=True),
        lax.psum_scatter(grad_sums[4], ("ctx", "ws"), scatter_dimension=0, tiled=True),
        lax.psum_scatter(grad_sums[5], ("ctx", "ws"), scatter_dimension=0, tiled=True),
        lax.psum_scatter(grad_sums[6], ("ctx", "ws"), scatter_dimension=0, tiled=True),
        lax.psum_scatter(grad_sums[7], ("ctx", "ws"), scatter_dimension=0, tiled=True),
        lax.psum_scatter(grad_sums[8], ("ctx", "ws"), scatter_dimension=0, tiled=True),
    )
    return (
        jnp.stack(layer_outs),
        jnp.stack(input_grads),
        owned_grads[0],
        owned_grads[1],
        owned_grads[2],
        owned_grads[3],
        owned_grads[4],
        owned_grads[5],
        owned_grads[6],
        owned_grads[7],
        owned_grads[8],
    )


MESH = pl.DeviceIdType.MESH
NEG = -1e30
WIDE = 128
VMEM_LIMIT = 61 * 1024 * 1024


def fits_fast(mesh):
    return mesh.shape["ctx"] == 8 and mesh.shape["ws"] == 4


def place():
    c = lax.axis_index("ctx")
    w = lax.axis_index("ws")
    return c // 2, lax.rem(c, 2), w // 2, lax.rem(w, 2)


def device(z, y, x, k):
    return (z * 2 + y, x * 2 + k)


def greet(zn):
    z, y, x, k = place()
    others = [device(lax.rem(z + j, zn), y, x, k) for j in range(1, zn)]
    others += [device(z, y, 1 - x, k), device(z, 1 - y, x, k), device(z, y, x, 1 - k)]
    barrier = pltpu.get_barrier_semaphore()
    for other in others:
        pl.semaphore_signal(barrier, inc=1, device_id=other, device_id_type=MESH)
    pl.semaphore_wait(barrier, len(others))


def remote(src, dst, send, recv, where):
    return pltpu.make_async_remote_copy(
        src_ref=src, dst_ref=dst, send_sem=send, recv_sem=recv, device_id=where, device_id_type=MESH
    )


class Gather:
    SEMS = 12

    def __init__(self, src, dst, send, recv, zn):
        z, y, x, k = place()
        own = dst.at[z, y, x, k]
        hz = zn // 2
        xn, yn, sib = device(z, y, 1 - x, k), device(z, 1 - y, x, k), device(z, y, x, 1 - k)

        def push(i, ref, where):
            return remote(ref, ref, send.at[i], recv.at[i], where)

        def col(yy, xx, lo=0, n=zn):
            return dst.at[pl.ds(lo, n), yy, xx, k]

        self.local = pltpu.make_async_copy(src(z), own, send.at[0])
        self.along = []
        for j in range(1, zn):
            zz = lax.rem(z + j, zn)
            self.along.append(remote(src(zz), own, send.at[j], recv.at[j], device(zz, y, x, k)))
        self.cols = [push(4, col(y, x), xn), push(5, col(y, x), yn)]
        self.corner = [push(7, col(1 - y, x, 0, hz), xn), push(8, col(y, 1 - x, hz, hz), yn)]
        self.twin_own = push(6, col(y, x), sib)
        self.twin_cols = [push(9, col(y, 1 - x), sib), push(10, col(1 - y, x), sib)]
        self.twin_corner = push(11, col(1 - y, 1 - x), sib)

    def stage(self, n):
        if n == 0:
            self.local.start()
            for c in self.along:
                c.start()
        elif n == 1:
            self.local.wait()
            for c in self.along:
                c.wait_recv()
            for c in self.cols:
                c.start()
            self.twin_own.start()
        elif n == 2:
            for c in self.cols:
                c.wait_recv()
            for c in self.corner:
                c.start()
            for c in self.twin_cols:
                c.start()
        elif n == 3:
            for c in self.corner:
                c.wait_recv()
            self.twin_corner.start()
        elif n == 4:
            for c in [self.twin_own] + self.twin_cols + [self.twin_corner]:
                c.wait_recv()
            for c in (
                self.along
                + self.cols
                + self.corner
                + [self.twin_own]
                + self.twin_cols
                + [self.twin_corner]
            ):
                c.wait_send()


def stage_step(items, offsets, t, between=None):
    for n, offset in enumerate(offsets):
        if 0 <= t - offset < len(items):
            if items[t - offset] is not None:
                items[t - offset].stage(n)
            if between is not None:
                between()


FIRST_STAGES = (0, 1, 2, 3, 4)
GATHER_STAGES = (0, 1, 2, 3, 4)
GATHER_FROM = 3
GATHER_CUTS = [(1, 1), (1, 2), (1, 2), (2, 1), (1, 1)]
SUM_STAGES = (0, 1, 2, 3)


def portions(step, total, parts):
    done = [0]

    def call(all_=False):
        upto = total if all_ else min(total, done[0] + -(-total // parts))
        if upto > done[0]:
            lax.fori_loop(done[0], upto, step, 0)
            done[0] = upto

    return call


def pieces_of(rows, cols, nrow, ncol):
    return [
        (i * (rows // nrow), rows // nrow, j * (cols // ncol), cols // ncol)
        for i in range(nrow)
        for j in range(ncol)
    ]


def gather_item(ref, out, r0, nr, c0, nc, send, recv, zn):
    src = ref.at[pl.ds(r0, nr), pl.ds(c0, nc)]
    dst = out.at[:, :, :, :, pl.ds(r0, nr), pl.ds(c0, nc)]
    return Gather(lambda zz: src, dst, send, recv, zn)


class Exchange:
    def __init__(self, src, dst, send, recv, zn):
        z, y, x, k = place()
        self.local = pltpu.make_async_copy(src(z), dst(z), send.at[0])
        self.along = []
        for j in range(1, zn):
            zz = lax.rem(z + j, zn)
            self.along.append(remote(src(zz), dst(z), send.at[j], recv.at[j], device(zz, y, x, k)))

    def start(self):
        self.local.start()
        for c in self.along:
            c.start()

    def arrived(self):
        self.local.wait()
        for c in self.along:
            c.wait_recv()

    def sent(self):
        for c in self.along:
            c.wait_send()


class Scatter:
    SEMS = 10

    @staticmethod
    def scratch(zn, nr, nc):
        b = jnp.bfloat16
        return [
            pltpu.VMEM((zn, 2, 2, nr, nc), b),
            pltpu.VMEM((zn, 2, 2, nr, nc), b),
            pltpu.VMEM((2, zn // 2, nr, nc), b),
            pltpu.VMEM((2, zn, nr, nc), b),
            pltpu.VMEM((zn - 1, nr, nc), b),
        ]

    def __init__(self, part, out, bufs, send, recv, zn, give=None):
        z, y, x, k = self.at = place()
        self.zn = zn
        hz = zn // 2
        xn, yn, sib = device(z, y, 1 - x, k), device(z, 1 - y, x, k), device(z, y, x, 1 - k)
        self.held, self.twin, self.corners, self.colsums, self.ends = held, twin, corners, colsums, ends = bufs
        self.out = out
        self.load = None
        if give is None:
            self.load = pltpu.make_async_copy(part.at[:, :, :, k], held, send.at[0])
            give = part.at[:, :, :, 1 - k]
        self.to_twin = remote(give, twin, send.at[1], recv.at[1], sib)
        self.to_corner = [
            remote(held.at[pl.ds(0, hz), 1 - y, 1 - x], corners.at[0], send.at[2], recv.at[2], yn),
            remote(held.at[pl.ds(hz, hz), 1 - y, 1 - x], corners.at[1], send.at[3], recv.at[3], xn),
        ]
        self.to_col = [
            remote(held.at[:, y, 1 - x], colsums.at[0], send.at[4], recv.at[4], xn),
            remote(held.at[:, 1 - y, x], colsums.at[1], send.at[5], recv.at[5], yn),
        ]
        self.along = []
        for j in range(1, zn):
            zz = lax.rem(z + j, zn)
            dst = out.at[z] if ends is None else ends.at[j - 1]
            self.along.append(
                remote(held.at[zz, y, x], dst, send.at[5 + j], recv.at[5 + j], device(zz, y, x, k))
            )
        self.last = pltpu.make_async_copy(held.at[z, y, x], out.at[z], send.at[0]) if ends is None else None

    def stage(self, n):
        z, y, x, k = self.at
        zn, hz = self.zn, self.zn // 2
        held = self.held
        if n == 0:
            self.to_twin.start()
            if self.load is not None:
                self.load.start()
        elif n == 1:
            if self.load is not None:
                self.load.wait()
            self.to_twin.wait_recv()

            def add(i, _):
                for yy in range(2):
                    for xx in range(2):
                        held[i, yy, xx] = held[i, yy, xx] + self.twin[i, yy, xx]
                return 0

            lax.fori_loop(0, zn, add, 0)
            for c in self.to_corner:
                c.start()
        elif n == 2:
            for c in self.to_corner:
                c.wait_recv()
            for i in range(hz):
                held[i, y, 1 - x] = held[i, y, 1 - x] + self.corners[0, i]
                held[hz + i, 1 - y, x] = held[hz + i, 1 - y, x] + self.corners[1, i]
            for c in self.to_col:
                c.start()
        elif n == 3:
            for c in self.to_col:
                c.wait_recv()

            def add(i, _):
                f = jnp.float32
                held[i, y, x] = (
                    held[i, y, x].astype(f) + self.colsums[0, i].astype(f) + self.colsums[1, i].astype(f)
                ).astype(jnp.bfloat16)
                return 0

            lax.fori_loop(0, zn, add, 0)
            for c in self.along:
                c.start()
            if self.last is not None:
                self.last.start()
        elif n == 4:
            for c in self.along:
                c.wait_recv()
            if self.last is not None:
                self.last.wait()
            else:
                total = held[z, y, x].astype(jnp.float32)
                for j in range(zn - 1):
                    total = total + self.ends[j].astype(jnp.float32)
                self.out[...] = total
            for c in [self.to_twin] + self.to_corner + self.to_col + self.along:
                c.wait_send()


NT = (((1,), (1,)), ((), ()))


def nt(a, b):
    return lax.dot_general(a, b, NT, preferred_element_type=jnp.float32)


PER = QUERY_HEADS // KEY_VALUE_HEADS
HALF_GROUPS = KEY_VALUE_HEADS // 2
HALF_HEADS = QUERY_HEADS // 2
KV_LANES = 2 * HALF_GROUPS * HEAD_SIZE


def lane_slot(n):
    return n // 2, n % 2


def key_slot(g):
    return lane_slot(g)


def value_slot(g):
    return lane_slot(HALF_GROUPS + g)


def pair_index(half, zp):
    return zp if half == 0 else 3 - zp


def pair_tile(src, g, half, zp):
    tiles = []
    for j in range(PER):
        lo = HEAD_SIZE * (PER * g + j)
        a = src[2 * zp, lo : lo + HEAD_SIZE, :].astype(jnp.float32)
        b = src[2 * zp + 1, lo : lo + HEAD_SIZE, :].astype(jnp.float32)
        low = lax.broadcasted_iota(jnp.int32, a.shape, 1) < WIDE // 2
        if half == 0:
            tiles.append(jnp.where(low, a, pltpu.roll(b, WIDE // 2, 1)))
        else:
            tiles.append(jnp.where(low, pltpu.roll(a, WIDE // 2, 1), b))
    return jnp.concatenate(tiles, axis=1)


def unpair(get, dst):
    for zp in range(2):
        for g in range(HALF_GROUPS):
            first, second = get(g, pair_index(0, zp)), get(g, pair_index(1, zp))
            for j in range(PER):
                lo = HEAD_SIZE * (PER * g + j)
                a, b = first[:, WIDE * j : WIDE * j + WIDE], second[:, WIDE * j : WIDE * j + WIDE]
                low = lax.broadcasted_iota(jnp.int32, a.shape, 1) < WIDE // 2
                even = jnp.where(low, a, pltpu.roll(b, WIDE // 2, 1))
                odd = jnp.where(low, pltpu.roll(a, WIDE // 2, 1), b)
                dst[2 * zp, lo : lo + HEAD_SIZE, :] = even.astype(dst.dtype)
                dst[2 * zp + 1, lo : lo + HEAD_SIZE, :] = odd.astype(dst.dtype)


def set_padded(dst, g, p, tile, side):
    tile = tile.astype(dst.dtype)
    dst[g, p, side * HEAD_SIZE : (side + 1) * HEAD_SIZE, :] = tile
    dst[g, p, (1 - side) * HEAD_SIZE : (2 - side) * HEAD_SIZE, :] = jnp.zeros_like(tile)


def walk(t, y, cn):
    b1, b2, b3 = 3 + y, 10 + 2 * y, 22 + y
    p = (t >= b1).astype(jnp.int32) + (t >= b2).astype(jnp.int32) + (t >= b3).astype(jnp.int32)
    j = t - jnp.where(p == 0, 0, jnp.where(p == 1, b1, jnp.where(p == 2, b2, b3)))
    zp = jnp.where(p < 2, p, 3 - p)
    low = jnp.where(p < 2, 4 * zp + y, 2 * cn - 3 - 4 * zp - y)
    late = (j >= cn).astype(jnp.int32)
    src = jnp.where(late == 1, 2 * cn - 1 - j, j)
    return p, j, src // 2, lax.rem(src, 2), pl.multiple_of(late * HEAD_SIZE, HEAD_SIZE), j >= low


STEPS = 38
FORWARD_PARTS, FORWARD_LEFT = 20, 3


def visible(p, j, y, w, cn, wn, rows):
    shape = (wn * rows, PER * WIDE)
    lane = lax.rem(lax.broadcasted_iota(jnp.int32, shape, 1), WIDE)
    zp = jnp.where(p < 2, p, 3 - p)
    c = 2 * (2 * zp + lane // rows) + y
    span = jnp.where(p < 2, c, 2 * cn - 1 - c)
    query = span * (wn * rows) + w * rows + lax.rem(lane, rows)
    key = j * (wn * rows) + lax.broadcasted_iota(jnp.int32, shape, 0)
    return key <= query


def key_block(kvg, zz, yy, late, rows, block):
    t = kvg[zz, yy, :, :, pl.ds(late, rows), WIDE * block : WIDE * block + WIDE]
    return t.reshape(4 * rows, WIDE)


def turned(t):
    return t.astype(jnp.float32).T.astype(t.dtype)


def by_span(body, kvg, cn, rows):
    def one(j, _):
        late = (j >= cn).astype(jnp.int32)
        src = jnp.where(late == 1, 2 * cn - 1 - j, j)
        at = pl.multiple_of(late * rows, rows)
        body(j, lambda b: key_block(kvg, src // 2, lax.rem(src, 2), at, rows, b))
        return 0

    lax.fori_loop(0, 2 * cn, one, 0)


def transposed(t):
    return jnp.concatenate([t[:, i : i + WIDE].T for i in range(0, t.shape[1], WIDE)], axis=0)


def unfold_rows(src, dst, rb):
    n = src.shape[0] // 16
    fold = 16 // rb
    cols = src.shape[1]
    shape = (n * rb, n * 16)
    row = lax.broadcasted_iota(jnp.int32, shape, 0)
    at = 16 * (row // rb) + lax.rem(row, rb)
    col = lax.broadcasted_iota(jnp.int32, shape, 1)
    for q in range(fold):
        pick = jnp.where(col == at + rb * q, 1.0, 0.0).astype(jnp.bfloat16)
        t = jnp.dot(pick, src[...], preferred_element_type=jnp.float32)
        dst[:, q * cols : (q + 1) * cols] = t.astype(dst.dtype)


def gather_attend(x, gy, tables, qkv, fold1, weights, cuts, collective_id):
    cn, wn = lax.axis_size("ctx"), lax.axis_size("ws")
    zn = cn // 2
    dn = cn * wn
    tokens = tables.shape[1]
    all_rows, width = x.shape
    mbs = all_rows // tokens
    qkv_w = qkv.shape[1]
    q_rows = qkv_w - 2 * KV_LANES
    rows = tokens // 2
    mine = q_rows // 2
    f32, b16 = jnp.float32, jnp.bfloat16
    ra = qkv.shape[0] // 16 * 16
    rb = qkv.shape[0] - ra
    wa = dn * ra
    wide1 = fold1.shape[1] * (16 // rb)
    own = ra + rb
    ff = weights[1].shape[1]
    step_cols = 3 * WIDE
    rest_w = -(-(width + 2 * ff) // (4 * step_cols)) * step_cols
    shapes = [(ra, width), (ra, ff), (ra, ff), weights[3].shape, (16, rest_w)]
    n = len(shapes)
    work = [(a, piece) for a in range(n) for piece in pieces_of(*shapes[a], *cuts[a])]
    groups = range(HALF_GROUPS)
    n_first = 3

    def kernel(*refs):
        x_raw, gy_raw, tab, qkv_ref, fold_ref, out_raw, gate_raw, up_raw, down_raw = refs[:9]
        at = 9
        x_ref, gy_out, order_out = refs[at : at + 3]
        at += 3
        o_out, q_out, kv_out, oh_out, lse_out, w_out, wb_out, hn_out, hnb_out, inv_out, gains_out = refs[at : at + 11]
        at += 11
        outs = refs[at : at + n]
        at += n
        (order, out_s, down_s, rest_s, wq, f1, wide, hn, q_s, kv_s, qh, kvg, oh, qpad, vt, m_s, l_s, acc) = refs[at : at + 18]
        send, recv, xs, xr, ks, kr, save = refs[at + 18 :]
        ins = [out_s, gate_raw, up_raw, down_s, rest_s]
        greet(zn)
        z, y, x_, k = place()
        w = 2 * x_ + k

        def lanes_of(zz):
            return kv_s.at[zz // 2, :, pl.ds(pl.multiple_of(lax.rem(zz, 2) * KV_LANES, WIDE), KV_LANES)]

        def heads_of(ref, zz):
            return ref.at[zz // 2, pl.ds(pl.multiple_of(lax.rem(zz, 2) * mine, 16), mine), :]

        items = [
            gather_item(fold_ref, f1, 0, 16, 0, fold1.shape[1], send.at[0], recv.at[0], zn),
            gather_item(qkv_ref, wq, 0, ra, 0, 2 * KV_LANES, send.at[1], recv.at[1], zn),
            gather_item(qkv_ref, wq, 0, ra, 2 * KV_LANES, q_rows, send.at[2], recv.at[2], zn),
        ]
        later = [
            gather_item(ins[a], outs[a], r0, nr, c0, nc, send.at[n_first + i], recv.at[n_first + i], zn)
            for i, (a, (r0, nr, c0, nc)) in enumerate(work)
        ]
        kvx = Gather(lanes_of, kvg, ks, kr, zn)
        qx = Exchange(lambda zz: heads_of(q_s, zz), lambda zz: qh.at[zz], xs.at[0], xr.at[0], zn)
        ox = Exchange(lambda zz: oh.at[zz], lambda zz: heads_of(o_out, zz), xs.at[1], xr.at[1], zn)

        def advance(s, between=None):
            stage_step(items, FIRST_STAGES, s)
            stage_step(later, GATHER_STAGES, s - GATHER_FROM, between)

        advance(0)
        for r in range(0, width, WIDE):
            new = r + lax.broadcasted_iota(jnp.int32, (WIDE, width), 0)
            old = jnp.where(
                new < wa, own * (new // ra) + lax.rem(new, ra), own * ((new - wa) // rb) + ra + lax.rem(new - wa, rb)
            )
            col = lax.broadcasted_iota(jnp.int32, (WIDE, width), 1)
            order[r : r + WIDE, :] = jnp.where(col == old, 1.0, 0.0).astype(b16)
        advance(1)
        out_s[...] = nt(out_raw[...], order[...]).astype(b16)
        down_s[...] = nt(down_raw[...], order[...]).astype(b16)
        columns = []
        for ref, cols in ((out_s, width), (gate_raw, ff), (up_raw, ff)):
            columns += [(ref, c) for c in range(0, cols, step_cols)]
        per = rest_w // step_cols
        row = lax.broadcasted_iota(jnp.int32, (16, own), 0)
        src = lax.broadcasted_iota(jnp.int32, (16, own), 1)
        for c in range(per):
            total = jnp.zeros((16, step_cols), f32)
            for q in range(16 // rb):
                if q * per + c < len(columns):
                    ref, lo = columns[q * per + c]
                    pick = jnp.where((row // rb == q) & (src == ra + lax.rem(row, rb)), 1.0, 0.0).astype(b16)
                    total = total + jnp.dot(pick, ref[:, lo : lo + step_cols], preferred_element_type=f32)
            rest_s[:, c * step_cols : (c + 1) * step_cols] = total.astype(b16)
        advance(2)
        x_ref[...] = nt(x_raw[...], order[...]).astype(b16)
        advance(3)
        gy_out[...] = nt(gy_raw[...], order[...]).astype(b16)
        save_order = pltpu.make_async_copy(order, order_out, save.at[5])
        save_order.start()
        xf = x_ref[...].astype(f32)
        inv = lax.rsqrt(jnp.mean(xf * xf, axis=-1, keepdims=True) + EPSILON)
        inv_out[...] = inv
        m_s[...] = jnp.full(m_s.shape, NEG, f32)
        l_s[...] = jnp.zeros(l_s.shape, f32)
        acc[...] = jnp.zeros(acc.shape, f32)
        advance(n_first + 1)
        unfold_rows(f1[...].reshape(dn * 16, fold1.shape[1]), wide, rb)
        lane = lax.broadcasted_iota(jnp.int32, (WIDE, width), 1)
        local = jnp.where(lane < wa, lax.rem(lane, ra), ra + lax.rem(lane - wa, rb))
        spread = jnp.where(lax.broadcasted_iota(jnp.int32, (WIDE, width), 0) == local, 1.0, 0.0).astype(b16)
        lines = jnp.dot(wide[:, wide1 - WIDE :], spread, preferred_element_type=f32)
        lane = lax.broadcasted_iota(jnp.int32, lines.shape, 1)
        owner = jnp.where(lane < wa, lane // ra, (lane - wa) // rb)
        line = lax.broadcasted_iota(jnp.int32, lines.shape, 0)
        for i in range(2):
            gains_out[i : i + 1, :] = jnp.sum(jnp.where(line == rb * owner + i, lines, 0.0), axis=0, keepdims=True)
        normed = xf * inv * gains_out[0:1, :]
        hn[...] = normed.astype(b16)
        hn_out[...] = transposed(normed[:, :wa]).astype(b16)
        hnb_out[...] = transposed(normed[:, wa:]).astype(b16)
        advance(n_first + 2)

        low_lanes = lax.broadcasted_iota(jnp.int32, (tokens, WIDE), 1) < HEAD_SIZE
        quarter = HEAD_SIZE // 2

        def turned_heads(t, kind):
            if kind == "still":
                return t
            cos, low, high = tab[0], tab[1], tab[2]
            r = t * cos + pltpu.roll(t, WIDE - quarter, 1) * low + pltpu.roll(t, quarter, 1) * high
            return r if kind == "turn" else jnp.where(low_lanes, r, t)

        def project(c):
            cols = slice(c * KV_LANES, (c + 1) * KV_LANES)
            t = jnp.dot(hn[:, :wa], wq[:, :, :, :, :, cols].reshape(wa, KV_LANES), preferred_element_type=f32)
            t = t + jnp.dot(hn[:, wa:], wide[:, cols], preferred_element_type=f32)
            kinds = ["turn", "mixed", "still"] if c < 2 else ["turn"] * 3
            for mb in range(mbs):
                for b in range(3):
                    r = turned_heads(t[mb * tokens : (mb + 1) * tokens, WIDE * b : WIDE * b + WIDE], kinds[b])
                    at = c * KV_LANES + WIDE * b
                    if c < 2:
                        kv_s[mb, :, at : at + WIDE] = r.astype(b16)
                    else:
                        at -= 2 * KV_LANES
                        q_s[mb, at : at + WIDE, :] = (r * HEAD_SIZE**-0.5).T.astype(b16)

        project(0)
        project(1)
        kvx.stage(0)
        advance(n_first + 3)
        for c in range(2, qkv_w // KV_LANES):
            project(c)
        qx.start()
        save_order.wait()
        saves = [
            pltpu.make_async_copy(wq, w_out, save.at[3]),
            pltpu.make_async_copy(wide.at[:, pl.ds(0, qkv_w)], wb_out, save.at[4]),
        ]
        for s in saves:
            s.start()
        kvx.stage(1)
        kvx.stage(2)
        advance(n_first + 4)
        kvx.stage(3)
        qx.arrived()
        for half in range(2):
            for zp in range(2):
                for g in groups:
                    set_padded(qpad, g, pair_index(half, zp), pair_tile(qh, g, half, zp), key_slot(g)[1])
        kvx.stage(4)

        def turn(j, block):
            flat = {b: turned(block(b)) for b in sorted({value_slot(g)[0] for g in groups})}
            for g in groups:
                b, side = value_slot(g)
                vt[j, g] = flat[b][side * HEAD_SIZE : (side + 1) * HEAD_SIZE]

        by_span(turn, kvg, cn, rows)
        saves += [
            pltpu.make_async_copy(qh, q_out, save.at[0]),
            pltpu.make_async_copy(kvg, kv_out, save.at[1]),
        ]
        for s in saves[2:]:
            s.start()

        def step(t, _):
            p, j, zz, yy, late, edge = walk(t, y, cn)

            def run(masked):
                seen = visible(p, j, y, w, cn, wn, rows) if masked else None
                for g in groups:
                    s = jnp.dot(
                        key_block(kvg, zz, yy, late, rows, key_slot(g)[0]), qpad[g, p], preferred_element_type=f32
                    )
                    if masked:
                        s = jnp.where(seen, s, NEG)
                    m_old = m_s[g, p]
                    m_new = jnp.maximum(m_old, jnp.max(s, axis=0, keepdims=True))
                    alpha = jnp.exp(m_old - m_new)
                    e = jnp.exp(s - m_new)
                    m_s[g, p] = m_new
                    l_s[g, p] = l_s[g, p] * alpha + jnp.sum(e, axis=0, keepdims=True)
                    acc[g, p] = acc[g, p] * alpha + jnp.dot(
                        vt[j, g], e.astype(b16), preferred_element_type=f32
                    )

            pl.when(edge)(lambda: run(True))
            pl.when(jnp.logical_not(edge))(lambda: run(False))
            return 0

        last = GATHER_FROM + len(later) + GATHER_STAGES[-1]
        start = n_first + 5
        attend = portions(step, STEPS, FORWARD_PARTS)
        for s in range(start, last):
            advance(s, attend if s <= last - FORWARD_LEFT else None)
            if s == last - FORWARD_LEFT:
                attend(True)
                unpair(lambda g, p: acc[g, p] / l_s[g, p], oh)
                ox.start()
                saves.append(pltpu.make_async_copy(oh, oh_out, save.at[2]))
                saves[-1].start()
                lse_out[...] = m_s[...] + jnp.log(l_s[...])
        ox.arrived()
        ox.sent()
        qx.sent()
        for s in saves:
            s.wait()

    stat = (HALF_GROUPS, 4, 1, PER * WIDE)
    block = (zn, mine, tokens)
    kv_shape = (zn, 2, 2, 2, tokens, KV_LANES)
    any_ = pl.BlockSpec(memory_space=pl.ANY)
    vmem = pl.BlockSpec(memory_space=pltpu.VMEM)
    sds = jax.ShapeDtypeStruct
    dma = pltpu.SemaphoreType.DMA
    return pl.pallas_call(
        kernel,
        out_shape=[
            sds(x.shape, b16),
            sds(x.shape, b16),
            sds((width, width), b16),
            sds((mbs, q_rows, tokens), b16),
            sds(block, b16),
            sds(kv_shape, b16),
            sds(block, b16),
            sds(stat, f32),
            sds((zn, 2, 2, 2, ra, qkv_w), b16),
            sds((dn * rb, qkv_w), b16),
            sds((wa, all_rows), b16),
            sds((width - wa, all_rows), b16),
            sds((all_rows, 1), f32),
            sds((2, width), f32),
        ]
        + [sds((zn, 2, 2, 2, *shapes[a]), b16) for a in range(n)],
        in_specs=[vmem] * 3 + [any_] * 2 + [vmem] * 4,
        out_specs=[vmem] * 2 + [any_] + [any_] * 4 + [vmem] + [any_] * 2 + [vmem] * 4 + [any_] * n,
        scratch_shapes=[
            pltpu.VMEM((width, width), b16),
            pltpu.VMEM(weights[0].shape, b16),
            pltpu.VMEM(weights[3].shape, b16),
            pltpu.VMEM((16, rest_w), b16),
            pltpu.VMEM((zn, 2, 2, 2, ra, qkv_w), b16),
            pltpu.VMEM((zn, 2, 2, 2, 16, fold1.shape[1]), b16),
            pltpu.VMEM((dn * rb, wide1), b16),
            pltpu.VMEM((all_rows, width), b16),
            pltpu.VMEM((mbs, q_rows, tokens), b16),
            pltpu.VMEM((mbs, tokens, 2 * KV_LANES), b16),
            pltpu.VMEM(block, b16),
            pltpu.VMEM(kv_shape, b16),
            pltpu.VMEM(block, b16),
            pltpu.VMEM((HALF_GROUPS, 4, WIDE, PER * WIDE), b16),
            pltpu.VMEM((2 * cn, HALF_GROUPS, HEAD_SIZE, wn * rows), b16),
            pltpu.VMEM(stat, f32),
            pltpu.VMEM(stat, f32),
            pltpu.VMEM((HALF_GROUPS, 4, HEAD_SIZE, PER * WIDE), f32),
            dma((n_first + len(work), Gather.SEMS)),
            dma((n_first + len(work), Gather.SEMS)),
            dma((2, zn)),
            dma((2, zn)),
            dma((Gather.SEMS,)),
            dma((Gather.SEMS,)),
            dma((6,)),
        ],
        compiler_params=pltpu.CompilerParams(
            collective_id=collective_id, has_side_effects=True, vmem_limit_bytes=VMEM_LIMIT
        ),
    )(x, gy, tables, qkv, fold1, *weights)


class Share:
    def __init__(self, src, own, other, local, send, recv, split):
        z, y, x, k = place()
        mine = src.at[:, :, :, k] if split else src
        theirs = src.at[:, :, :, 1 - k] if split else src
        self.load = None if mine is own else pltpu.make_async_copy(mine, own, local)
        self.swap = remote(theirs, other, send, recv, device(z, y, x, 1 - k))
        self.waited = False

    def start(self):
        if self.load is not None:
            self.load.start()
        self.swap.start()

    def ready(self):
        if not self.waited:
            if self.load is not None:
                self.load.wait()
            self.swap.wait_recv()
            self.waited = True

    def sent(self):
        self.swap.wait_send()


class Sum:
    SEMS = 8

    def __init__(self, make, held, bufs, out, send, recv, zn):
        z, y, x, k = self.at = place()
        self.make, self.held, self.out, self.zn = make, held, out, zn
        hz = zn // 2
        xn, yn = device(z, y, 1 - x, k), device(z, 1 - y, x, k)
        self.corners, self.colsums, self.ends = corners, colsums, ends = bufs
        self.to_corner = [
            remote(held.at[pl.ds(0, hz), 1 - y, 1 - x], corners.at[0], send.at[0], recv.at[0], yn),
            remote(held.at[pl.ds(hz, hz), 1 - y, 1 - x], corners.at[1], send.at[1], recv.at[1], xn),
        ]
        self.to_col = [
            remote(held.at[:, y, 1 - x], colsums.at[0], send.at[2], recv.at[2], xn),
            remote(held.at[:, 1 - y, x], colsums.at[1], send.at[3], recv.at[3], yn),
        ]
        self.along = []
        for j in range(1, zn):
            zz = lax.rem(z + j, zn)
            self.along.append(
                remote(held.at[zz, y, x], ends.at[j - 1], send.at[3 + j], recv.at[3 + j], device(zz, y, x, k))
            )

    @staticmethod
    def scratch(zn, nr, nc):
        b = jnp.bfloat16
        return [
            pltpu.VMEM((2, zn // 2, nr, nc), b),
            pltpu.VMEM((2, zn, nr, nc), b),
            pltpu.VMEM((zn - 1, nr, nc), b),
        ]

    def stage(self, n):
        z, y, x, k = self.at
        zn, hz, held = self.zn, self.zn // 2, self.held
        f32, b16 = jnp.float32, jnp.bfloat16
        if n == 0:
            self.make(held)
            for c in self.to_corner:
                c.start()
        elif n == 1:
            for c in self.to_corner:
                c.wait_recv()
            for i in range(hz):
                held[i, y, 1 - x] = held[i, y, 1 - x] + self.corners[0, i]
                held[hz + i, 1 - y, x] = held[hz + i, 1 - y, x] + self.corners[1, i]
            for c in self.to_col:
                c.start()
        elif n == 2:
            for c in self.to_col:
                c.wait_recv()
            for i in range(zn):
                held[i, y, x] = (
                    held[i, y, x].astype(f32)
                    + self.colsums[0, i].astype(f32)
                    + self.colsums[1, i].astype(f32)
                ).astype(b16)
            for c in self.along:
                c.start()
        elif n == 3:
            for c in self.along:
                c.wait_recv()
            total = held[z, y, x].astype(f32)
            for j in range(zn - 1):
                total = total + self.ends[j].astype(f32)
            self.out[...] = total
            for c in self.to_corner + self.to_col + self.along:
                c.wait_send()


FFN_CUTS = 2
ORDER = (0, 1, 2, 3, 4, 5, 6, 7, 8, 9, 10, 11)
BACK_SPAN, BACK_PARTS = 3, 10


def scatter_attend(do, qh, kvg, oh, lse, tables, lefts, rests, rights, plan, last, collective_id):
    cn, wn = lax.axis_size("ctx"), lax.axis_size("ws")
    zn = cn // 2
    mbs, q_rows, tokens = do.shape
    rows = tokens // 2
    mine = q_rows // 2
    all_rows = mbs * tokens
    f32, b16 = jnp.float32, jnp.bfloat16
    groups = range(HALF_GROUPS)
    scale = HEAD_SIZE**-0.5
    ff = rights[2].shape[1]
    width = rights[0].shape[1]
    qkv_w = q_rows + 2 * KV_LANES
    act_rows = lefts[0].shape[4]
    ra = lefts[1].shape[4]
    rest_w, qkv_rest_w = plan
    n_down = act_rows // ra
    sizes = (
        [(ra, width)] * n_down
        + [(ra, ff // FFN_CUTS)] * (2 * FFN_CUTS)
        + [(ra, width), (16, rest_w), (ra, 2 * KV_LANES), (ra, q_rows), (16, qkv_rest_w)]
    )
    max_cols = max(s[1] for s in sizes)
    ring = SUM_STAGES[-1] + 1
    scratch = []
    for nr, nc in sizes:
        scratch += Sum.scratch(zn, nr, nc)
    n_items = len(sizes)
    ins_all = [*lefts, *rests, *rights]
    n_in = len(ins_all)
    split = [True] * len(lefts) + [False] * (n_in - len(lefts))
    half = lambda a, s: (a.shape[:3] + a.shape[4:]) if s else a.shape
    shares = []
    for a, s in zip(ins_all, split):
        shares += [pltpu.VMEM(half(a, s), b16), pltpu.VMEM(half(a, s), b16)]
    outs_shape = [
        (act_rows, width), (ra, ff), (ra, ff), (ra, width), (16, rest_w), (ra, qkv_w), (16, qkv_rest_w)
    ]
    n_out = len(outs_shape)
    n_last = len(last)

    def kernel(*refs):
        do_ref, qh_ref, kvg_ref, oh_ref, lse_ref, tab = refs[:6]
        ins = refs[6 : 6 + n_in]
        at = 6 + n_in
        w_ref, r_ref, x_ref, inv_ref, gain_ref, gx1_ref, gain2_ref, order_ref = refs[at : at + n_last]
        at += n_last
        outs = refs[at : at + n_out]
        input_grad, total = refs[at + n_out : at + n_out + 2]
        rest = refs[at + n_out + 2 :]
        bufs, rest = rest[: len(scratch)], rest[len(scratch) :]
        pairs, rest = rest[: len(shares)], rest[len(shares) :]
        (held, gq, gq_other, dkv_in, oh, gh, give, got) = rest[:8]
        kb = rest[8:12]
        send, recv, ps, pr, pl_, xs, xr, ks, kr, gs, gr, loads = rest[12:]
        dqh, dq_in = gh, oh
        greet(zn)
        z, y, x, k = place()
        w = 2 * x + k

        def heads_of(ref, zz):
            return ref.at[zz // 2, pl.ds(pl.multiple_of(lax.rem(zz, 2) * mine, 16), mine), :]

        gx = Exchange(lambda zz: heads_of(do_ref, zz), lambda zz: gh.at[zz], xs.at[0], xr.at[0], zn)
        dx = Exchange(lambda zz: dqh.at[zz], lambda zz: dq_in.at[zz], xs.at[1], xr.at[1], zn)
        kvx = Scatter(None, dkv_in, tuple(kb) + (None,), ks, kr, zn, give)
        share = [
            Share(ins[i], pairs[2 * i], pairs[2 * i + 1], pl_.at[i], ps.at[i], pr.at[i], split[i])
            for i in range(n_in)
        ]
        gq_share = Share(gq, gq, gq_other, None, ps.at[n_in], pr.at[n_in], False)
        own = lambda i: pairs[2 * i]
        other = lambda i: pairs[2 * i + 1]
        ACT, H2, OT, HN, H2B, OTB, HNB, GY, GB, GG, GU = range(n_in)

        def product(left, right, lo, row0, needs):
            def make(dst):
                for i in needs:
                    share[i].ready()
                nr, nc = dst.shape[3:]
                lefts2 = [
                    r[:, :, :, row0 : row0 + nr, :].reshape(zn * 4 * nr, all_rows)
                    for r in (own(left), other(left))
                ]
                step = 3 * WIDE

                def cols(i, _):
                    at = pl.multiple_of(i * step, WIDE)
                    t = jnp.dot(lefts2[0], right[0][:, pl.ds(lo + at, step)], preferred_element_type=f32)
                    t = t + jnp.dot(lefts2[1], right[1][:, pl.ds(lo + at, step)], preferred_element_type=f32)
                    dst[:, :, :, :, pl.ds(at, step)] = t.astype(b16).reshape(zn, 2, 2, nr, step)
                    return 0

                lax.fori_loop(0, nc // step, cols, 0)

            return make

        def both(i):
            return (own(i), other(i))

        def fold4(quarters):
            row = lax.rem(lax.broadcasted_iota(jnp.int32, quarters[0].shape, 0), 8)
            here = k == 0

            def put(a, b):
                n = a.shape[0]
                low = jnp.where(here, a, pltpu.roll(a, n - 4, 0))
                high = jnp.where(here, pltpu.roll(b, 4, 0), b)
                t = jnp.where(row < 4, low, high)
                return t.reshape(zn * 4, 8, t.shape[1])

            t = jnp.concatenate([put(*quarters[:2]), put(*quarters[2:])], axis=1)
            return t.astype(b16).reshape(zn, 2, 2, 16, t.shape[2])

        def rest_product(dst):
            step = 3 * WIDE
            for i in (H2B, OTB, GB, GG, GU):
                share[i].ready()
            columns = []
            for left, right, n in ((OTB, GB, width), (H2B, GG, ff), (H2B, GU, ff)):
                columns += [(left, right, c) for c in range(0, n, step)]
            per = rest_w // step

            def one(entry):
                if entry is None:
                    return jnp.zeros((own(H2B).shape[0], step), f32)
                left, right, c = entry
                return jnp.dot(own(left)[...], own(right)[:, c : c + step], preferred_element_type=f32) + jnp.dot(
                    other(left)[...], other(right)[:, c : c + step], preferred_element_type=f32
                )

            for c in range(per):
                quarters = []
                for q in range(4):
                    at = q * per + c
                    quarters.append(one(columns[at] if at < len(columns) else None))
                dst[:, :, :, :, c * step : (c + 1) * step] = fold4(quarters)

        def qkv_rest_product(dst):
            for i in (HNB,):
                share[i].ready()
            gq_share.ready()
            quarters = []
            for q in range(4):
                lo, hi = q * qkv_rest_w, min((q + 1) * qkv_rest_w, qkv_w)
                t = jnp.dot(own(HNB)[...], gq[:, lo:hi], preferred_element_type=f32) + jnp.dot(
                    other(HNB)[...], gq_other[:, lo:hi], preferred_element_type=f32
                )
                if hi - lo < qkv_rest_w:
                    t = jnp.concatenate([t, jnp.zeros((t.shape[0], qkv_rest_w - hi + lo), f32)], axis=1)
                quarters.append(t)
            dst[...] = fold4(quarters)

        gq_both = (gq, gq_other)
        makes = [product(ACT, both(GY), 0, ra * i, (ACT, GY)) for i in range(n_down)]
        ffn_parts = [(g, i * (ff // FFN_CUTS), ff // FFN_CUTS) for g in (GG, GU) for i in range(FFN_CUTS)]
        makes += [product(H2, both(g), lo, 0, (H2, g)) for g, lo, _ in ffn_parts]
        makes += [product(OT, both(GB), 0, 0, (OT, GB)), rest_product]
        makes += [product(HN, gq_both, 0, 0, (HN,)), product(HN, gq_both, 2 * KV_LANES, 0, (HN,)), qkv_rest_product]
        targets = [outs[0].at[pl.ds(ra * i, ra), :] for i in range(n_down)]
        targets += [outs[1 if g == GG else 2].at[:, pl.ds(lo, n)] for g, lo, n in ffn_parts]
        targets += [outs[3], outs[4], outs[5].at[:, pl.ds(0, 2 * KV_LANES)], outs[5].at[:, pl.ds(2 * KV_LANES, q_rows)], outs[6]]
        items = []
        for i, (nr, nc) in enumerate(sizes):
            slot = held.at[ORDER.index(i) % ring, :, :, :, pl.ds(0, nr), pl.ds(0, nc)]
            items.append(
                Sum(makes[i], slot, bufs[3 * i : 3 * i + 3], targets[i], send.at[i], recv.at[i], zn)
            )
        load_o = pltpu.make_async_copy(oh_ref, oh, pl_.at[n_in])
        load_o.start()
        gx.start()
        for i in (ACT, GY, H2, GG, GU, OT, GB, H2B, OTB, HN, HNB):
            share[i].start()
        order = [None if i is None else items[i] for i in ORDER]
        at_qkv = ORDER.index(n_items - 3)
        n_back = BACK_SPAN
        stage_step(order, SUM_STAGES, 0)

        def attention_back(kvg, qh, qt, dot_, kt, delta, dq, dkv):
            load_kv = pltpu.make_async_copy(kvg_ref, kvg, loads.at[0])
            load_q = pltpu.make_async_copy(qh_ref, qh, loads.at[1])
            load_kv.start()
            load_q.start()
            dq[...] = jnp.zeros(dq.shape, f32)

            def clear(i, _):
                dkv[i] = jnp.zeros(dkv.shape[1:], f32)
                return 0

            lax.fori_loop(0, zn, clear, 0)
            def turn(j, block):
                flat = {b: turned(block(b)) for b in sorted({key_slot(g)[0] for g in groups})}
                for g in groups:
                    b, side = key_slot(g)
                    kt[j, g] = flat[b][side * HEAD_SIZE : (side + 1) * HEAD_SIZE]

            load_kv.wait()
            by_span(turn, kvg, cn, rows)
            stage_step(order, SUM_STAGES, 1)
            gx.arrived()
            load_o.wait()
            load_q.wait()
            for half_ in range(2):
                for zp in range(2):
                    p = pair_index(half_, zp)
                    for g in groups:
                        g_tile = pair_tile(gh, g, half_, zp)
                        o_tile = pair_tile(oh, g, half_, zp)
                        delta[g, p] = jnp.sum(g_tile * o_tile, axis=0, keepdims=True)
                        set_padded(qt, g, p, pair_tile(qh, g, half_, zp), key_slot(g)[1])
                        set_padded(dot_, g, p, g_tile, value_slot(g)[1])

            def step(t, _):
                p, j, zz, yy, late, edge = walk(t, y, cn)

                def run(masked):
                    seen = visible(p, j, y, w, cn, wn, rows) if masked else None
                    blocks = [key_block(kvg, zz, yy, late, rows, b) for b in range(KV_LANES // WIDE)]
                    sums = [None] * len(blocks)

                    def put(b, v):
                        sums[b] = v if sums[b] is None else sums[b] + v

                    for g in groups:
                        s = jnp.dot(blocks[key_slot(g)[0]], qt[g, p], preferred_element_type=f32)
                        if masked:
                            s = jnp.where(seen, s, NEG)
                        e = jnp.exp(s - lse_ref[g, p])
                        dp = jnp.dot(blocks[value_slot(g)[0]], dot_[g, p], preferred_element_type=f32)
                        ds = (e * (dp - delta[g, p])).astype(b16)
                        put(value_slot(g)[0], nt(e.astype(b16), dot_[g, p]))
                        put(key_slot(g)[0], nt(ds, qt[g, p]))
                        dq[g, p] += jnp.dot(kt[j, g], ds, preferred_element_type=f32)
                    for b, v in enumerate(sums):
                        dkv[zz, yy, :, :, pl.ds(late, rows), WIDE * b : WIDE * b + WIDE] += v.reshape(
                            2, 2, rows, WIDE
                        )

                pl.when(edge)(lambda: run(True))
                pl.when(jnp.logical_not(edge))(lambda: run(False))
                return 0

            attend = portions(step, STEPS, BACK_PARTS)
            for s in range(2, 2 + n_back):
                stage_step(order, SUM_STAGES, s, attend)
            attend(True)

            def pack(i, _):
                for yy in range(2):
                    for xx in range(2):
                        kb[0][i, yy, xx] = dkv[i, yy, xx, k].astype(b16)
                        give[i, yy, xx] = dkv[i, yy, xx, 1 - k].astype(b16)
                return 0

            lax.fori_loop(0, zn, pack, 0)
            kvx.stage(0)
            unpair(lambda g, p: dq[g, p] * scale, dqh)
            dx.start()

        stat = (HALF_GROUPS, 4, 1, PER * WIDE)
        tile = (HALF_GROUPS, 4, WIDE, PER * WIDE)
        pl.run_scoped(
            attention_back,
            pltpu.VMEM(kvg_ref.shape, b16),
            pltpu.VMEM(qh_ref.shape, b16),
            pltpu.VMEM(tile, b16),
            pltpu.VMEM(tile, b16),
            pltpu.VMEM((2 * cn, HALF_GROUPS, HEAD_SIZE, wn * rows), b16),
            pltpu.VMEM(stat, f32),
            pltpu.VMEM((HALF_GROUPS, 4, HEAD_SIZE, PER * WIDE), f32),
            pltpu.VMEM((zn, 2, 2, 2, tokens, KV_LANES), f32),
        )

        def rope_back():
            low_lanes = lax.broadcasted_iota(jnp.int32, (tokens, WIDE), 1) < HEAD_SIZE
            quarter = HEAD_SIZE // 2

            def back(t, kind):
                if kind == "still":
                    return t
                cos, low, high = tab[0], tab[1], tab[2]
                r = t * cos - pltpu.roll(t, WIDE - quarter, 1) * low - pltpu.roll(t, quarter, 1) * high
                return r if kind == "turn" else jnp.where(low_lanes, r, t)

            def heads_block(mb, at):
                n = max(0, min(WIDE, mine - at))
                parts = []
                if n:
                    parts.append(dq_in[2 * mb, at : at + n, :].astype(f32))
                if n < WIDE:
                    lo = at + n - mine
                    parts.append(dq_in[2 * mb + 1, lo : lo + WIDE - n, :].astype(f32))
                return parts[0] if len(parts) == 1 else jnp.concatenate(parts, axis=0)

            kinds = ["turn", "mixed", "still"]
            for mb in range(mbs):
                at = slice(mb * tokens, (mb + 1) * tokens)
                for hh in range(2):
                    for b in range(KV_LANES // WIDE):
                        t = dkv_in[2 * mb + hh, :, WIDE * b : WIDE * b + WIDE].astype(f32)
                        lo = hh * KV_LANES + WIDE * b
                        gq[at, lo : lo + WIDE] = back(t, kinds[b]).astype(b16)
                for b in range(q_rows // WIDE):
                    t = heads_block(mb, WIDE * b).T
                    lo = 2 * KV_LANES + WIDE * b
                    gq[at, lo : lo + WIDE] = back(t, "turn").astype(b16)

        def gains_and_input(w_s, r_s, order_s, x_s, gx_s, ghn, low):
            moves = [
                pltpu.make_async_copy(src, dst, loads.at[i])
                for i, (src, dst) in enumerate(
                    [(w_ref, w_s), (r_ref, r_s), (order_ref, order_s), (x_ref, x_s), (gx1_ref, gx_s)]
                )
            ]
            for c in moves:
                c.start()
            wa = w_s.shape[0]
            chips = [device(z, y, x, 1 - k), device(z, y, 1 - x, k), device(z, 1 - y, x, k)]
            steps = [remote(total, got.at[i], gs.at[i], gr.at[i], chips[i]) for i in range(3)]
            ends = [
                remote(total, got.at[2 + j], gs.at[2 + j], gr.at[2 + j], device(lax.rem(z + j, zn), y, x, k))
                for j in range(1, zn)
            ]

            def first():
                for c in moves:
                    c.wait()
                ghn[:, :wa] = nt(gq[...], w_s[...])
                ghn[:, wa:] = nt(gq[...], r_s[...])

            def second():
                xf, inv, grad = x_s[...].astype(f32), inv_ref[...], ghn[...]
                total[...] = jnp.zeros(total.shape, f32)
                total[0:1, :] = jnp.sum(grad * xf * inv, axis=0, keepdims=True)
                total[1:2, :] = gain2_ref[...]
                steps[0].start()
                weighted = grad * gain_ref[0:1, :]
                inner = jnp.mean(weighted * xf, axis=-1, keepdims=True)
                low[...] = (gx_s[...] + inv * weighted - xf * (inv * inv * inv) * inner).astype(b16)

            def add(i):
                steps[i].wait()
                total[...] = total[...] + got[i]
                for c in [steps[i + 1]] if i < 2 else ends:
                    c.start()

            def third():
                input_grad[...] = jnp.dot(low[...], order_s[...], preferred_element_type=f32).astype(b16)

            jobs = [first, second, lambda: (add(0), third()), lambda: add(1), lambda: add(2)]
            kv_stage = 1
            for s in range(2 + n_back, len(order) + SUM_STAGES[-1]):
                if s == at_qkv:
                    while kv_stage < 5:
                        kvx.stage(kv_stage)
                        kv_stage += 1
                    dx.arrived()
                    rope_back()
                    gq_share.start()
                    gq_share.ready()
                stage_step(order, SUM_STAGES, s)
                if kv_stage < 4:
                    kvx.stage(kv_stage)
                    kv_stage += 1
                if s >= at_qkv and jobs:
                    jobs.pop(0)()
            for job in jobs:
                job()
            for c in ends:
                c.wait()
            t = total[...]
            for j in range(1, zn):
                t = t + got[2 + j]
            total[...] = t

        pl.run_scoped(
            gains_and_input,
            pltpu.VMEM(w_ref.shape, b16),
            pltpu.VMEM(r_ref.shape, b16),
            pltpu.VMEM(order_ref.shape, b16),
            pltpu.VMEM(x_ref.shape, b16),
            pltpu.VMEM(gx1_ref.shape, f32),
            pltpu.VMEM(gx1_ref.shape, f32),
            pltpu.VMEM(x_ref.shape, b16),
        )
        dx.sent()
        gx.sent()
        gq_share.sent()
        for i in share:
            i.sent()

    block = (zn, mine, tokens)
    any_ = pl.BlockSpec(memory_space=pl.ANY)
    vmem = pl.BlockSpec(memory_space=pltpu.VMEM)
    dma = pltpu.SemaphoreType.DMA
    return pl.pallas_call(
        kernel,
        out_shape=[jax.ShapeDtypeStruct(s, f32) for s in outs_shape]
        + [jax.ShapeDtypeStruct((all_rows, width), b16), jax.ShapeDtypeStruct((8, width), f32)],
        in_specs=[any_, any_, any_, any_, vmem, vmem]
        + [any_] * n_in
        + [any_, any_, any_, vmem, vmem, any_, vmem, any_],
        out_specs=[vmem] * (n_out + 2),
        scratch_shapes=scratch
        + shares
        + [
            pltpu.VMEM((ring, zn, 2, 2, ra, max_cols), b16),
            pltpu.VMEM((all_rows, qkv_w), b16),
            pltpu.VMEM((all_rows, qkv_w), b16),
            pltpu.VMEM((zn, tokens, KV_LANES), b16),
            pltpu.VMEM(block, b16),
            pltpu.VMEM(block, b16),
            pltpu.VMEM((zn, 2, 2, tokens, KV_LANES), b16),
            pltpu.VMEM((2 + zn, 8, width), f32),
        ]
        + Scatter.scratch(zn, tokens, KV_LANES)[:4]
        + [
            dma((n_items, Sum.SEMS)),
            dma((n_items, Sum.SEMS)),
            dma((n_in + 1,)),
            dma((n_in + 1,)),
            dma((n_in + 1,)),
            dma((2, zn)),
            dma((2, zn)),
            dma((Scatter.SEMS,)),
            dma((Scatter.SEMS,)),
            dma((2 + zn,)),
            dma((2 + zn,)),
            dma((5,)),
        ],
        compiler_params=pltpu.CompilerParams(
            collective_id=collective_id, has_side_effects=True, vmem_limit_bytes=VMEM_LIMIT
        ),
    )(do, qh, kvg, oh, lse, tables, *ins_all, *last)


def ffn(o_t, x, gy, gain, order_t, out_a, gate_a, up_a, down, rest):
    f32, b16 = jnp.float32, jnp.bfloat16
    mbs, width, tokens = o_t.shape
    rows = mbs * tokens
    ff = gate_a.shape[1]
    wa = out_a.shape[0]
    wb = width - wa
    rb = wb * 16 // rest.shape[0]
    chunk = 4 * WIDE

    def kernel(o_ref, x_ref, gy_ref, gain_ref, order_hbm, out_hbm, gate_hbm, up_hbm, down_hbm, rest_hbm,
               y_ref, gx1_ref, gb_ref, gg_ref, gu_ref, act_ref, h2_ref, h2b_ref, op_ref, opb_ref, go_ref, gain_sum,
               order_s, out_s, gate_s, up_s, down_s, rest_s, wide, x1, h2, acc, gh, sems):
        loads = [
            pltpu.make_async_copy(src, dst, sems.at[i])
            for i, (src, dst) in enumerate(
                [(order_hbm, order_s), (rest_hbm, rest_s), (out_hbm, out_s), (gate_hbm, gate_s), (up_hbm, up_s), (down_hbm, down_s)]
            )
        ]
        for c in loads:
            c.start()
        loads[0].wait()
        for mb in range(mbs):
            at = slice(mb * tokens, (mb + 1) * tokens)
            t = jnp.dot(order_s[...], o_ref[mb], preferred_element_type=f32)
            op_ref[:, at] = t[:wa].astype(b16)
            opb_ref[:, at] = t[wa:].astype(b16)
            h2[at, :] = transposed_rows(t).astype(b16)
        loads[1].wait()
        unfold_rows(rest_s, wide, rb)
        loads[2].wait()
        x1[...] = (
            x_ref[...].astype(f32)
            + jnp.dot(h2[:, :wa], out_s[...], preferred_element_type=f32)
            + jnp.dot(h2[:, wa:], wide[:, :width], preferred_element_type=f32)
        )
        u = x1[...]
        inv = lax.rsqrt(jnp.mean(u * u, axis=-1, keepdims=True) + EPSILON)
        hidden = u * inv * gain_ref[1:2, :]
        h2[...] = hidden.astype(b16)
        h2_ref[...] = transposed(hidden[:, :wa]).astype(b16)
        h2b_ref[...] = transposed(hidden[:, wa:]).astype(b16)
        acc[...] = jnp.zeros(acc.shape, f32)
        gh[...] = jnp.zeros(gh.shape, f32)
        for c in loads[3:]:
            c.wait()

        def one(i, _):
            at = pl.multiple_of(i * chunk, WIDE)
            cols = pl.ds(at, chunk)
            gcols, ucols = pl.ds(width + at, chunk), pl.ds(width + ff + at, chunk)
            ha, hb = h2[:, :wa], h2[:, wa:]
            gate = jnp.dot(ha, gate_s[:, cols], preferred_element_type=f32) + jnp.dot(
                hb, wide[:, gcols], preferred_element_type=f32
            )
            up = jnp.dot(ha, up_s[:, cols], preferred_element_type=f32) + jnp.dot(
                hb, wide[:, ucols], preferred_element_type=f32
            )
            ga = nt(gy_ref[...], down_s[cols, :])
            sig = jax.nn.sigmoid(gate)
            silu = gate * sig
            act = silu * up
            g_gate = (ga * up * sig * (1.0 + gate * (1.0 - sig))).astype(b16)
            g_up = (ga * silu).astype(b16)
            gg_ref[:, cols] = g_gate
            gu_ref[:, cols] = g_up
            act_ref[cols, :] = transposed(act).astype(b16)
            acc[...] += jnp.dot(act.astype(b16), down_s[cols, :], preferred_element_type=f32)
            gh[:, :wa] += nt(g_gate, gate_s[:, cols]) + nt(g_up, up_s[:, cols])
            gh[:, wa:] += nt(g_gate, wide[:, gcols]) + nt(g_up, wide[:, ucols])
            return 0

        lax.fori_loop(0, ff // chunk, one, 0)
        y = (x1[...] + acc[...]).astype(b16)
        y_ref[...] = jnp.dot(y, order_s[...], preferred_element_type=f32).astype(b16)
        u = x1[...]
        inv = lax.rsqrt(jnp.mean(u * u, axis=-1, keepdims=True) + EPSILON)
        grad = gh[...]
        gain_sum[...] = jnp.sum(grad * u * inv, axis=0, keepdims=True)
        weighted = grad * gain_ref[1:2, :]
        inner = jnp.mean(weighted * u, axis=-1, keepdims=True)
        gx1 = inv * weighted - u * (inv * inv * inv) * inner + gy_ref[...].astype(f32)
        gx1_ref[...] = gx1
        gb = gx1.astype(b16)
        gb_ref[...] = jnp.dot(gb, order_s[...], preferred_element_type=f32).astype(b16)
        h2[:, :wa] = nt(gb, out_s[...]).astype(b16)
        h2[:, wa:] = nt(gb, wide[:, :width]).astype(b16)
        go = jnp.dot(h2[...], order_s[...], preferred_element_type=f32)
        for mb in range(mbs):
            go_ref[mb] = transposed(go[mb * tokens : (mb + 1) * tokens]).astype(b16)

    def transposed_rows(t):
        return jnp.concatenate([t[i : i + WIDE].T for i in range(0, t.shape[0], WIDE)], axis=1)

    any_ = pl.BlockSpec(memory_space=pl.ANY)
    vmem = pl.BlockSpec(memory_space=pltpu.VMEM)
    sds = jax.ShapeDtypeStruct
    return pl.pallas_call(
        kernel,
        out_shape=[
            sds((rows, width), b16),
            sds((rows, width), f32),
            sds((rows, width), b16),
            sds((rows, ff), b16),
            sds((rows, ff), b16),
            sds((ff, rows), b16),
            sds((wa, rows), b16),
            sds((wb, rows), b16),
            sds((wa, rows), b16),
            sds((wb, rows), b16),
            sds(o_t.shape, b16),
            sds((1, width), f32),
        ],
        in_specs=[vmem] * 4 + [any_] * 6,
        out_specs=[vmem] * 12,
        scratch_shapes=[
            pltpu.VMEM(order_t.shape, b16),
            pltpu.VMEM(out_a.shape, b16),
            pltpu.VMEM(gate_a.shape, b16),
            pltpu.VMEM(up_a.shape, b16),
            pltpu.VMEM(down.shape, b16),
            pltpu.VMEM(rest.shape, b16),
            pltpu.VMEM((wb, 16 // rb * rest.shape[1]), b16),
            pltpu.VMEM((rows, width), f32),
            pltpu.VMEM((rows, width), b16),
            pltpu.VMEM((rows, width), f32),
            pltpu.VMEM((rows, width), f32),
            pltpu.SemaphoreType.DMA((6,)),
        ],
        compiler_params=pltpu.CompilerParams(vmem_limit_bytes=VMEM_LIMIT),
    )(o_t, x, gy, gain, order_t, out_a, gate_a, up_a, down, rest)


def lane_tables(positions):
    quarter = HEAD_SIZE // 2
    frequency = 10000.0 ** (-2.0 * jnp.arange(quarter, dtype=jnp.float32) / HEAD_SIZE)
    angles = positions.astype(jnp.float32)[:, None] * frequency[None, :]
    cos, sin = jnp.cos(angles), jnp.sin(angles)
    none = jnp.zeros_like(sin)
    full = lambda a, b: jnp.concatenate([a, b, a, b], axis=1)
    return jnp.stack([full(cos, cos), full(-sin, none), full(none, sin)])


def fast_device(
    inputs,
    attn_gain,
    query_weight,
    key_matrix,
    value_matrix,
    out_weight,
    ffn_gain,
    gate_weight,
    up_weight,
    down_weight,
    cotangent,
):
    f32, b16 = jnp.float32, jnp.bfloat16
    cn, wn = lax.axis_size("ctx"), lax.axis_size("ws")
    dn = cn * wn
    zn = cn // 2
    mbs, tokens, width = inputs.shape
    own = query_weight.shape[0]
    ra = own // 16 * 16
    rb = own - ra
    q_width = query_weight.shape[1]
    hid = KEY_VALUE_HEADS * HEAD_SIZE
    ff = gate_weight.shape[1]
    rows = mbs * tokens
    wa = dn * ra

    fold = 16 // rb

    def folded(t):
        return t.reshape(t.shape[0], fold, -1).transpose(1, 0, 2).reshape(16, -1)

    qkv_w = q_width + 2 * hid
    pad1 = -qkv_w % (fold * WIDE)
    rest_w = width + 2 * ff
    pad2 = -rest_w % (fold * WIDE)
    half_hid = hid // 2
    qkv = jnp.concatenate(
        [
            key_matrix[:, :half_hid],
            value_matrix[:, :half_hid],
            key_matrix[:, half_hid:],
            value_matrix[:, half_hid:],
            query_weight,
        ],
        axis=1,
    )
    gains = jnp.stack([attn_gain, ffn_gain])
    gains = jnp.pad(gains, ((0, rb - 2), (0, pad1 - own)))
    b1 = folded(jnp.concatenate([qkv[ra:], gains], axis=1))
    flat = lambda t: t.reshape(-1, t.shape[-1])
    c, w = lax.axis_index("ctx"), lax.axis_index("ws")
    tables = lane_tables(query_places(c, w, tokens, cn, wn))
    (x_low, gy_low, order_t, o_t, qh, kvg, oh, lse, qkv_a, qkv_b, hn_t, hn_bt, inv1, gains, out_a, gate_a, up_a, down_a, b2g) = gather_attend(
        inputs.reshape(rows, width),
        cotangent.reshape(rows, width),
        tables,
        qkv,
        b1,
        [out_weight, gate_weight, up_weight, down_weight],
        GATHER_CUTS,
        2,
    )
    qkv_a, out_a, gate_a, up_a, down_w = map(flat, (qkv_a, out_a, gate_a, up_a, down_a))
    out, gx1, gb_plain, g_gate, g_up, act_t, h2_t, h2_bt, o_pt, o_pbt, go_t, gain2_sum = ffn(
        o_t, x_low, gy_low, gains, order_t, out_a, gate_a, up_a, down_w, flat(b2g)
    )
    gy_plain = cotangent.reshape(rows, width)
    left = lambda t: t.reshape(zn, 2, 2, 2, -1, rows)
    r_down, r_gate, r_up, r_out, r_b2, r_qkv, r_b1, input_grad, gain_sums = scatter_attend(
        go_t,
        qh,
        kvg,
        oh,
        lse,
        tables,
        [left(act_t), left(h2_t), left(o_pt), left(hn_t)],
        [h2_bt, o_pbt, hn_bt],
        [gy_plain, gb_plain, g_gate, g_up],
        ((rest_w + pad2) // fold, (qkv_w + pad1) // fold),
        [qkv_a, qkv_b, x_low, inv1, gains, gx1, gain2_sum, order_t],
        3,
    )
    device_at = c * wn + w

    def own_gain(t):
        first = lax.dynamic_slice(t, (device_at * ra,), (ra,))
        return jnp.concatenate([first, lax.dynamic_slice(t, (wa + device_at * rb,), (rb,))])

    def own_rows(t):
        return t.reshape(fold, rb, -1).transpose(1, 0, 2).reshape(rb, -1)

    e1, e2 = own_rows(r_b1), own_rows(r_b2)
    whole = lambda a, b: jnp.concatenate([a, b], axis=0)
    d_qkv = whole(r_qkv, e1[:, :qkv_w])
    return (
        out.reshape(inputs.shape),
        input_grad.reshape(inputs.shape),
        own_gain(gain_sums[0]),
        d_qkv[:, 2 * hid :],
        jnp.concatenate([d_qkv[:, :half_hid], d_qkv[:, hid : hid + half_hid]], axis=1),
        jnp.concatenate([d_qkv[:, half_hid:hid], d_qkv[:, hid + half_hid : 2 * hid]], axis=1),
        whole(r_out, e2[:, :width]),
        own_gain(gain_sums[1]),
        whole(r_gate, e2[:, width : width + ff]),
        whole(r_up, e2[:, width + ff : width + 2 * ff]),
        r_down,
    )


def solution(mesh):
    in_specs = (
        P(None, ("ctx", "ws"), None),
        P(("ctx", "ws")),
        P(("ctx", "ws"), None),
        P(("ctx", "ws"), None),
        P(("ctx", "ws"), None),
        P(("ctx", "ws"), None),
        P(("ctx", "ws")),
        P(("ctx", "ws"), None),
        P(("ctx", "ws"), None),
        P(("ctx", "ws"), None),
        P(None, ("ctx", "ws"), None),
    )
    out_specs = (
        P(None, ("ctx", "ws"), None),
        P(None, ("ctx", "ws"), None),
        P(("ctx", "ws")),
        P(("ctx", "ws"), None),
        P(("ctx", "ws"), None),
        P(("ctx", "ws"), None),
        P(("ctx", "ws"), None),
        P(("ctx", "ws")),
        P(("ctx", "ws"), None),
        P(("ctx", "ws"), None),
        P(("ctx", "ws"), None),
    )
    body = fast_device if fits_fast(mesh) else per_device
    return jax.shard_map(
        body, mesh=mesh, in_specs=in_specs, out_specs=out_specs, check_vma=False
    )
```

```python
import jax
import jax.numpy as jnp
from jax import lax
from jax.experimental import pallas as pl
from jax.experimental.pallas import tpu as pltpu
from jax.sharding import PartitionSpec as P
import functools

QUERY_HEADS = 18
KEY_VALUE_HEADS = 6
HEAD_SIZE = 64


EPSILON = 1e-05
MASKED_SCORE = -1e30


def shifted(block, axis, distance):
    devices = range(lax.axis_size(axis))
    route = [((i - distance) % len(devices), i) for i in devices]
    return lax.ppermute(block, axis, route)


def as_sent(x):

    def short(part):
        return part.astype(jnp.bfloat16) if part.dtype == jnp.float32 else part

    return jax.tree.map(short, x)


def matrix_multiply(left, right):
    return jnp.dot(left, right, preferred_element_type=jnp.float32)


def outer_sum(left, right):
    return jnp.einsum("ri,rj->ij", left, right, preferred_element_type=jnp.float32)


def back_product(gradient, weight):
    return jnp.einsum("rj,ij->ri", gradient, weight, preferred_element_type=jnp.float32)


def normalize(layer_rows, gain_vector):
    inverse = lax.rsqrt(jnp.mean(layer_rows * layer_rows, axis=-1, keepdims=True) + EPSILON)
    return (layer_rows * inverse * gain_vector, inverse)


def normalize_back(layer_rows, inverse, gain_vector, gradient):
    weighted = gradient * gain_vector
    inner_mean = jnp.mean(weighted * layer_rows, axis=-1, keepdims=True)
    row_grad = inverse * weighted - layer_rows * (inverse * inverse * inverse) * inner_mean
    gain_grad = jnp.sum(gradient * layer_rows * inverse, axis=0)
    return (row_grad, gain_grad)


def rotary_tables(token_positions):
    quarter = HEAD_SIZE // 2
    frequency = 10000.0 ** (-2.0 * jnp.arange(quarter, dtype=jnp.float32) / HEAD_SIZE)
    angles = token_positions.astype(jnp.float32)[:, None] * frequency[None, :]
    return (jnp.cos(angles)[:, None, :], jnp.sin(angles)[:, None, :])


def rotate(heads, cosine_table, sine_table):
    quarter = HEAD_SIZE // 2
    first_half = heads[..., :quarter]
    second_half = heads[..., quarter:]
    return jnp.concatenate(
        [
            first_half * cosine_table - second_half * sine_table,
            second_half * cosine_table + first_half * sine_table,
        ],
        axis=-1,
    )


def rotate_back(heads, cosine_table, sine_table):
    quarter = HEAD_SIZE // 2
    first_half = heads[..., :quarter]
    second_half = heads[..., quarter:]
    return jnp.concatenate(
        [
            first_half * cosine_table + second_half * sine_table,
            second_half * cosine_table - first_half * sine_table,
        ],
        axis=-1,
    )


def query_places(own_ctx, own_member, count_of_rows, ctx_count, device_count):
    rows_per_half = count_of_rows // 2
    local_index = jnp.arange(count_of_rows, dtype=jnp.int32)
    span_index = jnp.where(local_index < rows_per_half, own_ctx, 2 * ctx_count - 1 - own_ctx)
    return (
        span_index * (device_count * rows_per_half)
        + own_member * rows_per_half
        + local_index % rows_per_half
    )


def block_places(source_ctx, count_of_rows, ctx_count, device_count):
    rows_per_half = count_of_rows // 2
    member_index = jnp.arange(device_count, dtype=jnp.int32)[:, None, None]
    half_index = jnp.arange(2, dtype=jnp.int32)[None, :, None]
    inner_index = jnp.arange(rows_per_half, dtype=jnp.int32)[None, None, :]
    span_index = jnp.where(half_index == 0, source_ctx, 2 * ctx_count - 1 - source_ctx)
    return (
        span_index * (device_count * rows_per_half) + member_index * rows_per_half + inner_index
    ).reshape(-1)


def split_block(block_of_keys):
    hidden_width = KEY_VALUE_HEADS * HEAD_SIZE
    device_count, _, rows_per_half, _ = block_of_keys.shape
    rows_of_keys = block_of_keys[..., :hidden_width].reshape(
        device_count, 2, rows_per_half, KEY_VALUE_HEADS, HEAD_SIZE
    )
    rows_of_values = block_of_keys[..., hidden_width:].reshape(
        device_count, 2, rows_per_half, KEY_VALUE_HEADS, HEAD_SIZE
    )
    return (rows_of_keys, rows_of_values)


def attend(query_rows, rows_of_keys, rows_of_values, causal_visible):
    scores = jnp.einsum(
        "rgjd,kgd->grjk", query_rows, rows_of_keys, preferred_element_type=jnp.float32
    ) * HEAD_SIZE ** (-0.5)
    if causal_visible is not None:
        scores = jnp.where(causal_visible[None, :, None, :], scores, MASKED_SCORE)
    row_max = jnp.max(scores, axis=-1)
    exponentials = jnp.exp(scores - row_max[..., None])
    row_total = jnp.sum(exponentials, axis=-1)
    mixture = jnp.einsum(
        "grjk,kgd->rgjd",
        exponentials.astype(jnp.bfloat16),
        rows_of_values,
        preferred_element_type=jnp.float32,
    )
    return (jnp.transpose(row_max, (1, 0, 2)), jnp.transpose(row_total, (1, 0, 2)), mixture)


def empty_part(count_of_rows):
    queries_per_group = QUERY_HEADS // KEY_VALUE_HEADS
    return (
        jnp.full((count_of_rows, KEY_VALUE_HEADS, queries_per_group), MASKED_SCORE, jnp.float32),
        jnp.zeros((count_of_rows, KEY_VALUE_HEADS, queries_per_group), jnp.float32),
        jnp.zeros((count_of_rows, KEY_VALUE_HEADS, queries_per_group, HEAD_SIZE), jnp.float32),
    )


def combine(carried, incoming):
    carried_max, carried_total, carried_mix = carried
    incoming_max, incoming_total, incoming_mix = incoming
    new_max = jnp.maximum(carried_max, incoming_max)
    carried_scale = jnp.exp(carried_max - new_max)
    incoming_scale = jnp.exp(incoming_max - new_max)
    return (
        new_max,
        carried_total * carried_scale + incoming_total * incoming_scale,
        carried_mix * carried_scale[..., None] + incoming_mix * incoming_scale[..., None],
    )


def forward_block(carried, block_of_keys, source_ctx, own_ctx, query_rows, own_places, ctx_count):
    rows_of_keys, rows_of_values = split_block(block_of_keys)
    device_count, _, rows_per_half, _ = block_of_keys.shape

    def forward_earlier():
        return attend(
            query_rows,
            rows_of_keys[:, 0].reshape(-1, KEY_VALUE_HEADS, HEAD_SIZE),
            rows_of_values[:, 0].reshape(-1, KEY_VALUE_HEADS, HEAD_SIZE),
            None,
        )

    def forward_later():
        late_part = attend(
            query_rows[rows_per_half:],
            rows_of_keys.reshape(-1, KEY_VALUE_HEADS, HEAD_SIZE),
            rows_of_values.reshape(-1, KEY_VALUE_HEADS, HEAD_SIZE),
            None,
        )
        early_part = empty_part(rows_per_half)
        return tuple(
            (
                jnp.concatenate([early_piece, late_piece], axis=0)
                for early_piece, late_piece in zip(early_part, late_part)
            )
        )

    def forward_diagonal():
        key_places = block_places(source_ctx, 2 * rows_per_half, ctx_count, device_count)
        causal_visible = own_places[:, None] >= key_places[None, :]
        return attend(
            query_rows,
            rows_of_keys.reshape(-1, KEY_VALUE_HEADS, HEAD_SIZE),
            rows_of_values.reshape(-1, KEY_VALUE_HEADS, HEAD_SIZE),
            causal_visible,
        )

    branch_index = jnp.where(source_ctx == own_ctx, 2, jnp.where(source_ctx > own_ctx, 1, 0))
    return combine(
        carried, lax.switch(branch_index, [forward_earlier, forward_later, forward_diagonal])
    )


def attend_back(
    query_rows, attended_grad, log_total, delta_rows, rows_of_keys, rows_of_values, causal_visible
):
    scores = jnp.einsum(
        "rgjd,kgd->grjk", query_rows, rows_of_keys, preferred_element_type=jnp.float32
    ) * HEAD_SIZE ** (-0.5)
    if causal_visible is not None:
        scores = jnp.where(causal_visible[None, :, None, :], scores, MASKED_SCORE)
    probabilities = jnp.exp(scores - jnp.transpose(log_total, (1, 0, 2))[..., None])
    prob_grad = jnp.einsum(
        "rgjd,kgd->grjk", attended_grad, rows_of_values, preferred_element_type=jnp.float32
    )
    score_grad = (
        probabilities * (prob_grad - jnp.transpose(delta_rows, (1, 0, 2))[..., None])
    ).astype(jnp.bfloat16)
    query_part = jnp.einsum(
        "grjk,kgd->rgjd", score_grad, rows_of_keys, preferred_element_type=jnp.float32
    ) * HEAD_SIZE ** (-0.5)
    key_part = jnp.einsum(
        "grjk,rgjd->kgd", score_grad, query_rows, preferred_element_type=jnp.float32
    ) * HEAD_SIZE ** (-0.5)
    value_part = jnp.einsum(
        "grjk,rgjd->kgd",
        probabilities.astype(jnp.bfloat16),
        attended_grad,
        preferred_element_type=jnp.float32,
    )
    return (query_part, key_part, value_part)


def backward_block(
    block_of_keys,
    source_ctx,
    own_ctx,
    query_rows,
    attended_grad,
    log_total,
    delta_rows,
    own_places,
    ctx_count,
):
    rows_of_keys, rows_of_values = split_block(block_of_keys)
    device_count, _, rows_per_half, _ = block_of_keys.shape
    hidden_width = KEY_VALUE_HEADS * HEAD_SIZE

    def backward_earlier():
        query_part, key_part, value_part = attend_back(
            query_rows,
            attended_grad,
            log_total,
            delta_rows,
            rows_of_keys[:, 0].reshape(-1, KEY_VALUE_HEADS, HEAD_SIZE),
            rows_of_values[:, 0].reshape(-1, KEY_VALUE_HEADS, HEAD_SIZE),
            None,
        )
        early_grad = jnp.concatenate(
            [
                key_part.reshape(device_count, 1, rows_per_half, hidden_width),
                value_part.reshape(device_count, 1, rows_per_half, hidden_width),
            ],
            axis=-1,
        )
        return (query_part, jnp.concatenate([early_grad, jnp.zeros_like(early_grad)], axis=1))

    def backward_later():
        query_part, key_part, value_part = attend_back(
            query_rows[rows_per_half:],
            attended_grad[rows_per_half:],
            log_total[rows_per_half:],
            delta_rows[rows_per_half:],
            rows_of_keys.reshape(-1, KEY_VALUE_HEADS, HEAD_SIZE),
            rows_of_values.reshape(-1, KEY_VALUE_HEADS, HEAD_SIZE),
            None,
        )
        query_part = jnp.concatenate([jnp.zeros_like(query_part), query_part], axis=0)
        return (
            query_part,
            jnp.concatenate(
                [
                    key_part.reshape(device_count, 2, rows_per_half, hidden_width),
                    value_part.reshape(device_count, 2, rows_per_half, hidden_width),
                ],
                axis=-1,
            ),
        )

    def backward_diagonal():
        key_places = block_places(source_ctx, 2 * rows_per_half, ctx_count, device_count)
        causal_visible = own_places[:, None] >= key_places[None, :]
        query_part, key_part, value_part = attend_back(
            query_rows,
            attended_grad,
            log_total,
            delta_rows,
            rows_of_keys.reshape(-1, KEY_VALUE_HEADS, HEAD_SIZE),
            rows_of_values.reshape(-1, KEY_VALUE_HEADS, HEAD_SIZE),
            causal_visible,
        )
        return (
            query_part,
            jnp.concatenate(
                [
                    key_part.reshape(device_count, 2, rows_per_half, hidden_width),
                    value_part.reshape(device_count, 2, rows_per_half, hidden_width),
                ],
                axis=-1,
            ),
        )

    branch_index = jnp.where(source_ctx == own_ctx, 2, jnp.where(source_ctx > own_ctx, 1, 0))
    return lax.switch(branch_index, [backward_earlier, backward_later, backward_diagonal])


def per_device(
    inputs,
    attn_gain,
    query_weight,
    key_matrix,
    value_matrix,
    out_weight,
    ffn_gain,
    gate_weight,
    up_weight,
    down_weight,
    cotangent,
):
    ctx_count = lax.axis_size("ctx")
    device_count = lax.axis_size("ws")
    own_ctx = lax.axis_index("ctx")
    own_member = lax.axis_index("ws")
    micro_count, count_of_rows, _ = inputs.shape
    rows_per_half = count_of_rows // 2
    queries_per_group = QUERY_HEADS // KEY_VALUE_HEADS
    hidden_width = KEY_VALUE_HEADS * HEAD_SIZE
    own_places = query_places(own_ctx, own_member, count_of_rows, ctx_count, device_count)
    cosine_table, sine_table = rotary_tables(own_places)
    grad_sums = None
    layer_outs = []
    input_grads = []
    for micro_batch in range(micro_count):
        gathered = (
            lax.all_gather(attn_gain, ("ctx", "ws"), axis=0, tiled=True),
            lax.all_gather(query_weight, ("ctx", "ws"), axis=0, tiled=True),
            lax.all_gather(key_matrix, ("ctx", "ws"), axis=0, tiled=True),
            lax.all_gather(value_matrix, ("ctx", "ws"), axis=0, tiled=True),
            lax.all_gather(out_weight, ("ctx", "ws"), axis=0, tiled=True),
            lax.all_gather(ffn_gain, ("ctx", "ws"), axis=0, tiled=True),
            lax.all_gather(gate_weight, ("ctx", "ws"), axis=0, tiled=True),
            lax.all_gather(up_weight, ("ctx", "ws"), axis=0, tiled=True),
            lax.all_gather(down_weight, ("ctx", "ws"), axis=0, tiled=True),
        )
        (
            full_attn_gain,
            full_query,
            complete_key,
            full_value,
            full_out,
            full_ffn_gain,
            full_gate,
            full_up,
            full_down,
        ) = gathered
        first_gain = full_attn_gain.astype(jnp.float32)
        second_gain = full_ffn_gain.astype(jnp.float32)
        layer_rows = inputs[micro_batch].astype(jnp.float32)
        normalized_rows, first_inverse = normalize(layer_rows, first_gain)
        normalized_reduced = normalized_rows.astype(jnp.bfloat16)
        query_rows = rotate(
            matrix_multiply(normalized_reduced, full_query).reshape(
                count_of_rows, QUERY_HEADS, HEAD_SIZE
            ),
            cosine_table,
            sine_table,
        )
        query_rows = query_rows.astype(jnp.bfloat16).reshape(
            count_of_rows, KEY_VALUE_HEADS, queries_per_group, HEAD_SIZE
        )
        rows_of_keys = rotate(
            matrix_multiply(normalized_reduced, complete_key).reshape(
                count_of_rows, KEY_VALUE_HEADS, HEAD_SIZE
            ),
            cosine_table,
            sine_table,
        ).astype(jnp.bfloat16)
        rows_of_values = matrix_multiply(normalized_reduced, full_value).astype(jnp.bfloat16)
        local_block = jnp.concatenate(
            [rows_of_keys.reshape(count_of_rows, hidden_width), rows_of_values], axis=-1
        )
        group_block = lax.all_gather(local_block, "ws", axis=0, tiled=True).reshape(
            device_count, 2, rows_per_half, 2 * hidden_width
        )

        def fold_step(carried, shard_piece):

            def visit_block(state_now, block_entry):
                block_of_keys, source_ctx = block_entry
                return (
                    forward_block(
                        state_now,
                        block_of_keys,
                        source_ctx,
                        own_ctx,
                        query_rows,
                        own_places,
                        ctx_count,
                    ),
                    None,
                )

            source_list = jnp.arange(shard_piece.shape[0], dtype=jnp.int32)
            result_state, _ = lax.scan(visit_block, carried, (shard_piece, source_list))
            return result_state

        row_max, row_total, mixture = fold_step(
            empty_part(count_of_rows), lax.all_gather(group_block[None], "ctx", axis=0, tiled=True)
        )
        attended = mixture / row_total[..., None]
        log_total = row_max + jnp.log(row_total)
        attended_low = attended.astype(jnp.bfloat16).reshape(count_of_rows, QUERY_HEADS * HEAD_SIZE)
        middle = layer_rows + matrix_multiply(attended_low, full_out)
        hidden, second_inverse = normalize(middle, second_gain)
        hidden_low = hidden.astype(jnp.bfloat16)
        gate_rows = matrix_multiply(hidden_low, full_gate)
        up_rows = matrix_multiply(hidden_low, full_up)
        sigmoid_gate = jax.nn.sigmoid(gate_rows)
        silu_gate = gate_rows * sigmoid_gate
        activated = (silu_gate * up_rows).astype(jnp.bfloat16)
        layer_outs.append((middle + matrix_multiply(activated, full_down)).astype(jnp.bfloat16))
        upstream_low = cotangent[micro_batch]
        upstream = upstream_low.astype(jnp.float32)
        down_sum = outer_sum(activated, upstream_low)
        act_grad = back_product(upstream_low, full_down)
        gate_low = (
            act_grad * up_rows * sigmoid_gate * (1.0 + gate_rows * (1.0 - sigmoid_gate))
        ).astype(jnp.bfloat16)
        up_low = (act_grad * silu_gate).astype(jnp.bfloat16)
        gate_sum = outer_sum(hidden_low, gate_low)
        up_sum = outer_sum(hidden_low, up_low)
        hidden_grad = back_product(gate_low, full_gate) + back_product(up_low, full_up)
        middle_part, ffn_gain_sum = normalize_back(middle, second_inverse, second_gain, hidden_grad)
        middle_grad = middle_part + upstream
        branch_low = middle_grad.astype(jnp.bfloat16)
        out_sum = outer_sum(attended_low, branch_low)
        attended_grad = (
            back_product(branch_low, full_out)
            .reshape(count_of_rows, KEY_VALUE_HEADS, queries_per_group, HEAD_SIZE)
            .astype(jnp.bfloat16)
        )
        delta_rows = jnp.sum(attended_grad.astype(jnp.float32) * attended, axis=-1)

        def cycle_step(turn_index, carried):
            block_of_keys, block_grad, query_total = carried
            source_ctx = (own_ctx - turn_index) % ctx_count
            query_part, block_part = backward_block(
                block_of_keys,
                source_ctx,
                own_ctx,
                query_rows,
                attended_grad,
                log_total,
                delta_rows,
                own_places,
                ctx_count,
            )
            block_grad = block_grad + block_part
            next_block = shifted(block_of_keys, "ctx", 1)
            next_grad = shifted(as_sent(block_grad), "ctx", 1).astype(block_grad.dtype)
            return (next_block, next_grad, query_total + query_part)

        cycle_start = (
            group_block,
            jnp.zeros(group_block.shape, jnp.float32),
            jnp.zeros((count_of_rows, KEY_VALUE_HEADS, queries_per_group, HEAD_SIZE), jnp.float32),
        )
        _, block_grad, query_total = lax.fori_loop(0, ctx_count, cycle_step, cycle_start)
        local_gradient = (
            lax.psum_scatter(block_grad.astype(jnp.bfloat16), "ws", scatter_dimension=0, tiled=True)
            .astype(jnp.float32)
            .reshape(count_of_rows, 2 * hidden_width)
        )
        key_low = rotate_back(
            local_gradient[:, :hidden_width].reshape(count_of_rows, KEY_VALUE_HEADS, HEAD_SIZE),
            cosine_table,
            sine_table,
        )
        key_low = key_low.astype(jnp.bfloat16).reshape(count_of_rows, hidden_width)
        value_low = local_gradient[:, hidden_width:].astype(jnp.bfloat16)
        query_low = rotate_back(
            query_total.reshape(count_of_rows, QUERY_HEADS, HEAD_SIZE), cosine_table, sine_table
        )
        query_low = query_low.astype(jnp.bfloat16).reshape(count_of_rows, QUERY_HEADS * HEAD_SIZE)
        query_sum = outer_sum(normalized_reduced, query_low)
        key_sum = outer_sum(normalized_reduced, key_low)
        value_sum = outer_sum(normalized_reduced, value_low)
        normed_grad = (
            back_product(query_low, full_query)
            + back_product(key_low, complete_key)
            + back_product(value_low, full_value)
        )
        input_part, attn_gain_sum = normalize_back(
            layer_rows, first_inverse, first_gain, normed_grad
        )
        input_grads.append((middle_grad + input_part).astype(jnp.bfloat16))
        batch_terms = (
            attn_gain_sum,
            query_sum,
            key_sum,
            value_sum,
            out_sum,
            ffn_gain_sum,
            gate_sum,
            up_sum,
            down_sum,
        )
        if grad_sums is None:
            grad_sums = batch_terms
        else:
            grad_sums = tuple(
                (
                    earlier_sum + batch_term
                    for earlier_sum, batch_term in zip(grad_sums, batch_terms)
                )
            )
    owned_grads = (
        lax.psum_scatter(grad_sums[0], ("ctx", "ws"), scatter_dimension=0, tiled=True),
        lax.psum_scatter(grad_sums[1], ("ctx", "ws"), scatter_dimension=0, tiled=True),
        lax.psum_scatter(grad_sums[2], ("ctx", "ws"), scatter_dimension=0, tiled=True),
        lax.psum_scatter(grad_sums[3], ("ctx", "ws"), scatter_dimension=0, tiled=True),
        lax.psum_scatter(grad_sums[4], ("ctx", "ws"), scatter_dimension=0, tiled=True),
        lax.psum_scatter(grad_sums[5], ("ctx", "ws"), scatter_dimension=0, tiled=True),
        lax.psum_scatter(grad_sums[6], ("ctx", "ws"), scatter_dimension=0, tiled=True),
        lax.psum_scatter(grad_sums[7], ("ctx", "ws"), scatter_dimension=0, tiled=True),
        lax.psum_scatter(grad_sums[8], ("ctx", "ws"), scatter_dimension=0, tiled=True),
    )
    return (
        jnp.stack(layer_outs),
        jnp.stack(input_grads),
        owned_grads[0],
        owned_grads[1],
        owned_grads[2],
        owned_grads[3],
        owned_grads[4],
        owned_grads[5],
        owned_grads[6],
        owned_grads[7],
        owned_grads[8],
    )


MESH = pl.DeviceIdType.MESH
NEG = -1e30
WIDE = 128
VMEM_LIMIT = 62 * 1024 * 1024


def fits_fast(mesh):
    return mesh.shape["ctx"] == 8 and mesh.shape["ws"] == 4


def place():
    c = lax.axis_index("ctx")
    w = lax.axis_index("ws")
    return c // 2, lax.rem(c, 2), w // 2, lax.rem(w, 2)


def device(z, y, x, k):
    return (z * 2 + y, x * 2 + k)


def greet(zn):
    z, y, x, k = place()
    others = [device(lax.rem(z + j, zn), y, x, k) for j in range(1, zn)]
    others += [device(z, y, 1 - x, k), device(z, 1 - y, x, k), device(z, y, x, 1 - k)]
    barrier = pltpu.get_barrier_semaphore()
    for other in others:
        pl.semaphore_signal(barrier, inc=1, device_id=other, device_id_type=MESH)
    pl.semaphore_wait(barrier, len(others))


def remote(src, dst, send, recv, where):
    return pltpu.make_async_remote_copy(
        src_ref=src, dst_ref=dst, send_sem=send, recv_sem=recv, device_id=where, device_id_type=MESH
    )


class Gather:
    SEMS = 12

    def __init__(self, src, dst, send, recv, zn):
        z, y, x, k = place()
        own = dst.at[z, y, x, k]
        hz = zn // 2
        xn, yn, sib = device(z, y, 1 - x, k), device(z, 1 - y, x, k), device(z, y, x, 1 - k)

        def push(i, ref, where):
            return remote(ref, ref, send.at[i], recv.at[i], where)

        def col(yy, xx, lo=0, n=zn):
            return dst.at[pl.ds(lo, n), yy, xx, k]

        self.local = pltpu.make_async_copy(src(z), own, send.at[0])
        self.along = []
        for j in range(1, zn):
            zz = lax.rem(z + j, zn)
            self.along.append(remote(src(zz), own, send.at[j], recv.at[j], device(zz, y, x, k)))
        self.cols = [push(4, col(y, x), xn), push(5, col(y, x), yn)]
        self.corner = [push(7, col(1 - y, x, 0, hz), xn), push(8, col(y, 1 - x, hz, hz), yn)]
        self.twin_own = push(6, col(y, x), sib)
        self.twin_cols = [push(9, col(y, 1 - x), sib), push(10, col(1 - y, x), sib)]
        self.twin_corner = push(11, col(1 - y, 1 - x), sib)

    def stage(self, n):
        if n == 0:
            self.local.start()
            for c in self.along:
                c.start()
        elif n == 1:
            self.local.wait()
            for c in self.along:
                c.wait_recv()
            for c in self.cols:
                c.start()
            self.twin_own.start()
        elif n == 2:
            for c in self.cols:
                c.wait_recv()
            for c in self.corner:
                c.start()
            for c in self.twin_cols:
                c.start()
        elif n == 3:
            for c in self.corner:
                c.wait_recv()
            self.twin_corner.start()
        elif n == 4:
            for c in [self.twin_own] + self.twin_cols + [self.twin_corner]:
                c.wait_recv()
            for c in (
                self.along
                + self.cols
                + self.corner
                + [self.twin_own]
                + self.twin_cols
                + [self.twin_corner]
            ):
                c.wait_send()


def stage_step(items, offsets, t, between=None):
    for n, offset in enumerate(offsets):
        if 0 <= t - offset < len(items):
            if items[t - offset] is not None:
                items[t - offset].stage(n)
            if between is not None:
                between()


FIRST_STAGES = (0, 1, 2, 3, 4)
GATHER_STAGES = (0, 1, 2, 3, 4)
GATHER_FROM = 3
GATHER_CUTS = [(1, 1), (1, 2), (1, 2), (2, 1), (1, 1)]
SUM_STAGES = (0, 1, 2, 3)


def portions(step, total, parts):
    done = [0]

    def call(all_=False):
        upto = total if all_ else min(total, done[0] + -(-total // parts))
        if upto > done[0]:
            lax.fori_loop(done[0], upto, step, 0)
            done[0] = upto

    return call


def pieces_of(rows, cols, nrow, ncol):
    return [
        (i * (rows // nrow), rows // nrow, j * (cols // ncol), cols // ncol)
        for i in range(nrow)
        for j in range(ncol)
    ]


def gather_item(ref, out, r0, nr, c0, nc, send, recv, zn):
    src = ref.at[pl.ds(r0, nr), pl.ds(c0, nc)]
    dst = out.at[:, :, :, :, pl.ds(r0, nr), pl.ds(c0, nc)]
    return Gather(lambda zz: src, dst, send, recv, zn)


class Exchange:
    def __init__(self, src, dst, send, recv, zn):
        z, y, x, k = place()
        self.local = pltpu.make_async_copy(src(z), dst(z), send.at[0])
        self.along = []
        for j in range(1, zn):
            zz = lax.rem(z + j, zn)
            self.along.append(remote(src(zz), dst(z), send.at[j], recv.at[j], device(zz, y, x, k)))

    def start(self):
        self.local.start()
        for c in self.along:
            c.start()

    def arrived(self):
        self.local.wait()
        for c in self.along:
            c.wait_recv()

    def sent(self):
        for c in self.along:
            c.wait_send()


class Scatter:
    SEMS = 10

    @staticmethod
    def scratch(zn, nr, nc):
        b = jnp.bfloat16
        return [
            pltpu.VMEM((zn, 2, 2, nr, nc), b),
            pltpu.VMEM((zn, 2, 2, nr, nc), b),
            pltpu.VMEM((2, zn // 2, nr, nc), b),
            pltpu.VMEM((2, zn, nr, nc), b),
            pltpu.VMEM((zn - 1, nr, nc), b),
        ]

    def __init__(self, part, out, bufs, send, recv, zn, give=None):
        z, y, x, k = self.at = place()
        self.zn = zn
        hz = zn // 2
        xn, yn, sib = device(z, y, 1 - x, k), device(z, 1 - y, x, k), device(z, y, x, 1 - k)
        self.held, self.twin, self.corners, self.colsums, self.ends = held, twin, corners, colsums, ends = bufs
        self.out = out
        self.load = None
        if give is None:
            self.load = pltpu.make_async_copy(part.at[:, :, :, k], held, send.at[0])
            give = part.at[:, :, :, 1 - k]
        self.to_twin = remote(give, twin, send.at[1], recv.at[1], sib)
        self.to_corner = [
            remote(held.at[pl.ds(0, hz), 1 - y, 1 - x], corners.at[0], send.at[2], recv.at[2], yn),
            remote(held.at[pl.ds(hz, hz), 1 - y, 1 - x], corners.at[1], send.at[3], recv.at[3], xn),
        ]
        self.to_col = [
            remote(held.at[:, y, 1 - x], colsums.at[0], send.at[4], recv.at[4], xn),
            remote(held.at[:, 1 - y, x], colsums.at[1], send.at[5], recv.at[5], yn),
        ]
        self.along = []
        for j in range(1, zn):
            zz = lax.rem(z + j, zn)
            dst = out.at[z] if ends is None else ends.at[j - 1]
            self.along.append(
                remote(held.at[zz, y, x], dst, send.at[5 + j], recv.at[5 + j], device(zz, y, x, k))
            )
        self.last = pltpu.make_async_copy(held.at[z, y, x], out.at[z], send.at[0]) if ends is None else None

    def stage(self, n):
        z, y, x, k = self.at
        zn, hz = self.zn, self.zn // 2
        held = self.held
        if n == 0:
            self.to_twin.start()
            if self.load is not None:
                self.load.start()
        elif n == 1:
            if self.load is not None:
                self.load.wait()
            self.to_twin.wait_recv()

            def add(i, _):
                for yy in range(2):
                    for xx in range(2):
                        held[i, yy, xx] = held[i, yy, xx] + self.twin[i, yy, xx]
                return 0

            lax.fori_loop(0, zn, add, 0)
            for c in self.to_corner:
                c.start()
        elif n == 2:
            for c in self.to_corner:
                c.wait_recv()
            for i in range(hz):
                held[i, y, 1 - x] = held[i, y, 1 - x] + self.corners[0, i]
                held[hz + i, 1 - y, x] = held[hz + i, 1 - y, x] + self.corners[1, i]
            for c in self.to_col:
                c.start()
        elif n == 3:
            for c in self.to_col:
                c.wait_recv()

            def add(i, _):
                f = jnp.float32
                held[i, y, x] = (
                    held[i, y, x].astype(f) + self.colsums[0, i].astype(f) + self.colsums[1, i].astype(f)
                ).astype(jnp.bfloat16)
                return 0

            lax.fori_loop(0, zn, add, 0)
            for c in self.along:
                c.start()
            if self.last is not None:
                self.last.start()
        elif n == 4:
            for c in self.along:
                c.wait_recv()
            if self.last is not None:
                self.last.wait()
            else:
                total = held[z, y, x].astype(jnp.float32)
                for j in range(zn - 1):
                    total = total + self.ends[j].astype(jnp.float32)
                self.out[...] = total
            for c in [self.to_twin] + self.to_corner + self.to_col + self.along:
                c.wait_send()


NT = (((1,), (1,)), ((), ()))


def nt(a, b):
    return lax.dot_general(a, b, NT, preferred_element_type=jnp.float32)


PER = QUERY_HEADS // KEY_VALUE_HEADS
HALF_GROUPS = KEY_VALUE_HEADS // 2
HALF_HEADS = QUERY_HEADS // 2
KV_LANES = 2 * HALF_GROUPS * HEAD_SIZE


def lane_slot(n):
    return n // 2, n % 2


def key_slot(g):
    return lane_slot(g)


def value_slot(g):
    return lane_slot(HALF_GROUPS + g)


def pair_index(half, zp):
    return zp if half == 0 else 3 - zp


def pair_tile(src, g, half, zp):
    tiles = []
    for j in range(PER):
        lo = HEAD_SIZE * (PER * g + j)
        a = src[2 * zp, lo : lo + HEAD_SIZE, :].astype(jnp.float32)
        b = src[2 * zp + 1, lo : lo + HEAD_SIZE, :].astype(jnp.float32)
        low = lax.broadcasted_iota(jnp.int32, a.shape, 1) < WIDE // 2
        if half == 0:
            tiles.append(jnp.where(low, a, pltpu.roll(b, WIDE // 2, 1)))
        else:
            tiles.append(jnp.where(low, pltpu.roll(a, WIDE // 2, 1), b))
    return jnp.concatenate(tiles, axis=1)


def unpair(get, dst):
    for zp in range(2):
        for g in range(HALF_GROUPS):
            first, second = get(g, pair_index(0, zp)), get(g, pair_index(1, zp))
            for j in range(PER):
                lo = HEAD_SIZE * (PER * g + j)
                a, b = first[:, WIDE * j : WIDE * j + WIDE], second[:, WIDE * j : WIDE * j + WIDE]
                low = lax.broadcasted_iota(jnp.int32, a.shape, 1) < WIDE // 2
                even = jnp.where(low, a, pltpu.roll(b, WIDE // 2, 1))
                odd = jnp.where(low, pltpu.roll(a, WIDE // 2, 1), b)
                dst[2 * zp, lo : lo + HEAD_SIZE, :] = even.astype(dst.dtype)
                dst[2 * zp + 1, lo : lo + HEAD_SIZE, :] = odd.astype(dst.dtype)


GROUP_LANES = 3 * WIDE


def set_padded(dst, g, p, tile, side):
    tile = tile.astype(dst.dtype)
    cols = slice(g * GROUP_LANES, (g + 1) * GROUP_LANES)
    dst[p, side * HEAD_SIZE : (side + 1) * HEAD_SIZE, cols] = tile
    dst[p, (1 - side) * HEAD_SIZE : (2 - side) * HEAD_SIZE, cols] = jnp.zeros_like(tile)


def by_block(slot):
    runs = []
    for g in range(HALF_GROUPS):
        if runs and runs[-1][0] == slot(g)[0]:
            runs[-1][2] += 1
        else:
            runs.append([slot(g)[0], g, 1])
    return runs


def group_scores(block, right, p, slot):
    out = []
    for b, g, n in by_block(slot):
        t = jnp.dot(block(b), right[p, :, g * GROUP_LANES : (g + n) * GROUP_LANES], preferred_element_type=jnp.float32)
        out += [t[:, i * GROUP_LANES : (i + 1) * GROUP_LANES] for i in range(n)]
    return out


def group_sums(tiles, right, p, slot):
    sums = {}
    for b, g, n in by_block(slot):
        left = tiles[g] if n == 1 else jnp.concatenate(tiles[g : g + n], axis=1)
        sums[b] = nt(left, right[p, :, g * GROUP_LANES : (g + n) * GROUP_LANES])
    return sums


def walk(t, y, cn):
    b1, b2, b3 = 3 + y, 10 + 2 * y, 22 + y
    p = (t >= b1).astype(jnp.int32) + (t >= b2).astype(jnp.int32) + (t >= b3).astype(jnp.int32)
    j = t - jnp.where(p == 0, 0, jnp.where(p == 1, b1, jnp.where(p == 2, b2, b3)))
    zp = jnp.where(p < 2, p, 3 - p)
    low = jnp.where(p < 2, 4 * zp + y, 2 * cn - 3 - 4 * zp - y)
    late = (j >= cn).astype(jnp.int32)
    src = jnp.where(late == 1, 2 * cn - 1 - j, j)
    return p, j, src // 2, lax.rem(src, 2), pl.multiple_of(late * HEAD_SIZE, HEAD_SIZE), j >= low


STEPS = 38
FORWARD_PARTS, FORWARD_LEFT = 20, 3


def visible(p, j, y, w, cn, wn, rows):
    shape = (wn * rows, PER * WIDE)
    lane = lax.rem(lax.broadcasted_iota(jnp.int32, shape, 1), WIDE)
    zp = jnp.where(p < 2, p, 3 - p)
    c = 2 * (2 * zp + lane // rows) + y
    span = jnp.where(p < 2, c, 2 * cn - 1 - c)
    query = span * (wn * rows) + w * rows + lax.rem(lane, rows)
    key = j * (wn * rows) + lax.broadcasted_iota(jnp.int32, shape, 0)
    return key <= query


def key_block(kvg, zz, yy, late, rows, block):
    t = kvg[zz, yy, :, :, pl.ds(late, rows), WIDE * block : WIDE * block + WIDE]
    return t.reshape(4 * rows, WIDE)


def turned(t):
    return t.astype(jnp.float32).T.astype(t.dtype)


def by_span(body, kvg, cn, rows):
    def one(j, _):
        late = (j >= cn).astype(jnp.int32)
        src = jnp.where(late == 1, 2 * cn - 1 - j, j)
        at = pl.multiple_of(late * rows, rows)
        body(j, lambda b: key_block(kvg, src // 2, lax.rem(src, 2), at, rows, b))
        return 0

    lax.fori_loop(0, 2 * cn, one, 0)


def transposed(t):
    return jnp.concatenate([t[:, i : i + WIDE].T for i in range(0, t.shape[1], WIDE)], axis=0)


def unfold_rows(src, dst, rb):
    n = src.shape[0] // 16
    fold = 16 // rb
    cols = src.shape[1]
    shape = (n * rb, n * 16)
    row = lax.broadcasted_iota(jnp.int32, shape, 0)
    at = 16 * (row // rb) + lax.rem(row, rb)
    col = lax.broadcasted_iota(jnp.int32, shape, 1)
    for q in range(fold):
        pick = jnp.where(col == at + rb * q, 1.0, 0.0).astype(jnp.bfloat16)
        t = jnp.dot(pick, src[...], preferred_element_type=jnp.float32)
        dst[:, q * cols : (q + 1) * cols] = t.astype(dst.dtype)


def gather_attend(x, gy, tables, qkv, fold1, weights, cuts, collective_id):
    cn, wn = lax.axis_size("ctx"), lax.axis_size("ws")
    zn = cn // 2
    dn = cn * wn
    tokens = tables.shape[1]
    all_rows, width = x.shape
    mbs = all_rows // tokens
    qkv_w = qkv.shape[1]
    q_rows = qkv_w - 2 * KV_LANES
    rows = tokens // 2
    mine = q_rows // 2
    f32, b16 = jnp.float32, jnp.bfloat16
    ra = qkv.shape[0] // 16 * 16
    rb = qkv.shape[0] - ra
    wa = dn * ra
    wide1 = fold1.shape[1] * (16 // rb)
    own = ra + rb
    ff = weights[1].shape[1]
    step_cols = 3 * WIDE
    rest_w = -(-(width + 2 * ff) // (4 * step_cols)) * step_cols
    shapes = [(ra, width), (ra, ff), (ra, ff), weights[3].shape, (16, rest_w)]
    n = len(shapes)
    work = [(a, piece) for a in range(n) for piece in pieces_of(*shapes[a], *cuts[a])]
    groups = range(HALF_GROUPS)
    n_first = 3

    def kernel(*refs):
        x_raw, gy_raw, tab, qkv_ref, fold_ref, out_raw, gate_raw, up_raw, down_raw = refs[:9]
        at = 9
        x_ref, gy_out, order_out = refs[at : at + 3]
        at += 3
        o_out, q_out, kv_out, oh_out, lse_out, w_out, wb_out, hn_out, hnb_out, inv_out, gains_out = refs[at : at + 11]
        at += 11
        outs = refs[at : at + n]
        at += n
        (order, out_s, down_s, rest_s, wq, f1, wide, hn, q_s, kv_s, qh, kvg, oh, qpad, vt, m_s, l_s, acc) = refs[at : at + 18]
        send, recv, xs, xr, ks, kr, save = refs[at + 18 :]
        ins = [out_s, gate_raw, up_raw, down_s, rest_s]
        greet(zn)
        z, y, x_, k = place()
        w = 2 * x_ + k

        def lanes_of(zz):
            return kv_s.at[zz // 2, :, pl.ds(pl.multiple_of(lax.rem(zz, 2) * KV_LANES, WIDE), KV_LANES)]

        def heads_of(ref, zz):
            return ref.at[zz // 2, pl.ds(pl.multiple_of(lax.rem(zz, 2) * mine, 16), mine), :]

        items = [
            gather_item(fold_ref, f1, 0, 16, 0, fold1.shape[1], send.at[0], recv.at[0], zn),
            gather_item(qkv_ref, wq, 0, ra, 0, 2 * KV_LANES, send.at[1], recv.at[1], zn),
            gather_item(qkv_ref, wq, 0, ra, 2 * KV_LANES, q_rows, send.at[2], recv.at[2], zn),
        ]
        later = [
            gather_item(ins[a], outs[a], r0, nr, c0, nc, send.at[n_first + i], recv.at[n_first + i], zn)
            for i, (a, (r0, nr, c0, nc)) in enumerate(work)
        ]
        kvx = Gather(lanes_of, kvg, ks, kr, zn)
        qx = Exchange(lambda zz: heads_of(q_s, zz), lambda zz: qh.at[zz], xs.at[0], xr.at[0], zn)
        ox = Exchange(lambda zz: oh.at[zz], lambda zz: heads_of(o_out, zz), xs.at[1], xr.at[1], zn)

        def advance(s, between=None):
            stage_step(items, FIRST_STAGES, s)
            stage_step(later, GATHER_STAGES, s - GATHER_FROM, between)

        advance(0)
        for r in range(0, width, WIDE):
            new = r + lax.broadcasted_iota(jnp.int32, (WIDE, width), 0)
            old = jnp.where(
                new < wa, own * (new // ra) + lax.rem(new, ra), own * ((new - wa) // rb) + ra + lax.rem(new - wa, rb)
            )
            col = lax.broadcasted_iota(jnp.int32, (WIDE, width), 1)
            order[r : r + WIDE, :] = jnp.where(col == old, 1.0, 0.0).astype(b16)
        advance(1)
        out_s[...] = nt(out_raw[...], order[...]).astype(b16)
        down_s[...] = nt(down_raw[...], order[...]).astype(b16)
        columns = []
        for ref, cols in ((out_s, width), (gate_raw, ff), (up_raw, ff)):
            columns += [(ref, c) for c in range(0, cols, step_cols)]
        per = rest_w // step_cols
        row = lax.broadcasted_iota(jnp.int32, (16, own), 0)
        src = lax.broadcasted_iota(jnp.int32, (16, own), 1)
        for c in range(per):
            total = jnp.zeros((16, step_cols), f32)
            for q in range(16 // rb):
                if q * per + c < len(columns):
                    ref, lo = columns[q * per + c]
                    pick = jnp.where((row // rb == q) & (src == ra + lax.rem(row, rb)), 1.0, 0.0).astype(b16)
                    total = total + jnp.dot(pick, ref[:, lo : lo + step_cols], preferred_element_type=f32)
            rest_s[:, c * step_cols : (c + 1) * step_cols] = total.astype(b16)
        advance(2)
        x_ref[...] = nt(x_raw[...], order[...]).astype(b16)
        advance(3)
        gy_out[...] = nt(gy_raw[...], order[...]).astype(b16)
        save_order = pltpu.make_async_copy(order, order_out, save.at[5])
        save_order.start()
        xf = x_ref[...].astype(f32)
        inv = lax.rsqrt(jnp.mean(xf * xf, axis=-1, keepdims=True) + EPSILON)
        inv_out[...] = inv
        m_s[...] = jnp.full(m_s.shape, NEG, f32)
        l_s[...] = jnp.zeros(l_s.shape, f32)
        acc[...] = jnp.zeros(acc.shape, f32)
        advance(n_first + 1)
        unfold_rows(f1[...].reshape(dn * 16, fold1.shape[1]), wide, rb)
        lane = lax.broadcasted_iota(jnp.int32, (WIDE, width), 1)
        local = jnp.where(lane < wa, lax.rem(lane, ra), ra + lax.rem(lane - wa, rb))
        spread = jnp.where(lax.broadcasted_iota(jnp.int32, (WIDE, width), 0) == local, 1.0, 0.0).astype(b16)
        lines = jnp.dot(wide[:, wide1 - WIDE :], spread, preferred_element_type=f32)
        lane = lax.broadcasted_iota(jnp.int32, lines.shape, 1)
        owner = jnp.where(lane < wa, lane // ra, (lane - wa) // rb)
        line = lax.broadcasted_iota(jnp.int32, lines.shape, 0)
        for i in range(2):
            gains_out[i : i + 1, :] = jnp.sum(jnp.where(line == rb * owner + i, lines, 0.0), axis=0, keepdims=True)
        normed = xf * inv * gains_out[0:1, :]
        hn[...] = normed.astype(b16)
        hn_out[...] = transposed(normed[:, :wa]).astype(b16)
        hnb_out[...] = transposed(normed[:, wa:]).astype(b16)
        advance(n_first + 2)

        low_lanes = lax.broadcasted_iota(jnp.int32, (tokens, WIDE), 1) < HEAD_SIZE
        quarter = HEAD_SIZE // 2

        def turned_heads(t, kind):
            if kind == "still":
                return t
            cos, low, high = tab[0], tab[1], tab[2]
            r = t * cos + pltpu.roll(t, WIDE - quarter, 1) * low + pltpu.roll(t, quarter, 1) * high
            return r if kind == "turn" else jnp.where(low_lanes, r, t)

        def project(c):
            cols = slice(c * KV_LANES, (c + 1) * KV_LANES)
            t = jnp.dot(hn[:, :wa], wq[:, :, :, :, :, cols].reshape(wa, KV_LANES), preferred_element_type=f32)
            t = t + jnp.dot(hn[:, wa:], wide[:, cols], preferred_element_type=f32)
            kinds = ["turn", "mixed", "still"] if c < 2 else ["turn"] * 3
            for mb in range(mbs):
                for b in range(3):
                    r = turned_heads(t[mb * tokens : (mb + 1) * tokens, WIDE * b : WIDE * b + WIDE], kinds[b])
                    at = c * KV_LANES + WIDE * b
                    if c < 2:
                        kv_s[mb, :, at : at + WIDE] = r.astype(b16)
                    else:
                        at -= 2 * KV_LANES
                        q_s[mb, at : at + WIDE, :] = (r * HEAD_SIZE**-0.5).T.astype(b16)

        project(0)
        project(1)
        kvx.stage(0)
        advance(n_first + 3)
        for c in range(2, qkv_w // KV_LANES):
            project(c)
        qx.start()
        save_order.wait()
        saves = [
            pltpu.make_async_copy(wq, w_out, save.at[3]),
            pltpu.make_async_copy(wide.at[:, pl.ds(0, qkv_w)], wb_out, save.at[4]),
        ]
        for s in saves:
            s.start()
        kvx.stage(1)
        kvx.stage(2)
        advance(n_first + 4)
        kvx.stage(3)
        qx.arrived()
        for half in range(2):
            for zp in range(2):
                for g in groups:
                    set_padded(qpad, g, pair_index(half, zp), pair_tile(qh, g, half, zp), key_slot(g)[1])
        kvx.stage(4)

        def turn(j, block):
            flat = {b: turned(block(b)) for b in sorted({value_slot(g)[0] for g in groups})}
            for g in groups:
                b, side = value_slot(g)
                vt[j, g] = flat[b][side * HEAD_SIZE : (side + 1) * HEAD_SIZE]

        by_span(turn, kvg, cn, rows)
        saves += [
            pltpu.make_async_copy(qh, q_out, save.at[0]),
            pltpu.make_async_copy(kvg, kv_out, save.at[1]),
        ]
        for s in saves[2:]:
            s.start()

        def step(t, _):
            p, j, zz, yy, late, edge = walk(t, y, cn)

            def run(masked):
                seen = visible(p, j, y, w, cn, wn, rows) if masked else None
                scores = group_scores(lambda b: key_block(kvg, zz, yy, late, rows, b), qpad, p, key_slot)
                for g in groups:
                    s = scores[g]
                    if masked:
                        s = jnp.where(seen, s, NEG)
                    m_old = m_s[g, p]
                    m_new = jnp.maximum(m_old, jnp.max(s, axis=0, keepdims=True))
                    alpha = jnp.exp(m_old - m_new)
                    e = jnp.exp(s - m_new)
                    m_s[g, p] = m_new
                    l_s[g, p] = l_s[g, p] * alpha + jnp.sum(e, axis=0, keepdims=True)
                    acc[g, p] = acc[g, p] * alpha + jnp.dot(
                        vt[j, g], e.astype(b16), preferred_element_type=f32
                    )

            pl.when(edge)(lambda: run(True))
            pl.when(jnp.logical_not(edge))(lambda: run(False))
            return 0

        last = GATHER_FROM + len(later) + GATHER_STAGES[-1]
        start = n_first + 5
        attend = portions(step, STEPS, FORWARD_PARTS)
        for s in range(start, last):
            advance(s, attend if s <= last - FORWARD_LEFT else None)
            if s == last - FORWARD_LEFT:
                attend(True)
                unpair(lambda g, p: acc[g, p] / l_s[g, p], oh)
                ox.start()
                saves.append(pltpu.make_async_copy(oh, oh_out, save.at[2]))
                saves[-1].start()
                lse_out[...] = m_s[...] + jnp.log(l_s[...])
        ox.arrived()
        ox.sent()
        qx.sent()
        for s in saves:
            s.wait()

    stat = (HALF_GROUPS, 4, 1, PER * WIDE)
    block = (zn, mine, tokens)
    kv_shape = (zn, 2, 2, 2, tokens, KV_LANES)
    any_ = pl.BlockSpec(memory_space=pl.ANY)
    vmem = pl.BlockSpec(memory_space=pltpu.VMEM)
    sds = jax.ShapeDtypeStruct
    dma = pltpu.SemaphoreType.DMA
    return pl.pallas_call(
        kernel,
        out_shape=[
            sds(x.shape, b16),
            sds(x.shape, b16),
            sds((width, width), b16),
            sds((mbs, q_rows, tokens), b16),
            sds(block, b16),
            sds(kv_shape, b16),
            sds(block, b16),
            sds(stat, f32),
            sds((zn, 2, 2, 2, ra, qkv_w), b16),
            sds((dn * rb, qkv_w), b16),
            sds((wa, all_rows), b16),
            sds((width - wa, all_rows), b16),
            sds((all_rows, 1), f32),
            sds((2, width), f32),
        ]
        + [sds((zn, 2, 2, 2, *shapes[a]), b16) for a in range(n)],
        in_specs=[vmem] * 3 + [any_] * 2 + [vmem] * 4,
        out_specs=[vmem] * 2 + [any_] + [any_] * 4 + [vmem] + [any_] * 2 + [vmem] * 4 + [any_] * n,
        scratch_shapes=[
            pltpu.VMEM((width, width), b16),
            pltpu.VMEM(weights[0].shape, b16),
            pltpu.VMEM(weights[3].shape, b16),
            pltpu.VMEM((16, rest_w), b16),
            pltpu.VMEM((zn, 2, 2, 2, ra, qkv_w), b16),
            pltpu.VMEM((zn, 2, 2, 2, 16, fold1.shape[1]), b16),
            pltpu.VMEM((dn * rb, wide1), b16),
            pltpu.VMEM((all_rows, width), b16),
            pltpu.VMEM((mbs, q_rows, tokens), b16),
            pltpu.VMEM((mbs, tokens, 2 * KV_LANES), b16),
            pltpu.VMEM(block, b16),
            pltpu.VMEM(kv_shape, b16),
            pltpu.VMEM(block, b16),
            pltpu.VMEM((4, WIDE, HALF_GROUPS * PER * WIDE), b16),
            pltpu.VMEM((2 * cn, HALF_GROUPS, HEAD_SIZE, wn * rows), b16),
            pltpu.VMEM(stat, f32),
            pltpu.VMEM(stat, f32),
            pltpu.VMEM((HALF_GROUPS, 4, HEAD_SIZE, PER * WIDE), f32),
            dma((n_first + len(work), Gather.SEMS)),
            dma((n_first + len(work), Gather.SEMS)),
            dma((2, zn)),
            dma((2, zn)),
            dma((Gather.SEMS,)),
            dma((Gather.SEMS,)),
            dma((6,)),
        ],
        compiler_params=pltpu.CompilerParams(
            collective_id=collective_id, has_side_effects=True, vmem_limit_bytes=VMEM_LIMIT
        ),
    )(x, gy, tables, qkv, fold1, *weights)


class Share:
    def __init__(self, src, own, other, local, send, recv, split):
        z, y, x, k = place()
        mine = src.at[:, :, :, k] if split else src
        theirs = src.at[:, :, :, 1 - k] if split else src
        self.load = None if mine is own else pltpu.make_async_copy(mine, own, local)
        self.swap = remote(theirs, other, send, recv, device(z, y, x, 1 - k))
        self.waited = False

    def start(self):
        if self.load is not None:
            self.load.start()
        self.swap.start()

    def ready(self):
        if not self.waited:
            if self.load is not None:
                self.load.wait()
            self.swap.wait_recv()
            self.waited = True

    def sent(self):
        self.swap.wait_send()


class Sum:
    SEMS = 8

    def __init__(self, make, held, bufs, out, send, recv, zn):
        z, y, x, k = self.at = place()
        self.make, self.held, self.out, self.zn = make, held, out, zn
        hz = zn // 2
        xn, yn = device(z, y, 1 - x, k), device(z, 1 - y, x, k)
        self.corners, self.colsums, self.ends = corners, colsums, ends = bufs
        self.to_corner = [
            remote(held.at[pl.ds(0, hz), 1 - y, 1 - x], corners.at[0], send.at[0], recv.at[0], yn),
            remote(held.at[pl.ds(hz, hz), 1 - y, 1 - x], corners.at[1], send.at[1], recv.at[1], xn),
        ]
        self.to_col = [
            remote(held.at[:, y, 1 - x], colsums.at[0], send.at[2], recv.at[2], xn),
            remote(held.at[:, 1 - y, x], colsums.at[1], send.at[3], recv.at[3], yn),
        ]
        self.along = []
        for j in range(1, zn):
            zz = lax.rem(z + j, zn)
            self.along.append(
                remote(held.at[zz, y, x], ends.at[j - 1], send.at[3 + j], recv.at[3 + j], device(zz, y, x, k))
            )

    @staticmethod
    def scratch(zn, nr, nc):
        b = jnp.bfloat16
        return [
            pltpu.VMEM((2, zn // 2, nr, nc), b),
            pltpu.VMEM((2, zn, nr, nc), b),
            pltpu.VMEM((zn - 1, nr, nc), b),
        ]

    def stage(self, n):
        z, y, x, k = self.at
        zn, hz, held = self.zn, self.zn // 2, self.held
        f32, b16 = jnp.float32, jnp.bfloat16
        if n == 0:
            self.make(held)
            for c in self.to_corner:
                c.start()
        elif n == 1:
            for c in self.to_corner:
                c.wait_recv()
            for i in range(hz):
                held[i, y, 1 - x] = held[i, y, 1 - x] + self.corners[0, i]
                held[hz + i, 1 - y, x] = held[hz + i, 1 - y, x] + self.corners[1, i]
            for c in self.to_col:
                c.start()
        elif n == 2:
            for c in self.to_col:
                c.wait_recv()
            for i in range(zn):
                held[i, y, x] = (
                    held[i, y, x].astype(f32)
                    + self.colsums[0, i].astype(f32)
                    + self.colsums[1, i].astype(f32)
                ).astype(b16)
            for c in self.along:
                c.start()
        elif n == 3:
            for c in self.along:
                c.wait_recv()
            total = held[z, y, x].astype(f32)
            for j in range(zn - 1):
                total = total + self.ends[j].astype(f32)
            self.out[...] = total
            for c in self.to_corner + self.to_col + self.along:
                c.wait_send()


FFN_CUTS = 2
ORDER = (0, 1, 2, 3, 4, 5, 6, 7, 8, 9, 10, 11)
BACK_SPAN, BACK_PARTS = 3, 10


def scatter_attend(do, qh, kvg, oh, lse, tables, lefts, rests, rights, plan, last, collective_id):
    cn, wn = lax.axis_size("ctx"), lax.axis_size("ws")
    zn = cn // 2
    mbs, q_rows, tokens = do.shape
    rows = tokens // 2
    mine = q_rows // 2
    all_rows = mbs * tokens
    f32, b16 = jnp.float32, jnp.bfloat16
    groups = range(HALF_GROUPS)
    scale = HEAD_SIZE**-0.5
    ff = rights[2].shape[1]
    width = rights[0].shape[1]
    qkv_w = q_rows + 2 * KV_LANES
    act_rows = lefts[0].shape[4]
    ra = lefts[1].shape[4]
    rest_w, qkv_rest_w = plan
    n_down = act_rows // ra
    sizes = (
        [(ra, width)] * n_down
        + [(ra, ff // FFN_CUTS)] * (2 * FFN_CUTS)
        + [(ra, width), (16, rest_w), (ra, 2 * KV_LANES), (ra, q_rows), (16, qkv_rest_w)]
    )
    max_cols = max(s[1] for s in sizes)
    ring = SUM_STAGES[-1] + 1
    scratch = []
    for nr, nc in sizes:
        scratch += Sum.scratch(zn, nr, nc)
    n_items = len(sizes)
    ins_all = [*lefts, *rests, *rights]
    n_in = len(ins_all)
    split = [True] * len(lefts) + [False] * (n_in - len(lefts))
    half = lambda a, s: (a.shape[:3] + a.shape[4:]) if s else a.shape
    shares = []
    for a, s in zip(ins_all, split):
        shares += [pltpu.VMEM(half(a, s), b16), pltpu.VMEM(half(a, s), b16)]
    rb = rests[0].shape[0] // (cn * wn)
    own_rows = ra + rb
    outs_shape = [(act_rows, width), (own_rows, ff), (own_rows, ff), (own_rows, width), (own_rows, qkv_w)]
    n_out = len(outs_shape)
    n_last = len(last)

    def kernel(*refs):
        do_ref, qh_ref, kvg_ref, oh_ref, lse_ref, tab = refs[:6]
        ins = refs[6 : 6 + n_in]
        at = 6 + n_in
        w_ref, r_ref, x_ref, inv_ref, gain_ref, gx1_ref, gain2_ref, order_ref = refs[at : at + n_last]
        at += n_last
        outs = refs[at : at + n_out]
        input_grad, total = refs[at + n_out : at + n_out + 2]
        rest = refs[at + n_out + 2 :]
        bufs, rest = rest[: len(scratch)], rest[len(scratch) :]
        pairs, rest = rest[: len(shares)], rest[len(shares) :]
        (held, gq, gq_other, dkv_in, oh, gh, give, got) = rest[:8]
        kb = rest[8:12]
        rest_sum, qkv_rest_sum = rest[12:14]
        send, recv, ps, pr, pl_, xs, xr, ks, kr, gs, gr, loads = rest[14:]
        dqh, dq_in = gh, oh
        greet(zn)
        z, y, x, k = place()
        w = 2 * x + k

        def heads_of(ref, zz):
            return ref.at[zz // 2, pl.ds(pl.multiple_of(lax.rem(zz, 2) * mine, 16), mine), :]

        gx = Exchange(lambda zz: heads_of(do_ref, zz), lambda zz: gh.at[zz], xs.at[0], xr.at[0], zn)
        dx = Exchange(lambda zz: dqh.at[zz], lambda zz: dq_in.at[zz], xs.at[1], xr.at[1], zn)
        kvx = Scatter(None, dkv_in, tuple(kb) + (None,), ks, kr, zn, give)
        share = [
            Share(ins[i], pairs[2 * i], pairs[2 * i + 1], pl_.at[i], ps.at[i], pr.at[i], split[i])
            for i in range(n_in)
        ]
        gq_share = Share(gq, gq, gq_other, None, ps.at[n_in], pr.at[n_in], False)
        own = lambda i: pairs[2 * i]
        other = lambda i: pairs[2 * i + 1]
        ACT, H2, OT, HN, H2B, OTB, HNB, GY, GB, GG, GU = range(n_in)

        def product(left, right, lo, row0, needs):
            def make(dst):
                for i in needs:
                    share[i].ready()
                nr, nc = dst.shape[3:]
                lefts2 = [
                    r[:, :, :, row0 : row0 + nr, :].reshape(zn * 4 * nr, all_rows)
                    for r in (own(left), other(left))
                ]
                step = 3 * WIDE

                def cols(i, _):
                    at = pl.multiple_of(i * step, WIDE)
                    t = jnp.dot(lefts2[0], right[0][:, pl.ds(lo + at, step)], preferred_element_type=f32)
                    t = t + jnp.dot(lefts2[1], right[1][:, pl.ds(lo + at, step)], preferred_element_type=f32)
                    dst[:, :, :, :, pl.ds(at, step)] = t.astype(b16).reshape(zn, 2, 2, nr, step)
                    return 0

                lax.fori_loop(0, nc // step, cols, 0)

            return make

        def both(i):
            return (own(i), other(i))

        def fold4(quarters):
            row = lax.rem(lax.broadcasted_iota(jnp.int32, quarters[0].shape, 0), 8)
            here = k == 0

            def put(a, b):
                n = a.shape[0]
                low = jnp.where(here, a, pltpu.roll(a, n - 4, 0))
                high = jnp.where(here, pltpu.roll(b, 4, 0), b)
                t = jnp.where(row < 4, low, high)
                return t.reshape(zn * 4, 8, t.shape[1])

            t = jnp.concatenate([put(*quarters[:2]), put(*quarters[2:])], axis=1)
            return t.astype(b16).reshape(zn, 2, 2, 16, t.shape[2])

        def rest_product(dst):
            step = 3 * WIDE
            for i in (H2B, OTB, GB, GG, GU):
                share[i].ready()
            columns = []
            for left, right, n in ((OTB, GB, width), (H2B, GG, ff), (H2B, GU, ff)):
                columns += [(left, right, c) for c in range(0, n, step)]
            per = rest_w // step

            def one(entry):
                if entry is None:
                    return jnp.zeros((own(H2B).shape[0], step), f32)
                left, right, c = entry
                return jnp.dot(own(left)[...], own(right)[:, c : c + step], preferred_element_type=f32) + jnp.dot(
                    other(left)[...], other(right)[:, c : c + step], preferred_element_type=f32
                )

            for c in range(per):
                quarters = []
                for q in range(4):
                    at = q * per + c
                    quarters.append(one(columns[at] if at < len(columns) else None))
                dst[:, :, :, :, c * step : (c + 1) * step] = fold4(quarters)

        def qkv_rest_product(dst):
            for i in (HNB,):
                share[i].ready()
            gq_share.ready()
            quarters = []
            for q in range(4):
                lo, hi = q * qkv_rest_w, min((q + 1) * qkv_rest_w, qkv_w)
                t = jnp.dot(own(HNB)[...], gq[:, lo:hi], preferred_element_type=f32) + jnp.dot(
                    other(HNB)[...], gq_other[:, lo:hi], preferred_element_type=f32
                )
                if hi - lo < qkv_rest_w:
                    t = jnp.concatenate([t, jnp.zeros((t.shape[0], qkv_rest_w - hi + lo), f32)], axis=1)
                quarters.append(t)
            dst[...] = fold4(quarters)

        gq_both = (gq, gq_other)
        makes = [product(ACT, both(GY), 0, ra * i, (ACT, GY)) for i in range(n_down)]
        ffn_parts = [(g, i * (ff // FFN_CUTS), ff // FFN_CUTS) for g in (GG, GU) for i in range(FFN_CUTS)]
        makes += [product(H2, both(g), lo, 0, (H2, g)) for g, lo, _ in ffn_parts]
        makes += [product(OT, both(GB), 0, 0, (OT, GB)), rest_product]
        makes += [product(HN, gq_both, 0, 0, (HN,)), product(HN, gq_both, 2 * KV_LANES, 0, (HN,)), qkv_rest_product]
        targets = [outs[0].at[pl.ds(ra * i, ra), :] for i in range(n_down)]
        block_rows = pl.ds(0, ra)
        targets += [outs[1 if g == GG else 2].at[block_rows, pl.ds(lo, n)] for g, lo, n in ffn_parts]
        targets += [
            outs[3].at[block_rows, :],
            rest_sum,
            outs[4].at[block_rows, pl.ds(0, 2 * KV_LANES)],
            outs[4].at[block_rows, pl.ds(2 * KV_LANES, q_rows)],
            qkv_rest_sum,
        ]
        items = []
        for i, (nr, nc) in enumerate(sizes):
            slot = held.at[ORDER.index(i) % ring, :, :, :, pl.ds(0, nr), pl.ds(0, nc)]
            items.append(
                Sum(makes[i], slot, bufs[3 * i : 3 * i + 3], targets[i], send.at[i], recv.at[i], zn)
            )
        load_o = pltpu.make_async_copy(oh_ref, oh, pl_.at[n_in])
        load_o.start()
        gx.start()
        for i in (ACT, GY, H2, GG, GU, OT, GB, H2B, OTB, HN, HNB):
            share[i].start()
        order = [None if i is None else items[i] for i in ORDER]
        at_qkv = ORDER.index(n_items - 3)
        n_back = BACK_SPAN
        stage_step(order, SUM_STAGES, 0)

        def attention_back(kvg, qh, qt, dot_, kt, delta, dq, dkv):
            load_kv = pltpu.make_async_copy(kvg_ref, kvg, loads.at[0])
            load_q = pltpu.make_async_copy(qh_ref, qh, loads.at[1])
            load_kv.start()
            load_q.start()
            dq[...] = jnp.zeros(dq.shape, f32)

            def clear(i, _):
                dkv[i] = jnp.zeros(dkv.shape[1:], f32)
                return 0

            lax.fori_loop(0, zn, clear, 0)
            def turn(j, block):
                flat = {b: turned(block(b)) for b in sorted({key_slot(g)[0] for g in groups})}
                for g in groups:
                    b, side = key_slot(g)
                    kt[j, g] = flat[b][side * HEAD_SIZE : (side + 1) * HEAD_SIZE]

            load_kv.wait()
            by_span(turn, kvg, cn, rows)
            stage_step(order, SUM_STAGES, 1)
            gx.arrived()
            load_o.wait()
            load_q.wait()
            for half_ in range(2):
                for zp in range(2):
                    p = pair_index(half_, zp)
                    for g in groups:
                        g_tile = pair_tile(gh, g, half_, zp)
                        o_tile = pair_tile(oh, g, half_, zp)
                        delta[g, p] = jnp.sum(g_tile * o_tile, axis=0, keepdims=True)
                        set_padded(qt, g, p, pair_tile(qh, g, half_, zp), key_slot(g)[1])
                        set_padded(dot_, g, p, g_tile, value_slot(g)[1])

            def step(t, _):
                p, j, zz, yy, late, edge = walk(t, y, cn)

                def run(masked):
                    seen = visible(p, j, y, w, cn, wn, rows) if masked else None
                    blocks = [key_block(kvg, zz, yy, late, rows, b) for b in range(KV_LANES // WIDE)]
                    scores = group_scores(lambda b: blocks[b], qt, p, key_slot)
                    dps = group_scores(lambda b: blocks[b], dot_, p, value_slot)
                    es, dss = [], []
                    for g in groups:
                        s = scores[g]
                        if masked:
                            s = jnp.where(seen, s, NEG)
                        e = jnp.exp(s - lse_ref[g, p])
                        ds = (e * (dps[g] - delta[g, p])).astype(b16)
                        es.append(e.astype(b16))
                        dss.append(ds)
                        dq[g, p] += jnp.dot(kt[j, g], ds, preferred_element_type=f32)
                    sums = group_sums(es, dot_, p, value_slot)
                    for b, v in group_sums(dss, qt, p, key_slot).items():
                        sums[b] = sums[b] + v if b in sums else v
                    for b, v in sums.items():
                        dkv[zz, yy, :, :, pl.ds(late, rows), WIDE * b : WIDE * b + WIDE] += v.reshape(
                            2, 2, rows, WIDE
                        )

                pl.when(edge)(lambda: run(True))
                pl.when(jnp.logical_not(edge))(lambda: run(False))
                return 0

            attend = portions(step, STEPS, BACK_PARTS)
            for s in range(2, 2 + n_back):
                stage_step(order, SUM_STAGES, s, attend)
            attend(True)

            def pack(i, _):
                for yy in range(2):
                    for xx in range(2):
                        kb[0][i, yy, xx] = dkv[i, yy, xx, k].astype(b16)
                        give[i, yy, xx] = dkv[i, yy, xx, 1 - k].astype(b16)
                return 0

            lax.fori_loop(0, zn, pack, 0)
            kvx.stage(0)
            unpair(lambda g, p: dq[g, p] * scale, dqh)
            dx.start()

        stat = (HALF_GROUPS, 4, 1, PER * WIDE)
        tile = (4, WIDE, HALF_GROUPS * PER * WIDE)
        pl.run_scoped(
            attention_back,
            pltpu.VMEM(kvg_ref.shape, b16),
            pltpu.VMEM(qh_ref.shape, b16),
            pltpu.VMEM(tile, b16),
            pltpu.VMEM(tile, b16),
            pltpu.VMEM((2 * cn, HALF_GROUPS, HEAD_SIZE, wn * rows), b16),
            pltpu.VMEM(stat, f32),
            pltpu.VMEM((HALF_GROUPS, 4, HEAD_SIZE, PER * WIDE), f32),
            pltpu.VMEM((zn, 2, 2, 2, tokens, KV_LANES), f32),
        )

        def rope_back():
            low_lanes = lax.broadcasted_iota(jnp.int32, (tokens, WIDE), 1) < HEAD_SIZE
            quarter = HEAD_SIZE // 2

            def back(t, kind):
                if kind == "still":
                    return t
                cos, low, high = tab[0], tab[1], tab[2]
                r = t * cos - pltpu.roll(t, WIDE - quarter, 1) * low - pltpu.roll(t, quarter, 1) * high
                return r if kind == "turn" else jnp.where(low_lanes, r, t)

            def heads_block(mb, at):
                n = max(0, min(WIDE, mine - at))
                parts = []
                if n:
                    parts.append(dq_in[2 * mb, at : at + n, :].astype(f32))
                if n < WIDE:
                    lo = at + n - mine
                    parts.append(dq_in[2 * mb + 1, lo : lo + WIDE - n, :].astype(f32))
                return parts[0] if len(parts) == 1 else jnp.concatenate(parts, axis=0)

            kinds = ["turn", "mixed", "still"]
            for mb in range(mbs):
                at = slice(mb * tokens, (mb + 1) * tokens)
                for hh in range(2):
                    for b in range(KV_LANES // WIDE):
                        t = dkv_in[2 * mb + hh, :, WIDE * b : WIDE * b + WIDE].astype(f32)
                        lo = hh * KV_LANES + WIDE * b
                        gq[at, lo : lo + WIDE] = back(t, kinds[b]).astype(b16)
                for b in range(q_rows // WIDE):
                    t = heads_block(mb, WIDE * b).T
                    lo = 2 * KV_LANES + WIDE * b
                    gq[at, lo : lo + WIDE] = back(t, "turn").astype(b16)

        def gains_and_input(w_s, r_s, order_s, x_s, gx_s, ghn, low):
            moves = [
                pltpu.make_async_copy(src, dst, loads.at[i])
                for i, (src, dst) in enumerate(
                    [(w_ref, w_s), (r_ref, r_s), (order_ref, order_s), (x_ref, x_s), (gx1_ref, gx_s)]
                )
            ]
            for c in moves:
                c.start()
            wa = w_s.shape[0]
            chips = [device(z, y, x, 1 - k), device(z, y, 1 - x, k), device(z, 1 - y, x, k)]
            steps = [remote(total, got.at[i], gs.at[i], gr.at[i], chips[i]) for i in range(3)]
            ends = [
                remote(total, got.at[2 + j], gs.at[2 + j], gr.at[2 + j], device(lax.rem(z + j, zn), y, x, k))
                for j in range(1, zn)
            ]

            def first():
                for c in moves:
                    c.wait()
                ghn[:, :wa] = nt(gq[...], w_s[...])
                ghn[:, wa:] = nt(gq[...], r_s[...])

            def second():
                xf, inv, grad = x_s[...].astype(f32), inv_ref[...], ghn[...]
                total[...] = jnp.zeros(total.shape, f32)
                total[0:1, :] = jnp.sum(grad * xf * inv, axis=0, keepdims=True)
                total[1:2, :] = gain2_ref[...]
                steps[0].start()
                weighted = grad * gain_ref[0:1, :]
                inner = jnp.mean(weighted * xf, axis=-1, keepdims=True)
                low[...] = (gx_s[...] + inv * weighted - xf * (inv * inv * inv) * inner).astype(b16)

            def add(i):
                steps[i].wait()
                total[...] = total[...] + got[i]
                for c in [steps[i + 1]] if i < 2 else ends:
                    c.start()

            def third():
                input_grad[...] = jnp.dot(low[...], order_s[...], preferred_element_type=f32).astype(b16)

            jobs = [first, second, lambda: (add(0), third()), lambda: add(1), lambda: add(2)]
            kv_stage = 1
            for s in range(2 + n_back, len(order) + SUM_STAGES[-1]):
                if s == at_qkv:
                    while kv_stage < 5:
                        kvx.stage(kv_stage)
                        kv_stage += 1
                    dx.arrived()
                    rope_back()
                    gq_share.start()
                    gq_share.ready()
                stage_step(order, SUM_STAGES, s)
                if kv_stage < 4:
                    kvx.stage(kv_stage)
                    kv_stage += 1
                if s >= at_qkv and jobs:
                    jobs.pop(0)()
            for job in jobs:
                job()
            for c in ends:
                c.wait()
            t = total[...]
            for j in range(1, zn):
                t = t + got[2 + j]
            total[...] = t

        pl.run_scoped(
            gains_and_input,
            pltpu.VMEM(w_ref.shape, b16),
            pltpu.VMEM(r_ref.shape, b16),
            pltpu.VMEM(order_ref.shape, b16),
            pltpu.VMEM(x_ref.shape, b16),
            pltpu.VMEM(gx1_ref.shape, f32),
            pltpu.VMEM(gx1_ref.shape, f32),
            pltpu.VMEM(x_ref.shape, b16),
        )
        width3 = 3 * WIDE
        columns = []
        for ref, n in ((outs[3], width), (outs[1], ff), (outs[2], ff)):
            columns += [(ref, lo) for lo in range(0, n, width3)]
        per = rest_w // width3
        for i, (ref, lo) in enumerate(columns):
            q, at = i // per * rb, i % per * width3
            ref[ra:own_rows, lo : lo + width3] = rest_sum[q : q + rb, at : at + width3]
        for q in range(16 // rb):
            lo, hi = q * qkv_rest_w, min((q + 1) * qkv_rest_w, qkv_w)
            outs[4][ra:own_rows, lo:hi] = qkv_rest_sum[rb * q : rb * (q + 1), : hi - lo]
        dx.sent()
        gx.sent()
        gq_share.sent()
        for i in share:
            i.sent()

    block = (zn, mine, tokens)
    any_ = pl.BlockSpec(memory_space=pl.ANY)
    vmem = pl.BlockSpec(memory_space=pltpu.VMEM)
    dma = pltpu.SemaphoreType.DMA
    return pl.pallas_call(
        kernel,
        out_shape=[jax.ShapeDtypeStruct(s, f32) for s in outs_shape]
        + [jax.ShapeDtypeStruct((all_rows, width), b16), jax.ShapeDtypeStruct((8, width), f32)],
        in_specs=[any_, any_, any_, any_, vmem, vmem]
        + [any_] * n_in
        + [any_, any_, any_, vmem, vmem, any_, vmem, any_],
        out_specs=[vmem] * (n_out + 2),
        scratch_shapes=scratch
        + shares
        + [
            pltpu.VMEM((ring, zn, 2, 2, ra, max_cols), b16),
            pltpu.VMEM((all_rows, qkv_w), b16),
            pltpu.VMEM((all_rows, qkv_w), b16),
            pltpu.VMEM((zn, tokens, KV_LANES), b16),
            pltpu.VMEM(block, b16),
            pltpu.VMEM(block, b16),
            pltpu.VMEM((zn, 2, 2, tokens, KV_LANES), b16),
            pltpu.VMEM((2 + zn, 8, width), f32),
        ]
        + Scatter.scratch(zn, tokens, KV_LANES)[:4]
        + [
            pltpu.VMEM((16, rest_w), f32),
            pltpu.VMEM((16, qkv_rest_w), f32),
            dma((n_items, Sum.SEMS)),
            dma((n_items, Sum.SEMS)),
            dma((n_in + 1,)),
            dma((n_in + 1,)),
            dma((n_in + 1,)),
            dma((2, zn)),
            dma((2, zn)),
            dma((Scatter.SEMS,)),
            dma((Scatter.SEMS,)),
            dma((2 + zn,)),
            dma((2 + zn,)),
            dma((5,)),
        ],
        compiler_params=pltpu.CompilerParams(
            collective_id=collective_id, has_side_effects=True, vmem_limit_bytes=VMEM_LIMIT
        ),
    )(do, qh, kvg, oh, lse, tables, *ins_all, *last)


def ffn(o_t, x, gy, gain, order_t, out_a, gate_a, up_a, down, rest):
    f32, b16 = jnp.float32, jnp.bfloat16
    mbs, width, tokens = o_t.shape
    rows = mbs * tokens
    ff = gate_a.shape[1]
    wa = out_a.shape[0]
    wb = width - wa
    rb = wb * 16 // rest.shape[0]
    chunk = 4 * WIDE

    def kernel(o_ref, x_ref, gy_ref, gain_ref, order_hbm, out_hbm, gate_hbm, up_hbm, down_hbm, rest_hbm,
               y_ref, gx1_ref, gb_ref, gg_ref, gu_ref, act_ref, h2_ref, h2b_ref, op_ref, opb_ref, go_ref, gain_sum,
               order_s, out_s, gate_s, up_s, down_s, rest_s, wide, x1, h2, acc, gh, sems):
        loads = [
            pltpu.make_async_copy(src, dst, sems.at[i])
            for i, (src, dst) in enumerate(
                [(order_hbm, order_s), (rest_hbm, rest_s), (out_hbm, out_s), (gate_hbm, gate_s), (up_hbm, up_s), (down_hbm, down_s)]
            )
        ]
        for c in loads:
            c.start()
        loads[0].wait()
        for mb in range(mbs):
            at = slice(mb * tokens, (mb + 1) * tokens)
            t = jnp.dot(order_s[...], o_ref[mb], preferred_element_type=f32)
            op_ref[:, at] = t[:wa].astype(b16)
            opb_ref[:, at] = t[wa:].astype(b16)
            h2[at, :] = transposed_rows(t).astype(b16)
        loads[1].wait()
        unfold_rows(rest_s, wide, rb)
        loads[2].wait()
        x1[...] = (
            x_ref[...].astype(f32)
            + jnp.dot(h2[:, :wa], out_s[...], preferred_element_type=f32)
            + jnp.dot(h2[:, wa:], wide[:, :width], preferred_element_type=f32)
        )
        u = x1[...]
        inv = lax.rsqrt(jnp.mean(u * u, axis=-1, keepdims=True) + EPSILON)
        hidden = u * inv * gain_ref[1:2, :]
        h2[...] = hidden.astype(b16)
        h2_ref[...] = transposed(hidden[:, :wa]).astype(b16)
        h2b_ref[...] = transposed(hidden[:, wa:]).astype(b16)
        acc[...] = jnp.zeros(acc.shape, f32)
        gh[...] = jnp.zeros(gh.shape, f32)
        for c in loads[3:]:
            c.wait()

        def one(i, _):
            at = pl.multiple_of(i * chunk, WIDE)
            cols = pl.ds(at, chunk)
            gcols, ucols = pl.ds(width + at, chunk), pl.ds(width + ff + at, chunk)
            ha, hb = h2[:, :wa], h2[:, wa:]
            gate = jnp.dot(ha, gate_s[:, cols], preferred_element_type=f32) + jnp.dot(
                hb, wide[:, gcols], preferred_element_type=f32
            )
            up = jnp.dot(ha, up_s[:, cols], preferred_element_type=f32) + jnp.dot(
                hb, wide[:, ucols], preferred_element_type=f32
            )
            ga = nt(gy_ref[...], down_s[cols, :])
            sig = jax.nn.sigmoid(gate)
            silu = gate * sig
            act = silu * up
            g_gate = (ga * up * sig * (1.0 + gate * (1.0 - sig))).astype(b16)
            g_up = (ga * silu).astype(b16)
            gg_ref[:, cols] = g_gate
            gu_ref[:, cols] = g_up
            act_ref[cols, :] = transposed(act).astype(b16)
            acc[...] += jnp.dot(act.astype(b16), down_s[cols, :], preferred_element_type=f32)
            gh[:, :wa] += nt(g_gate, gate_s[:, cols]) + nt(g_up, up_s[:, cols])
            gh[:, wa:] += nt(g_gate, wide[:, gcols]) + nt(g_up, wide[:, ucols])
            return 0

        lax.fori_loop(0, ff // chunk, one, 0)
        y = (x1[...] + acc[...]).astype(b16)
        y_ref[...] = jnp.dot(y, order_s[...], preferred_element_type=f32).astype(b16)
        u = x1[...]
        inv = lax.rsqrt(jnp.mean(u * u, axis=-1, keepdims=True) + EPSILON)
        grad = gh[...]
        gain_sum[...] = jnp.sum(grad * u * inv, axis=0, keepdims=True)
        weighted = grad * gain_ref[1:2, :]
        inner = jnp.mean(weighted * u, axis=-1, keepdims=True)
        gx1 = inv * weighted - u * (inv * inv * inv) * inner + gy_ref[...].astype(f32)
        gx1_ref[...] = gx1
        gb = gx1.astype(b16)
        gb_ref[...] = jnp.dot(gb, order_s[...], preferred_element_type=f32).astype(b16)
        h2[:, :wa] = nt(gb, out_s[...]).astype(b16)
        h2[:, wa:] = nt(gb, wide[:, :width]).astype(b16)
        go = jnp.dot(h2[...], order_s[...], preferred_element_type=f32)
        for mb in range(mbs):
            go_ref[mb] = transposed(go[mb * tokens : (mb + 1) * tokens]).astype(b16)

    def transposed_rows(t):
        return jnp.concatenate([t[i : i + WIDE].T for i in range(0, t.shape[0], WIDE)], axis=1)

    any_ = pl.BlockSpec(memory_space=pl.ANY)
    vmem = pl.BlockSpec(memory_space=pltpu.VMEM)
    sds = jax.ShapeDtypeStruct
    return pl.pallas_call(
        kernel,
        out_shape=[
            sds((rows, width), b16),
            sds((rows, width), f32),
            sds((rows, width), b16),
            sds((rows, ff), b16),
            sds((rows, ff), b16),
            sds((ff, rows), b16),
            sds((wa, rows), b16),
            sds((wb, rows), b16),
            sds((wa, rows), b16),
            sds((wb, rows), b16),
            sds(o_t.shape, b16),
            sds((1, width), f32),
        ],
        in_specs=[vmem] * 4 + [any_] * 6,
        out_specs=[vmem] * 12,
        scratch_shapes=[
            pltpu.VMEM(order_t.shape, b16),
            pltpu.VMEM(out_a.shape, b16),
            pltpu.VMEM(gate_a.shape, b16),
            pltpu.VMEM(up_a.shape, b16),
            pltpu.VMEM(down.shape, b16),
            pltpu.VMEM(rest.shape, b16),
            pltpu.VMEM((wb, 16 // rb * rest.shape[1]), b16),
            pltpu.VMEM((rows, width), f32),
            pltpu.VMEM((rows, width), b16),
            pltpu.VMEM((rows, width), f32),
            pltpu.VMEM((rows, width), f32),
            pltpu.SemaphoreType.DMA((6,)),
        ],
        compiler_params=pltpu.CompilerParams(vmem_limit_bytes=VMEM_LIMIT),
    )(o_t, x, gy, gain, order_t, out_a, gate_a, up_a, down, rest)


def lane_tables(positions):
    quarter = HEAD_SIZE // 2
    frequency = 10000.0 ** (-2.0 * jnp.arange(quarter, dtype=jnp.float32) / HEAD_SIZE)
    angles = positions.astype(jnp.float32)[:, None] * frequency[None, :]
    cos, sin = jnp.cos(angles), jnp.sin(angles)
    none = jnp.zeros_like(sin)
    full = lambda a, b: jnp.concatenate([a, b, a, b], axis=1)
    return jnp.stack([full(cos, cos), full(-sin, none), full(none, sin)])


def fast_device(
    inputs,
    attn_gain,
    query_weight,
    key_matrix,
    value_matrix,
    out_weight,
    ffn_gain,
    gate_weight,
    up_weight,
    down_weight,
    cotangent,
):
    f32, b16 = jnp.float32, jnp.bfloat16
    cn, wn = lax.axis_size("ctx"), lax.axis_size("ws")
    dn = cn * wn
    zn = cn // 2
    mbs, tokens, width = inputs.shape
    own = query_weight.shape[0]
    ra = own // 16 * 16
    rb = own - ra
    q_width = query_weight.shape[1]
    hid = KEY_VALUE_HEADS * HEAD_SIZE
    ff = gate_weight.shape[1]
    rows = mbs * tokens
    wa = dn * ra

    fold = 16 // rb

    def folded(t):
        return t.reshape(t.shape[0], fold, -1).transpose(1, 0, 2).reshape(16, -1)

    qkv_w = q_width + 2 * hid
    pad1 = -qkv_w % (fold * WIDE)
    rest_w = width + 2 * ff
    pad2 = -rest_w % (fold * WIDE)
    half_hid = hid // 2
    qkv = jnp.concatenate(
        [
            key_matrix[:, :half_hid],
            value_matrix[:, :half_hid],
            key_matrix[:, half_hid:],
            value_matrix[:, half_hid:],
            query_weight,
        ],
        axis=1,
    )
    gains = jnp.stack([attn_gain, ffn_gain])
    gains = jnp.pad(gains, ((0, rb - 2), (0, pad1 - own)))
    b1 = folded(jnp.concatenate([qkv[ra:], gains], axis=1))
    flat = lambda t: t.reshape(-1, t.shape[-1])
    c, w = lax.axis_index("ctx"), lax.axis_index("ws")
    tables = lane_tables(query_places(c, w, tokens, cn, wn))
    (x_low, gy_low, order_t, o_t, qh, kvg, oh, lse, qkv_a, qkv_b, hn_t, hn_bt, inv1, gains, out_a, gate_a, up_a, down_a, b2g) = gather_attend(
        inputs.reshape(rows, width),
        cotangent.reshape(rows, width),
        tables,
        qkv,
        b1,
        [out_weight, gate_weight, up_weight, down_weight],
        GATHER_CUTS,
        2,
    )
    qkv_a, out_a, gate_a, up_a, down_w = map(flat, (qkv_a, out_a, gate_a, up_a, down_a))
    out, gx1, gb_plain, g_gate, g_up, act_t, h2_t, h2_bt, o_pt, o_pbt, go_t, gain2_sum = ffn(
        o_t, x_low, gy_low, gains, order_t, out_a, gate_a, up_a, down_w, flat(b2g)
    )
    gy_plain = cotangent.reshape(rows, width)
    left = lambda t: t.reshape(zn, 2, 2, 2, -1, rows)
    d_down, d_gate, d_up, d_out, d_qkv, input_grad, gain_sums = scatter_attend(
        go_t,
        qh,
        kvg,
        oh,
        lse,
        tables,
        [left(act_t), left(h2_t), left(o_pt), left(hn_t)],
        [h2_bt, o_pbt, hn_bt],
        [gy_plain, gb_plain, g_gate, g_up],
        ((rest_w + pad2) // fold, (qkv_w + pad1) // fold),
        [qkv_a, qkv_b, x_low, inv1, gains, gx1, gain2_sum, order_t],
        3,
    )
    device_at = c * wn + w

    def own_gain(t):
        first = lax.dynamic_slice(t, (device_at * ra,), (ra,))
        return jnp.concatenate([first, lax.dynamic_slice(t, (wa + device_at * rb,), (rb,))])

    return (
        out.reshape(inputs.shape),
        input_grad.reshape(inputs.shape),
        own_gain(gain_sums[0]),
        d_qkv[:, 2 * hid :],
        jnp.concatenate([d_qkv[:, :half_hid], d_qkv[:, hid : hid + half_hid]], axis=1),
        jnp.concatenate([d_qkv[:, half_hid:hid], d_qkv[:, hid + half_hid : 2 * hid]], axis=1),
        d_out,
        own_gain(gain_sums[1]),
        d_gate,
        d_up,
        d_down,
    )


def solution(mesh):
    in_specs = (
        P(None, ("ctx", "ws"), None),
        P(("ctx", "ws")),
        P(("ctx", "ws"), None),
        P(("ctx", "ws"), None),
        P(("ctx", "ws"), None),
        P(("ctx", "ws"), None),
        P(("ctx", "ws")),
        P(("ctx", "ws"), None),
        P(("ctx", "ws"), None),
        P(("ctx", "ws"), None),
        P(None, ("ctx", "ws"), None),
    )
    out_specs = (
        P(None, ("ctx", "ws"), None),
        P(None, ("ctx", "ws"), None),
        P(("ctx", "ws")),
        P(("ctx", "ws"), None),
        P(("ctx", "ws"), None),
        P(("ctx", "ws"), None),
        P(("ctx", "ws"), None),
        P(("ctx", "ws")),
        P(("ctx", "ws"), None),
        P(("ctx", "ws"), None),
        P(("ctx", "ws"), None),
    )
    body = fast_device if fits_fast(mesh) else per_device
    return jax.shard_map(
        body, mesh=mesh, in_specs=in_specs, out_specs=out_specs, check_vma=False
    )
```

```python
import jax
import jax.numpy as jnp
from jax import lax
from jax.experimental import pallas as pl
from jax.experimental.pallas import tpu as pltpu
from jax.sharding import PartitionSpec as P
import functools

QUERY_HEADS = 18
KEY_VALUE_HEADS = 6
HEAD_SIZE = 64


EPSILON = 1e-05
MASKED_SCORE = -1e30


def shifted(block, axis, distance):
    devices = range(lax.axis_size(axis))
    route = [((i - distance) % len(devices), i) for i in devices]
    return lax.ppermute(block, axis, route)


def as_sent(x):

    def short(part):
        return part.astype(jnp.bfloat16) if part.dtype == jnp.float32 else part

    return jax.tree.map(short, x)


def matrix_multiply(left, right):
    return jnp.dot(left, right, preferred_element_type=jnp.float32)


def outer_sum(left, right):
    return jnp.einsum("ri,rj->ij", left, right, preferred_element_type=jnp.float32)


def back_product(gradient, weight):
    return jnp.einsum("rj,ij->ri", gradient, weight, preferred_element_type=jnp.float32)


def normalize(layer_rows, gain_vector):
    inverse = lax.rsqrt(jnp.mean(layer_rows * layer_rows, axis=-1, keepdims=True) + EPSILON)
    return (layer_rows * inverse * gain_vector, inverse)


def normalize_back(layer_rows, inverse, gain_vector, gradient):
    weighted = gradient * gain_vector
    inner_mean = jnp.mean(weighted * layer_rows, axis=-1, keepdims=True)
    row_grad = inverse * weighted - layer_rows * (inverse * inverse * inverse) * inner_mean
    gain_grad = jnp.sum(gradient * layer_rows * inverse, axis=0)
    return (row_grad, gain_grad)


def rotary_tables(token_positions):
    quarter = HEAD_SIZE // 2
    frequency = 10000.0 ** (-2.0 * jnp.arange(quarter, dtype=jnp.float32) / HEAD_SIZE)
    angles = token_positions.astype(jnp.float32)[:, None] * frequency[None, :]
    return (jnp.cos(angles)[:, None, :], jnp.sin(angles)[:, None, :])


def rotate(heads, cosine_table, sine_table):
    quarter = HEAD_SIZE // 2
    first_half = heads[..., :quarter]
    second_half = heads[..., quarter:]
    return jnp.concatenate(
        [
            first_half * cosine_table - second_half * sine_table,
            second_half * cosine_table + first_half * sine_table,
        ],
        axis=-1,
    )


def rotate_back(heads, cosine_table, sine_table):
    quarter = HEAD_SIZE // 2
    first_half = heads[..., :quarter]
    second_half = heads[..., quarter:]
    return jnp.concatenate(
        [
            first_half * cosine_table + second_half * sine_table,
            second_half * cosine_table - first_half * sine_table,
        ],
        axis=-1,
    )


def query_places(own_ctx, own_member, count_of_rows, ctx_count, device_count):
    rows_per_half = count_of_rows // 2
    local_index = jnp.arange(count_of_rows, dtype=jnp.int32)
    span_index = jnp.where(local_index < rows_per_half, own_ctx, 2 * ctx_count - 1 - own_ctx)
    return (
        span_index * (device_count * rows_per_half)
        + own_member * rows_per_half
        + local_index % rows_per_half
    )


def block_places(source_ctx, count_of_rows, ctx_count, device_count):
    rows_per_half = count_of_rows // 2
    member_index = jnp.arange(device_count, dtype=jnp.int32)[:, None, None]
    half_index = jnp.arange(2, dtype=jnp.int32)[None, :, None]
    inner_index = jnp.arange(rows_per_half, dtype=jnp.int32)[None, None, :]
    span_index = jnp.where(half_index == 0, source_ctx, 2 * ctx_count - 1 - source_ctx)
    return (
        span_index * (device_count * rows_per_half) + member_index * rows_per_half + inner_index
    ).reshape(-1)


def split_block(block_of_keys):
    hidden_width = KEY_VALUE_HEADS * HEAD_SIZE
    device_count, _, rows_per_half, _ = block_of_keys.shape
    rows_of_keys = block_of_keys[..., :hidden_width].reshape(
        device_count, 2, rows_per_half, KEY_VALUE_HEADS, HEAD_SIZE
    )
    rows_of_values = block_of_keys[..., hidden_width:].reshape(
        device_count, 2, rows_per_half, KEY_VALUE_HEADS, HEAD_SIZE
    )
    return (rows_of_keys, rows_of_values)


def attend(query_rows, rows_of_keys, rows_of_values, causal_visible):
    scores = jnp.einsum(
        "rgjd,kgd->grjk", query_rows, rows_of_keys, preferred_element_type=jnp.float32
    ) * HEAD_SIZE ** (-0.5)
    if causal_visible is not None:
        scores = jnp.where(causal_visible[None, :, None, :], scores, MASKED_SCORE)
    row_max = jnp.max(scores, axis=-1)
    exponentials = jnp.exp(scores - row_max[..., None])
    row_total = jnp.sum(exponentials, axis=-1)
    mixture = jnp.einsum(
        "grjk,kgd->rgjd",
        exponentials.astype(jnp.bfloat16),
        rows_of_values,
        preferred_element_type=jnp.float32,
    )
    return (jnp.transpose(row_max, (1, 0, 2)), jnp.transpose(row_total, (1, 0, 2)), mixture)


def empty_part(count_of_rows):
    queries_per_group = QUERY_HEADS // KEY_VALUE_HEADS
    return (
        jnp.full((count_of_rows, KEY_VALUE_HEADS, queries_per_group), MASKED_SCORE, jnp.float32),
        jnp.zeros((count_of_rows, KEY_VALUE_HEADS, queries_per_group), jnp.float32),
        jnp.zeros((count_of_rows, KEY_VALUE_HEADS, queries_per_group, HEAD_SIZE), jnp.float32),
    )


def combine(carried, incoming):
    carried_max, carried_total, carried_mix = carried
    incoming_max, incoming_total, incoming_mix = incoming
    new_max = jnp.maximum(carried_max, incoming_max)
    carried_scale = jnp.exp(carried_max - new_max)
    incoming_scale = jnp.exp(incoming_max - new_max)
    return (
        new_max,
        carried_total * carried_scale + incoming_total * incoming_scale,
        carried_mix * carried_scale[..., None] + incoming_mix * incoming_scale[..., None],
    )


def forward_block(carried, block_of_keys, source_ctx, own_ctx, query_rows, own_places, ctx_count):
    rows_of_keys, rows_of_values = split_block(block_of_keys)
    device_count, _, rows_per_half, _ = block_of_keys.shape

    def forward_earlier():
        return attend(
            query_rows,
            rows_of_keys[:, 0].reshape(-1, KEY_VALUE_HEADS, HEAD_SIZE),
            rows_of_values[:, 0].reshape(-1, KEY_VALUE_HEADS, HEAD_SIZE),
            None,
        )

    def forward_later():
        late_part = attend(
            query_rows[rows_per_half:],
            rows_of_keys.reshape(-1, KEY_VALUE_HEADS, HEAD_SIZE),
            rows_of_values.reshape(-1, KEY_VALUE_HEADS, HEAD_SIZE),
            None,
        )
        early_part = empty_part(rows_per_half)
        return tuple(
            (
                jnp.concatenate([early_piece, late_piece], axis=0)
                for early_piece, late_piece in zip(early_part, late_part)
            )
        )

    def forward_diagonal():
        key_places = block_places(source_ctx, 2 * rows_per_half, ctx_count, device_count)
        causal_visible = own_places[:, None] >= key_places[None, :]
        return attend(
            query_rows,
            rows_of_keys.reshape(-1, KEY_VALUE_HEADS, HEAD_SIZE),
            rows_of_values.reshape(-1, KEY_VALUE_HEADS, HEAD_SIZE),
            causal_visible,
        )

    branch_index = jnp.where(source_ctx == own_ctx, 2, jnp.where(source_ctx > own_ctx, 1, 0))
    return combine(
        carried, lax.switch(branch_index, [forward_earlier, forward_later, forward_diagonal])
    )


def attend_back(
    query_rows, attended_grad, log_total, delta_rows, rows_of_keys, rows_of_values, causal_visible
):
    scores = jnp.einsum(
        "rgjd,kgd->grjk", query_rows, rows_of_keys, preferred_element_type=jnp.float32
    ) * HEAD_SIZE ** (-0.5)
    if causal_visible is not None:
        scores = jnp.where(causal_visible[None, :, None, :], scores, MASKED_SCORE)
    probabilities = jnp.exp(scores - jnp.transpose(log_total, (1, 0, 2))[..., None])
    prob_grad = jnp.einsum(
        "rgjd,kgd->grjk", attended_grad, rows_of_values, preferred_element_type=jnp.float32
    )
    score_grad = (
        probabilities * (prob_grad - jnp.transpose(delta_rows, (1, 0, 2))[..., None])
    ).astype(jnp.bfloat16)
    query_part = jnp.einsum(
        "grjk,kgd->rgjd", score_grad, rows_of_keys, preferred_element_type=jnp.float32
    ) * HEAD_SIZE ** (-0.5)
    key_part = jnp.einsum(
        "grjk,rgjd->kgd", score_grad, query_rows, preferred_element_type=jnp.float32
    ) * HEAD_SIZE ** (-0.5)
    value_part = jnp.einsum(
        "grjk,rgjd->kgd",
        probabilities.astype(jnp.bfloat16),
        attended_grad,
        preferred_element_type=jnp.float32,
    )
    return (query_part, key_part, value_part)


def backward_block(
    block_of_keys,
    source_ctx,
    own_ctx,
    query_rows,
    attended_grad,
    log_total,
    delta_rows,
    own_places,
    ctx_count,
):
    rows_of_keys, rows_of_values = split_block(block_of_keys)
    device_count, _, rows_per_half, _ = block_of_keys.shape
    hidden_width = KEY_VALUE_HEADS * HEAD_SIZE

    def backward_earlier():
        query_part, key_part, value_part = attend_back(
            query_rows,
            attended_grad,
            log_total,
            delta_rows,
            rows_of_keys[:, 0].reshape(-1, KEY_VALUE_HEADS, HEAD_SIZE),
            rows_of_values[:, 0].reshape(-1, KEY_VALUE_HEADS, HEAD_SIZE),
            None,
        )
        early_grad = jnp.concatenate(
            [
                key_part.reshape(device_count, 1, rows_per_half, hidden_width),
                value_part.reshape(device_count, 1, rows_per_half, hidden_width),
            ],
            axis=-1,
        )
        return (query_part, jnp.concatenate([early_grad, jnp.zeros_like(early_grad)], axis=1))

    def backward_later():
        query_part, key_part, value_part = attend_back(
            query_rows[rows_per_half:],
            attended_grad[rows_per_half:],
            log_total[rows_per_half:],
            delta_rows[rows_per_half:],
            rows_of_keys.reshape(-1, KEY_VALUE_HEADS, HEAD_SIZE),
            rows_of_values.reshape(-1, KEY_VALUE_HEADS, HEAD_SIZE),
            None,
        )
        query_part = jnp.concatenate([jnp.zeros_like(query_part), query_part], axis=0)
        return (
            query_part,
            jnp.concatenate(
                [
                    key_part.reshape(device_count, 2, rows_per_half, hidden_width),
                    value_part.reshape(device_count, 2, rows_per_half, hidden_width),
                ],
                axis=-1,
            ),
        )

    def backward_diagonal():
        key_places = block_places(source_ctx, 2 * rows_per_half, ctx_count, device_count)
        causal_visible = own_places[:, None] >= key_places[None, :]
        query_part, key_part, value_part = attend_back(
            query_rows,
            attended_grad,
            log_total,
            delta_rows,
            rows_of_keys.reshape(-1, KEY_VALUE_HEADS, HEAD_SIZE),
            rows_of_values.reshape(-1, KEY_VALUE_HEADS, HEAD_SIZE),
            causal_visible,
        )
        return (
            query_part,
            jnp.concatenate(
                [
                    key_part.reshape(device_count, 2, rows_per_half, hidden_width),
                    value_part.reshape(device_count, 2, rows_per_half, hidden_width),
                ],
                axis=-1,
            ),
        )

    branch_index = jnp.where(source_ctx == own_ctx, 2, jnp.where(source_ctx > own_ctx, 1, 0))
    return lax.switch(branch_index, [backward_earlier, backward_later, backward_diagonal])


def per_device(
    inputs,
    attn_gain,
    query_weight,
    key_matrix,
    value_matrix,
    out_weight,
    ffn_gain,
    gate_weight,
    up_weight,
    down_weight,
    cotangent,
):
    ctx_count = lax.axis_size("ctx")
    device_count = lax.axis_size("ws")
    own_ctx = lax.axis_index("ctx")
    own_member = lax.axis_index("ws")
    micro_count, count_of_rows, _ = inputs.shape
    rows_per_half = count_of_rows // 2
    queries_per_group = QUERY_HEADS // KEY_VALUE_HEADS
    hidden_width = KEY_VALUE_HEADS * HEAD_SIZE
    own_places = query_places(own_ctx, own_member, count_of_rows, ctx_count, device_count)
    cosine_table, sine_table = rotary_tables(own_places)
    grad_sums = None
    layer_outs = []
    input_grads = []
    for micro_batch in range(micro_count):
        gathered = (
            lax.all_gather(attn_gain, ("ctx", "ws"), axis=0, tiled=True),
            lax.all_gather(query_weight, ("ctx", "ws"), axis=0, tiled=True),
            lax.all_gather(key_matrix, ("ctx", "ws"), axis=0, tiled=True),
            lax.all_gather(value_matrix, ("ctx", "ws"), axis=0, tiled=True),
            lax.all_gather(out_weight, ("ctx", "ws"), axis=0, tiled=True),
            lax.all_gather(ffn_gain, ("ctx", "ws"), axis=0, tiled=True),
            lax.all_gather(gate_weight, ("ctx", "ws"), axis=0, tiled=True),
            lax.all_gather(up_weight, ("ctx", "ws"), axis=0, tiled=True),
            lax.all_gather(down_weight, ("ctx", "ws"), axis=0, tiled=True),
        )
        (
            full_attn_gain,
            full_query,
            complete_key,
            full_value,
            full_out,
            full_ffn_gain,
            full_gate,
            full_up,
            full_down,
        ) = gathered
        first_gain = full_attn_gain.astype(jnp.float32)
        second_gain = full_ffn_gain.astype(jnp.float32)
        layer_rows = inputs[micro_batch].astype(jnp.float32)
        normalized_rows, first_inverse = normalize(layer_rows, first_gain)
        normalized_reduced = normalized_rows.astype(jnp.bfloat16)
        query_rows = rotate(
            matrix_multiply(normalized_reduced, full_query).reshape(
                count_of_rows, QUERY_HEADS, HEAD_SIZE
            ),
            cosine_table,
            sine_table,
        )
        query_rows = query_rows.astype(jnp.bfloat16).reshape(
            count_of_rows, KEY_VALUE_HEADS, queries_per_group, HEAD_SIZE
        )
        rows_of_keys = rotate(
            matrix_multiply(normalized_reduced, complete_key).reshape(
                count_of_rows, KEY_VALUE_HEADS, HEAD_SIZE
            ),
            cosine_table,
            sine_table,
        ).astype(jnp.bfloat16)
        rows_of_values = matrix_multiply(normalized_reduced, full_value).astype(jnp.bfloat16)
        local_block = jnp.concatenate(
            [rows_of_keys.reshape(count_of_rows, hidden_width), rows_of_values], axis=-1
        )
        group_block = lax.all_gather(local_block, "ws", axis=0, tiled=True).reshape(
            device_count, 2, rows_per_half, 2 * hidden_width
        )

        def fold_step(carried, shard_piece):

            def visit_block(state_now, block_entry):
                block_of_keys, source_ctx = block_entry
                return (
                    forward_block(
                        state_now,
                        block_of_keys,
                        source_ctx,
                        own_ctx,
                        query_rows,
                        own_places,
                        ctx_count,
                    ),
                    None,
                )

            source_list = jnp.arange(shard_piece.shape[0], dtype=jnp.int32)
            result_state, _ = lax.scan(visit_block, carried, (shard_piece, source_list))
            return result_state

        row_max, row_total, mixture = fold_step(
            empty_part(count_of_rows), lax.all_gather(group_block[None], "ctx", axis=0, tiled=True)
        )
        attended = mixture / row_total[..., None]
        log_total = row_max + jnp.log(row_total)
        attended_low = attended.astype(jnp.bfloat16).reshape(count_of_rows, QUERY_HEADS * HEAD_SIZE)
        middle = layer_rows + matrix_multiply(attended_low, full_out)
        hidden, second_inverse = normalize(middle, second_gain)
        hidden_low = hidden.astype(jnp.bfloat16)
        gate_rows = matrix_multiply(hidden_low, full_gate)
        up_rows = matrix_multiply(hidden_low, full_up)
        sigmoid_gate = jax.nn.sigmoid(gate_rows)
        silu_gate = gate_rows * sigmoid_gate
        activated = (silu_gate * up_rows).astype(jnp.bfloat16)
        layer_outs.append((middle + matrix_multiply(activated, full_down)).astype(jnp.bfloat16))
        upstream_low = cotangent[micro_batch]
        upstream = upstream_low.astype(jnp.float32)
        down_sum = outer_sum(activated, upstream_low)
        act_grad = back_product(upstream_low, full_down)
        gate_low = (
            act_grad * up_rows * sigmoid_gate * (1.0 + gate_rows * (1.0 - sigmoid_gate))
        ).astype(jnp.bfloat16)
        up_low = (act_grad * silu_gate).astype(jnp.bfloat16)
        gate_sum = outer_sum(hidden_low, gate_low)
        up_sum = outer_sum(hidden_low, up_low)
        hidden_grad = back_product(gate_low, full_gate) + back_product(up_low, full_up)
        middle_part, ffn_gain_sum = normalize_back(middle, second_inverse, second_gain, hidden_grad)
        middle_grad = middle_part + upstream
        branch_low = middle_grad.astype(jnp.bfloat16)
        out_sum = outer_sum(attended_low, branch_low)
        attended_grad = (
            back_product(branch_low, full_out)
            .reshape(count_of_rows, KEY_VALUE_HEADS, queries_per_group, HEAD_SIZE)
            .astype(jnp.bfloat16)
        )
        delta_rows = jnp.sum(attended_grad.astype(jnp.float32) * attended, axis=-1)

        def cycle_step(turn_index, carried):
            block_of_keys, block_grad, query_total = carried
            source_ctx = (own_ctx - turn_index) % ctx_count
            query_part, block_part = backward_block(
                block_of_keys,
                source_ctx,
                own_ctx,
                query_rows,
                attended_grad,
                log_total,
                delta_rows,
                own_places,
                ctx_count,
            )
            block_grad = block_grad + block_part
            next_block = shifted(block_of_keys, "ctx", 1)
            next_grad = shifted(as_sent(block_grad), "ctx", 1).astype(block_grad.dtype)
            return (next_block, next_grad, query_total + query_part)

        cycle_start = (
            group_block,
            jnp.zeros(group_block.shape, jnp.float32),
            jnp.zeros((count_of_rows, KEY_VALUE_HEADS, queries_per_group, HEAD_SIZE), jnp.float32),
        )
        _, block_grad, query_total = lax.fori_loop(0, ctx_count, cycle_step, cycle_start)
        local_gradient = (
            lax.psum_scatter(block_grad.astype(jnp.bfloat16), "ws", scatter_dimension=0, tiled=True)
            .astype(jnp.float32)
            .reshape(count_of_rows, 2 * hidden_width)
        )
        key_low = rotate_back(
            local_gradient[:, :hidden_width].reshape(count_of_rows, KEY_VALUE_HEADS, HEAD_SIZE),
            cosine_table,
            sine_table,
        )
        key_low = key_low.astype(jnp.bfloat16).reshape(count_of_rows, hidden_width)
        value_low = local_gradient[:, hidden_width:].astype(jnp.bfloat16)
        query_low = rotate_back(
            query_total.reshape(count_of_rows, QUERY_HEADS, HEAD_SIZE), cosine_table, sine_table
        )
        query_low = query_low.astype(jnp.bfloat16).reshape(count_of_rows, QUERY_HEADS * HEAD_SIZE)
        query_sum = outer_sum(normalized_reduced, query_low)
        key_sum = outer_sum(normalized_reduced, key_low)
        value_sum = outer_sum(normalized_reduced, value_low)
        normed_grad = (
            back_product(query_low, full_query)
            + back_product(key_low, complete_key)
            + back_product(value_low, full_value)
        )
        input_part, attn_gain_sum = normalize_back(
            layer_rows, first_inverse, first_gain, normed_grad
        )
        input_grads.append((middle_grad + input_part).astype(jnp.bfloat16))
        batch_terms = (
            attn_gain_sum,
            query_sum,
            key_sum,
            value_sum,
            out_sum,
            ffn_gain_sum,
            gate_sum,
            up_sum,
            down_sum,
        )
        if grad_sums is None:
            grad_sums = batch_terms
        else:
            grad_sums = tuple(
                (
                    earlier_sum + batch_term
                    for earlier_sum, batch_term in zip(grad_sums, batch_terms)
                )
            )
    owned_grads = (
        lax.psum_scatter(grad_sums[0], ("ctx", "ws"), scatter_dimension=0, tiled=True),
        lax.psum_scatter(grad_sums[1], ("ctx", "ws"), scatter_dimension=0, tiled=True),
        lax.psum_scatter(grad_sums[2], ("ctx", "ws"), scatter_dimension=0, tiled=True),
        lax.psum_scatter(grad_sums[3], ("ctx", "ws"), scatter_dimension=0, tiled=True),
        lax.psum_scatter(grad_sums[4], ("ctx", "ws"), scatter_dimension=0, tiled=True),
        lax.psum_scatter(grad_sums[5], ("ctx", "ws"), scatter_dimension=0, tiled=True),
        lax.psum_scatter(grad_sums[6], ("ctx", "ws"), scatter_dimension=0, tiled=True),
        lax.psum_scatter(grad_sums[7], ("ctx", "ws"), scatter_dimension=0, tiled=True),
        lax.psum_scatter(grad_sums[8], ("ctx", "ws"), scatter_dimension=0, tiled=True),
    )
    return (
        jnp.stack(layer_outs),
        jnp.stack(input_grads),
        owned_grads[0],
        owned_grads[1],
        owned_grads[2],
        owned_grads[3],
        owned_grads[4],
        owned_grads[5],
        owned_grads[6],
        owned_grads[7],
        owned_grads[8],
    )


MESH = pl.DeviceIdType.MESH
NEG = -1e30
WIDE = 128
VMEM_LIMIT = 62 * 1024 * 1024


def fits_fast(mesh):
    return mesh.shape["ctx"] == 8 and mesh.shape["ws"] == 4


def place():
    c = lax.axis_index("ctx")
    w = lax.axis_index("ws")
    return c // 2, lax.rem(c, 2), w // 2, lax.rem(w, 2)


def device(z, y, x, k):
    return (z * 2 + y, x * 2 + k)


def greet(zn):
    z, y, x, k = place()
    others = [device(lax.rem(z + j, zn), y, x, k) for j in range(1, zn)]
    others += [device(z, y, 1 - x, k), device(z, 1 - y, x, k), device(z, y, x, 1 - k)]
    barrier = pltpu.get_barrier_semaphore()
    for other in others:
        pl.semaphore_signal(barrier, inc=1, device_id=other, device_id_type=MESH)
    pl.semaphore_wait(barrier, len(others))


def remote(src, dst, send, recv, where):
    return pltpu.make_async_remote_copy(
        src_ref=src, dst_ref=dst, send_sem=send, recv_sem=recv, device_id=where, device_id_type=MESH
    )


class Gather:
    SEMS = 12

    def __init__(self, src, dst, send, recv, zn):
        z, y, x, k = place()
        own = dst.at[z, y, x, k]
        hz = zn // 2
        xn, yn, sib = device(z, y, 1 - x, k), device(z, 1 - y, x, k), device(z, y, x, 1 - k)

        def push(i, ref, where):
            return remote(ref, ref, send.at[i], recv.at[i], where)

        def col(yy, xx, lo=0, n=zn):
            return dst.at[pl.ds(lo, n), yy, xx, k]

        self.local = pltpu.make_async_copy(src(z), own, send.at[0])
        self.along = []
        for j in range(1, zn):
            zz = lax.rem(z + j, zn)
            self.along.append(remote(src(zz), own, send.at[j], recv.at[j], device(zz, y, x, k)))
        self.cols = [push(4, col(y, x), xn), push(5, col(y, x), yn)]
        self.corner = [push(7, col(1 - y, x, 0, hz), xn), push(8, col(y, 1 - x, hz, hz), yn)]
        self.twin_own = push(6, col(y, x), sib)
        self.twin_cols = [push(9, col(y, 1 - x), sib), push(10, col(1 - y, x), sib)]
        self.twin_corner = push(11, col(1 - y, 1 - x), sib)

    def stage(self, n):
        if n == 0:
            self.local.start()
            for c in self.along:
                c.start()
        elif n == 1:
            self.local.wait()
            for c in self.along:
                c.wait_recv()
            for c in self.cols:
                c.start()
            self.twin_own.start()
        elif n == 2:
            for c in self.cols:
                c.wait_recv()
            for c in self.corner:
                c.start()
            for c in self.twin_cols:
                c.start()
        elif n == 3:
            for c in self.corner:
                c.wait_recv()
            self.twin_corner.start()
        elif n == 4:
            for c in [self.twin_own] + self.twin_cols + [self.twin_corner]:
                c.wait_recv()
            for c in (
                self.along
                + self.cols
                + self.corner
                + [self.twin_own]
                + self.twin_cols
                + [self.twin_corner]
            ):
                c.wait_send()


def stage_step(items, offsets, t, between=None):
    for n, offset in enumerate(offsets):
        if 0 <= t - offset < len(items):
            if items[t - offset] is not None:
                items[t - offset].stage(n)
            if between is not None:
                between()


FIRST_STAGES = (0, 1, 2, 3, 4)
GATHER_STAGES = (0, 1, 2, 3, 4)
GATHER_FROM = 3
GATHER_CUTS = [(1, 1), (1, 2), (1, 2), (2, 1), (1, 1)]
SUM_STAGES = (0, 1, 2, 3)


def portions(step, total, parts):
    done = [0]

    def call(all_=False):
        upto = total if all_ else min(total, done[0] + -(-total // parts))
        if upto > done[0]:
            lax.fori_loop(done[0], upto, step, 0)
            done[0] = upto

    return call


def pieces_of(rows, cols, nrow, ncol):
    return [
        (i * (rows // nrow), rows // nrow, j * (cols // ncol), cols // ncol)
        for i in range(nrow)
        for j in range(ncol)
    ]


def gather_item(ref, out, r0, nr, c0, nc, send, recv, zn):
    src = ref.at[pl.ds(r0, nr), pl.ds(c0, nc)]
    dst = out.at[:, :, :, :, pl.ds(r0, nr), pl.ds(c0, nc)]
    return Gather(lambda zz: src, dst, send, recv, zn)


class Exchange:
    def __init__(self, src, dst, send, recv, zn):
        z, y, x, k = place()
        self.local = pltpu.make_async_copy(src(z), dst(z), send.at[0])
        self.along = []
        for j in range(1, zn):
            zz = lax.rem(z + j, zn)
            self.along.append(remote(src(zz), dst(z), send.at[j], recv.at[j], device(zz, y, x, k)))

    def start(self):
        self.local.start()
        for c in self.along:
            c.start()

    def arrived(self):
        self.local.wait()
        for c in self.along:
            c.wait_recv()

    def sent(self):
        for c in self.along:
            c.wait_send()


class Scatter:
    SEMS = 10

    @staticmethod
    def scratch(zn, nr, nc):
        b = jnp.bfloat16
        return [
            pltpu.VMEM((zn, 2, 2, nr, nc), b),
            pltpu.VMEM((zn, 2, 2, nr, nc), b),
            pltpu.VMEM((2, zn // 2, nr, nc), b),
            pltpu.VMEM((2, zn, nr, nc), b),
            pltpu.VMEM((zn - 1, nr, nc), b),
        ]

    def __init__(self, part, out, bufs, send, recv, zn, give=None):
        z, y, x, k = self.at = place()
        self.zn = zn
        hz = zn // 2
        xn, yn, sib = device(z, y, 1 - x, k), device(z, 1 - y, x, k), device(z, y, x, 1 - k)
        self.held, self.twin, self.corners, self.colsums, self.ends = held, twin, corners, colsums, ends = bufs
        self.out = out
        self.load = None
        if give is None:
            self.load = pltpu.make_async_copy(part.at[:, :, :, k], held, send.at[0])
            give = part.at[:, :, :, 1 - k]
        self.to_twin = remote(give, twin, send.at[1], recv.at[1], sib)
        self.to_corner = [
            remote(held.at[pl.ds(0, hz), 1 - y, 1 - x], corners.at[0], send.at[2], recv.at[2], yn),
            remote(held.at[pl.ds(hz, hz), 1 - y, 1 - x], corners.at[1], send.at[3], recv.at[3], xn),
        ]
        self.to_col = [
            remote(held.at[:, y, 1 - x], colsums.at[0], send.at[4], recv.at[4], xn),
            remote(held.at[:, 1 - y, x], colsums.at[1], send.at[5], recv.at[5], yn),
        ]
        self.along = []
        for j in range(1, zn):
            zz = lax.rem(z + j, zn)
            dst = out.at[z] if ends is None else ends.at[j - 1]
            self.along.append(
                remote(held.at[zz, y, x], dst, send.at[5 + j], recv.at[5 + j], device(zz, y, x, k))
            )
        self.last = pltpu.make_async_copy(held.at[z, y, x], out.at[z], send.at[0]) if ends is None else None

    def stage(self, n):
        z, y, x, k = self.at
        zn, hz = self.zn, self.zn // 2
        held = self.held
        if n == 0:
            self.to_twin.start()
            if self.load is not None:
                self.load.start()
        elif n == 1:
            if self.load is not None:
                self.load.wait()
            self.to_twin.wait_recv()

            def add(i, _):
                for yy in range(2):
                    for xx in range(2):
                        held[i, yy, xx] = held[i, yy, xx] + self.twin[i, yy, xx]
                return 0

            lax.fori_loop(0, zn, add, 0)
            for c in self.to_corner:
                c.start()
        elif n == 2:
            for c in self.to_corner:
                c.wait_recv()
            for i in range(hz):
                held[i, y, 1 - x] = held[i, y, 1 - x] + self.corners[0, i]
                held[hz + i, 1 - y, x] = held[hz + i, 1 - y, x] + self.corners[1, i]
            for c in self.to_col:
                c.start()
        elif n == 3:
            for c in self.to_col:
                c.wait_recv()

            def add(i, _):
                f = jnp.float32
                held[i, y, x] = (
                    held[i, y, x].astype(f) + self.colsums[0, i].astype(f) + self.colsums[1, i].astype(f)
                ).astype(jnp.bfloat16)
                return 0

            lax.fori_loop(0, zn, add, 0)
            for c in self.along:
                c.start()
            if self.last is not None:
                self.last.start()
        elif n == 4:
            for c in self.along:
                c.wait_recv()
            if self.last is not None:
                self.last.wait()
            else:
                total = held[z, y, x].astype(jnp.float32)
                for j in range(zn - 1):
                    total = total + self.ends[j].astype(jnp.float32)
                self.out[...] = total
            for c in [self.to_twin] + self.to_corner + self.to_col + self.along:
                c.wait_send()


NT = (((1,), (1,)), ((), ()))


def nt(a, b):
    return lax.dot_general(a, b, NT, preferred_element_type=jnp.float32)


PER = QUERY_HEADS // KEY_VALUE_HEADS
HALF_GROUPS = KEY_VALUE_HEADS // 2
HALF_HEADS = QUERY_HEADS // 2
KV_LANES = 2 * HALF_GROUPS * HEAD_SIZE


def lane_slot(n):
    return n // 2, n % 2


def key_slot(g):
    return lane_slot(g)


def value_slot(g):
    return lane_slot(HALF_GROUPS + g)


def pair_index(half, zp):
    return zp if half == 0 else 3 - zp


def pair_tile(src, g, half, zp):
    tiles = []
    for j in range(PER):
        lo = HEAD_SIZE * (PER * g + j)
        a = src[2 * zp, lo : lo + HEAD_SIZE, :].astype(jnp.float32)
        b = src[2 * zp + 1, lo : lo + HEAD_SIZE, :].astype(jnp.float32)
        low = lax.broadcasted_iota(jnp.int32, a.shape, 1) < WIDE // 2
        if half == 0:
            tiles.append(jnp.where(low, a, pltpu.roll(b, WIDE // 2, 1)))
        else:
            tiles.append(jnp.where(low, pltpu.roll(a, WIDE // 2, 1), b))
    return jnp.concatenate(tiles, axis=1)


def unpair(get, dst):
    for zp in range(2):
        for g in range(HALF_GROUPS):
            first, second = get(g, pair_index(0, zp)), get(g, pair_index(1, zp))
            for j in range(PER):
                lo = HEAD_SIZE * (PER * g + j)
                a, b = first[:, WIDE * j : WIDE * j + WIDE], second[:, WIDE * j : WIDE * j + WIDE]
                low = lax.broadcasted_iota(jnp.int32, a.shape, 1) < WIDE // 2
                even = jnp.where(low, a, pltpu.roll(b, WIDE // 2, 1))
                odd = jnp.where(low, pltpu.roll(a, WIDE // 2, 1), b)
                dst[2 * zp, lo : lo + HEAD_SIZE, :] = even.astype(dst.dtype)
                dst[2 * zp + 1, lo : lo + HEAD_SIZE, :] = odd.astype(dst.dtype)


GROUP_LANES = 3 * WIDE


def set_padded(dst, g, p, tile, side):
    tile = tile.astype(dst.dtype)
    cols = slice(g * GROUP_LANES, (g + 1) * GROUP_LANES)
    dst[p, side * HEAD_SIZE : (side + 1) * HEAD_SIZE, cols] = tile
    dst[p, (1 - side) * HEAD_SIZE : (2 - side) * HEAD_SIZE, cols] = jnp.zeros_like(tile)


def by_block(slot):
    runs = []
    for g in range(HALF_GROUPS):
        if runs and runs[-1][0] == slot(g)[0]:
            runs[-1][2] += 1
        else:
            runs.append([slot(g)[0], g, 1])
    return runs


def group_scores(block, right, p, slot):
    out = []
    for b, g, n in by_block(slot):
        t = jnp.dot(block(b), right[p, :, g * GROUP_LANES : (g + n) * GROUP_LANES], preferred_element_type=jnp.float32)
        out += [t[:, i * GROUP_LANES : (i + 1) * GROUP_LANES] for i in range(n)]
    return out


def group_sums(tiles, right, p, slot):
    sums = {}
    for b, g, n in by_block(slot):
        left = tiles[g] if n == 1 else jnp.concatenate(tiles[g : g + n], axis=1)
        sums[b] = nt(left, right[p, :, g * GROUP_LANES : (g + n) * GROUP_LANES])
    return sums


def walk(t, y, cn):
    b1, b2, b3 = 3 + y, 10 + 2 * y, 22 + y
    p = (t >= b1).astype(jnp.int32) + (t >= b2).astype(jnp.int32) + (t >= b3).astype(jnp.int32)
    j = t - jnp.where(p == 0, 0, jnp.where(p == 1, b1, jnp.where(p == 2, b2, b3)))
    zp = jnp.where(p < 2, p, 3 - p)
    low = jnp.where(p < 2, 4 * zp + y, 2 * cn - 3 - 4 * zp - y)
    late = (j >= cn).astype(jnp.int32)
    src = jnp.where(late == 1, 2 * cn - 1 - j, j)
    return p, j, src // 2, lax.rem(src, 2), pl.multiple_of(late * HEAD_SIZE, HEAD_SIZE), j >= low


STEPS = 38
FORWARD_PARTS, FORWARD_LEFT = 20, 3


def visible(p, j, y, w, cn, wn, rows):
    shape = (wn * rows, PER * WIDE)
    lane = lax.rem(lax.broadcasted_iota(jnp.int32, shape, 1), WIDE)
    zp = jnp.where(p < 2, p, 3 - p)
    c = 2 * (2 * zp + lane // rows) + y
    span = jnp.where(p < 2, c, 2 * cn - 1 - c)
    query = span * (wn * rows) + w * rows + lax.rem(lane, rows)
    key = j * (wn * rows) + lax.broadcasted_iota(jnp.int32, shape, 0)
    return key <= query


def key_block(kvg, zz, yy, late, rows, block):
    t = kvg[zz, yy, :, :, pl.ds(late, rows), WIDE * block : WIDE * block + WIDE]
    return t.reshape(4 * rows, WIDE)


def turned(t):
    return t.astype(jnp.float32).T.astype(t.dtype)


def by_span(body, kvg, cn, rows):
    def one(j, _):
        late = (j >= cn).astype(jnp.int32)
        src = jnp.where(late == 1, 2 * cn - 1 - j, j)
        at = pl.multiple_of(late * rows, rows)
        body(j, lambda b: key_block(kvg, src // 2, lax.rem(src, 2), at, rows, b))
        return 0

    lax.fori_loop(0, 2 * cn, one, 0)


def transposed(t):
    return jnp.concatenate([t[:, i : i + WIDE].T for i in range(0, t.shape[1], WIDE)], axis=0)


def unfold_rows(src, dst, rb):
    n = src.shape[0] // 16
    fold = 16 // rb
    cols = src.shape[1]
    shape = (n * rb, n * 16)
    row = lax.broadcasted_iota(jnp.int32, shape, 0)
    at = 16 * (row // rb) + lax.rem(row, rb)
    col = lax.broadcasted_iota(jnp.int32, shape, 1)
    for q in range(fold):
        pick = jnp.where(col == at + rb * q, 1.0, 0.0).astype(jnp.bfloat16)
        t = jnp.dot(pick, src[...], preferred_element_type=jnp.float32)
        dst[:, q * cols : (q + 1) * cols] = t.astype(dst.dtype)


def gather_attend(x, gy, tables, qkv, fold1, weights, cuts, collective_id):
    cn, wn = lax.axis_size("ctx"), lax.axis_size("ws")
    zn = cn // 2
    dn = cn * wn
    tokens = tables.shape[1]
    all_rows, width = x.shape
    mbs = all_rows // tokens
    qkv_w = qkv.shape[1]
    q_rows = qkv_w - 2 * KV_LANES
    rows = tokens // 2
    mine = q_rows // 2
    f32, b16 = jnp.float32, jnp.bfloat16
    ra = qkv.shape[0] // 16 * 16
    rb = qkv.shape[0] - ra
    wa = dn * ra
    wide1 = fold1.shape[1] * (16 // rb)
    own = ra + rb
    ff = weights[1].shape[1]
    step_cols = 3 * WIDE
    rest_w = -(-(width + 2 * ff) // (4 * step_cols)) * step_cols
    shapes = [(ra, width), (ra, ff), (ra, ff), weights[3].shape, (16, rest_w)]
    n = len(shapes)
    work = [(a, piece) for a in range(n) for piece in pieces_of(*shapes[a], *cuts[a])]
    groups = range(HALF_GROUPS)
    n_first = 3

    def kernel(*refs):
        x_raw, gy_raw, tab, qkv_ref, fold_ref, out_raw, gate_raw, up_raw, down_raw = refs[:9]
        at = 9
        x_ref, gy_out, order_out = refs[at : at + 3]
        at += 3
        o_out, q_out, kv_out, oh_out, lse_out, w_out, wb_out, hn_out, hnb_out, inv_out, gains_out = refs[at : at + 11]
        at += 11
        outs = refs[at : at + n]
        at += n
        (order, out_s, down_s, rest_s, wq, f1, wide, hn, q_s, kv_s, qh, kvg, oh, qpad, vt, m_s, l_s, acc) = refs[at : at + 18]
        send, recv, xs, xr, ks, kr, save = refs[at + 18 :]
        ins = [out_s, gate_raw, up_raw, down_s, rest_s]
        greet(zn)
        z, y, x_, k = place()
        w = 2 * x_ + k

        def lanes_of(zz):
            return kv_s.at[zz // 2, :, pl.ds(pl.multiple_of(lax.rem(zz, 2) * KV_LANES, WIDE), KV_LANES)]

        def heads_of(ref, zz):
            return ref.at[zz // 2, pl.ds(pl.multiple_of(lax.rem(zz, 2) * mine, 16), mine), :]

        items = [
            gather_item(fold_ref, f1, 0, 16, 0, fold1.shape[1], send.at[0], recv.at[0], zn),
            gather_item(qkv_ref, wq, 0, ra, 0, 2 * KV_LANES, send.at[1], recv.at[1], zn),
            gather_item(qkv_ref, wq, 0, ra, 2 * KV_LANES, q_rows, send.at[2], recv.at[2], zn),
        ]
        later = [
            gather_item(ins[a], outs[a], r0, nr, c0, nc, send.at[n_first + i], recv.at[n_first + i], zn)
            for i, (a, (r0, nr, c0, nc)) in enumerate(work)
        ]
        kvx = Gather(lanes_of, kvg, ks, kr, zn)
        qx = Exchange(lambda zz: heads_of(q_s, zz), lambda zz: qh.at[zz], xs.at[0], xr.at[0], zn)
        ox = Exchange(lambda zz: oh.at[zz], lambda zz: heads_of(o_out, zz), xs.at[1], xr.at[1], zn)

        def advance(s, between=None):
            stage_step(items, FIRST_STAGES, s)
            stage_step(later, GATHER_STAGES, s - GATHER_FROM, between)

        advance(0)
        for r in range(0, width, WIDE):
            new = r + lax.broadcasted_iota(jnp.int32, (WIDE, width), 0)
            old = jnp.where(
                new < wa, own * (new // ra) + lax.rem(new, ra), own * ((new - wa) // rb) + ra + lax.rem(new - wa, rb)
            )
            col = lax.broadcasted_iota(jnp.int32, (WIDE, width), 1)
            order[r : r + WIDE, :] = jnp.where(col == old, 1.0, 0.0).astype(b16)
        advance(1)
        out_s[...] = nt(out_raw[...], order[...]).astype(b16)
        down_s[...] = nt(down_raw[...], order[...]).astype(b16)
        columns = []
        for ref, cols in ((out_s, width), (gate_raw, ff), (up_raw, ff)):
            columns += [(ref, c) for c in range(0, cols, step_cols)]
        per = rest_w // step_cols
        row = lax.broadcasted_iota(jnp.int32, (16, own), 0)
        src = lax.broadcasted_iota(jnp.int32, (16, own), 1)
        for c in range(per):
            total = jnp.zeros((16, step_cols), f32)
            for q in range(16 // rb):
                if q * per + c < len(columns):
                    ref, lo = columns[q * per + c]
                    pick = jnp.where((row // rb == q) & (src == ra + lax.rem(row, rb)), 1.0, 0.0).astype(b16)
                    total = total + jnp.dot(pick, ref[:, lo : lo + step_cols], preferred_element_type=f32)
            rest_s[:, c * step_cols : (c + 1) * step_cols] = total.astype(b16)
        advance(2)
        x_ref[...] = nt(x_raw[...], order[...]).astype(b16)
        advance(3)
        gy_out[...] = nt(gy_raw[...], order[...]).astype(b16)
        save_order = pltpu.make_async_copy(order, order_out, save.at[5])
        save_order.start()
        xf = x_ref[...].astype(f32)
        inv = lax.rsqrt(jnp.mean(xf * xf, axis=-1, keepdims=True) + EPSILON)
        inv_out[...] = inv
        m_s[...] = jnp.full(m_s.shape, NEG, f32)
        l_s[...] = jnp.zeros(l_s.shape, f32)
        acc[...] = jnp.zeros(acc.shape, f32)
        advance(n_first + 1)
        unfold_rows(f1[...].reshape(dn * 16, fold1.shape[1]), wide, rb)
        lane = lax.broadcasted_iota(jnp.int32, (WIDE, width), 1)
        local = jnp.where(lane < wa, lax.rem(lane, ra), ra + lax.rem(lane - wa, rb))
        spread = jnp.where(lax.broadcasted_iota(jnp.int32, (WIDE, width), 0) == local, 1.0, 0.0).astype(b16)
        lines = jnp.dot(wide[:, wide1 - WIDE :], spread, preferred_element_type=f32)
        lane = lax.broadcasted_iota(jnp.int32, lines.shape, 1)
        owner = jnp.where(lane < wa, lane // ra, (lane - wa) // rb)
        line = lax.broadcasted_iota(jnp.int32, lines.shape, 0)
        for i in range(2):
            gains_out[i : i + 1, :] = jnp.sum(jnp.where(line == rb * owner + i, lines, 0.0), axis=0, keepdims=True)
        normed = xf * inv * gains_out[0:1, :]
        hn[...] = normed.astype(b16)
        hn_out[...] = transposed(normed[:, :wa]).astype(b16)
        hnb_out[...] = transposed(normed[:, wa:]).astype(b16)
        advance(n_first + 2)

        low_lanes = lax.broadcasted_iota(jnp.int32, (tokens, WIDE), 1) < HEAD_SIZE
        quarter = HEAD_SIZE // 2

        def turned_heads(t, kind):
            if kind == "still":
                return t
            cos, low, high = tab[0], tab[1], tab[2]
            r = t * cos + pltpu.roll(t, WIDE - quarter, 1) * low + pltpu.roll(t, quarter, 1) * high
            return r if kind == "turn" else jnp.where(low_lanes, r, t)

        def project(c):
            cols = slice(c * KV_LANES, (c + 1) * KV_LANES)
            t = jnp.dot(hn[:, :wa], wq[:, :, :, :, :, cols].reshape(wa, KV_LANES), preferred_element_type=f32)
            t = t + jnp.dot(hn[:, wa:], wide[:, cols], preferred_element_type=f32)
            kinds = ["turn", "mixed", "still"] if c < 2 else ["turn"] * 3
            for mb in range(mbs):
                for b in range(3):
                    r = turned_heads(t[mb * tokens : (mb + 1) * tokens, WIDE * b : WIDE * b + WIDE], kinds[b])
                    at = c * KV_LANES + WIDE * b
                    if c < 2:
                        kv_s[mb, :, at : at + WIDE] = r.astype(b16)
                    else:
                        at -= 2 * KV_LANES
                        q_s[mb, at : at + WIDE, :] = (r * HEAD_SIZE**-0.5).T.astype(b16)

        project(0)
        project(1)
        kvx.stage(0)
        advance(n_first + 3)
        for c in range(2, qkv_w // KV_LANES):
            project(c)
        qx.start()
        save_order.wait()
        saves = [
            pltpu.make_async_copy(wq, w_out, save.at[3]),
            pltpu.make_async_copy(wide.at[:, pl.ds(0, qkv_w)], wb_out, save.at[4]),
        ]
        for s in saves:
            s.start()
        kvx.stage(1)
        kvx.stage(2)
        advance(n_first + 4)
        kvx.stage(3)
        qx.arrived()
        for half in range(2):
            for zp in range(2):
                for g in groups:
                    set_padded(qpad, g, pair_index(half, zp), pair_tile(qh, g, half, zp), key_slot(g)[1])
        kvx.stage(4)

        def turn(j, block):
            flat = {b: turned(block(b)) for b in sorted({value_slot(g)[0] for g in groups})}
            for g in groups:
                b, side = value_slot(g)
                vt[j, g] = flat[b][side * HEAD_SIZE : (side + 1) * HEAD_SIZE]

        by_span(turn, kvg, cn, rows)
        saves += [
            pltpu.make_async_copy(qh, q_out, save.at[0]),
            pltpu.make_async_copy(kvg, kv_out, save.at[1]),
        ]
        for s in saves[2:]:
            s.start()

        def step(t, _):
            p, j, zz, yy, late, edge = walk(t, y, cn)

            def run(masked):
                seen = visible(p, j, y, w, cn, wn, rows) if masked else None
                scores = group_scores(lambda b: key_block(kvg, zz, yy, late, rows, b), qpad, p, key_slot)
                for g in groups:
                    s = scores[g]
                    if masked:
                        s = jnp.where(seen, s, NEG)
                    m_old = m_s[g, p]
                    m_new = jnp.maximum(m_old, jnp.max(s, axis=0, keepdims=True))
                    alpha = jnp.exp(m_old - m_new)
                    e = jnp.exp(s - m_new)
                    m_s[g, p] = m_new
                    l_s[g, p] = l_s[g, p] * alpha + jnp.sum(e, axis=0, keepdims=True)
                    acc[g, p] = acc[g, p] * alpha + jnp.dot(
                        vt[j, g], e.astype(b16), preferred_element_type=f32
                    )

            pl.when(edge)(lambda: run(True))
            pl.when(jnp.logical_not(edge))(lambda: run(False))
            return 0

        last = GATHER_FROM + len(later) + GATHER_STAGES[-1]
        start = n_first + 5
        attend = portions(step, STEPS, FORWARD_PARTS)
        for s in range(start, last):
            advance(s, attend if s <= last - FORWARD_LEFT else None)
            if s == last - FORWARD_LEFT:
                attend(True)
                unpair(lambda g, p: acc[g, p] / l_s[g, p], oh)
                ox.start()
                saves.append(pltpu.make_async_copy(oh, oh_out, save.at[2]))
                saves[-1].start()
                lse_out[...] = m_s[...] + jnp.log(l_s[...])
        ox.arrived()
        ox.sent()
        qx.sent()
        for s in saves:
            s.wait()

    stat = (HALF_GROUPS, 4, 1, PER * WIDE)
    block = (zn, mine, tokens)
    kv_shape = (zn, 2, 2, 2, tokens, KV_LANES)
    any_ = pl.BlockSpec(memory_space=pl.ANY)
    vmem = pl.BlockSpec(memory_space=pltpu.VMEM)
    sds = jax.ShapeDtypeStruct
    dma = pltpu.SemaphoreType.DMA
    return pl.pallas_call(
        kernel,
        out_shape=[
            sds(x.shape, b16),
            sds(x.shape, b16),
            sds((width, width), b16),
            sds((mbs, q_rows, tokens), b16),
            sds(block, b16),
            sds(kv_shape, b16),
            sds(block, b16),
            sds(stat, f32),
            sds((zn, 2, 2, 2, ra, qkv_w), b16),
            sds((dn * rb, qkv_w), b16),
            sds((wa, all_rows), b16),
            sds((width - wa, all_rows), b16),
            sds((all_rows, 1), f32),
            sds((2, width), f32),
        ]
        + [sds((zn, 2, 2, 2, *shapes[a]), b16) for a in range(n)],
        in_specs=[vmem] * 3 + [any_] * 2 + [vmem] * 4,
        out_specs=[vmem] * 2 + [any_] + [any_] * 4 + [vmem] + [any_] * 2 + [vmem] * 4 + [any_] * n,
        scratch_shapes=[
            pltpu.VMEM((width, width), b16),
            pltpu.VMEM(weights[0].shape, b16),
            pltpu.VMEM(weights[3].shape, b16),
            pltpu.VMEM((16, rest_w), b16),
            pltpu.VMEM((zn, 2, 2, 2, ra, qkv_w), b16),
            pltpu.VMEM((zn, 2, 2, 2, 16, fold1.shape[1]), b16),
            pltpu.VMEM((dn * rb, wide1), b16),
            pltpu.VMEM((all_rows, width), b16),
            pltpu.VMEM((mbs, q_rows, tokens), b16),
            pltpu.VMEM((mbs, tokens, 2 * KV_LANES), b16),
            pltpu.VMEM(block, b16),
            pltpu.VMEM(kv_shape, b16),
            pltpu.VMEM(block, b16),
            pltpu.VMEM((4, WIDE, HALF_GROUPS * PER * WIDE), b16),
            pltpu.VMEM((2 * cn, HALF_GROUPS, HEAD_SIZE, wn * rows), b16),
            pltpu.VMEM(stat, f32),
            pltpu.VMEM(stat, f32),
            pltpu.VMEM((HALF_GROUPS, 4, HEAD_SIZE, PER * WIDE), f32),
            dma((n_first + len(work), Gather.SEMS)),
            dma((n_first + len(work), Gather.SEMS)),
            dma((2, zn)),
            dma((2, zn)),
            dma((Gather.SEMS,)),
            dma((Gather.SEMS,)),
            dma((6,)),
        ],
        compiler_params=pltpu.CompilerParams(
            collective_id=collective_id, has_side_effects=True, vmem_limit_bytes=VMEM_LIMIT
        ),
    )(x, gy, tables, qkv, fold1, *weights)


class Share:
    def __init__(self, src, own, other, local, send, recv, split):
        z, y, x, k = place()
        mine = src.at[:, :, :, k] if split else src
        theirs = src.at[:, :, :, 1 - k] if split else src
        self.load = None if mine is own else pltpu.make_async_copy(mine, own, local)
        self.swap = remote(theirs, other, send, recv, device(z, y, x, 1 - k))
        self.waited = False

    def start(self):
        if self.load is not None:
            self.load.start()
        self.swap.start()

    def ready(self):
        if not self.waited:
            if self.load is not None:
                self.load.wait()
            self.swap.wait_recv()
            self.waited = True

    def sent(self):
        self.swap.wait_send()


class Sum:
    SEMS = 8

    def __init__(self, make, held, bufs, out, send, recv, zn):
        z, y, x, k = self.at = place()
        self.make, self.held, self.out, self.zn = make, held, out, zn
        hz = zn // 2
        xn, yn = device(z, y, 1 - x, k), device(z, 1 - y, x, k)
        self.corners, self.colsums, self.ends = corners, colsums, ends = bufs
        self.to_corner = [
            remote(held.at[pl.ds(0, hz), 1 - y, 1 - x], corners.at[0], send.at[0], recv.at[0], yn),
            remote(held.at[pl.ds(hz, hz), 1 - y, 1 - x], corners.at[1], send.at[1], recv.at[1], xn),
        ]
        self.to_col = [
            remote(held.at[:, y, 1 - x], colsums.at[0], send.at[2], recv.at[2], xn),
            remote(held.at[:, 1 - y, x], colsums.at[1], send.at[3], recv.at[3], yn),
        ]
        self.along = []
        for j in range(1, zn):
            zz = lax.rem(z + j, zn)
            self.along.append(
                remote(held.at[zz, y, x], ends.at[j - 1], send.at[3 + j], recv.at[3 + j], device(zz, y, x, k))
            )

    @staticmethod
    def scratch(zn, nr, nc):
        b = jnp.bfloat16
        return [
            pltpu.VMEM((2, zn // 2, nr, nc), b),
            pltpu.VMEM((2, zn, nr, nc), b),
            pltpu.VMEM((zn - 1, nr, nc), b),
        ]

    def stage(self, n):
        z, y, x, k = self.at
        zn, hz, held = self.zn, self.zn // 2, self.held
        f32, b16 = jnp.float32, jnp.bfloat16
        if n == 0:
            self.make(held)
            for c in self.to_corner:
                c.start()
        elif n == 1:
            for c in self.to_corner:
                c.wait_recv()
            for i in range(hz):
                held[i, y, 1 - x] = held[i, y, 1 - x] + self.corners[0, i]
                held[hz + i, 1 - y, x] = held[hz + i, 1 - y, x] + self.corners[1, i]
            for c in self.to_col:
                c.start()
        elif n == 2:
            for c in self.to_col:
                c.wait_recv()
            for i in range(zn):
                held[i, y, x] = (
                    held[i, y, x].astype(f32)
                    + self.colsums[0, i].astype(f32)
                    + self.colsums[1, i].astype(f32)
                ).astype(b16)
            for c in self.along:
                c.start()
        elif n == 3:
            for c in self.along:
                c.wait_recv()
            total = held[z, y, x].astype(f32)
            for j in range(zn - 1):
                total = total + self.ends[j].astype(f32)
            self.out[...] = total
            for c in self.to_corner + self.to_col + self.along:
                c.wait_send()


FFN_CUTS = 2
ORDER = (0, 1, 2, 3, 4, 5, 6, 7, 8, 9, 10, 11)
BACK_SPAN, BACK_PARTS = 3, 10


def scatter_attend(do, qh, kvg, oh, lse, tables, lefts, rests, rights, plan, last, collective_id):
    cn, wn = lax.axis_size("ctx"), lax.axis_size("ws")
    zn = cn // 2
    mbs, q_rows, tokens = do.shape
    rows = tokens // 2
    mine = q_rows // 2
    all_rows = mbs * tokens
    f32, b16 = jnp.float32, jnp.bfloat16
    groups = range(HALF_GROUPS)
    scale = HEAD_SIZE**-0.5
    ff = rights[2].shape[1]
    width = rights[0].shape[1]
    qkv_w = q_rows + 2 * KV_LANES
    act_rows = lefts[0].shape[4]
    ra = lefts[1].shape[4]
    rest_w, qkv_rest_w = plan
    n_down = act_rows // ra
    sizes = (
        [(ra, width)] * n_down
        + [(ra, ff // FFN_CUTS)] * (2 * FFN_CUTS)
        + [(ra, width), (16, rest_w), (ra, 2 * KV_LANES), (ra, q_rows), (16, qkv_rest_w)]
    )
    max_cols = max(s[1] for s in sizes)
    ring = SUM_STAGES[-1] + 1
    scratch = []
    for nr, nc in sizes:
        scratch += Sum.scratch(zn, nr, nc)
    n_items = len(sizes)
    ins_all = [*lefts, *rests, *rights]
    n_in = len(ins_all)
    split = [True] * len(lefts) + [False] * (n_in - len(lefts))
    half = lambda a, s: (a.shape[:3] + a.shape[4:]) if s else a.shape
    shares = []
    for a, s in zip(ins_all, split):
        shares += [pltpu.VMEM(half(a, s), b16), pltpu.VMEM(half(a, s), b16)]
    rb = rests[0].shape[0] // (cn * wn)
    own_rows = ra + rb
    outs_shape = [(act_rows, width), (own_rows, ff), (own_rows, ff), (own_rows, width), (own_rows, qkv_w)]
    n_out = len(outs_shape)
    n_last = len(last)

    def kernel(*refs):
        do_ref, qh_ref, kvg_ref, oh_ref, lse_ref, tab = refs[:6]
        ins = refs[6 : 6 + n_in]
        at = 6 + n_in
        w_ref, r_ref, x_ref, inv_ref, gain_ref, gx1_ref, gain2_ref, order_ref = refs[at : at + n_last]
        at += n_last
        outs = refs[at : at + n_out]
        input_grad, total = refs[at + n_out : at + n_out + 2]
        rest = refs[at + n_out + 2 :]
        bufs, rest = rest[: len(scratch)], rest[len(scratch) :]
        pairs, rest = rest[: len(shares)], rest[len(shares) :]
        (held, gq, gq_other, dkv_in, oh, gh, give, got) = rest[:8]
        kb = rest[8:12]
        rest_sum, qkv_rest_sum = rest[12:14]
        send, recv, ps, pr, pl_, xs, xr, ks, kr, gs, gr, loads = rest[14:]
        dqh, dq_in = gh, oh
        greet(zn)
        z, y, x, k = place()
        w = 2 * x + k

        def heads_of(ref, zz):
            return ref.at[zz // 2, pl.ds(pl.multiple_of(lax.rem(zz, 2) * mine, 16), mine), :]

        gx = Exchange(lambda zz: heads_of(do_ref, zz), lambda zz: gh.at[zz], xs.at[0], xr.at[0], zn)
        dx = Exchange(lambda zz: dqh.at[zz], lambda zz: dq_in.at[zz], xs.at[1], xr.at[1], zn)
        kvx = Scatter(None, dkv_in, tuple(kb) + (None,), ks, kr, zn, give)
        share = [
            Share(ins[i], pairs[2 * i], pairs[2 * i + 1], pl_.at[i], ps.at[i], pr.at[i], split[i])
            for i in range(n_in)
        ]
        gq_share = Share(gq, gq, gq_other, None, ps.at[n_in], pr.at[n_in], False)
        own = lambda i: pairs[2 * i]
        other = lambda i: pairs[2 * i + 1]
        ACT, H2, OT, HN, H2B, OTB, HNB, GY, GB, GG, GU = range(n_in)

        def product(left, right, lo, row0, needs):
            def make(dst):
                for i in needs:
                    share[i].ready()
                nr, nc = dst.shape[3:]
                lefts2 = [
                    r[:, :, :, row0 : row0 + nr, :].reshape(zn * 4 * nr, all_rows)
                    for r in (own(left), other(left))
                ]
                step = 3 * WIDE

                def cols(i, _):
                    at = pl.multiple_of(i * step, WIDE)
                    t = jnp.dot(lefts2[0], right[0][:, pl.ds(lo + at, step)], preferred_element_type=f32)
                    t = t + jnp.dot(lefts2[1], right[1][:, pl.ds(lo + at, step)], preferred_element_type=f32)
                    dst[:, :, :, :, pl.ds(at, step)] = t.astype(b16).reshape(zn, 2, 2, nr, step)
                    return 0

                lax.fori_loop(0, nc // step, cols, 0)

            return make

        def both(i):
            return (own(i), other(i))

        def fold4(quarters):
            row = lax.rem(lax.broadcasted_iota(jnp.int32, quarters[0].shape, 0), 8)
            here = k == 0

            def put(a, b):
                n = a.shape[0]
                low = jnp.where(here, a, pltpu.roll(a, n - 4, 0))
                high = jnp.where(here, pltpu.roll(b, 4, 0), b)
                t = jnp.where(row < 4, low, high)
                return t.reshape(zn * 4, 8, t.shape[1])

            t = jnp.concatenate([put(*quarters[:2]), put(*quarters[2:])], axis=1)
            return t.astype(b16).reshape(zn, 2, 2, 16, t.shape[2])

        def rest_product(dst):
            step = 3 * WIDE
            for i in (H2B, OTB, GB, GG, GU):
                share[i].ready()
            columns = []
            for left, right, n in ((OTB, GB, width), (H2B, GG, ff), (H2B, GU, ff)):
                columns += [(left, right, c) for c in range(0, n, step)]
            per = rest_w // step

            def one(entry):
                if entry is None:
                    return jnp.zeros((own(H2B).shape[0], step), f32)
                left, right, c = entry
                return jnp.dot(own(left)[...], own(right)[:, c : c + step], preferred_element_type=f32) + jnp.dot(
                    other(left)[...], other(right)[:, c : c + step], preferred_element_type=f32
                )

            for c in range(per):
                quarters = []
                for q in range(4):
                    at = q * per + c
                    quarters.append(one(columns[at] if at < len(columns) else None))
                dst[:, :, :, :, c * step : (c + 1) * step] = fold4(quarters)

        def qkv_rest_product(dst):
            for i in (HNB,):
                share[i].ready()
            gq_share.ready()
            quarters = []
            for q in range(4):
                lo, hi = q * qkv_rest_w, min((q + 1) * qkv_rest_w, qkv_w)
                t = jnp.dot(own(HNB)[...], gq[:, lo:hi], preferred_element_type=f32) + jnp.dot(
                    other(HNB)[...], gq_other[:, lo:hi], preferred_element_type=f32
                )
                if hi - lo < qkv_rest_w:
                    t = jnp.concatenate([t, jnp.zeros((t.shape[0], qkv_rest_w - hi + lo), f32)], axis=1)
                quarters.append(t)
            dst[...] = fold4(quarters)

        gq_both = (gq, gq_other)
        makes = [product(ACT, both(GY), 0, ra * i, (ACT, GY)) for i in range(n_down)]
        ffn_parts = [(g, i * (ff // FFN_CUTS), ff // FFN_CUTS) for g in (GG, GU) for i in range(FFN_CUTS)]
        makes += [product(H2, both(g), lo, 0, (H2, g)) for g, lo, _ in ffn_parts]
        makes += [product(OT, both(GB), 0, 0, (OT, GB)), rest_product]
        makes += [product(HN, gq_both, 0, 0, (HN,)), product(HN, gq_both, 2 * KV_LANES, 0, (HN,)), qkv_rest_product]
        targets = [outs[0].at[pl.ds(ra * i, ra), :] for i in range(n_down)]
        block_rows = pl.ds(0, ra)
        targets += [outs[1 if g == GG else 2].at[block_rows, pl.ds(lo, n)] for g, lo, n in ffn_parts]
        targets += [
            outs[3].at[block_rows, :],
            rest_sum,
            outs[4].at[block_rows, pl.ds(0, 2 * KV_LANES)],
            outs[4].at[block_rows, pl.ds(2 * KV_LANES, q_rows)],
            qkv_rest_sum,
        ]
        items = []
        for i, (nr, nc) in enumerate(sizes):
            slot = held.at[ORDER.index(i) % ring, :, :, :, pl.ds(0, nr), pl.ds(0, nc)]
            items.append(
                Sum(makes[i], slot, bufs[3 * i : 3 * i + 3], targets[i], send.at[i], recv.at[i], zn)
            )
        load_o = pltpu.make_async_copy(oh_ref, oh, pl_.at[n_in])
        load_o.start()
        gx.start()
        for i in (ACT, GY, H2, GG, GU, OT, GB, H2B, OTB, HN, HNB):
            share[i].start()
        order = [None if i is None else items[i] for i in ORDER]
        at_qkv = ORDER.index(n_items - 3)
        n_back = BACK_SPAN
        stage_step(order, SUM_STAGES, 0)

        def attention_back(kvg, qh, qt, dot_, kt, delta, dq, dkv):
            load_kv = pltpu.make_async_copy(kvg_ref, kvg, loads.at[0])
            load_q = pltpu.make_async_copy(qh_ref, qh, loads.at[1])
            load_kv.start()
            load_q.start()
            dq[...] = jnp.zeros(dq.shape, f32)

            def clear(i, _):
                dkv[i] = jnp.zeros(dkv.shape[1:], f32)
                return 0

            lax.fori_loop(0, zn, clear, 0)
            def turn(j, block):
                flat = {b: turned(block(b)) for b in sorted({key_slot(g)[0] for g in groups})}
                for g in groups:
                    b, side = key_slot(g)
                    kt[j, g] = flat[b][side * HEAD_SIZE : (side + 1) * HEAD_SIZE]

            load_kv.wait()
            by_span(turn, kvg, cn, rows)
            stage_step(order, SUM_STAGES, 1)
            gx.arrived()
            load_o.wait()
            load_q.wait()
            for half_ in range(2):
                for zp in range(2):
                    p = pair_index(half_, zp)
                    for g in groups:
                        g_tile = pair_tile(gh, g, half_, zp)
                        o_tile = pair_tile(oh, g, half_, zp)
                        delta[g, p] = jnp.sum(g_tile * o_tile, axis=0, keepdims=True)
                        set_padded(qt, g, p, pair_tile(qh, g, half_, zp), key_slot(g)[1])
                        set_padded(dot_, g, p, g_tile, value_slot(g)[1])

            def step(t, _):
                p, j, zz, yy, late, edge = walk(t, y, cn)

                def run(masked):
                    seen = visible(p, j, y, w, cn, wn, rows) if masked else None
                    blocks = [key_block(kvg, zz, yy, late, rows, b) for b in range(KV_LANES // WIDE)]
                    scores = group_scores(lambda b: blocks[b], qt, p, key_slot)
                    dps = group_scores(lambda b: blocks[b], dot_, p, value_slot)
                    es, dss = [], []
                    for g in groups:
                        s = scores[g]
                        if masked:
                            s = jnp.where(seen, s, NEG)
                        e = jnp.exp(s - lse_ref[g, p])
                        ds = (e * (dps[g] - delta[g, p])).astype(b16)
                        es.append(e.astype(b16))
                        dss.append(ds)
                        dq[g, p] += jnp.dot(kt[j, g], ds, preferred_element_type=f32)
                    sums = group_sums(es, dot_, p, value_slot)
                    for b, v in group_sums(dss, qt, p, key_slot).items():
                        sums[b] = sums[b] + v if b in sums else v
                    for b, v in sums.items():
                        dkv[zz, yy, :, :, pl.ds(late, rows), WIDE * b : WIDE * b + WIDE] += v.reshape(
                            2, 2, rows, WIDE
                        )

                pl.when(edge)(lambda: run(True))
                pl.when(jnp.logical_not(edge))(lambda: run(False))
                return 0

            attend = portions(step, STEPS, BACK_PARTS)
            for s in range(2, 2 + n_back):
                stage_step(order, SUM_STAGES, s, attend)
            attend(True)

            def pack(i, _):
                for yy in range(2):
                    for xx in range(2):
                        kb[0][i, yy, xx] = dkv[i, yy, xx, k].astype(b16)
                        give[i, yy, xx] = dkv[i, yy, xx, 1 - k].astype(b16)
                return 0

            lax.fori_loop(0, zn, pack, 0)
            kvx.stage(0)
            unpair(lambda g, p: dq[g, p] * scale, dqh)
            dx.start()

        stat = (HALF_GROUPS, 4, 1, PER * WIDE)
        tile = (4, WIDE, HALF_GROUPS * PER * WIDE)
        pl.run_scoped(
            attention_back,
            pltpu.VMEM(kvg_ref.shape, b16),
            pltpu.VMEM(qh_ref.shape, b16),
            pltpu.VMEM(tile, b16),
            pltpu.VMEM(tile, b16),
            pltpu.VMEM((2 * cn, HALF_GROUPS, HEAD_SIZE, wn * rows), b16),
            pltpu.VMEM(stat, f32),
            pltpu.VMEM((HALF_GROUPS, 4, HEAD_SIZE, PER * WIDE), f32),
            pltpu.VMEM((zn, 2, 2, 2, tokens, KV_LANES), f32),
        )

        def rope_back():
            low_lanes = lax.broadcasted_iota(jnp.int32, (tokens, WIDE), 1) < HEAD_SIZE
            quarter = HEAD_SIZE // 2

            def back(t, kind):
                if kind == "still":
                    return t
                cos, low, high = tab[0], tab[1], tab[2]
                r = t * cos - pltpu.roll(t, WIDE - quarter, 1) * low - pltpu.roll(t, quarter, 1) * high
                return r if kind == "turn" else jnp.where(low_lanes, r, t)

            def heads_block(mb, at):
                n = max(0, min(WIDE, mine - at))
                parts = []
                if n:
                    parts.append(dq_in[2 * mb, at : at + n, :].astype(f32))
                if n < WIDE:
                    lo = at + n - mine
                    parts.append(dq_in[2 * mb + 1, lo : lo + WIDE - n, :].astype(f32))
                return parts[0] if len(parts) == 1 else jnp.concatenate(parts, axis=0)

            kinds = ["turn", "mixed", "still"]
            for mb in range(mbs):
                at = slice(mb * tokens, (mb + 1) * tokens)
                for hh in range(2):
                    for b in range(KV_LANES // WIDE):
                        t = dkv_in[2 * mb + hh, :, WIDE * b : WIDE * b + WIDE].astype(f32)
                        lo = hh * KV_LANES + WIDE * b
                        gq[at, lo : lo + WIDE] = back(t, kinds[b]).astype(b16)
                for b in range(q_rows // WIDE):
                    t = heads_block(mb, WIDE * b).T
                    lo = 2 * KV_LANES + WIDE * b
                    gq[at, lo : lo + WIDE] = back(t, "turn").astype(b16)

        def gains_and_input(w_s, r_s, order_s, x_s, gx_s, ghn, low):
            moves = [
                pltpu.make_async_copy(src, dst, loads.at[i])
                for i, (src, dst) in enumerate(
                    [(w_ref, w_s), (r_ref, r_s), (order_ref, order_s), (x_ref, x_s), (gx1_ref, gx_s)]
                )
            ]
            for c in moves:
                c.start()
            wa = w_s.shape[0]
            chips = [device(z, y, x, 1 - k), device(z, y, 1 - x, k), device(z, 1 - y, x, k)]
            steps = [remote(total, got.at[i], gs.at[i], gr.at[i], chips[i]) for i in range(3)]
            ends = [
                remote(total, got.at[2 + j], gs.at[2 + j], gr.at[2 + j], device(lax.rem(z + j, zn), y, x, k))
                for j in range(1, zn)
            ]

            def first():
                for c in moves:
                    c.wait()
                ghn[:, :wa] = nt(gq[...], w_s[...])
                ghn[:, wa:] = nt(gq[...], r_s[...])

            def second():
                xf, inv, grad = x_s[...].astype(f32), inv_ref[...], ghn[...]
                total[...] = jnp.zeros(total.shape, f32)
                total[0:1, :] = jnp.sum(grad * xf * inv, axis=0, keepdims=True)
                total[1:2, :] = gain2_ref[...]
                steps[0].start()
                weighted = grad * gain_ref[0:1, :]
                inner = jnp.mean(weighted * xf, axis=-1, keepdims=True)
                low[...] = (gx_s[...] + inv * weighted - xf * (inv * inv * inv) * inner).astype(b16)

            def add(i):
                steps[i].wait()
                total[...] = total[...] + got[i]
                for c in [steps[i + 1]] if i < 2 else ends:
                    c.start()

            def third():
                input_grad[...] = jnp.dot(low[...], order_s[...], preferred_element_type=f32).astype(b16)

            jobs = [first, second, lambda: (add(0), third()), lambda: add(1), lambda: add(2)]
            kv_stage = 1
            for s in range(2 + n_back, len(order) + SUM_STAGES[-1]):
                if s == at_qkv:
                    while kv_stage < 5:
                        kvx.stage(kv_stage)
                        kv_stage += 1
                    dx.arrived()
                    rope_back()
                    gq_share.start()
                    gq_share.ready()
                stage_step(order, SUM_STAGES, s)
                if kv_stage < 4:
                    kvx.stage(kv_stage)
                    kv_stage += 1
                if s >= at_qkv and jobs:
                    jobs.pop(0)()
            for job in jobs:
                job()
            for c in ends:
                c.wait()
            t = total[...]
            for j in range(1, zn):
                t = t + got[2 + j]
            total[...] = t

        pl.run_scoped(
            gains_and_input,
            pltpu.VMEM(w_ref.shape, b16),
            pltpu.VMEM(r_ref.shape, b16),
            pltpu.VMEM(order_ref.shape, b16),
            pltpu.VMEM(x_ref.shape, b16),
            pltpu.VMEM(gx1_ref.shape, f32),
            pltpu.VMEM(gx1_ref.shape, f32),
            pltpu.VMEM(x_ref.shape, b16),
        )
        width3 = 3 * WIDE
        columns = []
        for ref, n in ((outs[3], width), (outs[1], ff), (outs[2], ff)):
            columns += [(ref, lo) for lo in range(0, n, width3)]
        per = rest_w // width3
        for i, (ref, lo) in enumerate(columns):
            q, at = i // per * rb, i % per * width3
            ref[ra:own_rows, lo : lo + width3] = rest_sum[q : q + rb, at : at + width3]
        for q in range(16 // rb):
            lo, hi = q * qkv_rest_w, min((q + 1) * qkv_rest_w, qkv_w)
            outs[4][ra:own_rows, lo:hi] = qkv_rest_sum[rb * q : rb * (q + 1), : hi - lo]
        dx.sent()
        gx.sent()
        gq_share.sent()
        for i in share:
            i.sent()

    block = (zn, mine, tokens)
    any_ = pl.BlockSpec(memory_space=pl.ANY)
    vmem = pl.BlockSpec(memory_space=pltpu.VMEM)
    dma = pltpu.SemaphoreType.DMA
    return pl.pallas_call(
        kernel,
        out_shape=[jax.ShapeDtypeStruct(s, f32) for s in outs_shape]
        + [jax.ShapeDtypeStruct((all_rows, width), b16), jax.ShapeDtypeStruct((8, width), f32)],
        in_specs=[any_, any_, any_, any_, vmem, vmem]
        + [any_] * n_in
        + [any_, any_, any_, vmem, vmem, any_, vmem, any_],
        out_specs=[vmem] * (n_out + 2),
        scratch_shapes=scratch
        + shares
        + [
            pltpu.VMEM((ring, zn, 2, 2, ra, max_cols), b16),
            pltpu.VMEM((all_rows, qkv_w), b16),
            pltpu.VMEM((all_rows, qkv_w), b16),
            pltpu.VMEM((zn, tokens, KV_LANES), b16),
            pltpu.VMEM(block, b16),
            pltpu.VMEM(block, b16),
            pltpu.VMEM((zn, 2, 2, tokens, KV_LANES), b16),
            pltpu.VMEM((2 + zn, 8, width), f32),
        ]
        + Scatter.scratch(zn, tokens, KV_LANES)[:4]
        + [
            pltpu.VMEM((16, rest_w), f32),
            pltpu.VMEM((16, qkv_rest_w), f32),
            dma((n_items, Sum.SEMS)),
            dma((n_items, Sum.SEMS)),
            dma((n_in + 1,)),
            dma((n_in + 1,)),
            dma((n_in + 1,)),
            dma((2, zn)),
            dma((2, zn)),
            dma((Scatter.SEMS,)),
            dma((Scatter.SEMS,)),
            dma((2 + zn,)),
            dma((2 + zn,)),
            dma((5,)),
        ],
        compiler_params=pltpu.CompilerParams(
            collective_id=collective_id, has_side_effects=True, vmem_limit_bytes=VMEM_LIMIT
        ),
    )(do, qh, kvg, oh, lse, tables, *ins_all, *last)


def ffn(o_t, x, gy, gain, order_t, out_a, gate_a, up_a, down, rest):
    f32, b16 = jnp.float32, jnp.bfloat16
    mbs, width, tokens = o_t.shape
    rows = mbs * tokens
    ff = gate_a.shape[1]
    wa = out_a.shape[0]
    wb = width - wa
    rb = wb * 16 // rest.shape[0]
    chunk = 4 * WIDE

    def kernel(o_ref, x_ref, gy_ref, gain_ref, order_hbm, out_hbm, gate_hbm, up_hbm, down_hbm, rest_hbm,
               y_ref, gx1_ref, gb_ref, gg_ref, gu_ref, act_ref, h2_ref, h2b_ref, op_ref, opb_ref, go_ref, gain_sum,
               order_s, out_s, gate_s, up_s, down_s, rest_s, wide, x1, h2, acc, gh, sems):
        loads = [
            pltpu.make_async_copy(src, dst, sems.at[i])
            for i, (src, dst) in enumerate(
                [(order_hbm, order_s), (rest_hbm, rest_s), (out_hbm, out_s), (gate_hbm, gate_s), (up_hbm, up_s), (down_hbm, down_s)]
            )
        ]
        for c in loads[:3]:
            c.start()
        loads[0].wait()
        for c in loads[3:]:
            c.start()
        for mb in range(mbs):
            at = slice(mb * tokens, (mb + 1) * tokens)
            t = jnp.dot(order_s[...], o_ref[mb], preferred_element_type=f32)
            op_ref[:, at] = t[:wa].astype(b16)
            opb_ref[:, at] = t[wa:].astype(b16)
            h2[at, :] = transposed_rows(t).astype(b16)
        loads[1].wait()
        unfold_rows(rest_s, wide, rb)
        loads[2].wait()
        x1[...] = (
            x_ref[...].astype(f32)
            + jnp.dot(h2[:, :wa], out_s[...], preferred_element_type=f32)
            + jnp.dot(h2[:, wa:], wide[:, :width], preferred_element_type=f32)
        )
        u = x1[...]
        inv = lax.rsqrt(jnp.mean(u * u, axis=-1, keepdims=True) + EPSILON)
        hidden = u * inv * gain_ref[1:2, :]
        h2[...] = hidden.astype(b16)
        h2_ref[...] = transposed(hidden[:, :wa]).astype(b16)
        h2b_ref[...] = transposed(hidden[:, wa:]).astype(b16)
        acc[...] = jnp.zeros(acc.shape, f32)
        gh[...] = jnp.zeros(gh.shape, f32)
        for c in loads[3:]:
            c.wait()

        def one(i, _):
            at = pl.multiple_of(i * chunk, WIDE)
            cols = pl.ds(at, chunk)
            gcols, ucols = pl.ds(width + at, chunk), pl.ds(width + ff + at, chunk)
            ha, hb = h2[:, :wa], h2[:, wa:]
            gate = jnp.dot(ha, gate_s[:, cols], preferred_element_type=f32) + jnp.dot(
                hb, wide[:, gcols], preferred_element_type=f32
            )
            up = jnp.dot(ha, up_s[:, cols], preferred_element_type=f32) + jnp.dot(
                hb, wide[:, ucols], preferred_element_type=f32
            )
            ga = nt(gy_ref[...], down_s[cols, :])
            sig = jax.nn.sigmoid(gate)
            silu = gate * sig
            act = silu * up
            g_gate = (ga * up * sig * (1.0 + gate * (1.0 - sig))).astype(b16)
            g_up = (ga * silu).astype(b16)
            gg_ref[:, cols] = g_gate
            gu_ref[:, cols] = g_up
            act_ref[cols, :] = transposed(act).astype(b16)
            acc[...] += jnp.dot(act.astype(b16), down_s[cols, :], preferred_element_type=f32)
            gh[:, :wa] += nt(g_gate, gate_s[:, cols]) + nt(g_up, up_s[:, cols])
            gh[:, wa:] += nt(g_gate, wide[:, gcols]) + nt(g_up, wide[:, ucols])
            return 0

        lax.fori_loop(0, ff // chunk, one, 0)
        y = (x1[...] + acc[...]).astype(b16)
        y_ref[...] = jnp.dot(y, order_s[...], preferred_element_type=f32).astype(b16)
        u = x1[...]
        inv = lax.rsqrt(jnp.mean(u * u, axis=-1, keepdims=True) + EPSILON)
        grad = gh[...]
        gain_sum[...] = jnp.sum(grad * u * inv, axis=0, keepdims=True)
        weighted = grad * gain_ref[1:2, :]
        inner = jnp.mean(weighted * u, axis=-1, keepdims=True)
        gx1 = inv * weighted - u * (inv * inv * inv) * inner + gy_ref[...].astype(f32)
        gx1_ref[...] = gx1
        gb = gx1.astype(b16)
        gb_ref[...] = jnp.dot(gb, order_s[...], preferred_element_type=f32).astype(b16)
        h2[:, :wa] = nt(gb, out_s[...]).astype(b16)
        h2[:, wa:] = nt(gb, wide[:, :width]).astype(b16)
        go = jnp.dot(h2[...], order_s[...], preferred_element_type=f32)
        for mb in range(mbs):
            go_ref[mb] = transposed(go[mb * tokens : (mb + 1) * tokens]).astype(b16)

    def transposed_rows(t):
        return jnp.concatenate([t[i : i + WIDE].T for i in range(0, t.shape[0], WIDE)], axis=1)

    any_ = pl.BlockSpec(memory_space=pl.ANY)
    vmem = pl.BlockSpec(memory_space=pltpu.VMEM)
    sds = jax.ShapeDtypeStruct
    return pl.pallas_call(
        kernel,
        out_shape=[
            sds((rows, width), b16),
            sds((rows, width), f32),
            sds((rows, width), b16),
            sds((rows, ff), b16),
            sds((rows, ff), b16),
            sds((ff, rows), b16),
            sds((wa, rows), b16),
            sds((wb, rows), b16),
            sds((wa, rows), b16),
            sds((wb, rows), b16),
            sds(o_t.shape, b16),
            sds((1, width), f32),
        ],
        in_specs=[vmem] * 4 + [any_] * 6,
        out_specs=[vmem] * 12,
        scratch_shapes=[
            pltpu.VMEM(order_t.shape, b16),
            pltpu.VMEM(out_a.shape, b16),
            pltpu.VMEM(gate_a.shape, b16),
            pltpu.VMEM(up_a.shape, b16),
            pltpu.VMEM(down.shape, b16),
            pltpu.VMEM(rest.shape, b16),
            pltpu.VMEM((wb, 16 // rb * rest.shape[1]), b16),
            pltpu.VMEM((rows, width), f32),
            pltpu.VMEM((rows, width), b16),
            pltpu.VMEM((rows, width), f32),
            pltpu.VMEM((rows, width), f32),
            pltpu.SemaphoreType.DMA((6,)),
        ],
        compiler_params=pltpu.CompilerParams(vmem_limit_bytes=VMEM_LIMIT),
    )(o_t, x, gy, gain, order_t, out_a, gate_a, up_a, down, rest)


def lane_tables(positions):
    quarter = HEAD_SIZE // 2
    frequency = 10000.0 ** (-2.0 * jnp.arange(quarter, dtype=jnp.float32) / HEAD_SIZE)
    angles = positions.astype(jnp.float32)[:, None] * frequency[None, :]
    cos, sin = jnp.cos(angles), jnp.sin(angles)
    none = jnp.zeros_like(sin)
    full = lambda a, b: jnp.concatenate([a, b, a, b], axis=1)
    return jnp.stack([full(cos, cos), full(-sin, none), full(none, sin)])


def fast_device(
    inputs,
    attn_gain,
    query_weight,
    key_matrix,
    value_matrix,
    out_weight,
    ffn_gain,
    gate_weight,
    up_weight,
    down_weight,
    cotangent,
):
    f32, b16 = jnp.float32, jnp.bfloat16
    cn, wn = lax.axis_size("ctx"), lax.axis_size("ws")
    dn = cn * wn
    zn = cn // 2
    mbs, tokens, width = inputs.shape
    own = query_weight.shape[0]
    ra = own // 16 * 16
    rb = own - ra
    q_width = query_weight.shape[1]
    hid = KEY_VALUE_HEADS * HEAD_SIZE
    ff = gate_weight.shape[1]
    rows = mbs * tokens
    wa = dn * ra

    fold = 16 // rb

    def folded(t):
        return t.reshape(t.shape[0], fold, -1).transpose(1, 0, 2).reshape(16, -1)

    qkv_w = q_width + 2 * hid
    pad1 = -qkv_w % (fold * WIDE)
    rest_w = width + 2 * ff
    pad2 = -rest_w % (fold * WIDE)
    half_hid = hid // 2
    qkv = jnp.concatenate(
        [
            key_matrix[:, :half_hid],
            value_matrix[:, :half_hid],
            key_matrix[:, half_hid:],
            value_matrix[:, half_hid:],
            query_weight,
        ],
        axis=1,
    )
    gains = jnp.stack([attn_gain, ffn_gain])
    gains = jnp.pad(gains, ((0, rb - 2), (0, pad1 - own)))
    b1 = folded(jnp.concatenate([qkv[ra:], gains], axis=1))
    flat = lambda t: t.reshape(-1, t.shape[-1])
    c, w = lax.axis_index("ctx"), lax.axis_index("ws")
    tables = lane_tables(query_places(c, w, tokens, cn, wn))
    (x_low, gy_low, order_t, o_t, qh, kvg, oh, lse, qkv_a, qkv_b, hn_t, hn_bt, inv1, gains, out_a, gate_a, up_a, down_a, b2g) = gather_attend(
        inputs.reshape(rows, width),
        cotangent.reshape(rows, width),
        tables,
        qkv,
        b1,
        [out_weight, gate_weight, up_weight, down_weight],
        GATHER_CUTS,
        2,
    )
    qkv_a, out_a, gate_a, up_a, down_w = map(flat, (qkv_a, out_a, gate_a, up_a, down_a))
    out, gx1, gb_plain, g_gate, g_up, act_t, h2_t, h2_bt, o_pt, o_pbt, go_t, gain2_sum = ffn(
        o_t, x_low, gy_low, gains, order_t, out_a, gate_a, up_a, down_w, flat(b2g)
    )
    gy_plain = cotangent.reshape(rows, width)
    left = lambda t: t.reshape(zn, 2, 2, 2, -1, rows)
    d_down, d_gate, d_up, d_out, d_qkv, input_grad, gain_sums = scatter_attend(
        go_t,
        qh,
        kvg,
        oh,
        lse,
        tables,
        [left(act_t), left(h2_t), left(o_pt), left(hn_t)],
        [h2_bt, o_pbt, hn_bt],
        [gy_plain, gb_plain, g_gate, g_up],
        ((rest_w + pad2) // fold, (qkv_w + pad1) // fold),
        [qkv_a, qkv_b, x_low, inv1, gains, gx1, gain2_sum, order_t],
        3,
    )
    device_at = c * wn + w

    def own_gain(t):
        first = lax.dynamic_slice(t, (device_at * ra,), (ra,))
        return jnp.concatenate([first, lax.dynamic_slice(t, (wa + device_at * rb,), (rb,))])

    return (
        out.reshape(inputs.shape),
        input_grad.reshape(inputs.shape),
        own_gain(gain_sums[0]),
        d_qkv[:, 2 * hid :],
        jnp.concatenate([d_qkv[:, :half_hid], d_qkv[:, hid : hid + half_hid]], axis=1),
        jnp.concatenate([d_qkv[:, half_hid:hid], d_qkv[:, hid + half_hid : 2 * hid]], axis=1),
        d_out,
        own_gain(gain_sums[1]),
        d_gate,
        d_up,
        d_down,
    )


def solution(mesh):
    in_specs = (
        P(None, ("ctx", "ws"), None),
        P(("ctx", "ws")),
        P(("ctx", "ws"), None),
        P(("ctx", "ws"), None),
        P(("ctx", "ws"), None),
        P(("ctx", "ws"), None),
        P(("ctx", "ws")),
        P(("ctx", "ws"), None),
        P(("ctx", "ws"), None),
        P(("ctx", "ws"), None),
        P(None, ("ctx", "ws"), None),
    )
    out_specs = (
        P(None, ("ctx", "ws"), None),
        P(None, ("ctx", "ws"), None),
        P(("ctx", "ws")),
        P(("ctx", "ws"), None),
        P(("ctx", "ws"), None),
        P(("ctx", "ws"), None),
        P(("ctx", "ws"), None),
        P(("ctx", "ws")),
        P(("ctx", "ws"), None),
        P(("ctx", "ws"), None),
        P(("ctx", "ws"), None),
    )
    body = fast_device if fits_fast(mesh) else per_device
    return jax.shard_map(
        body, mesh=mesh, in_specs=in_specs, out_specs=out_specs, check_vma=False
    )
```
